32 devices in a mesh: seq: 8 (over z, y), head: 4 (over x, core).
Axes of the slice: x: 2, y: 2, z: 4, core: 2. Of those that a mesh axis runs over, the one named last changes fastest.
Arguments:
- rotated_query_rows: bfloat16 [4096, 4096], P(('seq', 'head')), may hold values from -8 to 8
- rotated_key_rows: bfloat16 [4096, 2048], P(('seq', 'head')), may hold values from -8 to 8
- value_matrix: bfloat16 [4096, 2048], P(('seq', 'head')), may hold values from -6 to 6
- output_gradient: bfloat16 [4096, 4096], P(('seq', 'head')), may hold values from -6 to 6
- doc_lengths: int32 [8], replicated, may hold values from 1 to 2048, 4096 in all
Outputs:
- attended: bfloat16 [4096, 4096], P(('seq', 'head'))
- query_grad: bfloat16 [4096, 4096], P(('seq', 'head'))
- key_gradient: bfloat16 [4096, 2048], P(('seq', 'head'))
- value_gradient: bfloat16 [4096, 2048], P(('seq', 'head'))
The draws below stay inside these ranges and needn't reach their ends.
Inputs may be any that keep to these rules, and one draw needn't show every extreme that they name: `doc_lengths`: the lengths of the 8 documents packed in order; they sum to 4096 and the longest has 2048 tokens.
All inputs are finite; a program needn't handle non-finite values.
Results may differ from the reference program's by a relative error of at most 0.02.
Values may be sent and summed in bfloat16 or wider, within the bound.
No kernel may reach another device: no remote copies, remote signals or barrier semaphores. Data moves between devices by JAX's collectives and lax.ppermute only.
A program may use at most 128 MiB of HBM per device.

```python
import math
import jax
import jax.numpy as jnp
import numpy as np
from jax import lax

QUERY_HEADS = 16
KEY_VALUE_HEADS = 8
HEAD_WIDTH = 256
WINDOW_LENGTH = 1024
MOST_DOC = 2048
STREAM_TOKENS = 4096
DOCS = 8


def draw_rotated_query_rows(key, part):
    own_key = jax.random.fold_in(key, 1)
    column_positions = QUERY_HEADS * HEAD_WIDTH
    drawn = jnp.clip(jax.random.normal(own_key, (STREAM_TOKENS, column_positions)), -6.0, 6.0)
    return drawn.astype(jnp.bfloat16)


def draw_rotated_key_rows(key, part):
    own_key = jax.random.fold_in(key, 2)
    column_positions = KEY_VALUE_HEADS * HEAD_WIDTH
    drawn = jnp.clip(jax.random.normal(own_key, (STREAM_TOKENS, column_positions)), -6.0, 6.0)
    return drawn.astype(jnp.bfloat16)


def levels(key, dims, shards, low, high):
    gain, own = 1.0, jax.random.fold_in(key, 6)
    for position, blocks in shards:
        heights = jnp.exp(jax.random.uniform(jax.random.fold_in(own, position), (blocks,), jnp.float32, low / len(shards), high / len(shards)))
        gain = gain * jnp.repeat(heights, dims[position] // blocks).reshape([-1 if axis == position else 1 for axis in range(len(dims))])
    return gain


def split_up(amount, total, reach, lean):
    portions = [(1 << 20) // math.isqrt(rank ** lean) + 1 for rank in range(2, amount + 1)]
    rest, holding = total - reach - (amount - 1), [1] * (amount - 1)
    while rest > 0:
        candidates = [i for i in range(amount - 1) if holding[i] < reach]
        pool, remaining = sum([portions[i] for i in candidates]), rest
        for i in candidates:
            extra = min(reach - holding[i], max(1, remaining * portions[i] // pool), rest)
            holding[i] = holding[i] + extra
            rest = rest - extra
    return np.array([reach] + holding)


def uneven_parts(rng, amount, total, limit, slope):
    if amount == 2:
        one = jax.random.randint(rng, (), max(1, total - limit), min(limit, total - 1) + 1)
        return jnp.stack([one, total - one])
    tallies = jnp.asarray(split_up(amount, total, limit, slope), jnp.int32)
    couples = (amount - 1) // 2
    donor, receiver = tallies[1:1 + 2 * couples:2], tallies[2:2 + 2 * couples:2]
    slack = jnp.minimum(donor - 1, limit - receiver)
    moved = jax.random.randint(jax.random.fold_in(rng, 1), (couples,), 0, 1 << 20) % (slack + 1)
    tallies = tallies.at[1:1 + 2 * couples:2].set(donor - moved).at[2:2 + 2 * couples:2].set(receiver + moved)
    return tallies[jax.random.permutation(jax.random.fold_in(rng, 2), amount)]


def bell_draw(key, shape, spread, bound, shards=(), held_as=jnp.bfloat16):
    loudness = levels(key, shape, shards, -0.22, 0.18) if shards else 1.0
    result = jax.random.normal(key, shape, jnp.float32) * spread * loudness
    return jnp.minimum(jnp.maximum(result, -bound), bound).astype(held_as)


def setup_inputs(seed: int = 0) -> dict:
    seeds = jax.random.split(jax.random.key(seed), 6)
    rotated_query_rows = draw_rotated_query_rows(jax.random.fold_in(seeds[5], 71), 0)
    rotated_key_rows = draw_rotated_key_rows(jax.random.fold_in(seeds[5], 71), 0)
    value_matrix = bell_draw(seeds[2], (STREAM_TOKENS, KEY_VALUE_HEADS * HEAD_WIDTH), 1.0, 6.0, ((0, 32),))
    output_gradient = bell_draw(seeds[3], (STREAM_TOKENS, QUERY_HEADS * HEAD_WIDTH), 1.0, 6.0, ((0, 32),))
    doc_lengths = uneven_parts(seeds[4], DOCS, STREAM_TOKENS, MOST_DOC, 2).astype(jnp.int32)
    return dict(rotated_query_rows=rotated_query_rows, rotated_key_rows=rotated_key_rows, value_matrix=value_matrix, output_gradient=output_gradient, doc_lengths=doc_lengths)


def doc_index(positions, doc_lengths):
    starts = jnp.cumsum(doc_lengths) - doc_lengths
    counted = jnp.sum((starts[None, :] <= positions[:, None]).astype(jnp.int32), axis=1)
    return (counted - 1).astype(jnp.int32)


def reference(rotated_query_rows, rotated_key_rows, value_matrix, output_gradient, doc_lengths):
    token_total = rotated_query_rows.shape[0]
    group_width = QUERY_HEADS // KEY_VALUE_HEADS
    score_scale = HEAD_WIDTH ** -0.5
    key_span = 2 * WINDOW_LENGTH
    query_head_count = rotated_query_rows.reshape(token_total, KEY_VALUE_HEADS, group_width, HEAD_WIDTH)
    gradient_heads = output_gradient.reshape(token_total, KEY_VALUE_HEADS, group_width, HEAD_WIDTH)
    leading_padding = jnp.zeros((WINDOW_LENGTH, KEY_VALUE_HEADS, HEAD_WIDTH), jnp.bfloat16)
    key_head_count = jnp.concatenate([leading_padding, rotated_key_rows.reshape(token_total, KEY_VALUE_HEADS, HEAD_WIDTH)], axis=0)
    value_head_count = jnp.concatenate([leading_padding, value_matrix.reshape(token_total, KEY_VALUE_HEADS, HEAD_WIDTH)], axis=0)
    documents = doc_index(jnp.arange(-WINDOW_LENGTH, token_total, dtype=jnp.int32), doc_lengths)
    offsets = (jnp.arange(WINDOW_LENGTH, dtype=jnp.int32) + WINDOW_LENGTH)[:, None] - jnp.arange(key_span, dtype=jnp.int32)[None, :]

    def tile_step(carried, tile_index):
        key_gradient_sums, value_gradient_sums = carried
        first_row = (tile_index * WINDOW_LENGTH).astype(jnp.int32)
        query_tile = lax.dynamic_slice_in_dim(query_head_count, first_row, WINDOW_LENGTH, 0).astype(jnp.float32)
        grad_tile = lax.dynamic_slice_in_dim(gradient_heads, first_row, WINDOW_LENGTH, 0).astype(jnp.float32)
        key_tile = lax.dynamic_slice_in_dim(key_head_count, first_row, key_span, 0).astype(jnp.float32)
        value_tile = lax.dynamic_slice_in_dim(value_head_count, first_row, key_span, 0).astype(jnp.float32)
        query_docs = lax.dynamic_slice_in_dim(documents, first_row + WINDOW_LENGTH, WINDOW_LENGTH, 0)
        key_docs = lax.dynamic_slice_in_dim(documents, first_row, key_span, 0)
        visible = (query_docs[:, None] == key_docs[None, :]) & (offsets >= 0) & (offsets < WINDOW_LENGTH)
        scores = jnp.einsum("qhgd,khd->hgqk", query_tile, key_tile) * score_scale
        scores = jnp.where(visible[None, None], scores, -jnp.inf)
        row_max = jnp.max(scores, axis=3, keepdims=True)
        weights = jnp.exp(scores - row_max)
        probs_full = weights / jnp.sum(weights, axis=3, keepdims=True)
        probs_low = lax.optimization_barrier(probs_full.astype(jnp.bfloat16)).astype(jnp.float32)
        attended = jnp.einsum("hgqk,khd->qhgd", probs_low, value_tile).astype(jnp.bfloat16)
        row_delta = jnp.sum(grad_tile * attended.astype(jnp.float32), axis=3)
        value_part = jnp.einsum("hgqk,qhgd->khd", probs_low, grad_tile)
        grad_probs = jnp.einsum("qhgd,khd->hgqk", grad_tile, value_tile)
        grad_scores = probs_full * (grad_probs - jnp.transpose(row_delta, (1, 2, 0))[..., None])
        grad_low = lax.optimization_barrier(grad_scores.astype(jnp.bfloat16)).astype(jnp.float32)
        query_grad = (jnp.einsum("hgqk,khd->qhgd", grad_low, key_tile) * score_scale).astype(jnp.bfloat16)
        key_part = jnp.einsum("hgqk,qhgd->khd", grad_low, query_tile) * score_scale
        key_gradient_sums = lax.dynamic_update_slice_in_dim(
            key_gradient_sums, lax.dynamic_slice_in_dim(key_gradient_sums, first_row, key_span, 0) + key_part, first_row, 0)
        value_gradient_sums = lax.dynamic_update_slice_in_dim(
            value_gradient_sums, lax.dynamic_slice_in_dim(value_gradient_sums, first_row, key_span, 0) + value_part, first_row, 0)
        return (key_gradient_sums, value_gradient_sums), (attended, query_grad)

    vacant_sums = jnp.zeros((token_total + WINDOW_LENGTH, KEY_VALUE_HEADS, HEAD_WIDTH), jnp.float32)
    (key_gradient_sums, value_gradient_sums), (attended, query_grad) = lax.scan(
        tile_step, (vacant_sums, vacant_sums), jnp.arange(token_total // WINDOW_LENGTH, dtype=jnp.int32))
    attended = attended.reshape(token_total, QUERY_HEADS * HEAD_WIDTH)
    query_grad = query_grad.reshape(token_total, QUERY_HEADS * HEAD_WIDTH)
    key_gradient = key_gradient_sums[WINDOW_LENGTH:].astype(jnp.bfloat16).reshape(token_total, KEY_VALUE_HEADS * HEAD_WIDTH)
    value_gradient = value_gradient_sums[WINDOW_LENGTH:].astype(jnp.bfloat16).reshape(token_total, KEY_VALUE_HEADS * HEAD_WIDTH)
    return (attended, query_grad, key_gradient, value_gradient)
```

```python
import jax
import jax.numpy as jnp
from jax import lax
from jax.experimental import pallas as pl
from jax.experimental.pallas import tpu as pltpu
from jax.sharding import Mesh
from jax.sharding import PartitionSpec as P

HEAD_WIDTH = 256
WINDOW_LENGTH = 1024

TILE = 256
LOG2_E = 1.4426950408889634


def dot(left, right, contract):
    return lax.dot_general(
        left, right, ((contract[:1], contract[1:]), ((), ())), preferred_element_type=jnp.float32
    )


def attention_kernel(
    start_ref,
    lengths_ref,
    rows_ref,
    own_ref,
    earlier_ref,
    out_ref,
    own_grad_ref,
    earlier_grad_ref,
    kv,
    kv_turned,
    scores,
    grads,
    sums,
):
    step = pl.program_id(0)
    tiles = WINDOW_LENGTH // TILE
    span = tiles + 1
    width = HEAD_WIDTH
    score_scale = HEAD_WIDTH ** (-0.5)

    @pl.when(step == 0)
    def _():
        for tile in range(2 * tiles):
            source = earlier_ref if tile < tiles else own_ref
            part = source[pl.ds(tile % tiles * TILE, TILE), :]
            kv[tile] = part
            kv_turned[tile] = part.T
        sums[...] = jnp.zeros_like(sums)

    queries = jnp.concatenate([rows_ref[:, :width], rows_ref[:, width : 2 * width]], axis=0)
    cotangents = jnp.concatenate(
        [rows_ref[:, 2 * width : 3 * width], rows_ref[:, 3 * width :]], axis=0
    )
    columns = 2 * TILE

    first_row = start_ref[0] + step * TILE
    row = lax.broadcasted_iota(jnp.int32, (1, columns), 1) % TILE
    oldest = row - (WINDOW_LENGTH - 1)

    def passed(item, carried):
        begin, oldest = carried
        near = begin - first_row
        oldest = jnp.where(near <= row, jnp.maximum(oldest, near), oldest)
        return begin + lengths_ref[item], oldest

    _, oldest = lax.fori_loop(0, lengths_ref.shape[0], passed, (jnp.int32(0), oldest))
    key_row = lax.broadcasted_iota(jnp.int32, (TILE, columns), 0)

    top = jnp.full((1, columns), -jnp.inf, jnp.float32)
    for item in range(span):
        place = (item - tiles) * TILE
        tile_scores = dot(kv[step + item, :, :width], queries, (1, 1))
        seen = key_row >= oldest - place
        if item == tiles:
            seen = seen & (key_row <= row)
        tile_scores = jnp.where(seen, tile_scores, -jnp.inf)
        top = jnp.maximum(top, jnp.max(tile_scores, axis=0, keepdims=True))
        scores[item] = tile_scores

    total = jnp.zeros((1, columns), jnp.float32)
    for item in range(span):
        weights = jnp.exp2((scores[item] - top) * (score_scale * LOG2_E))
        total = total + jnp.sum(weights, axis=0, keepdims=True)
        scores[item] = weights
    share = 1.0 / total

    attended = jnp.zeros((width, columns), jnp.float32)
    for item in range(span):
        probs = scores[item] * share
        scores[item] = probs
        probs_low = probs.astype(jnp.bfloat16)
        attended = attended + dot(kv_turned[step + item, width:, :], probs_low, (1, 0))
        sums[step + item, :, width:] += dot(probs_low, cotangents, (1, 0))
        grads[item] = dot(kv[step + item, :, width:], cotangents, (1, 1))
    attended = attended.astype(jnp.bfloat16).astype(jnp.float32)
    turned = cotangents.astype(jnp.float32).T
    row_delta = jnp.sum(attended * turned, axis=0, keepdims=True)
    attended = attended.T.astype(jnp.bfloat16)
    out_ref[:, :width] = attended[:TILE]
    out_ref[:, width : 2 * width] = attended[TILE:]

    query_grad = jnp.zeros((width, columns), jnp.float32)
    for item in range(span):
        grad_low = (scores[item] * (grads[item] - row_delta)).astype(jnp.bfloat16)
        query_grad = query_grad + dot(kv_turned[step + item, :width, :], grad_low, (1, 0))
        sums[step + item, :, :width] += dot(grad_low, queries, (1, 0))
    query_grad = (query_grad * score_scale).T.astype(jnp.bfloat16)
    out_ref[:, 2 * width : 3 * width] = query_grad[:TILE]
    out_ref[:, 3 * width :] = query_grad[TILE:]

    @pl.when(step == pl.num_programs(0) - 1)
    def _():
        for tile in range(2 * tiles):
            target = earlier_grad_ref if tile < tiles else own_grad_ref
            rows = pl.ds(tile % tiles * TILE, TILE)
            target[rows, :width] = (sums[tile, :, :width] * score_scale).astype(target.dtype)
            target[rows, width:] = sums[tile, :, width:].astype(target.dtype)


def attention(start, doc_lengths, rows, own, earlier):
    block_rows = rows.shape[0]
    tiles = WINDOW_LENGTH // TILE
    width = HEAD_WIDTH
    flat = (block_rows, 2 * width)
    products = 5 * 2 * block_rows * 2 * (WINDOW_LENGTH + TILE) * width
    return pl.pallas_call(
        attention_kernel,
        grid=(block_rows // TILE,),
        in_specs=[
            pl.BlockSpec(memory_space=pltpu.SMEM),
            pl.BlockSpec(memory_space=pltpu.SMEM),
            pl.BlockSpec((TILE, 4 * width), lambda i: (i, 0)),
            pl.BlockSpec(flat, lambda i: (0, 0)),
            pl.BlockSpec(flat, lambda i: (0, 0)),
        ],
        out_specs=[
            pl.BlockSpec((TILE, 4 * width), lambda i: (i, 0)),
            pl.BlockSpec(flat, lambda i: (0, 0)),
            pl.BlockSpec(flat, lambda i: (0, 0)),
        ],
        out_shape=[
            jax.ShapeDtypeStruct((block_rows, 4 * width), jnp.bfloat16),
            jax.ShapeDtypeStruct(flat, jnp.float32),
            jax.ShapeDtypeStruct(flat, jnp.bfloat16),
        ],
        scratch_shapes=[
            pltpu.VMEM((2 * tiles, TILE, 2 * width), jnp.bfloat16),
            pltpu.VMEM((2 * tiles, 2 * width, TILE), jnp.bfloat16),
            pltpu.VMEM((tiles + 1, TILE, 2 * TILE), jnp.float32),
            pltpu.VMEM((tiles + 1, TILE, 2 * TILE), jnp.float32),
            pltpu.VMEM((2 * tiles, TILE, 2 * width), jnp.float32),
        ],
        compiler_params=pltpu.CompilerParams(vmem_limit_bytes=48 * 1024 * 1024),
        cost_estimate=pl.CostEstimate(
            flops=2 * products, bytes_accessed=block_rows * width * 30, transcendentals=0
        ),
    )(start, doc_lengths, rows, own, earlier)


def by_head(block, members):
    rows = block.shape[0]
    return block.reshape(rows, members, block.shape[1] // members).transpose(1, 0, 2)


def by_token(blocks):
    members, rows, columns = blocks.shape
    return blocks.transpose(1, 0, 2).reshape(rows, members * columns)


def exchanged(blocks):
    return lax.all_to_all(blocks, "member", split_axis=0, concat_axis=0, tiled=True)


def shards(rotated_query_rows, rotated_key_rows, value_matrix, output_gradient, doc_lengths):
    members = lax.axis_size("member")
    stretches = lax.axis_size("stretch")
    rows = rotated_query_rows.shape[0]
    block_rows = members * rows
    width = HEAD_WIDTH
    kv = jnp.concatenate(
        [by_head(rotated_key_rows, members), by_head(value_matrix, members)], axis=2
    )
    kv = exchanged(kv).reshape(block_rows, 2 * width)
    earlier = lax.ppermute(kv, "stretch", [(i, i + 1) for i in range(stretches - 1)])
    query_rows = jnp.concatenate(
        [by_head(rotated_query_rows, members), by_head(output_gradient, members)], axis=2
    )
    query_rows = exchanged(query_rows).reshape(block_rows, 4 * width)
    start = (lax.axis_index("stretch") * block_rows).astype(jnp.int32).reshape(1)
    results, own_grad, earlier_grad = attention(start, doc_lengths, query_rows, kv, earlier)
    later = lax.ppermute(earlier_grad, "stretch", [(i + 1, i) for i in range(stretches - 1)])
    results = exchanged(results.reshape(members, rows, 4 * width))
    kv_grad = (own_grad + later.astype(jnp.float32)).astype(jnp.bfloat16)
    kv_grad = exchanged(kv_grad.reshape(members, rows, 2 * width))
    return (
        by_token(results[:, :, : 2 * width]),
        by_token(results[:, :, 2 * width :]),
        by_token(kv_grad[:, :, :width]),
        by_token(kv_grad[:, :, width:]),
    )


def solution(mesh):
    members = 8
    grouped = Mesh(mesh.devices.reshape(-1, members), ("stretch", "member"))
    spread = P(("stretch", "member"), None)
    return jax.shard_map(
        shards,
        mesh=grouped,
        in_specs=(spread, spread, spread, spread, P()),
        out_specs=(spread, spread, spread, spread),
        check_vma=False,
    )
```

```python
import jax
import jax.numpy as jnp
from jax import lax
from jax.experimental import pallas as pl
from jax.experimental.pallas import tpu as pltpu
from jax.sharding import Mesh
from jax.sharding import PartitionSpec as P

HEAD_WIDTH = 256
WINDOW_LENGTH = 1024
MEMBERS = 8

TILE = 256
TILES = WINDOW_LENGTH // TILE
SPAN = TILES + 1
ROWS = WINDOW_LENGTH // MEMBERS
CHUNKS = TILE // ROWS
LOG2_E = 1.4426950408889634

ANYWHERE = pl.BlockSpec(memory_space=pl.ANY)
SCALARS = pl.BlockSpec(memory_space=pltpu.SMEM)


def dot(left, right, contract):
    return lax.dot_general(
        left, right, ((contract[:1], contract[1:]), ((), ())), preferred_element_type=jnp.float32
    )


def run_copies(pairs, semaphores):
    copies = [
        pltpu.make_async_copy(source, target, semaphores.at[item])
        for item, (source, target) in enumerate(pairs)
    ]
    for copy in copies:
        copy.start()
    for copy in copies:
        copy.wait()


def columns_of(ref, head, width):
    return ref.at[:, pl.ds(pl.multiple_of(head * width, width), width)]


def pack_kernel(first, place_ref, left_ref, right_ref, *refs):
    pieces, semaphores = refs[:-1], refs[-1]
    width = left_ref.shape[1] // MEMBERS
    pairs = []
    for item, piece in enumerate(pieces):
        head = place_ref[0] ^ (item + first)
        pairs.append((columns_of(left_ref, head, width), piece.at[:, pl.ds(0, width)]))
        pairs.append((columns_of(right_ref, head, width), piece.at[:, pl.ds(width, width)]))
    run_copies(pairs, semaphores)


def pack(place, left, right, first):
    rows, columns = left.shape
    pieces = MEMBERS - first
    piece = jax.ShapeDtypeStruct((rows, 2 * columns // MEMBERS), left.dtype)
    return pl.pallas_call(
        lambda *refs: pack_kernel(first, *refs),
        in_specs=[SCALARS, ANYWHERE, ANYWHERE],
        out_specs=[ANYWHERE] * pieces,
        out_shape=[piece] * pieces,
        scratch_shapes=[pltpu.SemaphoreType.DMA((2 * pieces,))],
        cost_estimate=pl.CostEstimate(
            flops=0, bytes_accessed=8 * rows * columns, transcendentals=0
        ),
    )(place, left, right)


def unpack_kernel(place_ref, *refs):
    pieces, (left_ref, right_ref, semaphores) = refs[:MEMBERS], refs[MEMBERS:]
    width = left_ref.shape[1] // MEMBERS
    pairs = []
    for item, piece in enumerate(pieces):
        head = place_ref[0] ^ item
        pairs.append((piece.at[:, pl.ds(0, width)], columns_of(left_ref, head, width)))
        pairs.append((piece.at[:, pl.ds(width, width)], columns_of(right_ref, head, width)))
    run_copies(pairs, semaphores)


def unpack(place, pieces):
    rows, columns = pieces[0].shape
    whole = jax.ShapeDtypeStruct((rows, MEMBERS * columns // 2), pieces[0].dtype)
    return pl.pallas_call(
        unpack_kernel,
        in_specs=[SCALARS] + [ANYWHERE] * MEMBERS,
        out_specs=[ANYWHERE] * 2,
        out_shape=[whole] * 2,
        scratch_shapes=[pltpu.SemaphoreType.DMA((2 * MEMBERS,))],
        cost_estimate=pl.CostEstimate(
            flops=0, bytes_accessed=4 * MEMBERS * rows * columns, transcendentals=0
        ),
    )(place, *pieces)


def attention_kernel(place_ref, lengths_ref, query_ref, cotangent_ref, *refs):
    row_pieces, refs = refs[: MEMBERS - 1], refs[MEMBERS - 1 :]
    own_pieces, earlier_pieces = refs[:MEMBERS], refs[MEMBERS : 2 * MEMBERS]
    refs = refs[2 * MEMBERS :]
    result_pieces, own_grads = refs[:MEMBERS], refs[MEMBERS : 2 * MEMBERS]
    earlier_grads, refs = refs[2 * MEMBERS : 3 * MEMBERS], refs[3 * MEMBERS :]
    rows, kv, results, sums, low_sums, kv_turned, scores, grads, semaphores = refs
    width = HEAD_WIDTH
    columns = CHUNKS * 2 * ROWS
    score_scale = HEAD_WIDTH ** (-0.5)
    member = place_ref[0]
    start = place_ref[1]

    pairs = [
        (columns_of(query_ref, member, 2 * width), rows.at[member, :, pl.ds(0, 2 * width)]),
        (
            columns_of(cotangent_ref, member, 2 * width),
            rows.at[member, :, pl.ds(2 * width, 2 * width)],
        ),
    ]
    for item in range(MEMBERS):
        chunk = member ^ item
        if item:
            pairs.append((row_pieces[item - 1], rows.at[chunk]))
        pairs.append((own_pieces[item], kv.at[MEMBERS + chunk]))
        pairs.append((earlier_pieces[item], kv.at[chunk]))
    run_copies(pairs, semaphores)

    sums[...] = jnp.zeros_like(sums)
    for tile in range(2 * TILES):
        part = kv[tile * CHUNKS : (tile + 1) * CHUNKS].reshape(TILE, 2 * width)
        kv_turned[tile] = part.T

    row = lax.broadcasted_iota(jnp.int32, (1, columns), 1) % TILE
    key_row = lax.broadcasted_iota(jnp.int32, (TILE, columns), 0)

    def tile_step(step, unused):
        chunks = pl.ds(step * CHUNKS, CHUNKS)

        def both(first):
            return jnp.concatenate(
                [
                    rows[chunks, :, head * width : (head + 1) * width].reshape(TILE, width)
                    for head in (first, first + 1)
                ],
                axis=0,
            )

        def key_tile(item, first):
            tile = pl.ds((step + item) * CHUNKS, CHUNKS)
            return kv[tile, :, first : first + width].reshape(TILE, width)

        def add(item, first, part):
            tile = pl.ds((step + item) * CHUNKS, CHUNKS)
            sums[tile, :, first : first + width] += part.reshape(CHUNKS, ROWS, width)

        queries = both(0)
        cotangents = both(2)
        first_row = start + step * TILE
        oldest = row - (WINDOW_LENGTH - 1)

        def passed(item, carried):
            begin, oldest = carried
            near = begin - first_row
            oldest = jnp.where(near <= row, jnp.maximum(oldest, near), oldest)
            return begin + lengths_ref[item], oldest

        _, oldest = lax.fori_loop(0, lengths_ref.shape[0], passed, (jnp.int32(0), oldest))

        top = jnp.full((1, columns), -jnp.inf, jnp.float32)
        for item in range(SPAN):
            place = (item - TILES) * TILE
            tile_scores = dot(key_tile(item, 0), queries, (1, 1))
            seen = key_row >= oldest - place
            if item == TILES:
                seen = seen & (key_row <= row)
            tile_scores = jnp.where(seen, tile_scores, -jnp.inf)
            top = jnp.maximum(top, jnp.max(tile_scores, axis=0, keepdims=True))
            scores[item] = tile_scores

        total = jnp.zeros((1, columns), jnp.float32)
        for item in range(SPAN):
            weights = jnp.exp2((scores[item] - top) * (score_scale * LOG2_E))
            total = total + jnp.sum(weights, axis=0, keepdims=True)
            scores[item] = weights
        share = 1.0 / total

        attended = jnp.zeros((width, columns), jnp.float32)
        for item in range(SPAN):
            probs = scores[item] * share
            scores[item] = probs
            probs_low = probs.astype(jnp.bfloat16)
            attended = attended + dot(kv_turned[step + item, width:, :], probs_low, (1, 0))
            add(item, width, dot(probs_low, cotangents, (1, 0)))
            grads[item] = dot(key_tile(item, width), cotangents, (1, 1))
        attended = attended.astype(jnp.bfloat16).astype(jnp.float32)
        turned = cotangents.astype(jnp.float32).T
        row_delta = jnp.sum(attended * turned, axis=0, keepdims=True)

        def put(first, part):
            part = part.T.astype(jnp.bfloat16).reshape(2 * CHUNKS, ROWS, width)
            results[chunks, :, first : first + width] = part[:CHUNKS]
            results[chunks, :, first + width : first + 2 * width] = part[CHUNKS:]

        put(0, attended)

        query_grad = jnp.zeros((width, columns), jnp.float32)
        for item in range(SPAN):
            grad_low = (scores[item] * (grads[item] - row_delta)).astype(jnp.bfloat16)
            query_grad = query_grad + dot(kv_turned[step + item, :width, :], grad_low, (1, 0))
            add(item, 0, dot(grad_low, queries, (1, 0)))
        put(2 * width, query_grad * score_scale)
        return unused

    lax.fori_loop(0, TILES, tile_step, 0)

    sums[:, :, :width] = sums[:, :, :width] * score_scale
    low_sums[...] = sums[:MEMBERS].astype(jnp.bfloat16)
    pairs = []
    for item in range(MEMBERS):
        chunk = member ^ item
        pairs.append((low_sums.at[chunk], earlier_grads[item]))
        pairs.append((sums.at[MEMBERS + chunk], own_grads[item]))
        pairs.append((results.at[chunk], result_pieces[item]))
    run_copies(pairs, semaphores)


def attention(place, doc_lengths, queries, cotangents, row_pieces, own, earlier):
    width = HEAD_WIDTH
    products = 5 * 2 * WINDOW_LENGTH * 2 * SPAN * TILE * width
    kv_piece = (ROWS, 2 * width)
    row_piece = jax.ShapeDtypeStruct((ROWS, 4 * width), jnp.bfloat16)
    outputs = pl.pallas_call(
        attention_kernel,
        in_specs=[SCALARS, SCALARS] + [ANYWHERE] * (3 * MEMBERS + 1),
        out_specs=[ANYWHERE] * (3 * MEMBERS),
        out_shape=[row_piece] * MEMBERS
        + [jax.ShapeDtypeStruct(kv_piece, jnp.float32)] * MEMBERS
        + [jax.ShapeDtypeStruct(kv_piece, jnp.bfloat16)] * MEMBERS,
        scratch_shapes=[
            pltpu.VMEM((MEMBERS, ROWS, 4 * width), jnp.bfloat16),
            pltpu.VMEM((2 * MEMBERS, *kv_piece), jnp.bfloat16),
            pltpu.VMEM((MEMBERS, ROWS, 4 * width), jnp.bfloat16),
            pltpu.VMEM((2 * MEMBERS, *kv_piece), jnp.float32),
            pltpu.VMEM((MEMBERS, *kv_piece), jnp.bfloat16),
            pltpu.VMEM((2 * TILES, 2 * width, TILE), jnp.bfloat16),
            pltpu.VMEM((SPAN, TILE, 2 * TILE), jnp.float32),
            pltpu.VMEM((SPAN, TILE, 2 * TILE), jnp.float32),
            pltpu.SemaphoreType.DMA((3 * MEMBERS + 1,)),
        ],
        compiler_params=pltpu.CompilerParams(vmem_limit_bytes=48 * 1024 * 1024),
        cost_estimate=pl.CostEstimate(
            flops=2 * products, bytes_accessed=WINDOW_LENGTH * width * 30, transcendentals=0
        ),
    )(place, doc_lengths, queries, cotangents, *row_pieces, *own, *earlier)
    return outputs[:MEMBERS], outputs[MEMBERS : 2 * MEMBERS], outputs[2 * MEMBERS :]


def swapped(piece, distance):
    return lax.ppermute(piece, "member", [(i, i ^ distance) for i in range(MEMBERS)])


def onward(piece, direction):
    stretches = lax.axis_size("stretch")
    lower = [(i, i + 1) for i in range(stretches - 1)]
    return lax.ppermute(
        piece, "stretch", lower if direction > 0 else [(j, i) for i, j in lower]
    )


def shards(rotated_query_rows, rotated_key_rows, value_matrix, output_gradient, doc_lengths):
    member = lax.axis_index("member")
    start = lax.axis_index("stretch") * WINDOW_LENGTH
    place = jnp.stack([member, start]).astype(jnp.int32)
    own = pack(place, rotated_key_rows, value_matrix, 0)
    own = [own[0]] + [swapped(own[distance], distance) for distance in range(1, MEMBERS)]
    earlier = [onward(piece, 1) for piece in own]
    row_pieces = pack(place, rotated_query_rows, output_gradient, 1)
    row_pieces = [swapped(row_pieces[item], item + 1) for item in range(MEMBERS - 1)]
    results, own_grads, earlier_grads = attention(
        place, doc_lengths, rotated_query_rows, output_gradient, row_pieces, own, earlier
    )
    later = [onward(piece, -1) for piece in earlier_grads]
    results = [results[0]] + [swapped(results[item], item) for item in range(1, MEMBERS)]
    kv_grads = [
        (own_grads[item] + later[item].astype(jnp.float32)).astype(jnp.bfloat16)
        for item in range(MEMBERS)
    ]
    kv_grads = [kv_grads[0]] + [swapped(kv_grads[item], item) for item in range(1, MEMBERS)]
    return (*unpack(place, results), *unpack(place, kv_grads))


def solution(mesh):
    grouped = Mesh(mesh.devices.reshape(-1, MEMBERS), ("stretch", "member"))
    spread = P(("stretch", "member"), None)
    return jax.shard_map(
        shards,
        mesh=grouped,
        in_specs=(spread, spread, spread, spread, P()),
        out_specs=(spread, spread, spread, spread),
        check_vma=False,
    )
```

```python
import jax
import jax.numpy as jnp
from jax import lax
from jax.experimental import pallas as pl
from jax.experimental.pallas import tpu as pltpu
from jax.sharding import Mesh
from jax.sharding import PartitionSpec as P

HEAD_WIDTH = 256
WINDOW_LENGTH = 1024
MEMBERS = 8

TILE = 256
TILES = WINDOW_LENGTH // TILE
SPAN = TILES + 1
ROWS = WINDOW_LENGTH // MEMBERS
CHUNKS = TILE // ROWS
COLUMNS = 2 * TILE
SCORE_SCALE = HEAD_WIDTH ** (-0.5)
LOG2_E = 1.4426950408889634

ANYWHERE = pl.BlockSpec(memory_space=pl.ANY)
SCALARS = pl.BlockSpec(memory_space=pltpu.SMEM)
VMEM_LIMIT = pltpu.CompilerParams(vmem_limit_bytes=48 * 1024 * 1024)


def dot(left, right, contract):
    return lax.dot_general(
        left, right, ((contract[:1], contract[1:]), ((), ())), preferred_element_type=jnp.float32
    )


def whole(shape):
    return pl.BlockSpec(shape, lambda *_: (0,) * len(shape))


def run_copies(pairs, semaphores):
    copies = [
        pltpu.make_async_copy(source, target, semaphores.at[item])
        for item, (source, target) in enumerate(pairs)
    ]
    for copy in copies:
        copy.start()
    for copy in copies:
        copy.wait()


def columns_of(ref, head, width):
    return ref.at[:, pl.ds(pl.multiple_of(head * width, width), width)]


def pack_kernel(place_ref, left_ref, right_ref, *refs):
    pieces, semaphores = refs[:-1], refs[-1]
    width = left_ref.shape[1] // MEMBERS
    pairs = []
    for item, piece in enumerate(pieces):
        head = place_ref[0] ^ item
        pairs.append((columns_of(left_ref, head, width), piece.at[:, pl.ds(0, width)]))
        pairs.append((columns_of(right_ref, head, width), piece.at[:, pl.ds(width, width)]))
    run_copies(pairs, semaphores)


def pack(place, left, right):
    rows, columns = left.shape
    piece = jax.ShapeDtypeStruct((rows, 2 * columns // MEMBERS), left.dtype)
    return pl.pallas_call(
        pack_kernel,
        in_specs=[SCALARS, whole(left.shape), whole(right.shape)],
        out_specs=[ANYWHERE] * MEMBERS,
        out_shape=[piece] * MEMBERS,
        scratch_shapes=[pltpu.SemaphoreType.DMA((2 * MEMBERS,))],
        compiler_params=VMEM_LIMIT,
        cost_estimate=pl.CostEstimate(
            flops=0, bytes_accessed=8 * rows * columns, transcendentals=0
        ),
    )(place, left, right)


def unpack_kernel(place_ref, *refs):
    pieces, (left_ref, right_ref, semaphores) = refs[:MEMBERS], refs[MEMBERS:]
    width = left_ref.shape[1] // MEMBERS
    pairs = []
    for item, piece in enumerate(pieces):
        head = place_ref[0] ^ item
        pairs.append((piece.at[:, pl.ds(0, width)], columns_of(left_ref, head, width)))
        pairs.append((piece.at[:, pl.ds(width, width)], columns_of(right_ref, head, width)))
    run_copies(pairs, semaphores)


def unpack(place, pieces):
    rows, columns = pieces[0].shape
    shape = (rows, MEMBERS * columns // 2)
    return pl.pallas_call(
        unpack_kernel,
        in_specs=[SCALARS] + [ANYWHERE] * MEMBERS,
        out_specs=[whole(shape)] * 2,
        out_shape=[jax.ShapeDtypeStruct(shape, pieces[0].dtype)] * 2,
        scratch_shapes=[pltpu.SemaphoreType.DMA((2 * MEMBERS,))],
        compiler_params=VMEM_LIMIT,
        cost_estimate=pl.CostEstimate(
            flops=0, bytes_accessed=4 * MEMBERS * rows * columns, transcendentals=0
        ),
    )(place, *pieces)


def row_copies(member, pieces, rows, semaphores):
    return [
        (member ^ item, pltpu.make_async_copy(piece, rows.at[member ^ item], semaphores.at[item]))
        for item, piece in enumerate(pieces)
    ]


def take_rows(step, copies):
    @pl.when(step == 0)
    def _():
        for _, copy in copies:
            copy.start()

    for chunk, copy in copies:
        pl.when(chunk // CHUNKS == step)(copy.wait)


def two_heads(rows, step, first):
    chunks = pl.ds(step * CHUNKS, CHUNKS)
    return jnp.concatenate(
        [
            rows[chunks, :, head * HEAD_WIDTH : (head + 1) * HEAD_WIDTH].reshape(TILE, HEAD_WIDTH)
            for head in (first, first + 1)
        ],
        axis=0,
    )


def key_tiles(target, earlier_ref, own_ref):
    for tile in range(TILES):
        target[tile] = earlier_ref[tile * TILE : (tile + 1) * TILE, :]
        target[TILES + tile] = own_ref[tile * TILE : (tile + 1) * TILE, :]


def put_sums(sums, earlier_ref, own_ref, scale):
    for tile in range(TILES):
        place = slice(tile * TILE, (tile + 1) * TILE)
        earlier_ref[place, :] = (sums[tile] * scale).astype(earlier_ref.dtype)
        own_ref[place, :] = sums[TILES + tile] * scale


def probs_kernel(place_ref, lengths_ref, earlier_ref, own_ref, *refs):
    pieces, refs = refs[:MEMBERS], refs[MEMBERS:]
    probs_ref, earlier_grad_ref, own_grad_ref, rows, keys, sums, scores, semaphores = refs
    step = pl.program_id(0)
    member = place_ref[0]
    copies = row_copies(member, pieces, rows, semaphores)

    take_rows(step, copies)

    @pl.when(step == 0)
    def _():
        key_tiles(keys, earlier_ref, own_ref)
        sums[...] = jnp.zeros_like(sums)

    queries = two_heads(rows, step, 0)
    cotangents = two_heads(rows, step, 2)
    row = lax.broadcasted_iota(jnp.int32, (1, COLUMNS), 1) % TILE
    key_row = lax.broadcasted_iota(jnp.int32, (TILE, COLUMNS), 0)
    first_row = place_ref[1] + step * TILE
    oldest = row - (WINDOW_LENGTH - 1)

    def passed(item, carried):
        begin, oldest = carried
        near = begin - first_row
        oldest = jnp.where(near <= row, jnp.maximum(oldest, near), oldest)
        return begin + lengths_ref[item], oldest

    _, oldest = lax.fori_loop(0, lengths_ref.shape[0], passed, (jnp.int32(0), oldest))

    top = jnp.full((1, COLUMNS), -jnp.inf, jnp.float32)
    for item in range(SPAN):
        place = (item - TILES) * TILE
        tile_scores = dot(keys[step + item], queries, (1, 1))
        seen = key_row >= oldest - place
        if item == TILES:
            seen = seen & (key_row <= row)
        tile_scores = jnp.where(seen, tile_scores, -jnp.inf)
        top = jnp.maximum(top, jnp.max(tile_scores, axis=0, keepdims=True))
        scores[item] = tile_scores

    total = jnp.zeros((1, COLUMNS), jnp.float32)
    for item in range(SPAN):
        weights = jnp.exp2((scores[item] - top) * (SCORE_SCALE * LOG2_E))
        total = total + jnp.sum(weights, axis=0, keepdims=True)
        scores[item] = weights
    share = 1.0 / total

    for item in range(SPAN):
        probs_low = (scores[item] * share).astype(jnp.bfloat16)
        probs_ref[0, item] = probs_low
        sums[step + item] += dot(probs_low, cotangents, (1, 0))

    @pl.when(step == TILES - 1)
    def _():
        put_sums(sums, earlier_grad_ref, own_grad_ref, 1.0)


def grads_kernel(
    place_ref, probs_ref, earlier_keys_ref, own_keys_ref, earlier_values_ref, own_values_ref, *refs
):
    pieces, refs = refs[:MEMBERS], refs[MEMBERS:]
    result_pieces, refs = refs[:MEMBERS], refs[MEMBERS:]
    earlier_grad_ref, own_grad_ref, refs = refs[0], refs[1], refs[2:]
    rows, values, keys_turned, values_turned, sums, grads, results, semaphores, sent = refs
    step = pl.program_id(0)
    member = place_ref[0]
    copies = row_copies(member, pieces, rows, semaphores)

    take_rows(step, copies)

    @pl.when(step == 0)
    def _():
        key_tiles(values, earlier_values_ref, own_values_ref)
        for tile in range(TILES):
            place = slice(tile * TILE, (tile + 1) * TILE)
            keys_turned[tile] = earlier_keys_ref[place, :].T
            keys_turned[TILES + tile] = own_keys_ref[place, :].T
            values_turned[tile] = earlier_values_ref[place, :].T
            values_turned[TILES + tile] = own_values_ref[place, :].T
        sums[...] = jnp.zeros_like(sums)

    queries = two_heads(rows, step, 0)
    cotangents = two_heads(rows, step, 2)

    attended = jnp.zeros((HEAD_WIDTH, COLUMNS), jnp.float32)
    for item in range(SPAN):
        attended = attended + dot(values_turned[step + item], probs_ref[0, item], (1, 0))
        grads[item] = dot(values[step + item], cotangents, (1, 1))
    attended = attended.astype(jnp.bfloat16).astype(jnp.float32)
    turned = cotangents.astype(jnp.float32).T
    row_delta = jnp.sum(attended * turned, axis=0, keepdims=True)

    def put(first, part):
        chunks = pl.ds(step * CHUNKS, CHUNKS)
        part = part.T.astype(jnp.bfloat16).reshape(2 * CHUNKS, ROWS, HEAD_WIDTH)
        results[chunks, :, first : first + HEAD_WIDTH] = part[:CHUNKS]
        results[chunks, :, first + HEAD_WIDTH : first + 2 * HEAD_WIDTH] = part[CHUNKS:]

    put(0, attended)

    query_grad = jnp.zeros((HEAD_WIDTH, COLUMNS), jnp.float32)
    for item in range(SPAN):
        probs = probs_ref[0, item].astype(jnp.float32)
        grad_low = (probs * (grads[item] - row_delta)).astype(jnp.bfloat16)
        query_grad = query_grad + dot(keys_turned[step + item], grad_low, (1, 0))
        sums[step + item] += dot(grad_low, queries, (1, 0))
    put(2 * HEAD_WIDTH, query_grad * SCORE_SCALE)

    outgoing = [
        (member ^ item, pltpu.make_async_copy(results.at[member ^ item], piece, sent.at[item]))
        for item, piece in enumerate(result_pieces)
    ]
    for chunk, copy in outgoing:
        pl.when(chunk // CHUNKS == step)(copy.start)

    @pl.when(step == TILES - 1)
    def _():
        put_sums(sums, earlier_grad_ref, own_grad_ref, SCORE_SCALE)
        for _, copy in outgoing:
            copy.wait()


def probs_call(place, doc_lengths, earlier, own, pieces):
    flat = (WINDOW_LENGTH, HEAD_WIDTH)
    block = (1, SPAN, TILE, COLUMNS)
    product = 2 * WINDOW_LENGTH * 2 * SPAN * TILE * HEAD_WIDTH
    return pl.pallas_call(
        probs_kernel,
        grid=(TILES,),
        in_specs=[SCALARS, SCALARS, whole(flat), whole(flat)] + [ANYWHERE] * MEMBERS,
        out_specs=[pl.BlockSpec(block, lambda i: (i, 0, 0, 0)), whole(flat), whole(flat)],
        out_shape=[
            jax.ShapeDtypeStruct((TILES, *block[1:]), jnp.bfloat16),
            jax.ShapeDtypeStruct(flat, jnp.bfloat16),
            jax.ShapeDtypeStruct(flat, jnp.float32),
        ],
        scratch_shapes=[
            pltpu.VMEM((MEMBERS, ROWS, 4 * HEAD_WIDTH), jnp.bfloat16),
            pltpu.VMEM((2 * TILES, TILE, HEAD_WIDTH), jnp.bfloat16),
            pltpu.VMEM((2 * TILES, TILE, HEAD_WIDTH), jnp.float32),
            pltpu.VMEM((SPAN, TILE, COLUMNS), jnp.float32),
            pltpu.SemaphoreType.DMA((MEMBERS,)),
        ],
        compiler_params=VMEM_LIMIT,
        cost_estimate=pl.CostEstimate(
            flops=4 * product, bytes_accessed=10 * 1024 * 1024, transcendentals=0
        ),
    )(place, doc_lengths, earlier, own, *pieces)


def grads_call(place, probs, earlier_keys, own_keys, earlier_values, own_values, pieces):
    flat = (WINDOW_LENGTH, HEAD_WIDTH)
    block = (1, SPAN, TILE, COLUMNS)
    product = 2 * WINDOW_LENGTH * 2 * SPAN * TILE * HEAD_WIDTH
    outputs = pl.pallas_call(
        grads_kernel,
        grid=(TILES,),
        in_specs=[SCALARS, pl.BlockSpec(block, lambda i: (i, 0, 0, 0))]
        + [whole(flat)] * 4
        + [ANYWHERE] * MEMBERS,
        out_specs=[ANYWHERE] * MEMBERS + [whole(flat), whole(flat)],
        out_shape=[jax.ShapeDtypeStruct((ROWS, 4 * HEAD_WIDTH), jnp.bfloat16)] * MEMBERS
        + [
            jax.ShapeDtypeStruct(flat, jnp.bfloat16),
            jax.ShapeDtypeStruct(flat, jnp.float32),
        ],
        scratch_shapes=[
            pltpu.VMEM((MEMBERS, ROWS, 4 * HEAD_WIDTH), jnp.bfloat16),
            pltpu.VMEM((2 * TILES, TILE, HEAD_WIDTH), jnp.bfloat16),
            pltpu.VMEM((2 * TILES, HEAD_WIDTH, TILE), jnp.bfloat16),
            pltpu.VMEM((2 * TILES, HEAD_WIDTH, TILE), jnp.bfloat16),
            pltpu.VMEM((2 * TILES, TILE, HEAD_WIDTH), jnp.float32),
            pltpu.VMEM((SPAN, TILE, COLUMNS), jnp.float32),
            pltpu.VMEM((MEMBERS, ROWS, 4 * HEAD_WIDTH), jnp.bfloat16),
            pltpu.SemaphoreType.DMA((MEMBERS,)),
            pltpu.SemaphoreType.DMA((MEMBERS,)),
        ],
        compiler_params=VMEM_LIMIT,
        cost_estimate=pl.CostEstimate(
            flops=6 * product, bytes_accessed=14 * 1024 * 1024, transcendentals=0
        ),
    )(place, probs, earlier_keys, own_keys, earlier_values, own_values, *pieces)
    return outputs[:MEMBERS], outputs[MEMBERS], outputs[MEMBERS + 1]


def swapped(pieces):
    return [pieces[0]] + [
        lax.ppermute(pieces[item], "member", [(i, i ^ item) for i in range(MEMBERS)])
        for item in range(1, MEMBERS)
    ]


def onward(block, direction):
    lower = [(i, i + 1) for i in range(lax.axis_size("stretch") - 1)]
    route = lower if direction > 0 else [(j, i) for i, j in lower]
    return lax.ppermute(block, "stretch", route)


def exchanged(blocks):
    return lax.all_to_all(blocks, "member", split_axis=0, concat_axis=0, tiled=True)


def to_heads(block):
    parts = block.reshape(ROWS, MEMBERS, HEAD_WIDTH).transpose(1, 0, 2)
    return exchanged(parts).reshape(WINDOW_LENGTH, HEAD_WIDTH)


def to_tokens(own, later):
    block = (own + later.astype(jnp.float32)).astype(jnp.bfloat16)
    parts = exchanged(block.reshape(MEMBERS, ROWS, HEAD_WIDTH))
    return parts.transpose(1, 0, 2).reshape(ROWS, MEMBERS * HEAD_WIDTH)


def shards(rotated_query_rows, rotated_key_rows, value_matrix, output_gradient, doc_lengths):
    member = lax.axis_index("member")
    start = lax.axis_index("stretch") * WINDOW_LENGTH
    place = jnp.stack([member, start]).astype(jnp.int32)
    keys = to_heads(rotated_key_rows)
    earlier_keys = onward(keys, 1)
    values = to_heads(value_matrix)
    earlier_values = onward(values, 1)
    pieces = swapped(pack(place, rotated_query_rows, output_gradient))
    probs, earlier_grad, value_grad = probs_call(place, doc_lengths, earlier_keys, keys, pieces)
    value_gradient = to_tokens(value_grad, onward(earlier_grad, -1))
    results, earlier_grad, key_grad = grads_call(
        place, probs, earlier_keys, keys, earlier_values, values, pieces
    )
    key_gradient = to_tokens(key_grad, onward(earlier_grad, -1))
    attended, query_grad = unpack(place, swapped(results))
    return attended, query_grad, key_gradient, value_gradient


def solution(mesh):
    grouped = Mesh(mesh.devices.reshape(-1, MEMBERS), ("stretch", "member"))
    spread = P(("stretch", "member"), None)
    return jax.shard_map(
        shards,
        mesh=grouped,
        in_specs=(spread, spread, spread, spread, P()),
        out_specs=(spread, spread, spread, spread),
        check_vma=False,
    )
```

```python
import jax
import jax.numpy as jnp
from jax import lax
from jax.experimental import pallas as pl
from jax.experimental.pallas import tpu as pltpu
from jax.sharding import Mesh
from jax.sharding import PartitionSpec as P

HEAD_WIDTH = 256
WINDOW_LENGTH = 1024
MEMBERS = 8
HALF = MEMBERS // 2

TILE = 256
TILES = WINDOW_LENGTH // TILE
SPAN = TILES + 1
ROWS = WINDOW_LENGTH // MEMBERS
CHUNKS = TILE // ROWS
COLUMNS = 2 * TILE
SCORE_SCALE = HEAD_WIDTH ** (-0.5)
LOG2_E = 1.4426950408889634

ANYWHERE = pl.BlockSpec(memory_space=pl.ANY)
SCALARS = pl.BlockSpec(memory_space=pltpu.SMEM)
VMEM_LIMIT = pltpu.CompilerParams(vmem_limit_bytes=60 * 1024 * 1024)


def dot(left, right, contract):
    return lax.dot_general(
        left, right, ((contract[:1], contract[1:]), ((), ())), preferred_element_type=jnp.float32
    )


def whole(shape):
    return pl.BlockSpec(shape, lambda *_: (0,) * len(shape))


def copies_of(pairs, semaphores):
    return [
        pltpu.make_async_copy(source, target, semaphores.at[item])
        for item, (source, target) in enumerate(pairs)
    ]


def run(copies):
    for copy in copies:
        copy.start()
    for copy in copies:
        copy.wait()


def columns_of(ref, head, width):
    return ref.at[:, pl.ds(pl.multiple_of(head * width, width), width)]


def pack_kernel(place_ref, left_ref, right_ref, *refs):
    pieces, semaphores = refs[:-1], refs[-1]
    width = left_ref.shape[1] // MEMBERS
    pairs = []
    for item, piece in enumerate(pieces):
        head = place_ref[0] ^ item
        pairs.append((columns_of(left_ref, head, width), piece.at[:, pl.ds(0, width)]))
        pairs.append((columns_of(right_ref, head, width), piece.at[:, pl.ds(width, width)]))
    run(copies_of(pairs, semaphores))


def pack(place, left, right):
    rows, columns = left.shape
    piece = jax.ShapeDtypeStruct((rows, 2 * columns // MEMBERS), left.dtype)
    return pl.pallas_call(
        pack_kernel,
        in_specs=[SCALARS, whole(left.shape), whole(right.shape)],
        out_specs=[ANYWHERE] * MEMBERS,
        out_shape=[piece] * MEMBERS,
        scratch_shapes=[pltpu.SemaphoreType.DMA((2 * MEMBERS,))],
        compiler_params=VMEM_LIMIT,
        cost_estimate=pl.CostEstimate(
            flops=0, bytes_accessed=8 * rows * columns, transcendentals=0
        ),
    )(place, left, right)


def unpack_kernel(place_ref, *refs):
    pieces, (left_ref, right_ref, semaphores) = refs[:MEMBERS], refs[MEMBERS:]
    width = left_ref.shape[1] // MEMBERS
    pairs = []
    for item, piece in enumerate(pieces):
        head = place_ref[0] ^ item
        pairs.append((piece.at[:, pl.ds(0, width)], columns_of(left_ref, head, width)))
        pairs.append((piece.at[:, pl.ds(width, width)], columns_of(right_ref, head, width)))
    run(copies_of(pairs, semaphores))


def unpack(place, pieces):
    rows, columns = pieces[0].shape
    shape = (rows, MEMBERS * columns // 2)
    return pl.pallas_call(
        unpack_kernel,
        in_specs=[SCALARS] + [ANYWHERE] * MEMBERS,
        out_specs=[whole(shape)] * 2,
        out_shape=[jax.ShapeDtypeStruct(shape, pieces[0].dtype)] * 2,
        scratch_shapes=[pltpu.SemaphoreType.DMA((2 * MEMBERS,))],
        compiler_params=VMEM_LIMIT,
        cost_estimate=pl.CostEstimate(
            flops=0, bytes_accessed=4 * MEMBERS * rows * columns, transcendentals=0
        ),
    )(place, *pieces)


def attention_kernel(place_ref, lengths_ref, rows_ref, *refs):
    own_halves, earlier_halves, out_ref = refs[:2], refs[2:4], refs[4]
    own_grads, earlier_grads, refs = refs[5:7], refs[7:9], refs[9:]
    kv, kv_turned, scores, grads, sums, low_sums, semaphores = refs
    step = pl.program_id(0)
    width = HEAD_WIDTH
    member = place_ref[0]

    @pl.when(step == 0)
    def _():
        pairs = []
        for item in range(MEMBERS):
            half, part, chunk = item // HALF, item % HALF, member ^ item
            pairs.append((earlier_halves[half].at[part], kv.at[chunk]))
            pairs.append((own_halves[half].at[part], kv.at[MEMBERS + chunk]))
        copies = copies_of(pairs, semaphores)
        for copy in copies:
            copy.start()
        sums[...] = jnp.zeros_like(sums)
        for copy in copies:
            copy.wait()
        for tile in range(2 * TILES):
            part = kv[tile * CHUNKS : (tile + 1) * CHUNKS].reshape(TILE, 2 * width)
            kv_turned[tile] = part.T

    def key_tile(item, first):
        tile = pl.ds((step + item) * CHUNKS, CHUNKS)
        return kv[tile, :, first : first + width].reshape(TILE, width)

    def add(item, first, part):
        tile = pl.ds((step + item) * CHUNKS, CHUNKS)
        sums[tile, :, first : first + width] += part.reshape(CHUNKS, ROWS, width)

    queries = jnp.concatenate([rows_ref[:, :width], rows_ref[:, width : 2 * width]], axis=0)
    cotangents = jnp.concatenate(
        [rows_ref[:, 2 * width : 3 * width], rows_ref[:, 3 * width :]], axis=0
    )

    first_row = place_ref[1] + step * TILE
    row = lax.broadcasted_iota(jnp.int32, (1, COLUMNS), 1) % TILE
    oldest = row - (WINDOW_LENGTH - 1)

    def passed(item, carried):
        begin, oldest = carried
        near = begin - first_row
        oldest = jnp.where(near <= row, jnp.maximum(oldest, near), oldest)
        return begin + lengths_ref[item], oldest

    _, oldest = lax.fori_loop(0, lengths_ref.shape[0], passed, (jnp.int32(0), oldest))
    key_row = lax.broadcasted_iota(jnp.int32, (TILE, COLUMNS), 0)

    top = jnp.full((1, COLUMNS), -jnp.inf, jnp.float32)
    for item in range(SPAN):
        place = (item - TILES) * TILE
        tile_scores = dot(key_tile(item, 0), queries, (1, 1))
        seen = key_row >= oldest - place
        if item == TILES:
            seen = seen & (key_row <= row)
        tile_scores = jnp.where(seen, tile_scores, -jnp.inf)
        top = jnp.maximum(top, jnp.max(tile_scores, axis=0, keepdims=True))
        scores[item] = tile_scores

    total = jnp.zeros((1, COLUMNS), jnp.float32)
    for item in range(SPAN):
        weights = jnp.exp2((scores[item] - top) * (SCORE_SCALE * LOG2_E))
        total = total + jnp.sum(weights, axis=0, keepdims=True)
        scores[item] = weights
    share = 1.0 / total

    attended = jnp.zeros((width, COLUMNS), jnp.float32)
    for item in range(SPAN):
        probs = scores[item] * share
        scores[item] = probs
        probs_low = probs.astype(jnp.bfloat16)
        attended = attended + dot(kv_turned[step + item, width:, :], probs_low, (1, 0))
        add(item, width, dot(probs_low, cotangents, (1, 0)))
        grads[item] = dot(key_tile(item, width), cotangents, (1, 1))
    attended = attended.astype(jnp.bfloat16).astype(jnp.float32)
    turned = cotangents.astype(jnp.float32).T
    row_delta = jnp.sum(attended * turned, axis=0, keepdims=True)
    attended = attended.T.astype(jnp.bfloat16)
    out_ref[:, :width] = attended[:TILE]
    out_ref[:, width : 2 * width] = attended[TILE:]

    query_grad = jnp.zeros((width, COLUMNS), jnp.float32)
    for item in range(SPAN):
        grad_low = (scores[item] * (grads[item] - row_delta)).astype(jnp.bfloat16)
        query_grad = query_grad + dot(kv_turned[step + item, :width, :], grad_low, (1, 0))
        add(item, 0, dot(grad_low, queries, (1, 0)))
    query_grad = (query_grad * SCORE_SCALE).T.astype(jnp.bfloat16)
    out_ref[:, 2 * width : 3 * width] = query_grad[:TILE]
    out_ref[:, 3 * width :] = query_grad[TILE:]

    @pl.when(step == TILES - 1)
    def _():
        sums[:, :, :width] = sums[:, :, :width] * SCORE_SCALE
        low_sums[...] = sums[:MEMBERS].astype(jnp.bfloat16)
        pairs = []
        for item in range(MEMBERS):
            half, part, chunk = item // HALF, item % HALF, member ^ item
            pairs.append((low_sums.at[chunk], earlier_grads[half].at[part]))
            pairs.append((sums.at[MEMBERS + chunk], own_grads[half].at[part]))
        run(copies_of(pairs, semaphores))


def attention(place, doc_lengths, rows, own, earlier):
    width = HEAD_WIDTH
    products = 5 * 2 * WINDOW_LENGTH * 2 * SPAN * TILE * width
    half = (HALF, ROWS, 2 * width)
    outputs = pl.pallas_call(
        attention_kernel,
        grid=(TILES,),
        in_specs=[SCALARS, SCALARS, pl.BlockSpec((TILE, 4 * width), lambda i: (i, 0))]
        + [ANYWHERE] * 4,
        out_specs=[pl.BlockSpec((TILE, 4 * width), lambda i: (i, 0))] + [ANYWHERE] * 4,
        out_shape=[jax.ShapeDtypeStruct(rows.shape, jnp.bfloat16)]
        + [jax.ShapeDtypeStruct(half, jnp.float32)] * 2
        + [jax.ShapeDtypeStruct(half, jnp.bfloat16)] * 2,
        scratch_shapes=[
            pltpu.VMEM((2 * MEMBERS, ROWS, 2 * width), jnp.bfloat16),
            pltpu.VMEM((2 * TILES, 2 * width, TILE), jnp.bfloat16),
            pltpu.VMEM((SPAN, TILE, COLUMNS), jnp.float32),
            pltpu.VMEM((SPAN, TILE, COLUMNS), jnp.float32),
            pltpu.VMEM((2 * MEMBERS, ROWS, 2 * width), jnp.float32),
            pltpu.VMEM((MEMBERS, ROWS, 2 * width), jnp.bfloat16),
            pltpu.SemaphoreType.DMA((2 * MEMBERS,)),
        ],
        compiler_params=VMEM_LIMIT,
        cost_estimate=pl.CostEstimate(
            flops=2 * products, bytes_accessed=WINDOW_LENGTH * width * 30, transcendentals=0
        ),
    )(place, doc_lengths, rows, *own, *earlier)
    return outputs[0], outputs[1:3], outputs[3:5]


def by_head(block):
    return block.reshape(ROWS, MEMBERS, block.shape[1] // MEMBERS).transpose(1, 0, 2)


def by_token(blocks):
    return blocks.transpose(1, 0, 2).reshape(ROWS, MEMBERS * blocks.shape[2])


def exchanged(blocks):
    return lax.all_to_all(blocks, "member", split_axis=0, concat_axis=0, tiled=True)


def swapped(piece, distance):
    if distance == 0:
        return piece
    return lax.ppermute(piece, "member", [(i, i ^ distance) for i in range(MEMBERS)])


def onward(block, direction):
    lower = [(i, i + 1) for i in range(lax.axis_size("stretch") - 1)]
    route = lower if direction > 0 else [(j, i) for i, j in lower]
    return lax.ppermute(block, "stretch", route)


def shards(rotated_query_rows, rotated_key_rows, value_matrix, output_gradient, doc_lengths):
    member = lax.axis_index("member")
    start = lax.axis_index("stretch") * WINDOW_LENGTH
    place = jnp.stack([member, start]).astype(jnp.int32)
    pieces = pack(place, rotated_key_rows, value_matrix)
    pieces, rotated_query_rows, output_gradient = lax.optimization_barrier(
        (pieces, rotated_query_rows, output_gradient)
    )
    pieces = [swapped(piece, item) for item, piece in enumerate(pieces)]
    own = [jnp.stack(pieces[:HALF]), jnp.stack(pieces[HALF:])]
    earlier = [onward(half, 1) for half in own]
    rows = jnp.concatenate([by_head(rotated_query_rows), by_head(output_gradient)], axis=2)
    rows = exchanged(rows).reshape(WINDOW_LENGTH, 4 * HEAD_WIDTH)
    results, own_grads, earlier_grads = attention(place, doc_lengths, rows, own, earlier)
    later = [None, None]
    later[1] = onward(earlier_grads[1], -1)
    later[0] = onward(earlier_grads[0], -1)
    results = exchanged(results.reshape(MEMBERS, ROWS, 4 * HEAD_WIDTH))
    pieces = [
        (own_grads[item // HALF][item % HALF] + later[item // HALF][item % HALF]).astype(
            jnp.bfloat16
        )
        for item in range(MEMBERS)
    ]
    pieces = [swapped(piece, item) for item, piece in enumerate(pieces)]
    key_gradient, value_gradient = unpack(place, pieces)
    return (
        by_token(results[:, :, : 2 * HEAD_WIDTH]),
        by_token(results[:, :, 2 * HEAD_WIDTH :]),
        key_gradient,
        value_gradient,
    )


def solution(mesh):
    grouped = Mesh(mesh.devices.reshape(-1, MEMBERS), ("stretch", "member"))
    spread = P(("stretch", "member"), None)
    return jax.shard_map(
        shards,
        mesh=grouped,
        in_specs=(spread, spread, spread, spread, P()),
        out_specs=(spread, spread, spread, spread),
        check_vma=False,
    )
```

```python
import jax
import jax.numpy as jnp
from jax import lax
from jax.experimental import pallas as pl
from jax.experimental.pallas import tpu as pltpu
from jax.sharding import Mesh
from jax.sharding import PartitionSpec as P

HEAD_WIDTH = 256
WINDOW_LENGTH = 1024
MEMBERS = 8
HALF = MEMBERS // 2

TILE = 256
TILES = WINDOW_LENGTH // TILE
SPAN = TILES + 1
ROWS = WINDOW_LENGTH // MEMBERS
CHUNKS = TILE // ROWS
COLUMNS = 2 * TILE
SCORE_SCALE = HEAD_WIDTH ** (-0.5)
LOG2_E = 1.4426950408889634

ANYWHERE = pl.BlockSpec(memory_space=pl.ANY)
SCALARS = pl.BlockSpec(memory_space=pltpu.SMEM)
VMEM_LIMIT = pltpu.CompilerParams(vmem_limit_bytes=62 * 1024 * 1024)


def dot(left, right, contract):
    return lax.dot_general(
        left, right, ((contract[:1], contract[1:]), ((), ())), preferred_element_type=jnp.float32
    )


def whole(shape):
    return pl.BlockSpec(shape, lambda *_: (0,) * len(shape))


def copies_of(pairs, semaphores):
    return [
        pltpu.make_async_copy(source, target, semaphores.at[item])
        for item, (source, target) in enumerate(pairs)
    ]


def run(copies):
    for copy in copies:
        copy.start()
    for copy in copies:
        copy.wait()


def columns_of(ref, head, width):
    return ref.at[:, pl.ds(pl.multiple_of(head * width, width), width)]


def pack_kernel(place_ref, left_ref, right_ref, *refs):
    pieces, semaphores = refs[:-1], refs[-1]
    width = left_ref.shape[1] // MEMBERS
    pairs = []
    for item, piece in enumerate(pieces):
        head = place_ref[0] ^ item
        pairs.append((columns_of(left_ref, head, width), piece.at[:, pl.ds(0, width)]))
        pairs.append((columns_of(right_ref, head, width), piece.at[:, pl.ds(width, width)]))
    run(copies_of(pairs, semaphores))


def pack(place, left, right):
    rows, columns = left.shape
    piece = jax.ShapeDtypeStruct((rows, 2 * columns // MEMBERS), left.dtype)
    return pl.pallas_call(
        pack_kernel,
        in_specs=[SCALARS, whole(left.shape), whole(right.shape)],
        out_specs=[ANYWHERE] * MEMBERS,
        out_shape=[piece] * MEMBERS,
        scratch_shapes=[pltpu.SemaphoreType.DMA((2 * MEMBERS,))],
        compiler_params=VMEM_LIMIT,
        cost_estimate=pl.CostEstimate(
            flops=0, bytes_accessed=8 * rows * columns, transcendentals=0
        ),
    )(place, left, right)


def unpack_kernel(place_ref, *refs):
    pieces, (left_ref, right_ref, semaphores) = refs[:MEMBERS], refs[MEMBERS:]
    width = left_ref.shape[1] // MEMBERS
    pairs = []
    for item, piece in enumerate(pieces):
        head = place_ref[0] ^ item
        pairs.append((piece.at[:, pl.ds(0, width)], columns_of(left_ref, head, width)))
        pairs.append((piece.at[:, pl.ds(width, width)], columns_of(right_ref, head, width)))
    run(copies_of(pairs, semaphores))


def unpack(place, pieces):
    rows, columns = pieces[0].shape
    shape = (rows, MEMBERS * columns // 2)
    return pl.pallas_call(
        unpack_kernel,
        in_specs=[SCALARS] + [ANYWHERE] * MEMBERS,
        out_specs=[whole(shape)] * 2,
        out_shape=[jax.ShapeDtypeStruct(shape, pieces[0].dtype)] * 2,
        scratch_shapes=[pltpu.SemaphoreType.DMA((2 * MEMBERS,))],
        compiler_params=VMEM_LIMIT,
        cost_estimate=pl.CostEstimate(
            flops=0, bytes_accessed=4 * MEMBERS * rows * columns, transcendentals=0
        ),
    )(place, *pieces)


def attention_kernel(place_ref, lengths_ref, *refs):
    row_pieces, refs = refs[:MEMBERS], refs[MEMBERS:]
    own_halves, earlier_halves, refs = refs[:2], refs[2:4], refs[4:]
    result_pieces, refs = refs[:MEMBERS], refs[MEMBERS:]
    own_grads, earlier_grads, refs = refs[:2], refs[2:4], refs[4:]
    rows, results, kv, kv_turned, scores, grads, sums, low_sums, semaphores, row_marks, sent = refs
    step = pl.program_id(0)
    width = HEAD_WIDTH
    member = place_ref[0]
    chunks = pl.ds(step * CHUNKS, CHUNKS)
    chunk_of = [member ^ item for item in range(MEMBERS)]
    arriving = copies_of(
        [(piece, rows.at[chunk]) for piece, chunk in zip(row_pieces, chunk_of)], row_marks
    )
    leaving = copies_of(
        [(results.at[chunk], piece) for piece, chunk in zip(result_pieces, chunk_of)], sent
    )

    @pl.when(step == 0)
    def _():
        for copy in arriving:
            copy.start()
        pairs = []
        for item in range(MEMBERS):
            half, part, chunk = item // HALF, item % HALF, chunk_of[item]
            pairs.append((earlier_halves[half].at[part], kv.at[chunk]))
            pairs.append((own_halves[half].at[part], kv.at[MEMBERS + chunk]))
        copies = copies_of(pairs, semaphores)
        for copy in copies:
            copy.start()
        sums[...] = jnp.zeros_like(sums)
        for copy in copies:
            copy.wait()
        for tile in range(2 * TILES):
            part = kv[tile * CHUNKS : (tile + 1) * CHUNKS].reshape(TILE, 2 * width)
            kv_turned[tile] = part.T

    for chunk, copy in zip(chunk_of, arriving):
        pl.when(chunk // CHUNKS == step)(copy.wait)

    def key_tile(item, first):
        tile = pl.ds((step + item) * CHUNKS, CHUNKS)
        return kv[tile, :, first : first + width].reshape(TILE, width)

    def add(item, first, part):
        tile = pl.ds((step + item) * CHUNKS, CHUNKS)
        sums[tile, :, first : first + width] += part.reshape(CHUNKS, ROWS, width)

    def both(first):
        return jnp.concatenate(
            [
                rows[chunks, :, head * width : (head + 1) * width].reshape(TILE, width)
                for head in (first, first + 1)
            ],
            axis=0,
        )

    def put(first, part):
        part = part.T.astype(jnp.bfloat16).reshape(2 * CHUNKS, ROWS, width)
        results[chunks, :, first : first + width] = part[:CHUNKS]
        results[chunks, :, first + width : first + 2 * width] = part[CHUNKS:]

    queries = both(0)
    cotangents = both(2)

    first_row = place_ref[1] + step * TILE
    row = lax.broadcasted_iota(jnp.int32, (1, COLUMNS), 1) % TILE
    oldest = row - (WINDOW_LENGTH - 1)

    def passed(item, carried):
        begin, oldest = carried
        near = begin - first_row
        oldest = jnp.where(near <= row, jnp.maximum(oldest, near), oldest)
        return begin + lengths_ref[item], oldest

    _, oldest = lax.fori_loop(0, lengths_ref.shape[0], passed, (jnp.int32(0), oldest))
    key_row = lax.broadcasted_iota(jnp.int32, (TILE, COLUMNS), 0)

    top = jnp.full((1, COLUMNS), -jnp.inf, jnp.float32)
    for item in range(SPAN):
        place = (item - TILES) * TILE
        tile_scores = dot(key_tile(item, 0), queries, (1, 1))
        seen = key_row >= oldest - place
        if item == TILES:
            seen = seen & (key_row <= row)
        tile_scores = jnp.where(seen, tile_scores, -jnp.inf)
        top = jnp.maximum(top, jnp.max(tile_scores, axis=0, keepdims=True))
        scores[item] = tile_scores

    total = jnp.zeros((1, COLUMNS), jnp.float32)
    for item in range(SPAN):
        weights = jnp.exp2((scores[item] - top) * (SCORE_SCALE * LOG2_E))
        total = total + jnp.sum(weights, axis=0, keepdims=True)
        scores[item] = weights
    share = 1.0 / total

    attended = jnp.zeros((width, COLUMNS), jnp.float32)
    for item in range(SPAN):
        probs = scores[item] * share
        scores[item] = probs
        probs_low = probs.astype(jnp.bfloat16)
        attended = attended + dot(kv_turned[step + item, width:, :], probs_low, (1, 0))
        add(item, width, dot(probs_low, cotangents, (1, 0)))
        grads[item] = dot(key_tile(item, width), cotangents, (1, 1))
    attended = attended.astype(jnp.bfloat16).astype(jnp.float32)
    turned = cotangents.astype(jnp.float32).T
    row_delta = jnp.sum(attended * turned, axis=0, keepdims=True)
    put(0, attended)

    query_grad = jnp.zeros((width, COLUMNS), jnp.float32)
    for item in range(SPAN):
        grad_low = (scores[item] * (grads[item] - row_delta)).astype(jnp.bfloat16)
        query_grad = query_grad + dot(kv_turned[step + item, :width, :], grad_low, (1, 0))
        add(item, 0, dot(grad_low, queries, (1, 0)))
    put(2 * width, query_grad * SCORE_SCALE)

    for chunk, copy in zip(chunk_of, leaving):
        pl.when(chunk // CHUNKS == step)(copy.start)

    @pl.when(step == TILES - 1)
    def _():
        sums[:, :, :width] = sums[:, :, :width] * SCORE_SCALE
        low_sums[...] = sums[:MEMBERS].astype(jnp.bfloat16)
        pairs = []
        for item in range(MEMBERS):
            half, part, chunk = item // HALF, item % HALF, chunk_of[item]
            pairs.append((low_sums.at[chunk], earlier_grads[half].at[part]))
            pairs.append((sums.at[MEMBERS + chunk], own_grads[half].at[part]))
        run(copies_of(pairs, semaphores))
        for copy in leaving:
            copy.wait()


def attention(place, doc_lengths, row_pieces, own, earlier):
    width = HEAD_WIDTH
    products = 5 * 2 * WINDOW_LENGTH * 2 * SPAN * TILE * width
    half = (HALF, ROWS, 2 * width)
    outputs = pl.pallas_call(
        attention_kernel,
        grid=(TILES,),
        in_specs=[SCALARS, SCALARS] + [ANYWHERE] * (MEMBERS + 4),
        out_specs=[ANYWHERE] * (MEMBERS + 4),
        out_shape=[jax.ShapeDtypeStruct((ROWS, 4 * width), jnp.bfloat16)] * MEMBERS
        + [jax.ShapeDtypeStruct(half, jnp.float32)] * 2
        + [jax.ShapeDtypeStruct(half, jnp.bfloat16)] * 2,
        scratch_shapes=[
            pltpu.VMEM((MEMBERS, ROWS, 4 * width), jnp.bfloat16),
            pltpu.VMEM((MEMBERS, ROWS, 4 * width), jnp.bfloat16),
            pltpu.VMEM((2 * MEMBERS, ROWS, 2 * width), jnp.bfloat16),
            pltpu.VMEM((2 * TILES, 2 * width, TILE), jnp.bfloat16),
            pltpu.VMEM((SPAN, TILE, COLUMNS), jnp.float32),
            pltpu.VMEM((SPAN, TILE, COLUMNS), jnp.float32),
            pltpu.VMEM((2 * MEMBERS, ROWS, 2 * width), jnp.float32),
            pltpu.VMEM((MEMBERS, ROWS, 2 * width), jnp.bfloat16),
            pltpu.SemaphoreType.DMA((2 * MEMBERS,)),
            pltpu.SemaphoreType.DMA((MEMBERS,)),
            pltpu.SemaphoreType.DMA((MEMBERS,)),
        ],
        compiler_params=VMEM_LIMIT,
        cost_estimate=pl.CostEstimate(
            flops=2 * products, bytes_accessed=WINDOW_LENGTH * width * 30, transcendentals=0
        ),
    )(place, doc_lengths, *row_pieces, *own, *earlier)
    return outputs[:MEMBERS], outputs[MEMBERS : MEMBERS + 2], outputs[MEMBERS + 2 :]


def swapped(pieces):
    return [pieces[0]] + [
        lax.ppermute(pieces[item], "member", [(i, i ^ item) for i in range(MEMBERS)])
        for item in range(1, MEMBERS)
    ]


def onward(block, direction):
    lower = [(i, i + 1) for i in range(lax.axis_size("stretch") - 1)]
    route = lower if direction > 0 else [(j, i) for i, j in lower]
    return lax.ppermute(block, "stretch", route)


def shards(rotated_query_rows, rotated_key_rows, value_matrix, output_gradient, doc_lengths):
    member = lax.axis_index("member")
    start = lax.axis_index("stretch") * WINDOW_LENGTH
    place = jnp.stack([member, start]).astype(jnp.int32)
    pieces = pack(place, rotated_key_rows, value_matrix)
    pieces, rotated_query_rows, output_gradient = lax.optimization_barrier(
        (pieces, rotated_query_rows, output_gradient)
    )
    pieces = swapped(pieces)
    own = [jnp.stack(pieces[:HALF]), jnp.stack(pieces[HALF:])]
    earlier = [onward(half, 1) for half in own]
    pieces = swapped(pack(place, rotated_query_rows, output_gradient))
    results, own_grads, earlier_grads = attention(place, doc_lengths, pieces, own, earlier)
    later = [onward(half, -1) for half in earlier_grads]
    results = swapped(results)
    pieces = [
        (own_grads[item // HALF][item % HALF] + later[item // HALF][item % HALF]).astype(
            jnp.bfloat16
        )
        for item in range(MEMBERS)
    ]
    pieces = swapped(pieces)
    return (*unpack(place, results), *unpack(place, pieces))


def solution(mesh):
    grouped = Mesh(mesh.devices.reshape(-1, MEMBERS), ("stretch", "member"))
    spread = P(("stretch", "member"), None)
    return jax.shard_map(
        shards,
        mesh=grouped,
        in_specs=(spread, spread, spread, spread, P()),
        out_specs=(spread, spread, spread, spread),
        check_vma=False,
    )
```

```python
import jax
import jax.numpy as jnp
from jax import lax
from jax.experimental import pallas as pl
from jax.experimental.pallas import tpu as pltpu
from jax.sharding import Mesh
from jax.sharding import PartitionSpec as P

HEAD_WIDTH = 256
WINDOW_LENGTH = 1024
MEMBERS = 8
HALF = MEMBERS // 2

TILE = 256
TILES = WINDOW_LENGTH // TILE
SPAN = TILES + 1
ROWS = WINDOW_LENGTH // MEMBERS
CHUNKS = TILE // ROWS
COLUMNS = 2 * TILE
SCORE_SCALE = HEAD_WIDTH ** (-0.5)
LOG2_E = 1.4426950408889634

ANYWHERE = pl.BlockSpec(memory_space=pl.ANY)
SCALARS = pl.BlockSpec(memory_space=pltpu.SMEM)
VMEM_LIMIT = pltpu.CompilerParams(vmem_limit_bytes=62 * 1024 * 1024)


def dot(left, right, contract):
    return lax.dot_general(
        left, right, ((contract[:1], contract[1:]), ((), ())), preferred_element_type=jnp.float32
    )


def whole(shape):
    return pl.BlockSpec(shape, lambda *_: (0,) * len(shape))


def copies_of(pairs, semaphores):
    return [
        pltpu.make_async_copy(source, target, semaphores.at[item])
        for item, (source, target) in enumerate(pairs)
    ]


def run(copies):
    for copy in copies:
        copy.start()
    for copy in copies:
        copy.wait()


def columns_of(ref, head, width):
    return ref.at[:, pl.ds(pl.multiple_of(head * width, width), width)]


def pack_kernel(place_ref, left_ref, right_ref, *refs):
    pieces, semaphores = refs[:-1], refs[-1]
    width = left_ref.shape[1] // MEMBERS
    pairs = []
    for item, piece in enumerate(pieces):
        head = place_ref[0] ^ item
        pairs.append((columns_of(left_ref, head, width), piece.at[:, pl.ds(0, width)]))
        pairs.append((columns_of(right_ref, head, width), piece.at[:, pl.ds(width, width)]))
    run(copies_of(pairs, semaphores))


def pack(place, left, right):
    rows, columns = left.shape
    piece = jax.ShapeDtypeStruct((rows, 2 * columns // MEMBERS), left.dtype)
    return pl.pallas_call(
        pack_kernel,
        in_specs=[SCALARS, whole(left.shape), whole(right.shape)],
        out_specs=[ANYWHERE] * MEMBERS,
        out_shape=[piece] * MEMBERS,
        scratch_shapes=[pltpu.SemaphoreType.DMA((2 * MEMBERS,))],
        compiler_params=VMEM_LIMIT,
        cost_estimate=pl.CostEstimate(
            flops=0, bytes_accessed=8 * rows * columns, transcendentals=0
        ),
    )(place, left, right)


def unpack_kernel(place_ref, *refs):
    pieces, (left_ref, right_ref, semaphores) = refs[:MEMBERS], refs[MEMBERS:]
    width = left_ref.shape[1] // MEMBERS
    pairs = []
    for item, piece in enumerate(pieces):
        head = place_ref[0] ^ item
        pairs.append((piece.at[:, pl.ds(0, width)], columns_of(left_ref, head, width)))
        pairs.append((piece.at[:, pl.ds(width, width)], columns_of(right_ref, head, width)))
    run(copies_of(pairs, semaphores))


def unpack(place, pieces):
    rows, columns = pieces[0].shape
    shape = (rows, MEMBERS * columns // 2)
    return pl.pallas_call(
        unpack_kernel,
        in_specs=[SCALARS] + [ANYWHERE] * MEMBERS,
        out_specs=[whole(shape)] * 2,
        out_shape=[jax.ShapeDtypeStruct(shape, pieces[0].dtype)] * 2,
        scratch_shapes=[pltpu.SemaphoreType.DMA((2 * MEMBERS,))],
        compiler_params=VMEM_LIMIT,
        cost_estimate=pl.CostEstimate(
            flops=0, bytes_accessed=4 * MEMBERS * rows * columns, transcendentals=0
        ),
    )(place, *pieces)


def attention_kernel(place_ref, lengths_ref, rows_ref, *refs):
    own_halves, earlier_halves, out_ref = refs[:2], refs[2:4], refs[4]
    own_grads, earlier_grads, refs = refs[5:7], refs[7:9], refs[9:]
    kv, kv_turned, scores, grads, sums, low_sums, semaphores = refs
    step = pl.program_id(0)
    width = HEAD_WIDTH
    member = place_ref[0]

    @pl.when(step == 0)
    def _():
        pairs = []
        for item in range(MEMBERS):
            half, part, chunk = item // HALF, item % HALF, member ^ item
            pairs.append((earlier_halves[half].at[part], kv.at[chunk]))
            pairs.append((own_halves[half].at[part], kv.at[MEMBERS + chunk]))
        copies = copies_of(pairs, semaphores)
        for copy in copies:
            copy.start()
        sums[...] = jnp.zeros_like(sums)
        for copy in copies:
            copy.wait()
        for tile in range(2 * TILES):
            part = kv[tile * CHUNKS : (tile + 1) * CHUNKS].reshape(TILE, 2 * width)
            kv_turned[tile] = part.T

    def key_tile(item, first):
        tile = pl.ds((step + item) * CHUNKS, CHUNKS)
        return kv[tile, :, first : first + width].reshape(TILE, width)

    def add(item, first, part):
        tile = pl.ds((step + item) * CHUNKS, CHUNKS)
        sums[tile, :, first : first + width] += part.reshape(CHUNKS, ROWS, width)

    queries = jnp.concatenate([rows_ref[:, :width], rows_ref[:, width : 2 * width]], axis=0)
    cotangents = jnp.concatenate(
        [rows_ref[:, 2 * width : 3 * width], rows_ref[:, 3 * width :]], axis=0
    )

    first_row = place_ref[1] + step * TILE
    row = lax.broadcasted_iota(jnp.int32, (1, COLUMNS), 1) % TILE
    oldest = row - (WINDOW_LENGTH - 1)

    def passed(item, carried):
        begin, oldest = carried
        near = begin - first_row
        oldest = jnp.where(near <= row, jnp.maximum(oldest, near), oldest)
        return begin + lengths_ref[item], oldest

    _, oldest = lax.fori_loop(0, lengths_ref.shape[0], passed, (jnp.int32(0), oldest))
    key_row = lax.broadcasted_iota(jnp.int32, (TILE, COLUMNS), 0)

    top = jnp.full((1, COLUMNS), -jnp.inf, jnp.float32)
    for item in range(SPAN):
        place = (item - TILES) * TILE
        tile_scores = dot(key_tile(item, 0), queries, (1, 1))
        seen = key_row >= oldest - place
        if item == TILES:
            seen = seen & (key_row <= row)
        tile_scores = jnp.where(seen, tile_scores, -jnp.inf)
        top = jnp.maximum(top, jnp.max(tile_scores, axis=0, keepdims=True))
        scores[item] = tile_scores

    total = jnp.zeros((1, COLUMNS), jnp.float32)
    for item in range(SPAN):
        weights = jnp.exp2((scores[item] - top) * (SCORE_SCALE * LOG2_E))
        total = total + jnp.sum(weights, axis=0, keepdims=True)
        scores[item] = weights
    share = 1.0 / total

    attended = jnp.zeros((width, COLUMNS), jnp.float32)
    for item in range(SPAN):
        probs = scores[item] * share
        scores[item] = probs
        probs_low = probs.astype(jnp.bfloat16)
        attended = attended + dot(kv_turned[step + item, width:, :], probs_low, (1, 0))
        add(item, width, dot(probs_low, cotangents, (1, 0)))
        grads[item] = dot(key_tile(item, width), cotangents, (1, 1))
    attended = attended.astype(jnp.bfloat16).astype(jnp.float32)
    turned = cotangents.astype(jnp.float32).T
    row_delta = jnp.sum(attended * turned, axis=0, keepdims=True)
    attended = attended.T.astype(jnp.bfloat16)
    out_ref[:, :width] = attended[:TILE]
    out_ref[:, width : 2 * width] = attended[TILE:]

    query_grad = jnp.zeros((width, COLUMNS), jnp.float32)
    for item in range(SPAN):
        grad_low = (scores[item] * (grads[item] - row_delta)).astype(jnp.bfloat16)
        query_grad = query_grad + dot(kv_turned[step + item, :width, :], grad_low, (1, 0))
        add(item, 0, dot(grad_low, queries, (1, 0)))
    query_grad = (query_grad * SCORE_SCALE).T.astype(jnp.bfloat16)
    out_ref[:, 2 * width : 3 * width] = query_grad[:TILE]
    out_ref[:, 3 * width :] = query_grad[TILE:]

    @pl.when(step == TILES - 1)
    def _():
        sums[:, :, :width] = sums[:, :, :width] * SCORE_SCALE
        low_sums[...] = sums[:MEMBERS].astype(jnp.bfloat16)
        pairs = []
        for item in range(MEMBERS):
            half, part, chunk = item // HALF, item % HALF, member ^ item
            pairs.append((low_sums.at[chunk], earlier_grads[half].at[part]))
            pairs.append((sums.at[MEMBERS + chunk], own_grads[half].at[part]))
        run(copies_of(pairs, semaphores))


def attention(place, doc_lengths, rows, own, earlier):
    width = HEAD_WIDTH
    products = 5 * 2 * WINDOW_LENGTH * 2 * SPAN * TILE * width
    half = (HALF, ROWS, 2 * width)
    outputs = pl.pallas_call(
        attention_kernel,
        grid=(TILES,),
        in_specs=[SCALARS, SCALARS, pl.BlockSpec((TILE, 4 * width), lambda i: (i, 0))]
        + [ANYWHERE] * 4,
        out_specs=[pl.BlockSpec((TILE, 4 * width), lambda i: (i, 0))] + [ANYWHERE] * 4,
        out_shape=[jax.ShapeDtypeStruct(rows.shape, jnp.bfloat16)]
        + [jax.ShapeDtypeStruct(half, jnp.float32)] * 2
        + [jax.ShapeDtypeStruct(half, jnp.bfloat16)] * 2,
        scratch_shapes=[
            pltpu.VMEM((2 * MEMBERS, ROWS, 2 * width), jnp.bfloat16),
            pltpu.VMEM((2 * TILES, 2 * width, TILE), jnp.bfloat16),
            pltpu.VMEM((SPAN, TILE, COLUMNS), jnp.float32),
            pltpu.VMEM((SPAN, TILE, COLUMNS), jnp.float32),
            pltpu.VMEM((2 * MEMBERS, ROWS, 2 * width), jnp.float32),
            pltpu.VMEM((MEMBERS, ROWS, 2 * width), jnp.bfloat16),
            pltpu.SemaphoreType.DMA((2 * MEMBERS,)),
        ],
        compiler_params=VMEM_LIMIT,
        cost_estimate=pl.CostEstimate(
            flops=2 * products, bytes_accessed=WINDOW_LENGTH * width * 30, transcendentals=0
        ),
    )(place, doc_lengths, rows, *own, *earlier)
    return outputs[0], outputs[1:3], outputs[3:5]


def by_head(block):
    return block.reshape(ROWS, MEMBERS, block.shape[1] // MEMBERS).transpose(1, 0, 2)


def by_token(blocks):
    return blocks.transpose(1, 0, 2).reshape(ROWS, MEMBERS * blocks.shape[2])


def exchanged(blocks):
    return lax.all_to_all(blocks, "member", split_axis=0, concat_axis=0, tiled=True)


def swapped(piece, distance):
    if distance == 0:
        return piece
    return lax.ppermute(piece, "member", [(i, i ^ distance) for i in range(MEMBERS)])


def onward(block, direction):
    lower = [(i, i + 1) for i in range(lax.axis_size("stretch") - 1)]
    route = lower if direction > 0 else [(j, i) for i, j in lower]
    return lax.ppermute(block, "stretch", route)


def shards(rotated_query_rows, rotated_key_rows, value_matrix, output_gradient, doc_lengths):
    member = lax.axis_index("member")
    start = lax.axis_index("stretch") * WINDOW_LENGTH
    place = jnp.stack([member, start]).astype(jnp.int32)
    pieces = pack(place, rotated_key_rows, value_matrix)
    pieces = [swapped(piece, item) for item, piece in enumerate(pieces)]
    rows = jnp.concatenate([by_head(rotated_query_rows), by_head(output_gradient)], axis=2)
    first, rows = lax.optimization_barrier((pieces[MEMBERS - 2 :], rows))
    pieces = pieces[: MEMBERS - 2] + first
    own = [jnp.stack(pieces[:HALF]), jnp.stack(pieces[HALF:])]
    earlier = [onward(half, 1) for half in own]
    rows = exchanged(rows).reshape(WINDOW_LENGTH, 4 * HEAD_WIDTH)
    results, own_grads, earlier_grads = attention(place, doc_lengths, rows, own, earlier)
    results = exchanged(results.reshape(MEMBERS, ROWS, 4 * HEAD_WIDTH))
    heavy = onward(earlier_grads[1], -1)
    heavy, light = lax.optimization_barrier((heavy, earlier_grads[0]))
    later = [onward(light, -1), heavy]
    pieces = [
        (own_grads[item // HALF][item % HALF] + later[item // HALF][item % HALF]).astype(
            jnp.bfloat16
        )
        for item in range(MEMBERS)
    ]
    pieces = [swapped(piece, item) for item, piece in enumerate(pieces)]
    key_gradient, value_gradient = unpack(place, pieces)
    return (
        by_token(results[:, :, : 2 * HEAD_WIDTH]),
        by_token(results[:, :, 2 * HEAD_WIDTH :]),
        key_gradient,
        value_gradient,
    )


def solution(mesh):
    grouped = Mesh(mesh.devices.reshape(-1, MEMBERS), ("stretch", "member"))
    spread = P(("stretch", "member"), None)
    return jax.shard_map(
        shards,
        mesh=grouped,
        in_specs=(spread, spread, spread, spread, P()),
        out_specs=(spread, spread, spread, spread),
        check_vma=False,
    )
```

```python
import jax
import jax.numpy as jnp
from jax import lax
from jax.experimental import pallas as pl
from jax.experimental.pallas import tpu as pltpu
from jax.sharding import Mesh
from jax.sharding import PartitionSpec as P

HEAD_WIDTH = 256
WINDOW_LENGTH = 1024
MEMBERS = 8
HALF = MEMBERS // 2
ORDER = (6, 7, 4, 2, 5, 3, 1, 0)

TILE = 256
TILES = WINDOW_LENGTH // TILE
SPAN = TILES + 1
ROWS = WINDOW_LENGTH // MEMBERS
CHUNKS = TILE // ROWS
COLUMNS = 2 * TILE
SCORE_SCALE = HEAD_WIDTH ** (-0.5)
LOG2_E = 1.4426950408889634

ANYWHERE = pl.BlockSpec(memory_space=pl.ANY)
SCALARS = pl.BlockSpec(memory_space=pltpu.SMEM)
VMEM_LIMIT = pltpu.CompilerParams(vmem_limit_bytes=64 * 1024 * 1024)


def dot(left, right, contract):
    return lax.dot_general(
        left, right, ((contract[:1], contract[1:]), ((), ())), preferred_element_type=jnp.float32
    )


def whole(shape):
    return pl.BlockSpec(shape, lambda *_: (0,) * len(shape))


def copies_of(pairs, semaphores):
    return [
        pltpu.make_async_copy(source, target, semaphores.at[item])
        for item, (source, target) in enumerate(pairs)
    ]


def run(copies):
    for copy in copies:
        copy.start()
    for copy in copies:
        copy.wait()


def columns_of(ref, head, width):
    return ref.at[:, pl.ds(pl.multiple_of(head * width, width), width)]


def pack_kernel(left_ref, right_ref, *refs):
    pieces, semaphores = refs[:-1], refs[-1]
    width = left_ref.shape[1] // MEMBERS
    member = lax.axis_index("member")
    pairs = []
    for item, piece in enumerate(pieces):
        head = member ^ item
        pairs.append((columns_of(left_ref, head, width), piece.at[:, pl.ds(0, width)]))
        pairs.append((columns_of(right_ref, head, width), piece.at[:, pl.ds(width, width)]))
    run(copies_of(pairs, semaphores))


def pack(left, right):
    rows, columns = left.shape
    piece = jax.ShapeDtypeStruct((rows, 2 * columns // MEMBERS), left.dtype)
    return pl.pallas_call(
        pack_kernel,
        in_specs=[whole(left.shape), whole(right.shape)],
        out_specs=[ANYWHERE] * MEMBERS,
        out_shape=[piece] * MEMBERS,
        scratch_shapes=[pltpu.SemaphoreType.DMA((2 * MEMBERS,))],
        compiler_params=VMEM_LIMIT,
        cost_estimate=pl.CostEstimate(
            flops=0, bytes_accessed=8 * rows * columns, transcendentals=0
        ),
    )(left, right)


def unpack_kernel(*refs):
    pieces, (left_ref, right_ref, semaphores) = refs[:MEMBERS], refs[MEMBERS:]
    width = left_ref.shape[1] // MEMBERS
    member = lax.axis_index("member")
    pairs = []
    for item, piece in zip(ORDER, pieces):
        head = member ^ item
        pairs.append((piece.at[:, pl.ds(0, width)], columns_of(left_ref, head, width)))
        pairs.append((piece.at[:, pl.ds(width, width)], columns_of(right_ref, head, width)))
    run(copies_of(pairs, semaphores))


def unpack(pieces):
    rows, columns = pieces[0].shape
    shape = (rows, MEMBERS * columns // 2)
    return pl.pallas_call(
        unpack_kernel,
        in_specs=[ANYWHERE] * MEMBERS,
        out_specs=[whole(shape)] * 2,
        out_shape=[jax.ShapeDtypeStruct(shape, pieces[0].dtype)] * 2,
        scratch_shapes=[pltpu.SemaphoreType.DMA((2 * MEMBERS,))],
        compiler_params=VMEM_LIMIT,
        cost_estimate=pl.CostEstimate(
            flops=0, bytes_accessed=4 * MEMBERS * rows * columns, transcendentals=0
        ),
    )(*[pieces[item] for item in ORDER])


def attention_kernel(lengths_ref, *refs):
    row_pieces, refs = refs[:MEMBERS], refs[MEMBERS:]
    own_halves, earlier_halves, refs = refs[:2], refs[2:4], refs[4:]
    result_pieces, refs = refs[:MEMBERS], refs[MEMBERS:]
    own_grads, earlier_grads, refs = refs[:2], refs[2:4], refs[4:]
    rows, results, kv, kv_turned, scores, grads, sums, low_sums, semaphores, row_marks, sent = refs
    step = pl.program_id(0)
    width = HEAD_WIDTH
    member = lax.axis_index("member")
    chunks = pl.ds(step * CHUNKS, CHUNKS)
    chunk_of = [member ^ item for item in range(MEMBERS)]
    arriving_chunks = [member ^ item for item in ORDER]
    arriving = copies_of(
        [(piece, rows.at[chunk]) for piece, chunk in zip(row_pieces, arriving_chunks)], row_marks
    )
    leaving = copies_of(
        [(results.at[chunk], piece) for piece, chunk in zip(result_pieces, chunk_of)], sent
    )

    @pl.when(step == 0)
    def _():
        for copy in arriving:
            copy.start()
        pairs = []
        for item in range(MEMBERS):
            half, part, chunk = item // HALF, item % HALF, chunk_of[item]
            pairs.append((earlier_halves[half].at[part], kv.at[chunk]))
            pairs.append((own_halves[half].at[part], kv.at[MEMBERS + chunk]))
        copies = copies_of(pairs, semaphores)
        for copy in copies:
            copy.start()
        sums[...] = jnp.zeros_like(sums)
        for copy in copies:
            copy.wait()
        for tile in range(2 * TILES):
            part = kv[tile * CHUNKS : (tile + 1) * CHUNKS].reshape(TILE, 2 * width)
            kv_turned[tile] = part.T

    for chunk, copy in zip(arriving_chunks, arriving):
        pl.when(chunk // CHUNKS == step)(copy.wait)

    def key_tile(item, first):
        tile = pl.ds((step + item) * CHUNKS, CHUNKS)
        return kv[tile, :, first : first + width].reshape(TILE, width)

    def add(item, first, part):
        tile = pl.ds((step + item) * CHUNKS, CHUNKS)
        sums[tile, :, first : first + width] += part.reshape(CHUNKS, ROWS, width)

    def both(first):
        return jnp.concatenate(
            [
                rows[chunks, :, head * width : (head + 1) * width].reshape(TILE, width)
                for head in (first, first + 1)
            ],
            axis=0,
        )

    def put(first, part):
        part = part.T.astype(jnp.bfloat16).reshape(2 * CHUNKS, ROWS, width)
        results[chunks, :, first : first + width] = part[:CHUNKS]
        results[chunks, :, first + width : first + 2 * width] = part[CHUNKS:]

    queries = both(0)
    cotangents = both(2)

    first_row = lax.axis_index("stretch") * WINDOW_LENGTH + step * TILE
    row = lax.broadcasted_iota(jnp.int32, (1, COLUMNS), 1) % TILE
    oldest = row - (WINDOW_LENGTH - 1)

    def passed(item, carried):
        begin, oldest = carried
        near = begin - first_row
        oldest = jnp.where(near <= row, jnp.maximum(oldest, near), oldest)
        return begin + lengths_ref[item], oldest

    _, oldest = lax.fori_loop(0, lengths_ref.shape[0], passed, (jnp.int32(0), oldest))
    key_row = lax.broadcasted_iota(jnp.int32, (TILE, COLUMNS), 0)

    top = jnp.full((1, COLUMNS), -jnp.inf, jnp.float32)
    for item in range(SPAN):
        place = (item - TILES) * TILE
        tile_scores = dot(key_tile(item, 0), queries, (1, 1))
        seen = key_row >= oldest - place
        if item == TILES:
            seen = seen & (key_row <= row)
        tile_scores = jnp.where(seen, tile_scores, -jnp.inf)
        top = jnp.maximum(top, jnp.max(tile_scores, axis=0, keepdims=True))
        scores[item] = tile_scores

    total = jnp.zeros((1, COLUMNS), jnp.float32)
    for item in range(SPAN):
        weights = jnp.exp2((scores[item] - top) * (SCORE_SCALE * LOG2_E))
        total = total + jnp.sum(weights, axis=0, keepdims=True)
        scores[item] = weights
    share = 1.0 / total

    attended = jnp.zeros((width, COLUMNS), jnp.float32)
    for item in range(SPAN):
        probs = scores[item] * share
        scores[item] = probs
        probs_low = probs.astype(jnp.bfloat16)
        attended = attended + dot(kv_turned[step + item, width:, :], probs_low, (1, 0))
        add(item, width, dot(probs_low, cotangents, (1, 0)))
        grads[item] = dot(key_tile(item, width), cotangents, (1, 1))
    attended = attended.astype(jnp.bfloat16).astype(jnp.float32)
    turned = cotangents.astype(jnp.float32).T
    row_delta = jnp.sum(attended * turned, axis=0, keepdims=True)
    put(0, attended)

    query_grad = jnp.zeros((width, COLUMNS), jnp.float32)
    for item in range(SPAN):
        grad_low = (scores[item] * (grads[item] - row_delta)).astype(jnp.bfloat16)
        query_grad = query_grad + dot(kv_turned[step + item, :width, :], grad_low, (1, 0))
        add(item, 0, dot(grad_low, queries, (1, 0)))
    put(2 * width, query_grad * SCORE_SCALE)

    for chunk, copy in zip(chunk_of, leaving):
        pl.when(chunk // CHUNKS == step)(copy.start)

    @pl.when(step == TILES - 1)
    def _():
        sums[:, :, :width] = sums[:, :, :width] * SCORE_SCALE
        low_sums[...] = sums[:MEMBERS].astype(jnp.bfloat16)
        pairs = []
        for item in range(MEMBERS):
            half, part, chunk = item // HALF, item % HALF, chunk_of[item]
            pairs.append((low_sums.at[chunk], earlier_grads[half].at[part]))
            pairs.append((sums.at[MEMBERS + chunk], own_grads[half].at[part]))
        run(copies_of(pairs, semaphores))
        for copy in leaving:
            copy.wait()


def attention(doc_lengths, row_pieces, own, earlier):
    width = HEAD_WIDTH
    products = 5 * 2 * WINDOW_LENGTH * 2 * SPAN * TILE * width
    half = (HALF, ROWS, 2 * width)
    outputs = pl.pallas_call(
        attention_kernel,
        grid=(TILES,),
        in_specs=[SCALARS] + [ANYWHERE] * (MEMBERS + 4),
        out_specs=[ANYWHERE] * (MEMBERS + 4),
        out_shape=[jax.ShapeDtypeStruct((ROWS, 4 * width), jnp.bfloat16)] * MEMBERS
        + [jax.ShapeDtypeStruct(half, jnp.float32)] * 2
        + [jax.ShapeDtypeStruct(half, jnp.bfloat16)] * 2,
        scratch_shapes=[
            pltpu.VMEM((MEMBERS, ROWS, 4 * width), jnp.bfloat16),
            pltpu.VMEM((MEMBERS, ROWS, 4 * width), jnp.bfloat16),
            pltpu.VMEM((2 * MEMBERS, ROWS, 2 * width), jnp.bfloat16),
            pltpu.VMEM((2 * TILES, 2 * width, TILE), jnp.bfloat16),
            pltpu.VMEM((SPAN, TILE, COLUMNS), jnp.float32),
            pltpu.VMEM((SPAN, TILE, COLUMNS), jnp.float32),
            pltpu.VMEM((2 * MEMBERS, ROWS, 2 * width), jnp.float32),
            pltpu.VMEM((MEMBERS, ROWS, 2 * width), jnp.bfloat16),
            pltpu.SemaphoreType.DMA((2 * MEMBERS,)),
            pltpu.SemaphoreType.DMA((MEMBERS,)),
            pltpu.SemaphoreType.DMA((MEMBERS,)),
        ],
        compiler_params=VMEM_LIMIT,
        cost_estimate=pl.CostEstimate(
            flops=2 * products, bytes_accessed=WINDOW_LENGTH * width * 30, transcendentals=0
        ),
    )(doc_lengths, *[row_pieces[item] for item in ORDER], *own, *earlier)
    return outputs[:MEMBERS], outputs[MEMBERS : MEMBERS + 2], outputs[MEMBERS + 2 :]


def swapped(pieces):
    moved = {0: pieces[0]}
    for item in ORDER[:-1]:
        route = [(i, i ^ item) for i in range(MEMBERS)]
        moved[item] = lax.ppermute(pieces[item], "member", route)
    return [moved[item] for item in range(MEMBERS)]


def onward(block, direction):
    lower = [(i, i + 1) for i in range(lax.axis_size("stretch") - 1)]
    route = lower if direction > 0 else [(j, i) for i, j in lower]
    return lax.ppermute(block, "stretch", route)


def shards(rotated_query_rows, rotated_key_rows, value_matrix, output_gradient, doc_lengths):
    pieces = pack(rotated_key_rows, value_matrix)
    pieces, rotated_query_rows, output_gradient = lax.optimization_barrier(
        (pieces, rotated_query_rows, output_gradient)
    )
    pieces = swapped(pieces)
    own = [jnp.stack(pieces[:HALF]), jnp.stack(pieces[HALF:])]
    earlier = [onward(half, 1) for half in own]
    pieces = swapped(pack(rotated_query_rows, output_gradient))
    results, own_grads, earlier_grads = attention(doc_lengths, pieces, own, earlier)
    later = [onward(half, -1) for half in earlier_grads]
    results = swapped(results)
    pieces = [
        (own_grads[item // HALF][item % HALF] + later[item // HALF][item % HALF]).astype(
            jnp.bfloat16
        )
        for item in range(MEMBERS)
    ]
    pieces = swapped(pieces)
    return (*unpack(results), *unpack(pieces))


def solution(mesh):
    grouped = Mesh(mesh.devices.reshape(-1, MEMBERS), ("stretch", "member"))
    spread = P(("stretch", "member"), None)
    return jax.shard_map(
        shards,
        mesh=grouped,
        in_specs=(spread, spread, spread, spread, P()),
        out_specs=(spread, spread, spread, spread),
        check_vma=False,
    )
```

```python
import jax
import jax.numpy as jnp
from jax import lax
from jax.experimental import pallas as pl
from jax.experimental.pallas import tpu as pltpu
from jax.sharding import Mesh
from jax.sharding import PartitionSpec as P

HEAD_WIDTH = 256
WINDOW_LENGTH = 1024
MEMBERS = 8
ORDER = (6, 7, 4, 2, 5, 3, 1, 0)

TILE = 256
TILES = WINDOW_LENGTH // TILE
SPAN = TILES + 1
ROWS = WINDOW_LENGTH // MEMBERS
CHUNKS = TILE // ROWS
COLUMNS = 2 * TILE
SCORE_SCALE = HEAD_WIDTH ** (-0.5)
LOG2_E = 1.4426950408889634

ANYWHERE = pl.BlockSpec(memory_space=pl.ANY)
SCALARS = pl.BlockSpec(memory_space=pltpu.SMEM)
VMEM_LIMIT = pltpu.CompilerParams(vmem_limit_bytes=64 * 1024 * 1024)


def dot(left, right, contract):
    return lax.dot_general(
        left, right, ((contract[:1], contract[1:]), ((), ())), preferred_element_type=jnp.float32
    )


def whole(shape):
    return pl.BlockSpec(shape, lambda *_: (0,) * len(shape))


def copies_of(pairs, semaphores):
    return [
        pltpu.make_async_copy(source, target, semaphores.at[item])
        for item, (source, target) in enumerate(pairs)
    ]


def run(copies):
    for copy in copies:
        copy.start()
    for copy in copies:
        copy.wait()


def columns_of(ref, head, width):
    return ref.at[:, pl.ds(pl.multiple_of(head * width, width), width)]


def pack_kernel(left_ref, right_ref, *refs):
    pieces, semaphores = refs[:-1], refs[-1]
    width = left_ref.shape[1] // MEMBERS
    member = lax.axis_index("member")
    pairs = []
    for item, piece in enumerate(pieces):
        head = member ^ item
        pairs.append((columns_of(left_ref, head, width), piece.at[:, pl.ds(0, width)]))
        pairs.append((columns_of(right_ref, head, width), piece.at[:, pl.ds(width, width)]))
    run(copies_of(pairs, semaphores))


def pack(left, right):
    rows, columns = left.shape
    piece = jax.ShapeDtypeStruct((rows, 2 * columns // MEMBERS), left.dtype)
    return pl.pallas_call(
        pack_kernel,
        in_specs=[whole(left.shape), whole(right.shape)],
        out_specs=[ANYWHERE] * MEMBERS,
        out_shape=[piece] * MEMBERS,
        scratch_shapes=[pltpu.SemaphoreType.DMA((2 * MEMBERS,))],
        compiler_params=VMEM_LIMIT,
        cost_estimate=pl.CostEstimate(
            flops=0, bytes_accessed=8 * rows * columns, transcendentals=0
        ),
    )(left, right)


def unpack_kernel(*refs):
    pieces, (left_ref, right_ref, semaphores) = refs[:MEMBERS], refs[MEMBERS:]
    width = left_ref.shape[1] // MEMBERS
    member = lax.axis_index("member")
    pairs = []
    for item, piece in zip(ORDER, pieces):
        head = member ^ item
        pairs.append((piece.at[:, pl.ds(0, width)], columns_of(left_ref, head, width)))
        pairs.append((piece.at[:, pl.ds(width, width)], columns_of(right_ref, head, width)))
    run(copies_of(pairs, semaphores))


def unpack(pieces):
    rows, columns = pieces[0].shape
    shape = (rows, MEMBERS * columns // 2)
    return pl.pallas_call(
        unpack_kernel,
        in_specs=[ANYWHERE] * MEMBERS,
        out_specs=[whole(shape)] * 2,
        out_shape=[jax.ShapeDtypeStruct(shape, pieces[0].dtype)] * 2,
        scratch_shapes=[pltpu.SemaphoreType.DMA((2 * MEMBERS,))],
        compiler_params=VMEM_LIMIT,
        cost_estimate=pl.CostEstimate(
            flops=0, bytes_accessed=4 * MEMBERS * rows * columns, transcendentals=0
        ),
    )(*[pieces[item] for item in ORDER])


def attention_kernel(
    lengths_ref,
    rows_ref,
    own_ref,
    earlier_ref,
    out_ref,
    own_grad_ref,
    earlier_grad_ref,
    kv,
    kv_turned,
    sums,
    low_sums,
    weights,
    grad_weights,
    *refs,
):
    scores, grads, (arrived, sent) = refs[:2], refs[2:4], refs[4:]
    step = pl.program_id(0)
    width = HEAD_WIDTH
    member = lax.axis_index("member")

    def arrival(chunk):
        own = chunk >= MEMBERS
        part = own_ref.at[member ^ (chunk - MEMBERS)] if own else earlier_ref.at[member ^ chunk]
        return pltpu.make_async_copy(part, kv.at[chunk], arrived.at[chunk])

    def turn(tile):
        part = kv[pl.ds(tile * CHUNKS, CHUNKS)].reshape(TILE, 2 * width)
        kv_turned[tile] = part.T

    @pl.when(step == 0)
    def _():
        for chunk in range(2 * MEMBERS):
            arrival(chunk).start()
        sums[: TILES * CHUNKS] = jnp.zeros((TILES * CHUNKS, ROWS, 2 * width), jnp.float32)
        for chunk in range(MEMBERS):
            arrival(chunk).wait()
        for tile in range(TILES):
            turn(tile)

    for part in range(CHUNKS):
        chunk = step * CHUNKS + part
        place = MEMBERS + chunk
        pltpu.make_async_copy(
            own_ref.at[member ^ chunk], kv.at[place], arrived.at[place]
        ).wait()
    turn(TILES + step)

    def key_tile(item, first):
        tile = pl.ds((step + item) * CHUNKS, CHUNKS)
        return kv[tile, :, first : first + width].reshape(TILE, width)

    def add(item, first, part):
        tile = pl.ds((step + item) * CHUNKS, CHUNKS)
        part = part.reshape(CHUNKS, ROWS, width)
        if item < TILES:
            part = sums[tile, :, first : first + width] + part
        sums[tile, :, first : first + width] = part

    queries = [rows_ref[:, head * width : (head + 1) * width] for head in range(2)]
    cotangents = [rows_ref[:, (2 + head) * width : (3 + head) * width] for head in range(2)]
    columns = [slice(head * TILE, (head + 1) * TILE) for head in range(2)]

    first_row = lax.axis_index("stretch") * WINDOW_LENGTH + step * TILE
    row = lax.broadcasted_iota(jnp.int32, (1, TILE), 1)
    oldest = row - (WINDOW_LENGTH - 1)

    def passed(item, carried):
        begin, oldest = carried
        near = begin - first_row
        oldest = jnp.where(near <= row, jnp.maximum(oldest, near), oldest)
        return begin + lengths_ref[item], oldest

    _, oldest = lax.fori_loop(0, lengths_ref.shape[0], passed, (jnp.int32(0), oldest))
    key_row = lax.broadcasted_iota(jnp.int32, (TILE, TILE), 0)

    def make_scores(head):
        top = jnp.full((1, TILE), -jnp.inf, jnp.float32)
        for item in range(SPAN):
            tile_scores = dot(key_tile(item, 0), queries[head], (1, 1))
            seen = key_row >= oldest - (item - TILES) * TILE
            if item == TILES:
                seen = seen & (key_row <= row)
            tile_scores = jnp.where(seen, tile_scores, -jnp.inf)
            top = jnp.maximum(top, jnp.max(tile_scores, axis=0, keepdims=True))
            scores[head][item] = tile_scores
        return top

    def make_weights(head, top):
        total = jnp.zeros((1, TILE), jnp.float32)
        for item in range(SPAN):
            part = jnp.exp2((scores[head][item] - top) * (SCORE_SCALE * LOG2_E))
            total = total + jnp.sum(part, axis=0, keepdims=True)
            weights[item, :, columns[head]] = part.astype(jnp.bfloat16)
        return 1.0 / total

    def make_grads(head):
        for item in range(SPAN):
            grads[head][item] = dot(key_tile(item, width), cotangents[head], (1, 1))

    def put(head, first, part):
        place = slice((first + head) * width, (first + head + 1) * width)
        out_ref[:, place] = part.T.astype(jnp.bfloat16)

    def attend(head, share):
        attended = jnp.zeros((width, TILE), jnp.float32)
        for item in range(SPAN):
            turned = kv_turned[step + item, width:, :]
            attended = attended + dot(turned, weights[item, :, columns[head]], (1, 0))
        attended = (attended * share).astype(jnp.bfloat16).astype(jnp.float32)
        put(head, 0, attended)
        turned = cotangents[head].astype(jnp.float32).T
        return jnp.sum(attended * turned, axis=0, keepdims=True)

    def make_query_grad(head, row_delta, share):
        query_grad = jnp.zeros((width, TILE), jnp.float32)
        for item in range(SPAN):
            part = weights[item, :, columns[head]].astype(jnp.float32)
            part = (part * (grads[head][item] - row_delta)).astype(jnp.bfloat16)
            grad_weights[item, :, columns[head]] = part
            query_grad = query_grad + dot(kv_turned[step + item, :width, :], part, (1, 0))
        put(head, 2, query_grad * (share * SCORE_SCALE))

    def scaled(parts, shares):
        scaled_parts = []
        for part, share in zip(parts, shares):
            down = jnp.broadcast_to(share, (8, TILE)).T[:, :1]
            scaled_parts.append((part.astype(jnp.float32) * down).astype(jnp.bfloat16))
        return jnp.concatenate(scaled_parts, axis=0)

    tops = [make_scores(0), make_scores(1)]
    shares = [make_weights(0, tops[0])]
    make_grads(0)
    shares.append(make_weights(1, tops[1]))
    make_grads(1)
    deltas = [attend(0, shares[0])]
    deltas.append(attend(1, shares[1]))
    make_query_grad(0, deltas[0], shares[0])
    cotangents_scaled = scaled(cotangents, shares)
    for item in range(SPAN):
        add(item, width, dot(weights[item], cotangents_scaled, (1, 0)))
    make_query_grad(1, deltas[1], shares[1])
    queries_scaled = scaled(queries, shares)
    for item in range(SPAN):
        add(item, 0, dot(grad_weights[item], queries_scaled, (1, 0)))

    def departure(step, part):
        chunk = step * CHUNKS + part
        return pltpu.make_async_copy(
            low_sums.at[chunk], earlier_grad_ref.at[member ^ chunk], sent.at[chunk]
        )

    for part in range(CHUNKS):
        chunk = step * CHUNKS + part
        low_sums[chunk, :, :width] = (sums[chunk, :, :width] * SCORE_SCALE).astype(jnp.bfloat16)
        low_sums[chunk, :, width:] = sums[chunk, :, width:].astype(jnp.bfloat16)
        departure(step, part).start()

    @pl.when(step == TILES - 1)
    def _():
        copies = []
        for chunk in range(MEMBERS):
            place = MEMBERS + chunk
            sums[place, :, :width] = sums[place, :, :width] * SCORE_SCALE
            copies.append(
                pltpu.make_async_copy(
                    sums.at[place], own_grad_ref.at[member ^ chunk], sent.at[place]
                )
            )
            copies[-1].start()
        for earlier_step in range(TILES):
            for part in range(CHUNKS):
                copies.append(departure(earlier_step, part))
        for copy in copies:
            copy.wait()


def attention(doc_lengths, rows, own, earlier):
    width = HEAD_WIDTH
    products = 5 * 2 * WINDOW_LENGTH * 2 * SPAN * TILE * width
    return pl.pallas_call(
        attention_kernel,
        grid=(TILES,),
        in_specs=[
            SCALARS,
            pl.BlockSpec((TILE, 4 * width), lambda i: (i, 0)),
            ANYWHERE,
            ANYWHERE,
        ],
        out_specs=[pl.BlockSpec((TILE, 4 * width), lambda i: (i, 0)), ANYWHERE, ANYWHERE],
        out_shape=[
            jax.ShapeDtypeStruct(rows.shape, jnp.bfloat16),
            jax.ShapeDtypeStruct(own.shape, jnp.float32),
            jax.ShapeDtypeStruct(own.shape, jnp.bfloat16),
        ],
        scratch_shapes=[
            pltpu.VMEM((2 * MEMBERS, ROWS, 2 * width), jnp.bfloat16),
            pltpu.VMEM((2 * TILES, 2 * width, TILE), jnp.bfloat16),
            pltpu.VMEM((2 * MEMBERS, ROWS, 2 * width), jnp.float32),
            pltpu.VMEM((MEMBERS, ROWS, 2 * width), jnp.bfloat16),
            pltpu.VMEM((SPAN, TILE, COLUMNS), jnp.bfloat16),
            pltpu.VMEM((SPAN, TILE, COLUMNS), jnp.bfloat16),
            pltpu.VMEM((SPAN, TILE, TILE), jnp.float32),
            pltpu.VMEM((SPAN, TILE, TILE), jnp.float32),
            pltpu.VMEM((SPAN, TILE, TILE), jnp.float32),
            pltpu.VMEM((SPAN, TILE, TILE), jnp.float32),
            pltpu.SemaphoreType.DMA((2 * MEMBERS,)),
            pltpu.SemaphoreType.DMA((2 * MEMBERS,)),
        ],
        compiler_params=VMEM_LIMIT,
        cost_estimate=pl.CostEstimate(
            flops=2 * products, bytes_accessed=WINDOW_LENGTH * width * 30, transcendentals=0
        ),
    )(doc_lengths, rows, own, earlier)


def by_head(block):
    return block.reshape(ROWS, MEMBERS, block.shape[1] // MEMBERS).transpose(1, 0, 2)


def by_token(blocks):
    return blocks.transpose(1, 0, 2).reshape(ROWS, MEMBERS * blocks.shape[2])


def exchanged(blocks):
    return lax.all_to_all(blocks, "member", split_axis=0, concat_axis=0, tiled=True)


def swapped(pieces):
    moved = {0: pieces[0]}
    for item in ORDER[:-1]:
        route = [(i, i ^ item) for i in range(MEMBERS)]
        moved[item] = lax.ppermute(pieces[item], "member", route)
    return [moved[item] for item in range(MEMBERS)]


def onward(block, direction):
    lower = [(i, i + 1) for i in range(lax.axis_size("stretch") - 1)]
    route = lower if direction > 0 else [(j, i) for i, j in lower]
    return lax.ppermute(block, "stretch", route)


def shards(rotated_query_rows, rotated_key_rows, value_matrix, output_gradient, doc_lengths):
    pieces = swapped(pack(rotated_key_rows, value_matrix))
    rows = jnp.concatenate([by_head(rotated_query_rows), by_head(output_gradient)], axis=2)
    pieces, rows = lax.optimization_barrier((pieces, rows))
    own = jnp.stack(pieces)
    earlier = onward(own, 1)
    rows = exchanged(rows).reshape(WINDOW_LENGTH, 4 * HEAD_WIDTH)
    results, own_grad, earlier_grad = attention(doc_lengths, rows, own, earlier)
    later = onward(earlier_grad, -1)
    results = exchanged(results.reshape(MEMBERS, ROWS, 4 * HEAD_WIDTH))
    attended = by_token(results[:, :, : 2 * HEAD_WIDTH])
    query_grad = by_token(results[:, :, 2 * HEAD_WIDTH :])
    sums = (own_grad + later.astype(jnp.float32)).astype(jnp.bfloat16)
    pieces = swapped([sums[item] for item in range(MEMBERS)])
    attended, query_grad, pieces = lax.optimization_barrier((attended, query_grad, pieces))
    return (attended, query_grad, *unpack(pieces))


def solution(mesh):
    grouped = Mesh(mesh.devices.reshape(-1, MEMBERS), ("stretch", "member"))
    spread = P(("stretch", "member"), None)
    return jax.shard_map(
        shards,
        mesh=grouped,
        in_specs=(spread, spread, spread, spread, P()),
        out_specs=(spread, spread, spread, spread),
        check_vma=False,
    )
```

```python
import jax
import jax.numpy as jnp
from jax import lax
from jax.experimental import pallas as pl
from jax.experimental.pallas import tpu as pltpu
from jax.sharding import Mesh
from jax.sharding import PartitionSpec as P

HEAD_WIDTH = 256
WINDOW_LENGTH = 1024
MEMBERS = 8
HALF = MEMBERS // 2
FAR = MEMBERS - 1

TILE = 256
TILES = WINDOW_LENGTH // TILE
SPAN = TILES + 1
KEYS = SPAN * TILE
ROWS = WINDOW_LENGTH // MEMBERS
CHUNKS = TILE // ROWS
COLUMNS = 2 * TILE
SCORE_SCALE = HEAD_WIDTH ** (-0.5)
LOG2_E = 1.4426950408889634

ANYWHERE = pl.BlockSpec(memory_space=pl.ANY)
SCALARS = pl.BlockSpec(memory_space=pltpu.SMEM)
VMEM_LIMIT = pltpu.CompilerParams(vmem_limit_bytes=64 * 1024 * 1024)


def dot(left, right, contract):
    return lax.dot_general(
        left, right, ((contract[:1], contract[1:]), ((), ())), preferred_element_type=jnp.float32
    )


def whole(shape):
    return pl.BlockSpec(shape, lambda *_: (0,) * len(shape))


def copies_of(pairs, semaphores):
    return [
        pltpu.make_async_copy(source, target, semaphores.at[item])
        for item, (source, target) in enumerate(pairs)
    ]


def run(copies):
    for copy in copies:
        copy.start()
    for copy in copies:
        copy.wait()


def columns_of(ref, head, width):
    return ref.at[:, pl.ds(pl.multiple_of(head * width, width), width)]


def pack_kernel(left_ref, right_ref, *refs):
    pieces, semaphores = refs[:-1], refs[-1]
    width = left_ref.shape[1] // MEMBERS
    member = lax.axis_index("member")
    pairs = []
    for item, piece in enumerate(pieces):
        head = member ^ (FAR - item)
        pairs.append((columns_of(left_ref, head, width), piece.at[:, pl.ds(0, width)]))
        pairs.append((columns_of(right_ref, head, width), piece.at[:, pl.ds(width, width)]))
    run(copies_of(pairs, semaphores))


def pack(left, right):
    rows, columns = left.shape
    piece = jax.ShapeDtypeStruct((rows, 2 * columns // MEMBERS), left.dtype)
    return pl.pallas_call(
        pack_kernel,
        in_specs=[whole(left.shape), whole(right.shape)],
        out_specs=[ANYWHERE] * MEMBERS,
        out_shape=[piece] * MEMBERS,
        scratch_shapes=[pltpu.SemaphoreType.DMA((2 * MEMBERS,))],
        compiler_params=VMEM_LIMIT,
        cost_estimate=pl.CostEstimate(
            flops=0, bytes_accessed=8 * rows * columns, transcendentals=0
        ),
    )(left, right)


def unpack_kernel(*refs):
    pieces, (left_ref, right_ref, semaphores) = refs[:MEMBERS], refs[MEMBERS:]
    width = left_ref.shape[1] // MEMBERS
    member = lax.axis_index("member")
    pairs = []
    for item, piece in enumerate(pieces):
        head = member ^ (FAR - item)
        pairs.append((piece.at[:, pl.ds(0, width)], columns_of(left_ref, head, width)))
        pairs.append((piece.at[:, pl.ds(width, width)], columns_of(right_ref, head, width)))
    run(copies_of(pairs, semaphores))


def unpack(pieces):
    rows, columns = pieces[0].shape
    shape = (rows, MEMBERS * columns // 2)
    return pl.pallas_call(
        unpack_kernel,
        in_specs=[ANYWHERE] * MEMBERS,
        out_specs=[whole(shape)] * 2,
        out_shape=[jax.ShapeDtypeStruct(shape, pieces[0].dtype)] * 2,
        scratch_shapes=[pltpu.SemaphoreType.DMA((2 * MEMBERS,))],
        compiler_params=VMEM_LIMIT,
        cost_estimate=pl.CostEstimate(
            flops=0, bytes_accessed=4 * MEMBERS * rows * columns, transcendentals=0
        ),
    )(*pieces)


def attention_kernel(lengths_ref, rows_ref, *refs):
    own_halves, earlier_halves, out_ref, refs = refs[:2], refs[2:4], refs[4], refs[5:]
    own_grads, earlier_grads, refs = refs[:2], refs[2:4], refs[4:]
    kv, kv_turned, sums, low_sums, weights, grad_weights, refs = *refs[:6], refs[6:]
    scores, grads, (arrived, sent) = refs[:2], refs[2:4], refs[4:]
    step = pl.program_id(0)
    width = HEAD_WIDTH
    member = lax.axis_index("member")

    def arrivals():
        pairs = []
        for item in range(MEMBERS):
            half, part, chunk = item // HALF, item % HALF, member ^ (FAR - item)
            pairs.append((earlier_halves[half].at[part], kv.at[chunk], arrived.at[chunk]))
            place = MEMBERS + chunk
            pairs.append((own_halves[half].at[part], kv.at[place], arrived.at[place]))
        return [pltpu.make_async_copy(*pair) for pair in pairs]

    def await_chunk(place):
        pltpu.make_async_copy(own_halves[0].at[0], kv.at[place], arrived.at[place]).wait()

    def turn(tile):
        part = kv[pl.ds(tile * CHUNKS, CHUNKS)].reshape(TILE, 2 * width)
        kv_turned[:, pl.ds(pl.multiple_of(tile * TILE, TILE), TILE)] = part.T

    @pl.when(step == 0)
    def _():
        for copy in arrivals():
            copy.start()
        sums[: TILES * CHUNKS] = jnp.zeros((TILES * CHUNKS, ROWS, 2 * width), jnp.float32)
        for chunk in range(MEMBERS):
            await_chunk(chunk)
        for tile in range(TILES):
            turn(tile)

    for part in range(CHUNKS):
        await_chunk(MEMBERS + step * CHUNKS + part)
    turn(TILES + step)

    def window(first):
        part = kv[pl.ds(step * CHUNKS, SPAN * CHUNKS), :, first : first + width]
        return part.reshape(KEYS, width)

    def turned_window(first):
        place = pl.ds(pl.multiple_of(step * TILE, TILE), KEYS)
        return kv_turned[first : first + width, place]

    def add(first, part):
        part = part.reshape(SPAN * CHUNKS, ROWS, width)
        known = TILES * CHUNKS
        old = pl.ds(step * CHUNKS, known)
        sums[old, :, first : first + width] += part[:known]
        new = pl.ds(step * CHUNKS + known, CHUNKS)
        sums[new, :, first : first + width] = part[known:]

    queries = [rows_ref[:, head * width : (head + 1) * width] for head in range(2)]
    cotangents = [rows_ref[:, (2 + head) * width : (3 + head) * width] for head in range(2)]
    columns = [slice(head * TILE, (head + 1) * TILE) for head in range(2)]
    tiles = [slice(item * TILE, (item + 1) * TILE) for item in range(SPAN)]

    first_row = lax.axis_index("stretch") * WINDOW_LENGTH + step * TILE
    row = lax.broadcasted_iota(jnp.int32, (1, TILE), 1)
    oldest = row - (WINDOW_LENGTH - 1)

    def passed(item, carried):
        begin, oldest = carried
        near = begin - first_row
        oldest = jnp.where(near <= row, jnp.maximum(oldest, near), oldest)
        return begin + lengths_ref[item], oldest

    _, oldest = lax.fori_loop(0, lengths_ref.shape[0], passed, (jnp.int32(0), oldest))
    key_row = lax.broadcasted_iota(jnp.int32, (TILE, TILE), 0)

    def seen(item):
        visible = key_row >= oldest - (item - TILES) * TILE
        return visible & (key_row <= row) if item == TILES else visible

    def make_scores(head):
        scores[head][...] = dot(window(0), queries[head], (1, 1))

    def make_weights(head):
        top = jnp.full((1, TILE), -jnp.inf, jnp.float32)
        for item, tile in enumerate(tiles):
            part = jnp.where(seen(item), scores[head][tile], -jnp.inf)
            top = jnp.maximum(top, jnp.max(part, axis=0, keepdims=True))
        total = jnp.zeros((1, TILE), jnp.float32)
        for item, tile in enumerate(tiles):
            part = jnp.exp2((scores[head][tile] - top) * (SCORE_SCALE * LOG2_E))
            part = jnp.where(seen(item), part, 0.0)
            total = total + jnp.sum(part, axis=0, keepdims=True)
            weights[tile, columns[head]] = part.astype(jnp.bfloat16)
        return 1.0 / total

    def make_grads(head):
        grads[head][...] = dot(window(width), cotangents[head], (1, 1))

    def put(head, first, part):
        place = slice((first + head) * width, (first + head + 1) * width)
        out_ref[:, place] = part.T.astype(jnp.bfloat16)

    def attend(head, share):
        attended = dot(turned_window(width), weights[:, columns[head]], (1, 0))
        attended = (attended * share).astype(jnp.bfloat16).astype(jnp.float32)
        put(head, 0, attended)
        turned = cotangents[head].astype(jnp.float32).T
        return jnp.sum(attended * turned, axis=0, keepdims=True)

    def weigh_grads(head, row_delta):
        for tile in tiles:
            part = weights[tile, columns[head]].astype(jnp.float32)
            part = (part * (grads[head][tile] - row_delta)).astype(jnp.bfloat16)
            grad_weights[tile, columns[head]] = part

    def make_query_grad(head, share):
        query_grad = dot(turned_window(0), grad_weights[:, columns[head]], (1, 0))
        put(head, 2, query_grad * (share * SCORE_SCALE))

    def scaled(parts, shares):
        scaled_parts = []
        for part, share in zip(parts, shares):
            down = jnp.broadcast_to(share, (8, TILE)).T[:, :1]
            scaled_parts.append((part.astype(jnp.float32) * down).astype(jnp.bfloat16))
        return jnp.concatenate(scaled_parts, axis=0)

    make_scores(0)
    make_scores(1)
    shares = [make_weights(0)]
    make_grads(0)
    shares.append(make_weights(1))
    make_grads(1)
    deltas = [attend(0, shares[0])]
    deltas.append(attend(1, shares[1]))
    weigh_grads(0, deltas[0])
    add(width, dot(weights[...], scaled(cotangents, shares), (1, 0)))
    make_query_grad(0, shares[0])
    weigh_grads(1, deltas[1])
    make_query_grad(1, shares[1])
    add(0, dot(grad_weights[...], scaled(queries, shares), (1, 0)))

    def departures():
        pairs = []
        for item in range(MEMBERS):
            half, part, chunk = item // HALF, item % HALF, member ^ (FAR - item)
            target = earlier_grads[half].at[part]
            pairs.append((chunk, (low_sums.at[chunk], target, sent.at[chunk])))
        return [(chunk, pltpu.make_async_copy(*pair)) for chunk, pair in pairs]

    for part in range(CHUNKS):
        chunk = step * CHUNKS + part
        low_sums[chunk, :, :width] = (sums[chunk, :, :width] * SCORE_SCALE).astype(jnp.bfloat16)
        low_sums[chunk, :, width:] = sums[chunk, :, width:].astype(jnp.bfloat16)
    for chunk, copy in departures():
        pl.when(chunk // CHUNKS == step)(copy.start)

    @pl.when(step == TILES - 1)
    def _():
        copies = [copy for _, copy in departures()]
        for chunk in range(MEMBERS, 2 * MEMBERS):
            sums[chunk, :, :width] = sums[chunk, :, :width] * SCORE_SCALE
        for item in range(MEMBERS):
            half, part, place = item // HALF, item % HALF, MEMBERS + (member ^ (FAR - item))
            target = own_grads[half].at[part]
            copies.append(pltpu.make_async_copy(sums.at[place], target, sent.at[place]))
            copies[-1].start()
        for copy in copies:
            copy.wait()


def attention(doc_lengths, rows, own, earlier):
    width = HEAD_WIDTH
    products = 6 * 2 * WINDOW_LENGTH * 2 * KEYS * width
    half = (HALF, ROWS, 2 * width)
    outputs = pl.pallas_call(
        attention_kernel,
        grid=(TILES,),
        in_specs=[SCALARS, pl.BlockSpec((TILE, 4 * width), lambda i: (i, 0))] + [ANYWHERE] * 4,
        out_specs=[pl.BlockSpec((TILE, 4 * width), lambda i: (i, 0))] + [ANYWHERE] * 4,
        out_shape=[jax.ShapeDtypeStruct(rows.shape, jnp.bfloat16)]
        + [jax.ShapeDtypeStruct(half, jnp.float32)] * 2
        + [jax.ShapeDtypeStruct(half, jnp.bfloat16)] * 2,
        scratch_shapes=[
            pltpu.VMEM((2 * MEMBERS, ROWS, 2 * width), jnp.bfloat16),
            pltpu.VMEM((2 * width, 2 * WINDOW_LENGTH), jnp.bfloat16),
            pltpu.VMEM((2 * MEMBERS, ROWS, 2 * width), jnp.float32),
            pltpu.VMEM((MEMBERS, ROWS, 2 * width), jnp.bfloat16),
            pltpu.VMEM((KEYS, COLUMNS), jnp.bfloat16),
            pltpu.VMEM((KEYS, COLUMNS), jnp.bfloat16),
            pltpu.VMEM((KEYS, TILE), jnp.float32),
            pltpu.VMEM((KEYS, TILE), jnp.float32),
            pltpu.VMEM((KEYS, TILE), jnp.float32),
            pltpu.VMEM((KEYS, TILE), jnp.float32),
            pltpu.SemaphoreType.DMA((2 * MEMBERS,)),
            pltpu.SemaphoreType.DMA((2 * MEMBERS,)),
        ],
        compiler_params=VMEM_LIMIT,
        cost_estimate=pl.CostEstimate(
            flops=2 * products, bytes_accessed=WINDOW_LENGTH * width * 30, transcendentals=0
        ),
    )(doc_lengths, rows, *own, *earlier)
    return outputs[0], outputs[1:3], outputs[3:]


def by_head(block):
    return block.reshape(ROWS, MEMBERS, block.shape[1] // MEMBERS).transpose(1, 0, 2)


def by_token(blocks):
    return blocks.transpose(1, 0, 2).reshape(ROWS, MEMBERS * blocks.shape[2])


def exchanged(blocks):
    return lax.all_to_all(blocks, "member", split_axis=0, concat_axis=0, tiled=True)


def swapped(pieces):
    moved = []
    for item in range(FAR):
        route = [(i, i ^ (FAR - item)) for i in range(MEMBERS)]
        moved.append(lax.ppermute(pieces[item], "member", route))
    return moved + [pieces[FAR]]


def onward(block, direction):
    lower = [(i, i + 1) for i in range(lax.axis_size("stretch") - 1)]
    route = lower if direction > 0 else [(j, i) for i, j in lower]
    return lax.ppermute(block, "stretch", route)


def shards(rotated_query_rows, rotated_key_rows, value_matrix, output_gradient, doc_lengths):
    pieces = swapped(pack(rotated_key_rows, value_matrix))
    rows = jnp.concatenate([by_head(rotated_query_rows), by_head(output_gradient)], axis=2)
    pieces, rows = lax.optimization_barrier((pieces, rows))
    own = [jnp.stack(pieces[:HALF]), jnp.stack(pieces[HALF:])]
    earlier = [onward(half, 1) for half in own]
    rows = exchanged(rows).reshape(WINDOW_LENGTH, 4 * HEAD_WIDTH)
    results, own_grads, earlier_grads = attention(doc_lengths, rows, own, earlier)
    later = [onward(half, -1) for half in earlier_grads]
    results = exchanged(results.reshape(MEMBERS, ROWS, 4 * HEAD_WIDTH))
    attended = by_token(results[:, :, : 2 * HEAD_WIDTH])
    query_grad = by_token(results[:, :, 2 * HEAD_WIDTH :])
    sums = [
        (own_grads[half] + later[half].astype(jnp.float32)).astype(jnp.bfloat16)
        for half in range(2)
    ]
    pieces = swapped([sums[item // HALF][item % HALF] for item in range(MEMBERS)])
    attended, query_grad, pieces = lax.optimization_barrier((attended, query_grad, pieces))
    return (attended, query_grad, *unpack(pieces))


def solution(mesh):
    grouped = Mesh(mesh.devices.reshape(-1, MEMBERS), ("stretch", "member"))
    spread = P(("stretch", "member"), None)
    return jax.shard_map(
        shards,
        mesh=grouped,
        in_specs=(spread, spread, spread, spread, P()),
        out_specs=(spread, spread, spread, spread),
        check_vma=False,
    )
```

```python
import jax
import jax.numpy as jnp
from jax import lax
from jax.experimental import pallas as pl
from jax.experimental.pallas import tpu as pltpu
from jax.sharding import Mesh
from jax.sharding import PartitionSpec as P

HEAD_WIDTH = 256
WINDOW_LENGTH = 1024
MEMBERS = 8
HALF = MEMBERS // 2
FAR = MEMBERS - 1

TILE = 256
TILES = WINDOW_LENGTH // TILE
SPAN = TILES + 1
KEYS = SPAN * TILE
ROWS = WINDOW_LENGTH // MEMBERS
CHUNKS = TILE // ROWS
COLUMNS = 2 * TILE
SCORE_SCALE = HEAD_WIDTH ** (-0.5)
LOG2_E = 1.4426950408889634

ANYWHERE = pl.BlockSpec(memory_space=pl.ANY)
IN_HBM = pl.BlockSpec(memory_space=pltpu.HBM)
SCALARS = pl.BlockSpec(memory_space=pltpu.SMEM)
VMEM_LIMIT = pltpu.CompilerParams(vmem_limit_bytes=64 * 1024 * 1024)


def dot(left, right, contract):
    return lax.dot_general(
        left, right, ((contract[:1], contract[1:]), ((), ())), preferred_element_type=jnp.float32
    )


def whole(shape):
    return pl.BlockSpec(shape, lambda *_: (0,) * len(shape))


def copies_of(pairs, semaphores):
    return [
        pltpu.make_async_copy(source, target, semaphores.at[item])
        for item, (source, target) in enumerate(pairs)
    ]


def run(copies):
    for copy in copies:
        copy.start()
    for copy in copies:
        copy.wait()


def columns_of(ref, head, width):
    return ref.at[:, pl.ds(pl.multiple_of(head * width, width), width)]


def pack_kernel(left_ref, right_ref, *refs):
    pieces, semaphores = refs[:-1], refs[-1]
    width = left_ref.shape[1] // MEMBERS
    member = lax.axis_index("member")
    pairs = []
    for item, piece in enumerate(pieces):
        head = member ^ (FAR - item)
        pairs.append((columns_of(left_ref, head, width), piece.at[:, pl.ds(0, width)]))
        pairs.append((columns_of(right_ref, head, width), piece.at[:, pl.ds(width, width)]))
    run(copies_of(pairs, semaphores))


def pack(left, right):
    rows, columns = left.shape
    piece = jax.ShapeDtypeStruct((rows, 2 * columns // MEMBERS), left.dtype)
    return pl.pallas_call(
        pack_kernel,
        in_specs=[whole(left.shape), whole(right.shape)],
        out_specs=[ANYWHERE] * MEMBERS,
        out_shape=[piece] * MEMBERS,
        scratch_shapes=[pltpu.SemaphoreType.DMA((2 * MEMBERS,))],
        compiler_params=VMEM_LIMIT,
        cost_estimate=pl.CostEstimate(
            flops=0, bytes_accessed=8 * rows * columns, transcendentals=0
        ),
    )(left, right)


def unpack_kernel(*refs):
    pieces, (left_ref, right_ref, semaphores) = refs[:MEMBERS], refs[MEMBERS:]
    width = left_ref.shape[1] // MEMBERS
    member = lax.axis_index("member")
    pairs = []
    for item, piece in enumerate(pieces):
        head = member ^ (FAR - item)
        pairs.append((piece.at[:, pl.ds(0, width)], columns_of(left_ref, head, width)))
        pairs.append((piece.at[:, pl.ds(width, width)], columns_of(right_ref, head, width)))
    run(copies_of(pairs, semaphores))


def unpack(pieces):
    rows, columns = pieces[0].shape
    shape = (rows, MEMBERS * columns // 2)
    return pl.pallas_call(
        unpack_kernel,
        in_specs=[ANYWHERE] * MEMBERS,
        out_specs=[whole(shape)] * 2,
        out_shape=[jax.ShapeDtypeStruct(shape, pieces[0].dtype)] * 2,
        scratch_shapes=[pltpu.SemaphoreType.DMA((2 * MEMBERS,))],
        compiler_params=VMEM_LIMIT,
        cost_estimate=pl.CostEstimate(
            flops=0, bytes_accessed=4 * MEMBERS * rows * columns, transcendentals=0
        ),
    )(*pieces)


def key_copies(own_halves, earlier_halves, kv, arrived):
    member = lax.axis_index("member")
    copies = []
    for item in range(MEMBERS):
        half, part, chunk = item // HALF, item % HALF, member ^ (FAR - item)
        for halves, place in ((earlier_halves, chunk), (own_halves, MEMBERS + chunk)):
            copies.append(
                pltpu.make_async_copy(halves[half].at[part], kv.at[place], arrived.at[place])
            )
    return copies


def await_keys(step, own_halves, earlier_halves, kv, arrived, turn):
    def await_chunk(place):
        pltpu.make_async_copy(own_halves[0].at[0], kv.at[place], arrived.at[place]).wait()

    @pl.when(step == 0)
    def _():
        for chunk in range(MEMBERS):
            await_chunk(chunk)
        for tile in range(TILES):
            turn(tile)

    for part in range(CHUNKS):
        await_chunk(MEMBERS + step * CHUNKS + part)
    turn(TILES + step)


def key_tile(kv, tile, first):
    chunks = pl.ds(tile * CHUNKS, CHUNKS)
    return kv[chunks, :, first : first + HEAD_WIDTH].reshape(TILE, HEAD_WIDTH)


def add_tile(sums, step, item, part):
    chunks = pl.ds((step + item) * CHUNKS, CHUNKS)
    part = part.reshape(CHUNKS, ROWS, HEAD_WIDTH)
    sums[chunks] = sums[chunks] + part if item < TILES else part


def send_sums(step, scale, sums, low_sums, own_grad, earlier_grad, sent):
    member = lax.axis_index("member")

    def departure(chunk):
        return pltpu.make_async_copy(
            low_sums.at[chunk], earlier_grad.at[FAR - (member ^ chunk)], sent.at[chunk]
        )

    for part in range(CHUNKS):
        chunk = step * CHUNKS + part
        low_sums[chunk] = (sums[chunk] * scale).astype(jnp.bfloat16)
        departure(chunk).start()

    @pl.when(step == TILES - 1)
    def _():
        copies = []
        for chunk in range(MEMBERS):
            place = MEMBERS + chunk
            if scale != 1.0:
                sums[place] = sums[place] * scale
            target = own_grad.at[FAR - (member ^ chunk)]
            copies.append(pltpu.make_async_copy(sums.at[place], target, sent.at[place]))
            copies[-1].start()
        for copy in copies + [departure(chunk) for chunk in range(MEMBERS)]:
            copy.wait()


def heads_of(rows_ref, first):
    return [
        rows_ref[:, head * HEAD_WIDTH : (head + 1) * HEAD_WIDTH] for head in (first, first + 1)
    ]


def turned_heads(parts):
    return jnp.concatenate([part.T for part in parts], axis=1)


def scaled_heads(parts, share):
    scaled = []
    for head, part in enumerate(parts):
        own = share[:, head * TILE : (head + 1) * TILE]
        down = jnp.broadcast_to(own, (8, TILE)).T[:, :1]
        scaled.append((part.astype(jnp.float32) * down).astype(jnp.bfloat16))
    return jnp.concatenate(scaled, axis=0)


def put_heads(out_ref, part):
    part = part.astype(jnp.bfloat16)
    out_ref[:, :HEAD_WIDTH] = part[:, :TILE].T
    out_ref[:, HEAD_WIDTH:] = part[:, TILE:].T


def window_of(turned, step):
    return turned[:, pl.ds(pl.multiple_of(step * TILE, TILE), KEYS)]


def turn_tile(kv, turned, first):
    def turn(tile):
        place = pl.ds(pl.multiple_of(tile * TILE, TILE), TILE)
        turned[:, place] = key_tile(kv, tile, first).T

    return turn


def attended_kernel(lengths_ref, rows_ref, *refs):
    own_halves, earlier_halves, refs = refs[:2], refs[2:4], refs[4:]
    attended_ref, weights_ref, stats_ref, own_grad, earlier_grad = refs[:5]
    kv, turned, sums, low_sums, scores, arrived, sent = refs[5:]
    step = pl.program_id(0)

    @pl.when(step == 0)
    def _():
        for copy in key_copies(own_halves, earlier_halves, kv, arrived):
            copy.start()
        sums[:MEMBERS] = jnp.zeros((MEMBERS, ROWS, HEAD_WIDTH), jnp.float32)

    await_keys(
        step, own_halves, earlier_halves, kv, arrived, turn_tile(kv, turned, HEAD_WIDTH)
    )
    queries = turned_heads(heads_of(rows_ref, 0))
    cotangents = heads_of(rows_ref, 2)

    first_row = lax.axis_index("stretch") * WINDOW_LENGTH + step * TILE
    row = lax.broadcasted_iota(jnp.int32, (1, COLUMNS), 1) % TILE
    oldest = row - (WINDOW_LENGTH - 1)

    def passed(item, carried):
        begin, oldest = carried
        near = begin - first_row
        oldest = jnp.where(near <= row, jnp.maximum(oldest, near), oldest)
        return begin + lengths_ref[item], oldest

    _, oldest = lax.fori_loop(0, lengths_ref.shape[0], passed, (jnp.int32(0), oldest))
    key_row = lax.broadcasted_iota(jnp.int32, (TILE, COLUMNS), 0)

    top = jnp.full((1, COLUMNS), -jnp.inf, jnp.float32)
    for item in range(SPAN):
        part = dot(key_tile(kv, step + item, 0), queries, (1, 0))
        seen = key_row >= oldest - (item - TILES) * TILE
        if item == TILES:
            seen = seen & (key_row <= row)
        part = jnp.where(seen, part, -jnp.inf)
        top = jnp.maximum(top, jnp.max(part, axis=0, keepdims=True))
        scores[item] = part

    total = jnp.zeros((1, COLUMNS), jnp.float32)
    for item in range(SPAN):
        part = jnp.exp2((scores[item] - top) * (SCORE_SCALE * LOG2_E))
        total = total + jnp.sum(part, axis=0, keepdims=True)
        weights_ref[0, item * TILE : (item + 1) * TILE, :] = part.astype(jnp.bfloat16)
    share = 1.0 / total

    attended = dot(window_of(turned, step), weights_ref[0], (1, 0)) * share
    scaled = scaled_heads(cotangents, share)
    for item in range(SPAN):
        part = weights_ref[0, item * TILE : (item + 1) * TILE, :]
        add_tile(sums, step, item, dot(part, scaled, (1, 0)))
    attended = attended.astype(jnp.bfloat16)
    put_heads(attended_ref, attended)
    products = attended.astype(jnp.float32) * turned_heads(cotangents).astype(jnp.float32)
    stats_ref[0, :1, :] = share
    stats_ref[0, 1:2, :] = jnp.sum(products, axis=0, keepdims=True)

    send_sums(step, 1.0, sums, low_sums, own_grad, earlier_grad, sent)


def gradient_kernel(rows_ref, weights_ref, stats_ref, *refs):
    own_halves, earlier_halves, refs = refs[:2], refs[2:4], refs[4:]
    query_grad_ref, own_grad, earlier_grad = refs[:3]
    kv, turned, sums, low_sums, grad_weights, arrived, sent = refs[3:]
    step = pl.program_id(0)

    @pl.when(step == 0)
    def _():
        for copy in key_copies(own_halves, earlier_halves, kv, arrived):
            copy.start()
        sums[:MEMBERS] = jnp.zeros((MEMBERS, ROWS, HEAD_WIDTH), jnp.float32)

    await_keys(step, own_halves, earlier_halves, kv, arrived, turn_tile(kv, turned, 0))
    cotangents = turned_heads(heads_of(rows_ref, 2))
    share = stats_ref[0, :1, :]
    row_delta = stats_ref[0, 1:2, :]
    scaled = scaled_heads(heads_of(rows_ref, 0), share)

    for item in range(SPAN):
        place = slice(item * TILE, (item + 1) * TILE)
        part = dot(key_tile(kv, step + item, HEAD_WIDTH), cotangents, (1, 0)) - row_delta
        part = (weights_ref[0, place, :].astype(jnp.float32) * part).astype(jnp.bfloat16)
        grad_weights[place, :] = part
        add_tile(sums, step, item, dot(part, scaled, (1, 0)))
    query_grad = dot(window_of(turned, step), grad_weights[...], (1, 0))
    put_heads(query_grad_ref, query_grad * (share * SCORE_SCALE))

    send_sums(step, SCORE_SCALE, sums, low_sums, own_grad, earlier_grad, sent)


ROWS_BLOCK = pl.BlockSpec((TILE, 4 * HEAD_WIDTH), lambda i: (i, 0))
HEADS_BLOCK = pl.BlockSpec((TILE, 2 * HEAD_WIDTH), lambda i: (i, 0))
WEIGHTS_BLOCK = pl.BlockSpec((1, KEYS, COLUMNS), lambda i: (i, 0, 0))
STATS_BLOCK = pl.BlockSpec((1, 8, COLUMNS), lambda i: (i, 0, 0))
HEADS_SHAPE = jax.ShapeDtypeStruct((WINDOW_LENGTH, 2 * HEAD_WIDTH), jnp.bfloat16)
GRAD_SHAPES = [
    jax.ShapeDtypeStruct((MEMBERS, ROWS, HEAD_WIDTH), dtype)
    for dtype in (jnp.float32, jnp.bfloat16)
]
KEY_SCRATCH = [
    pltpu.VMEM((2 * MEMBERS, ROWS, 2 * HEAD_WIDTH), jnp.bfloat16),
    pltpu.VMEM((HEAD_WIDTH, 2 * WINDOW_LENGTH), jnp.bfloat16),
    pltpu.VMEM((2 * MEMBERS, ROWS, HEAD_WIDTH), jnp.float32),
    pltpu.VMEM((MEMBERS, ROWS, HEAD_WIDTH), jnp.bfloat16),
]
MARKS = [pltpu.SemaphoreType.DMA((2 * MEMBERS,))] * 2
COST = pl.CostEstimate(
    flops=3 * 2 * WINDOW_LENGTH * 2 * KEYS * HEAD_WIDTH,
    bytes_accessed=12 * 1024 * 1024,
    transcendentals=0,
)


def attended_call(doc_lengths, rows, own, earlier):
    return pl.pallas_call(
        attended_kernel,
        grid=(TILES,),
        in_specs=[SCALARS, ROWS_BLOCK] + [IN_HBM] * 4,
        out_specs=[HEADS_BLOCK, WEIGHTS_BLOCK, STATS_BLOCK] + [IN_HBM] * 2,
        out_shape=[
            HEADS_SHAPE,
            jax.ShapeDtypeStruct((TILES, KEYS, COLUMNS), jnp.bfloat16),
            jax.ShapeDtypeStruct((TILES, 8, COLUMNS), jnp.float32),
        ]
        + GRAD_SHAPES,
        scratch_shapes=KEY_SCRATCH + [pltpu.VMEM((SPAN, TILE, COLUMNS), jnp.float32)] + MARKS,
        compiler_params=VMEM_LIMIT,
        cost_estimate=COST,
    )(doc_lengths, rows, *own, *earlier)


def gradient_call(rows, weights, stats, own, earlier):
    return pl.pallas_call(
        gradient_kernel,
        grid=(TILES,),
        in_specs=[ROWS_BLOCK, WEIGHTS_BLOCK, STATS_BLOCK] + [IN_HBM] * 4,
        out_specs=[HEADS_BLOCK] + [IN_HBM] * 2,
        out_shape=[HEADS_SHAPE] + GRAD_SHAPES,
        scratch_shapes=KEY_SCRATCH + [pltpu.VMEM((KEYS, COLUMNS), jnp.bfloat16)] + MARKS,
        compiler_params=VMEM_LIMIT,
        cost_estimate=COST,
    )(rows, weights, stats, *own, *earlier)


def by_head(block):
    return block.reshape(ROWS, MEMBERS, block.shape[1] // MEMBERS).transpose(1, 0, 2)


def by_token(blocks):
    return blocks.transpose(1, 0, 2).reshape(ROWS, MEMBERS * blocks.shape[2])


def exchanged(blocks):
    return lax.all_to_all(blocks, "member", split_axis=0, concat_axis=0, tiled=True)


def swapped(pieces):
    moved = []
    for item in range(FAR):
        route = [(i, i ^ (FAR - item)) for i in range(MEMBERS)]
        moved.append(lax.ppermute(pieces[item], "member", route))
    return moved + [pieces[FAR]]


def onward(block, direction):
    lower = [(i, i + 1) for i in range(lax.axis_size("stretch") - 1)]
    route = lower if direction > 0 else [(j, i) for i, j in lower]
    return lax.ppermute(block, "stretch", route)


def shards(rotated_query_rows, rotated_key_rows, value_matrix, output_gradient, doc_lengths):
    pieces = swapped(pack(rotated_key_rows, value_matrix))
    rows = jnp.concatenate([by_head(rotated_query_rows), by_head(output_gradient)], axis=2)
    pieces, rows = lax.optimization_barrier((pieces, rows))
    own = [jnp.stack(pieces[:HALF]), jnp.stack(pieces[HALF:])]
    earlier = [onward(half, 1) for half in own]
    rows = exchanged(rows).reshape(WINDOW_LENGTH, 4 * HEAD_WIDTH)
    attended, weights, stats, own_values, earlier_values = attended_call(
        doc_lengths, rows, own, earlier
    )
    later_values = onward(earlier_values, -1)
    attended = by_token(exchanged(attended.reshape(MEMBERS, ROWS, 2 * HEAD_WIDTH)))
    query_grad, own_keys, earlier_keys = gradient_call(rows, weights, stats, own, earlier)
    later_keys = onward(earlier_keys, -1)
    query_grad = by_token(exchanged(query_grad.reshape(MEMBERS, ROWS, 2 * HEAD_WIDTH)))
    sums = jnp.concatenate([own_keys + later_keys, own_values + later_values], axis=2)
    sums = sums.astype(jnp.bfloat16)
    pieces = swapped([sums[item] for item in range(MEMBERS)])
    attended, query_grad, pieces = lax.optimization_barrier((attended, query_grad, pieces))
    return (attended, query_grad, *unpack(pieces))


def solution(mesh):
    grouped = Mesh(mesh.devices.reshape(-1, MEMBERS), ("stretch", "member"))
    spread = P(("stretch", "member"), None)
    return jax.shard_map(
        shards,
        mesh=grouped,
        in_specs=(spread, spread, spread, spread, P()),
        out_specs=(spread, spread, spread, spread),
        check_vma=False,
    )
```

```python
import jax
import jax.numpy as jnp
from jax import lax
from jax.experimental import pallas as pl
from jax.experimental.pallas import tpu as pltpu
from jax.sharding import Mesh
from jax.sharding import PartitionSpec as P

HEAD_WIDTH = 256
WINDOW_LENGTH = 1024
MEMBERS = 8
PAIRS = MEMBERS // 2
FAR = MEMBERS - 1

TILE = 256
TILES = WINDOW_LENGTH // TILE
SPAN = TILES + 1
KEYS = SPAN * TILE
ROWS = WINDOW_LENGTH // MEMBERS
CHUNKS = TILE // ROWS
COLUMNS = 2 * TILE
SCORE_SCALE = HEAD_WIDTH ** (-0.5)
LOG2_E = 1.4426950408889634

ANYWHERE = pl.BlockSpec(memory_space=pl.ANY)
IN_HBM = pl.BlockSpec(memory_space=pltpu.HBM)
SCALARS = pl.BlockSpec(memory_space=pltpu.SMEM)
VMEM_LIMIT = pltpu.CompilerParams(vmem_limit_bytes=64 * 1024 * 1024)


def dot(left, right, contract):
    return lax.dot_general(
        left, right, ((contract[:1], contract[1:]), ((), ())), preferred_element_type=jnp.float32
    )


def whole(shape):
    return pl.BlockSpec(shape, lambda *_: (0,) * len(shape))


def copies_of(pairs, semaphores):
    return [
        pltpu.make_async_copy(source, target, semaphores.at[item])
        for item, (source, target) in enumerate(pairs)
    ]


def run(copies):
    for copy in copies:
        copy.start()
    for copy in copies:
        copy.wait()


def columns_of(ref, head, width):
    return ref.at[:, pl.ds(pl.multiple_of(head * width, width), width)]


def unpack_kernel(*refs):
    pieces, (left_ref, right_ref, semaphores) = refs[:MEMBERS], refs[MEMBERS:]
    width = left_ref.shape[1] // MEMBERS
    member = lax.axis_index("member")
    pairs = []
    for item, piece in enumerate(pieces):
        head = member ^ (FAR - item)
        pairs.append((piece.at[:, pl.ds(0, width)], columns_of(left_ref, head, width)))
        pairs.append((piece.at[:, pl.ds(width, width)], columns_of(right_ref, head, width)))
    run(copies_of(pairs, semaphores))


def unpack(pieces):
    rows, columns = pieces[0].shape
    shape = (rows, MEMBERS * columns // 2)
    return pl.pallas_call(
        unpack_kernel,
        in_specs=[ANYWHERE] * MEMBERS,
        out_specs=[whole(shape)] * 2,
        out_shape=[jax.ShapeDtypeStruct(shape, pieces[0].dtype)] * 2,
        scratch_shapes=[pltpu.SemaphoreType.DMA((2 * MEMBERS,))],
        compiler_params=VMEM_LIMIT,
        cost_estimate=pl.CostEstimate(
            flops=0, bytes_accessed=4 * MEMBERS * rows * columns, transcendentals=0
        ),
    )(*pieces)


def pair_copies(left_ref, right_ref, buffer, rows, parity):
    pair = lax.axis_index("member") // 2
    width = left_ref.shape[1] // MEMBERS
    copies = []
    for item in range(PAIRS):
        head = 2 * (pair ^ (PAIRS - 1 - item)) + parity
        for ref, place in ((left_ref, 0), (right_ref, width)):
            target = buffer.at[item, rows, pl.ds(place, width)]
            copies.append((columns_of(ref, head, width), target))
    return copies


def pack_kernel(keys_ref, values_ref, queries_ref, cotangents_ref, *refs):
    pieces, away_ref, refs = refs[:MEMBERS], refs[MEMBERS], refs[MEMBERS + 1 :]
    key_buffer, row_buffer, arrived, sent = refs
    member = lax.axis_index("member")
    width = HEAD_WIDTH
    pairs = []
    for item in range(MEMBERS):
        head = member ^ (FAR - item)
        for ref, place in ((keys_ref, 0), (values_ref, width)):
            target = key_buffer.at[item, :, pl.ds(place, width)]
            pairs.append((columns_of(ref, head, width), target))
    parity = 1 - member % 2
    pairs += pair_copies(queries_ref, cotangents_ref, row_buffer, pl.ds(0, ROWS), parity)
    arriving = copies_of(pairs, arrived)
    leaving = copies_of(
        [(key_buffer.at[item], piece) for item, piece in enumerate(pieces)]
        + [(row_buffer, away_ref)],
        sent,
    )
    for copy in arriving:
        copy.start()
    for item in range(MEMBERS):
        arriving[2 * item].wait()
        arriving[2 * item + 1].wait()
        leaving[item].start()
    for copy in arriving[2 * MEMBERS :]:
        copy.wait()
    leaving[MEMBERS].start()
    for copy in leaving:
        copy.wait()


def pack(keys, values, queries, cotangents):
    key_shape = (ROWS, 2 * HEAD_WIDTH)
    row_shape = (PAIRS, ROWS, 4 * HEAD_WIDTH)
    outputs = pl.pallas_call(
        pack_kernel,
        in_specs=[IN_HBM] * 4,
        out_specs=[IN_HBM] * (MEMBERS + 1),
        out_shape=[jax.ShapeDtypeStruct(key_shape, jnp.bfloat16)] * MEMBERS
        + [jax.ShapeDtypeStruct(row_shape, jnp.bfloat16)],
        scratch_shapes=[
            pltpu.VMEM((MEMBERS, *key_shape), jnp.bfloat16),
            pltpu.VMEM(row_shape, jnp.bfloat16),
            pltpu.SemaphoreType.DMA((2 * MEMBERS + 2 * PAIRS,)),
            pltpu.SemaphoreType.DMA((MEMBERS + 1,)),
        ],
        compiler_params=VMEM_LIMIT,
        cost_estimate=pl.CostEstimate(
            flops=0, bytes_accessed=8 * 1024 * 1024, transcendentals=0
        ),
    )(keys, values, queries, cotangents)
    return outputs[:MEMBERS], outputs[MEMBERS]


def pair_join_kernel(left_ref, right_ref, back_ref, *refs):
    pieces, (buffer, arrived, sent) = refs[:PAIRS], refs[PAIRS:]
    parity = lax.axis_index("member") % 2
    own_rows = pl.ds(pl.multiple_of(parity * ROWS, ROWS), ROWS)
    other_rows = pl.ds(pl.multiple_of((1 - parity) * ROWS, ROWS), ROWS)
    pairs = pair_copies(left_ref, right_ref, buffer, own_rows, parity)
    pairs += [(back_ref.at[item], buffer.at[item, other_rows]) for item in range(PAIRS)]
    arriving = copies_of(pairs, arrived)
    leaving = copies_of([(buffer.at[item], piece) for item, piece in enumerate(pieces)], sent)
    for copy in arriving:
        copy.start()
    for item in range(PAIRS):
        for place in (2 * item, 2 * item + 1, 2 * PAIRS + item):
            arriving[place].wait()
        leaving[item].start()
    for copy in leaving:
        copy.wait()


def pair_join(left, right, back):
    width = back.shape[2]
    piece = jax.ShapeDtypeStruct((2 * ROWS, width), back.dtype)
    return pl.pallas_call(
        pair_join_kernel,
        in_specs=[IN_HBM] * 3,
        out_specs=[IN_HBM] * PAIRS,
        out_shape=[piece] * PAIRS,
        scratch_shapes=[
            pltpu.VMEM((PAIRS, 2 * ROWS, width), back.dtype),
            pltpu.SemaphoreType.DMA((3 * PAIRS,)),
            pltpu.SemaphoreType.DMA((PAIRS,)),
        ],
        compiler_params=VMEM_LIMIT,
        cost_estimate=pl.CostEstimate(
            flops=0, bytes_accessed=8 * PAIRS * ROWS * width, transcendentals=0
        ),
    )(left, right, back)


def pair_split_kernel(*refs):
    pieces, (away_ref, semaphores) = refs[:PAIRS], refs[PAIRS:]
    parity = 1 - lax.axis_index("member") % 2
    rows = pl.ds(pl.multiple_of(parity * ROWS, ROWS), ROWS)
    run(
        copies_of(
            [(piece.at[rows], away_ref.at[item]) for item, piece in enumerate(pieces)], semaphores
        )
    )


def pair_split(pieces):
    shape = (PAIRS, ROWS, pieces[0].shape[1])
    return pl.pallas_call(
        pair_split_kernel,
        in_specs=[IN_HBM] * PAIRS,
        out_specs=whole(shape),
        out_shape=jax.ShapeDtypeStruct(shape, pieces[0].dtype),
        scratch_shapes=[pltpu.SemaphoreType.DMA((PAIRS,))],
        compiler_params=VMEM_LIMIT,
        cost_estimate=pl.CostEstimate(
            flops=0, bytes_accessed=4 * ROWS * PAIRS * shape[2], transcendentals=0
        ),
    )(*pieces)


def pair_unpack_kernel(*refs):
    pieces, back_ref, refs = refs[:PAIRS], refs[PAIRS], refs[PAIRS + 1 :]
    left_ref, right_ref, semaphores = refs
    member = lax.axis_index("member")
    pair, parity = member // 2, member % 2
    rows = pl.ds(pl.multiple_of(parity * ROWS, ROWS), ROWS)
    width = left_ref.shape[1] // MEMBERS
    pairs = []
    for item, piece in enumerate(pieces):
        for source, head in (
            (piece.at[rows], 2 * (pair ^ (PAIRS - 1 - item)) + parity),
            (back_ref.at[item], 2 * (pair ^ (PAIRS - 1 - item)) + 1 - parity),
        ):
            for ref, place in ((left_ref, 0), (right_ref, width)):
                pairs.append((source.at[:, pl.ds(place, width)], columns_of(ref, head, width)))
    run(copies_of(pairs, semaphores))


def pair_unpack(pieces, back):
    shape = (ROWS, MEMBERS * back.shape[2] // 2)
    return pl.pallas_call(
        pair_unpack_kernel,
        in_specs=[IN_HBM] * (PAIRS + 1),
        out_specs=[whole(shape)] * 2,
        out_shape=[jax.ShapeDtypeStruct(shape, back.dtype)] * 2,
        scratch_shapes=[pltpu.SemaphoreType.DMA((4 * PAIRS,))],
        compiler_params=VMEM_LIMIT,
        cost_estimate=pl.CostEstimate(
            flops=0, bytes_accessed=8 * shape[0] * shape[1], transcendentals=0
        ),
    )(*pieces, back)


def attention_kernel(lengths_ref, *refs):
    row_pieces, refs = refs[:PAIRS], refs[PAIRS:]
    own_ref, earlier_ref, refs = refs[0], refs[1], refs[2:]
    result_pieces, refs = refs[:PAIRS], refs[PAIRS:]
    own_grad_ref, earlier_grad_ref, refs = refs[0], refs[1], refs[2:]
    rows, results, kv, kv_turned, sums, low_sums, weights, grad_weights = refs[:8]
    refs = refs[8:]
    scores, grads, (arrived, sent, row_marks, result_marks) = refs[:2], refs[2:4], refs[4:]
    step = pl.program_id(0)
    width = HEAD_WIDTH
    member = lax.axis_index("member")
    pair = member // 2

    def row_copy(item):
        tile = pair ^ (PAIRS - 1 - item)
        return pltpu.make_async_copy(row_pieces[item], rows.at[tile], row_marks.at[tile])

    def result_copy(item):
        tile = pair ^ (PAIRS - 1 - item)
        return pltpu.make_async_copy(results.at[tile], result_pieces[item], result_marks.at[tile])

    def arrivals():
        pairs = []
        for item in range(MEMBERS):
            chunk = member ^ (FAR - item)
            pairs.append((earlier_ref.at[item], kv.at[chunk], arrived.at[chunk]))
            place = MEMBERS + chunk
            pairs.append((own_ref.at[item], kv.at[place], arrived.at[place]))
        return [pltpu.make_async_copy(*pair) for pair in pairs]

    def await_chunk(place):
        pltpu.make_async_copy(own_ref.at[0], kv.at[place], arrived.at[place]).wait()

    def turn(tile):
        part = kv[pl.ds(tile * CHUNKS, CHUNKS)].reshape(TILE, 2 * width)
        kv_turned[:, pl.ds(pl.multiple_of(tile * TILE, TILE), TILE)] = part.T

    @pl.when(step == 0)
    def _():
        for copy in arrivals():
            copy.start()
        for item in range(PAIRS):
            row_copy(item).start()
        sums[:MEMBERS] = jnp.zeros((MEMBERS, ROWS, 2 * width), jnp.float32)
        for chunk in range(MEMBERS):
            await_chunk(chunk)
        for tile in range(TILES):
            turn(tile)

    for part in range(CHUNKS):
        await_chunk(MEMBERS + step * CHUNKS + part)
    pltpu.make_async_copy(row_pieces[0], rows.at[step], row_marks.at[step]).wait()
    turn(TILES + step)

    def key_tile(item, first):
        tile = pl.ds((step + item) * CHUNKS, CHUNKS)
        return kv[tile, :, first : first + width].reshape(TILE, width)

    def turned_window(first):
        place = pl.ds(pl.multiple_of(step * TILE, TILE), KEYS)
        return kv_turned[first : first + width, place]

    def add(item, first, part):
        tile = pl.ds((step + item) * CHUNKS, CHUNKS)
        part = part.reshape(CHUNKS, ROWS, width)
        if item < TILES:
            part = sums[tile, :, first : first + width] + part
        sums[tile, :, first : first + width] = part

    queries = [rows[step, :, head * width : (head + 1) * width] for head in range(2)]
    cotangents = [rows[step, :, (2 + head) * width : (3 + head) * width] for head in range(2)]
    queries_turned = [part.T for part in queries]
    cotangents_turned = [part.T for part in cotangents]
    columns = [slice(head * TILE, (head + 1) * TILE) for head in range(2)]
    tiles = [slice(item * TILE, (item + 1) * TILE) for item in range(SPAN)]

    first_row = lax.axis_index("stretch") * WINDOW_LENGTH + step * TILE
    row = lax.broadcasted_iota(jnp.int32, (1, TILE), 1)
    oldest = row - (WINDOW_LENGTH - 1)

    def passed(item, carried):
        begin, oldest = carried
        near = begin - first_row
        oldest = jnp.where(near <= row, jnp.maximum(oldest, near), oldest)
        return begin + lengths_ref[item], oldest

    _, oldest = lax.fori_loop(0, lengths_ref.shape[0], passed, (jnp.int32(0), oldest))
    key_row = lax.broadcasted_iota(jnp.int32, (TILE, TILE), 0)

    tops = [jnp.full((1, TILE), -jnp.inf, jnp.float32)] * 2
    totals = [jnp.zeros((1, TILE), jnp.float32)] * 2

    def score(head, item):
        part = dot(key_tile(item, 0), queries_turned[head], (1, 0))
        seen = key_row >= oldest - (item - TILES) * TILE
        if item == TILES:
            seen = seen & (key_row <= row)
        part = jnp.where(seen, part, -jnp.inf)
        tops[head] = jnp.maximum(tops[head], jnp.max(part, axis=0, keepdims=True))
        scores[head][item] = part

    def weigh(head, item):
        part = jnp.exp2((scores[head][item] - tops[head]) * (SCORE_SCALE * LOG2_E))
        totals[head] = totals[head] + jnp.sum(part, axis=0, keepdims=True)
        weights[tiles[item], columns[head]] = part.astype(jnp.bfloat16)

    def grade(head, item):
        grads[head][item] = dot(key_tile(item, width), cotangents_turned[head], (1, 0))

    def put(head, first, part):
        place = slice((first + head) * width, (first + head + 1) * width)
        results[step, :, place] = part.astype(jnp.bfloat16).T

    def attend(head, share):
        attended = dot(turned_window(width), weights[:, columns[head]], (1, 0))
        attended = (attended * share).astype(jnp.bfloat16)
        put(head, 0, attended)
        products = attended.astype(jnp.float32) * cotangents_turned[head].astype(jnp.float32)
        return jnp.sum(products, axis=0, keepdims=True)

    def weigh_grad(head, item, row_delta):
        part = weights[tiles[item], columns[head]].astype(jnp.float32)
        part = (part * (grads[head][item] - row_delta)).astype(jnp.bfloat16)
        grad_weights[tiles[item], columns[head]] = part

    def make_query_grad(head, share):
        query_grad = dot(turned_window(0), grad_weights[:, columns[head]], (1, 0))
        put(head, 2, query_grad * (share * SCORE_SCALE))

    def scaled(parts, shares):
        scaled_parts = []
        for part, share in zip(parts, shares):
            down = jnp.broadcast_to(share, (8, TILE)).T[:, :1]
            scaled_parts.append((part.astype(jnp.float32) * down).astype(jnp.bfloat16))
        return jnp.concatenate(scaled_parts, axis=0)

    for item in range(SPAN):
        score(0, item)
    for item in range(SPAN):
        score(1, item)
        weigh(0, item)
    for item in range(SPAN):
        grade(0, item)
        weigh(1, item)
    shares = [1.0 / total for total in totals]
    delta = attend(0, shares[0])
    for item in range(SPAN):
        grade(1, item)
        weigh_grad(0, item, delta)
    delta = attend(1, shares[1])
    cotangents_scaled = scaled(cotangents, shares)
    queries_scaled = scaled(queries, shares)
    for item in range(SPAN):
        add(item, width, dot(weights[tiles[item]], cotangents_scaled, (1, 0)))
        weigh_grad(1, item, delta)
    make_query_grad(0, shares[0])
    make_query_grad(1, shares[1])
    for item in range(SPAN):
        add(item, 0, dot(grad_weights[tiles[item]], queries_scaled, (1, 0)))

    def departures():
        pairs = []
        for item in range(MEMBERS):
            chunk = member ^ (FAR - item)
            target = earlier_grad_ref.at[item]
            pairs.append((chunk, (low_sums.at[chunk], target, sent.at[chunk])))
        return [(chunk, pltpu.make_async_copy(*parts)) for chunk, parts in pairs]

    for part in range(CHUNKS):
        chunk = step * CHUNKS + part
        low_sums[chunk, :, :width] = (sums[chunk, :, :width] * SCORE_SCALE).astype(jnp.bfloat16)
        low_sums[chunk, :, width:] = sums[chunk, :, width:].astype(jnp.bfloat16)
    for chunk, copy in departures():
        pl.when(chunk // CHUNKS == step)(copy.start)
    for item in range(PAIRS):
        pl.when((pair ^ (PAIRS - 1 - item)) == step)(result_copy(item).start)

    @pl.when(step == TILES - 1)
    def _():
        copies = [copy for _, copy in departures()]
        copies += [result_copy(item) for item in range(PAIRS)]
        for chunk in range(MEMBERS, 2 * MEMBERS):
            sums[chunk, :, :width] = sums[chunk, :, :width] * SCORE_SCALE
        for item in range(MEMBERS):
            place = MEMBERS + (member ^ (FAR - item))
            target = own_grad_ref.at[item]
            copies.append(pltpu.make_async_copy(sums.at[place], target, sent.at[place]))
            copies[-1].start()
        for copy in copies:
            copy.wait()


def attention(doc_lengths, row_pieces, own, earlier):
    width = HEAD_WIDTH
    products = 6 * 2 * WINDOW_LENGTH * 2 * KEYS * width
    whole_shape = (MEMBERS, ROWS, 2 * width)
    outputs = pl.pallas_call(
        attention_kernel,
        grid=(TILES,),
        in_specs=[SCALARS] + [IN_HBM] * (PAIRS + 2),
        out_specs=[IN_HBM] * (PAIRS + 2),
        out_shape=[jax.ShapeDtypeStruct((TILE, 4 * width), jnp.bfloat16)] * PAIRS
        + [jax.ShapeDtypeStruct(whole_shape, dtype) for dtype in (jnp.float32, jnp.bfloat16)],
        scratch_shapes=[
            pltpu.VMEM((TILES, TILE, 4 * width), jnp.bfloat16),
            pltpu.VMEM((TILES, TILE, 4 * width), jnp.bfloat16),
            pltpu.VMEM((2 * MEMBERS, ROWS, 2 * width), jnp.bfloat16),
            pltpu.VMEM((2 * width, 2 * WINDOW_LENGTH), jnp.bfloat16),
            pltpu.VMEM((2 * MEMBERS, ROWS, 2 * width), jnp.float32),
            pltpu.VMEM((MEMBERS, ROWS, 2 * width), jnp.bfloat16),
            pltpu.VMEM((KEYS, COLUMNS), jnp.bfloat16),
            pltpu.VMEM((KEYS, COLUMNS), jnp.bfloat16),
        ]
        + [pltpu.VMEM((SPAN, TILE, TILE), jnp.float32)] * 4
        + [
            pltpu.SemaphoreType.DMA((2 * MEMBERS,)),
            pltpu.SemaphoreType.DMA((2 * MEMBERS,)),
            pltpu.SemaphoreType.DMA((TILES,)),
            pltpu.SemaphoreType.DMA((TILES,)),
        ],
        compiler_params=VMEM_LIMIT,
        cost_estimate=pl.CostEstimate(
            flops=2 * products, bytes_accessed=WINDOW_LENGTH * width * 30, transcendentals=0
        ),
    )(doc_lengths, *row_pieces, own, earlier)
    return outputs[:PAIRS], outputs[PAIRS], outputs[PAIRS + 1]


def between(block, distance):
    return lax.ppermute(block, "member", [(i, i ^ distance) for i in range(MEMBERS)])


def pair_swapped(pieces):
    last = PAIRS - 1
    return [between(pieces[item], 2 * (last - item)) for item in range(last)] + [pieces[last]]


def swapped(pieces):
    return [between(pieces[item], FAR - item) for item in range(FAR)] + [pieces[FAR]]


def onward(block, direction):
    lower = [(i, i + 1) for i in range(lax.axis_size("stretch") - 1)]
    route = lower if direction > 0 else [(j, i) for i, j in lower]
    return lax.ppermute(block, "stretch", route)


def shards(rotated_query_rows, rotated_key_rows, value_matrix, output_gradient, doc_lengths):
    pieces, away = pack(
        rotated_key_rows, value_matrix, rotated_query_rows, output_gradient
    )
    pieces = swapped(pieces)
    back = between(away, 1)
    rows = pair_join(rotated_query_rows, output_gradient, back)
    pieces, rows = lax.optimization_barrier((pieces, rows))
    own = jnp.stack(pieces)
    earlier = onward(own, 1)
    rows = pair_swapped(rows)
    results, own_grad, earlier_grad = attention(doc_lengths, rows, own, earlier)
    later = onward(earlier_grad, -1)
    results = pair_swapped(results)
    attended, query_grad = pair_unpack(results, between(pair_split(results), 1))
    sums = (own_grad + later.astype(jnp.float32)).astype(jnp.bfloat16)
    pieces = swapped([sums[item] for item in range(MEMBERS)])
    attended, query_grad, pieces = lax.optimization_barrier((attended, query_grad, pieces))
    return (attended, query_grad, *unpack(pieces))


def solution(mesh):
    grouped = Mesh(mesh.devices.reshape(-1, MEMBERS), ("stretch", "member"))
    spread = P(("stretch", "member"), None)
    return jax.shard_map(
        shards,
        mesh=grouped,
        in_specs=(spread, spread, spread, spread, P()),
        out_specs=(spread, spread, spread, spread),
        check_vma=False,
    )
```

```python
import jax
import jax.numpy as jnp
from jax import lax
from jax.experimental import pallas as pl
from jax.experimental.pallas import tpu as pltpu
from jax.sharding import Mesh
from jax.sharding import PartitionSpec as P

HEAD_WIDTH = 256
WINDOW_LENGTH = 1024
MEMBERS = 8
HALF = MEMBERS // 2
FAR = MEMBERS - 1

TILE = 256
TILES = WINDOW_LENGTH // TILE
SPAN = TILES + 1
KEYS = SPAN * TILE
ROWS = WINDOW_LENGTH // MEMBERS
CHUNKS = TILE // ROWS
COLUMNS = 2 * TILE
SCORE_SCALE = HEAD_WIDTH ** (-0.5)
LOG2_E = 1.4426950408889634

ANYWHERE = pl.BlockSpec(memory_space=pl.ANY)
IN_HBM = pl.BlockSpec(memory_space=pltpu.HBM)
SCALARS = pl.BlockSpec(memory_space=pltpu.SMEM)
VMEM_LIMIT = pltpu.CompilerParams(vmem_limit_bytes=64 * 1024 * 1024)


def dot(left, right, contract):
    return lax.dot_general(
        left, right, ((contract[:1], contract[1:]), ((), ())), preferred_element_type=jnp.float32
    )


def whole(shape):
    return pl.BlockSpec(shape, lambda *_: (0,) * len(shape))


def copies_of(pairs, semaphores):
    return [
        pltpu.make_async_copy(source, target, semaphores.at[item])
        for item, (source, target) in enumerate(pairs)
    ]


def run(copies):
    for copy in copies:
        copy.start()
    for copy in copies:
        copy.wait()


def columns_of(ref, head, width):
    return ref.at[:, pl.ds(pl.multiple_of(head * width, width), width)]


def pack_kernel(left_ref, right_ref, *refs):
    pieces, semaphores = refs[:-1], refs[-1]
    width = left_ref.shape[1] // MEMBERS
    member = lax.axis_index("member")
    pairs = []
    for item, piece in enumerate(pieces):
        head = member ^ (FAR - item)
        pairs.append((columns_of(left_ref, head, width), piece.at[:, pl.ds(0, width)]))
        pairs.append((columns_of(right_ref, head, width), piece.at[:, pl.ds(width, width)]))
    run(copies_of(pairs, semaphores))


def pack(left, right):
    rows, columns = left.shape
    piece = jax.ShapeDtypeStruct((rows, 2 * columns // MEMBERS), left.dtype)
    return pl.pallas_call(
        pack_kernel,
        in_specs=[whole(left.shape), whole(right.shape)],
        out_specs=[ANYWHERE] * MEMBERS,
        out_shape=[piece] * MEMBERS,
        scratch_shapes=[pltpu.SemaphoreType.DMA((2 * MEMBERS,))],
        compiler_params=VMEM_LIMIT,
        cost_estimate=pl.CostEstimate(
            flops=0, bytes_accessed=8 * rows * columns, transcendentals=0
        ),
    )(left, right)


def unpack_kernel(*refs):
    pieces, (left_ref, right_ref, semaphores) = refs[:MEMBERS], refs[MEMBERS:]
    width = left_ref.shape[1] // MEMBERS
    member = lax.axis_index("member")
    pairs = []
    for item, piece in enumerate(pieces):
        head = member ^ (FAR - item)
        pairs.append((piece.at[:, pl.ds(0, width)], columns_of(left_ref, head, width)))
        pairs.append((piece.at[:, pl.ds(width, width)], columns_of(right_ref, head, width)))
    run(copies_of(pairs, semaphores))


def unpack(pieces):
    rows, columns = pieces[0].shape
    shape = (rows, MEMBERS * columns // 2)
    return pl.pallas_call(
        unpack_kernel,
        in_specs=[ANYWHERE] * MEMBERS,
        out_specs=[whole(shape)] * 2,
        out_shape=[jax.ShapeDtypeStruct(shape, pieces[0].dtype)] * 2,
        scratch_shapes=[pltpu.SemaphoreType.DMA((2 * MEMBERS,))],
        compiler_params=VMEM_LIMIT,
        cost_estimate=pl.CostEstimate(
            flops=0, bytes_accessed=4 * MEMBERS * rows * columns, transcendentals=0
        ),
    )(*pieces)


def key_copies(own_halves, earlier_halves, kv, arrived):
    member = lax.axis_index("member")
    copies = []
    for item in range(MEMBERS):
        half, part, chunk = item // HALF, item % HALF, member ^ (FAR - item)
        for halves, place in ((earlier_halves, chunk), (own_halves, MEMBERS + chunk)):
            copies.append(
                pltpu.make_async_copy(halves[half].at[part], kv.at[place], arrived.at[place])
            )
    return copies


def await_keys(step, own_halves, earlier_halves, kv, arrived, turn):
    def await_chunk(place):
        pltpu.make_async_copy(own_halves[0].at[0], kv.at[place], arrived.at[place]).wait()

    @pl.when(step == 0)
    def _():
        for chunk in range(MEMBERS):
            await_chunk(chunk)
        for tile in range(TILES):
            turn(tile)

    for part in range(CHUNKS):
        await_chunk(MEMBERS + step * CHUNKS + part)
    turn(TILES + step)


def key_tile(kv, tile, first):
    chunks = pl.ds(tile * CHUNKS, CHUNKS)
    return kv[chunks, :, first : first + HEAD_WIDTH].reshape(TILE, HEAD_WIDTH)


def add_tile(sums, step, item, part):
    chunks = pl.ds((step + item) * CHUNKS, CHUNKS)
    part = part.reshape(CHUNKS, ROWS, HEAD_WIDTH)
    sums[chunks] = sums[chunks] + part if item < TILES else part


def send_sums(step, scale, sums, low_sums, own_grad, earlier_grad, sent):
    member = lax.axis_index("member")

    def departure(chunk):
        return pltpu.make_async_copy(
            low_sums.at[chunk], earlier_grad.at[FAR - (member ^ chunk)], sent.at[chunk]
        )

    for part in range(CHUNKS):
        chunk = step * CHUNKS + part
        low_sums[chunk] = (sums[chunk] * scale).astype(jnp.bfloat16)
        departure(chunk).start()

    @pl.when(step == TILES - 1)
    def _():
        copies = []
        for chunk in range(MEMBERS):
            place = MEMBERS + chunk
            if scale != 1.0:
                sums[place] = sums[place] * scale
            target = own_grad.at[FAR - (member ^ chunk)]
            copies.append(pltpu.make_async_copy(sums.at[place], target, sent.at[place]))
            copies[-1].start()
        for copy in copies + [departure(chunk) for chunk in range(MEMBERS)]:
            copy.wait()


def heads_of(rows_ref, first):
    return [
        rows_ref[:, head * HEAD_WIDTH : (head + 1) * HEAD_WIDTH] for head in (first, first + 1)
    ]


def turned_heads(parts):
    return jnp.concatenate([part.T for part in parts], axis=1)


def scaled_heads(parts, share):
    scaled = []
    for head, part in enumerate(parts):
        own = share[:, head * TILE : (head + 1) * TILE]
        down = jnp.broadcast_to(own, (8, TILE)).T[:, :1]
        scaled.append((part.astype(jnp.float32) * down).astype(jnp.bfloat16))
    return jnp.concatenate(scaled, axis=0)


def put_heads(out_ref, part):
    part = part.astype(jnp.bfloat16)
    out_ref[:, :HEAD_WIDTH] = part[:, :TILE].T
    out_ref[:, HEAD_WIDTH:] = part[:, TILE:].T


def window_of(turned, step):
    return turned[:, pl.ds(pl.multiple_of(step * TILE, TILE), KEYS)]


def turn_tile(kv, turned, first):
    def turn(tile):
        place = pl.ds(pl.multiple_of(tile * TILE, TILE), TILE)
        turned[:, place] = key_tile(kv, tile, first).T

    return turn


def attended_kernel(lengths_ref, rows_ref, *refs):
    own_halves, earlier_halves, refs = refs[:2], refs[2:4], refs[4:]
    attended_ref, weights_ref, stats_ref, own_grad, earlier_grad = refs[:5]
    kv, turned, sums, low_sums, scores, arrived, sent = refs[5:]
    step = pl.program_id(0)

    @pl.when(step == 0)
    def _():
        for copy in key_copies(own_halves, earlier_halves, kv, arrived):
            copy.start()
        sums[:MEMBERS] = jnp.zeros((MEMBERS, ROWS, HEAD_WIDTH), jnp.float32)

    await_keys(
        step, own_halves, earlier_halves, kv, arrived, turn_tile(kv, turned, HEAD_WIDTH)
    )
    queries = turned_heads(heads_of(rows_ref, 0))
    cotangents = heads_of(rows_ref, 2)

    first_row = lax.axis_index("stretch") * WINDOW_LENGTH + step * TILE
    row = lax.broadcasted_iota(jnp.int32, (1, COLUMNS), 1) % TILE
    oldest = row - (WINDOW_LENGTH - 1)

    def passed(item, carried):
        begin, oldest = carried
        near = begin - first_row
        oldest = jnp.where(near <= row, jnp.maximum(oldest, near), oldest)
        return begin + lengths_ref[item], oldest

    _, oldest = lax.fori_loop(0, lengths_ref.shape[0], passed, (jnp.int32(0), oldest))
    key_row = lax.broadcasted_iota(jnp.int32, (TILE, COLUMNS), 0)

    top = jnp.full((1, COLUMNS), -jnp.inf, jnp.float32)
    for item in range(SPAN):
        part = dot(key_tile(kv, step + item, 0), queries, (1, 0))
        seen = key_row >= oldest - (item - TILES) * TILE
        if item == TILES:
            seen = seen & (key_row <= row)
        part = jnp.where(seen, part, -jnp.inf)
        top = jnp.maximum(top, jnp.max(part, axis=0, keepdims=True))
        scores[item] = part

    total = jnp.zeros((1, COLUMNS), jnp.float32)
    for item in range(SPAN):
        part = jnp.exp2((scores[item] - top) * (SCORE_SCALE * LOG2_E))
        total = total + jnp.sum(part, axis=0, keepdims=True)
        weights_ref[0, item * TILE : (item + 1) * TILE, :] = part.astype(jnp.bfloat16)
    share = 1.0 / total

    attended = dot(window_of(turned, step), weights_ref[0], (1, 0)) * share
    scaled = scaled_heads(cotangents, share)
    for item in range(SPAN):
        part = weights_ref[0, item * TILE : (item + 1) * TILE, :]
        add_tile(sums, step, item, dot(part, scaled, (1, 0)))
    attended = attended.astype(jnp.bfloat16)
    put_heads(attended_ref, attended)
    products = attended.astype(jnp.float32) * turned_heads(cotangents).astype(jnp.float32)
    stats_ref[0, :1, :] = share
    stats_ref[0, 1:2, :] = jnp.sum(products, axis=0, keepdims=True)

    send_sums(step, 1.0, sums, low_sums, own_grad, earlier_grad, sent)


def gradient_kernel(rows_ref, weights_ref, stats_ref, *refs):
    own_halves, earlier_halves, refs = refs[:2], refs[2:4], refs[4:]
    query_grad_ref, own_grad, earlier_grad = refs[:3]
    kv, turned, sums, low_sums, grad_weights, arrived, sent = refs[3:]
    step = pl.program_id(0)

    @pl.when(step == 0)
    def _():
        for copy in key_copies(own_halves, earlier_halves, kv, arrived):
            copy.start()
        sums[:MEMBERS] = jnp.zeros((MEMBERS, ROWS, HEAD_WIDTH), jnp.float32)

    await_keys(step, own_halves, earlier_halves, kv, arrived, turn_tile(kv, turned, 0))
    cotangents = turned_heads(heads_of(rows_ref, 2))
    share = stats_ref[0, :1, :]
    row_delta = stats_ref[0, 1:2, :]
    scaled = scaled_heads(heads_of(rows_ref, 0), share)

    for item in range(SPAN):
        place = slice(item * TILE, (item + 1) * TILE)
        part = dot(key_tile(kv, step + item, HEAD_WIDTH), cotangents, (1, 0)) - row_delta
        part = (weights_ref[0, place, :].astype(jnp.float32) * part).astype(jnp.bfloat16)
        grad_weights[place, :] = part
        add_tile(sums, step, item, dot(part, scaled, (1, 0)))
    query_grad = dot(window_of(turned, step), grad_weights[...], (1, 0))
    put_heads(query_grad_ref, query_grad * (share * SCORE_SCALE))

    send_sums(step, SCORE_SCALE, sums, low_sums, own_grad, earlier_grad, sent)


ROWS_BLOCK = pl.BlockSpec((TILE, 4 * HEAD_WIDTH), lambda i: (i, 0))
HEADS_BLOCK = pl.BlockSpec((TILE, 2 * HEAD_WIDTH), lambda i: (i, 0))
WEIGHTS_BLOCK = pl.BlockSpec((1, KEYS, COLUMNS), lambda i: (i, 0, 0))
STATS_BLOCK = pl.BlockSpec((1, 8, COLUMNS), lambda i: (i, 0, 0))
HEADS_SHAPE = jax.ShapeDtypeStruct((WINDOW_LENGTH, 2 * HEAD_WIDTH), jnp.bfloat16)
GRAD_SHAPES = [
    jax.ShapeDtypeStruct((MEMBERS, ROWS, HEAD_WIDTH), dtype)
    for dtype in (jnp.float32, jnp.bfloat16)
]
KEY_SCRATCH = [
    pltpu.VMEM((2 * MEMBERS, ROWS, 2 * HEAD_WIDTH), jnp.bfloat16),
    pltpu.VMEM((HEAD_WIDTH, 2 * WINDOW_LENGTH), jnp.bfloat16),
    pltpu.VMEM((2 * MEMBERS, ROWS, HEAD_WIDTH), jnp.float32),
    pltpu.VMEM((MEMBERS, ROWS, HEAD_WIDTH), jnp.bfloat16),
]
MARKS = [pltpu.SemaphoreType.DMA((2 * MEMBERS,))] * 2
COST = pl.CostEstimate(
    flops=3 * 2 * WINDOW_LENGTH * 2 * KEYS * HEAD_WIDTH,
    bytes_accessed=12 * 1024 * 1024,
    transcendentals=0,
)


def attended_call(doc_lengths, rows, own, earlier):
    return pl.pallas_call(
        attended_kernel,
        grid=(TILES,),
        in_specs=[SCALARS, ROWS_BLOCK] + [IN_HBM] * 4,
        out_specs=[HEADS_BLOCK, WEIGHTS_BLOCK, STATS_BLOCK] + [IN_HBM] * 2,
        out_shape=[
            HEADS_SHAPE,
            jax.ShapeDtypeStruct((TILES, KEYS, COLUMNS), jnp.bfloat16),
            jax.ShapeDtypeStruct((TILES, 8, COLUMNS), jnp.float32),
        ]
        + GRAD_SHAPES,
        scratch_shapes=KEY_SCRATCH + [pltpu.VMEM((SPAN, TILE, COLUMNS), jnp.float32)] + MARKS,
        compiler_params=VMEM_LIMIT,
        cost_estimate=COST,
    )(doc_lengths, rows, *own, *earlier)


def gradient_call(rows, weights, stats, own, earlier):
    return pl.pallas_call(
        gradient_kernel,
        grid=(TILES,),
        in_specs=[ROWS_BLOCK, WEIGHTS_BLOCK, STATS_BLOCK] + [IN_HBM] * 4,
        out_specs=[HEADS_BLOCK] + [IN_HBM] * 2,
        out_shape=[HEADS_SHAPE] + GRAD_SHAPES,
        scratch_shapes=KEY_SCRATCH + [pltpu.VMEM((KEYS, COLUMNS), jnp.bfloat16)] + MARKS,
        compiler_params=VMEM_LIMIT,
        cost_estimate=COST,
    )(rows, weights, stats, *own, *earlier)


def by_head(block):
    return block.reshape(ROWS, MEMBERS, block.shape[1] // MEMBERS).transpose(1, 0, 2)


def by_token(blocks):
    return blocks.transpose(1, 0, 2).reshape(ROWS, MEMBERS * blocks.shape[2])


def exchanged(blocks):
    return lax.all_to_all(blocks, "member", split_axis=0, concat_axis=0, tiled=True)


def swapped(pieces):
    moved = []
    for item in range(FAR):
        route = [(i, i ^ (FAR - item)) for i in range(MEMBERS)]
        moved.append(lax.ppermute(pieces[item], "member", route))
    return moved + [pieces[FAR]]


def onward(block, direction):
    lower = [(i, i + 1) for i in range(lax.axis_size("stretch") - 1)]
    route = lower if direction > 0 else [(j, i) for i, j in lower]
    return lax.ppermute(block, "stretch", route)


def shards(rotated_query_rows, rotated_key_rows, value_matrix, output_gradient, doc_lengths):
    pieces = swapped(pack(rotated_key_rows, value_matrix))
    rows = jnp.concatenate([by_head(rotated_query_rows), by_head(output_gradient)], axis=2)
    pieces, rows = lax.optimization_barrier((pieces, rows))
    own = [jnp.stack(pieces[:HALF]), jnp.stack(pieces[HALF:])]
    earlier = [onward(half, 1) for half in own]
    rows = exchanged(rows).reshape(WINDOW_LENGTH, 4 * HEAD_WIDTH)
    attended, weights, stats, own_values, earlier_values = attended_call(
        doc_lengths, rows, own, earlier
    )
    later_values = onward(earlier_values, -1)
    attended = exchanged(attended.reshape(MEMBERS, ROWS, 2 * HEAD_WIDTH))
    query_grad, own_keys, earlier_keys = gradient_call(rows, weights, stats, own, earlier)
    attended, later_values, query_grad, earlier_keys = lax.optimization_barrier(
        (attended, later_values, query_grad, earlier_keys)
    )
    attended = by_token(attended)
    later_keys = onward(earlier_keys, -1)
    query_grad = by_token(exchanged(query_grad.reshape(MEMBERS, ROWS, 2 * HEAD_WIDTH)))
    sums = jnp.concatenate([own_keys + later_keys, own_values + later_values], axis=2)
    sums = sums.astype(jnp.bfloat16)
    pieces = swapped([sums[item] for item in range(MEMBERS)])
    attended, query_grad, pieces = lax.optimization_barrier((attended, query_grad, pieces))
    return (attended, query_grad, *unpack(pieces))


def solution(mesh):
    grouped = Mesh(mesh.devices.reshape(-1, MEMBERS), ("stretch", "member"))
    spread = P(("stretch", "member"), None)
    return jax.shard_map(
        shards,
        mesh=grouped,
        in_specs=(spread, spread, spread, spread, P()),
        out_specs=(spread, spread, spread, spread),
        check_vma=False,
    )
```

```python
import jax
import jax.numpy as jnp
from jax import lax
from jax.experimental import pallas as pl
from jax.experimental.pallas import tpu as pltpu
from jax.sharding import Mesh
from jax.sharding import PartitionSpec as P

HEAD_WIDTH = 256
WINDOW_LENGTH = 1024
MEMBERS = 8
HALF = MEMBERS // 2
DISTANCES = (7, 6, 5, 4, 3, 2, 1, 0)
BACK_DISTANCES = (7, 6, 5, 4, 0, 1, 2, 3)

TILE = 256
TILES = WINDOW_LENGTH // TILE
SPAN = TILES + 1
KEYS = SPAN * TILE
ROWS = WINDOW_LENGTH // MEMBERS
CHUNKS = TILE // ROWS
COLUMNS = 2 * TILE
SCORE_SCALE = HEAD_WIDTH ** (-0.5)
LOG2_E = 1.4426950408889634

IN_HBM = pl.BlockSpec(memory_space=pltpu.HBM)
SCALARS = pl.BlockSpec(memory_space=pltpu.SMEM)
VMEM_LIMIT = pltpu.CompilerParams(vmem_limit_bytes=64 * 1024 * 1024)


def dot(left, right, contract):
    return lax.dot_general(
        left, right, ((contract[:1], contract[1:]), ((), ())), preferred_element_type=jnp.float32
    )


def copies_of(pairs, semaphores):
    return [
        pltpu.make_async_copy(source, target, semaphores.at[item])
        for item, (source, target) in enumerate(pairs)
    ]


def columns_of(ref, head, width):
    return ref.at[:, pl.ds(pl.multiple_of(head * width, width), width)]


def staged(arriving, leaving):
    for copies in arriving:
        for copy in copies:
            copy.start()
    for copies, onward in zip(arriving, leaving):
        for copy in copies:
            copy.wait()
        for copy in onward:
            copy.start()
    for onward in leaving:
        for copy in onward:
            copy.wait()


def pack_kernel(left_ref, right_ref, *refs):
    pieces, (buffer, arrived, sent) = refs[:MEMBERS], refs[MEMBERS:]
    member = lax.axis_index("member")
    width = left_ref.shape[1] // MEMBERS
    arriving, leaving = [], []
    for item, distance in enumerate(DISTANCES):
        head = member ^ distance
        pairs = [
            (columns_of(left_ref, head, width), buffer.at[item, :, pl.ds(0, width)]),
            (columns_of(right_ref, head, width), buffer.at[item, :, pl.ds(width, width)]),
        ]
        arriving.append(copies_of(pairs, arrived.at[item]))
        leaving.append([pltpu.make_async_copy(buffer.at[item], pieces[item], sent.at[item])])
    staged(arriving, leaving)


def pack(left, right):
    rows, columns = left.shape
    shape = (rows, 2 * columns // MEMBERS)
    return pl.pallas_call(
        pack_kernel,
        in_specs=[IN_HBM] * 2,
        out_specs=[IN_HBM] * MEMBERS,
        out_shape=[jax.ShapeDtypeStruct(shape, left.dtype)] * MEMBERS,
        scratch_shapes=[
            pltpu.VMEM((MEMBERS, *shape), left.dtype),
            pltpu.SemaphoreType.DMA((MEMBERS, 2)),
            pltpu.SemaphoreType.DMA((MEMBERS,)),
        ],
        compiler_params=VMEM_LIMIT,
        cost_estimate=pl.CostEstimate(
            flops=0, bytes_accessed=8 * rows * columns, transcendentals=0
        ),
    )(left, right)


def unpack_kernel(*refs):
    pieces, refs = refs[:MEMBERS], refs[MEMBERS:]
    left_ref, right_ref, buffer, arrived, sent = refs
    member = lax.axis_index("member")
    width = left_ref.shape[1] // MEMBERS
    arriving, leaving = [], []
    for item, distance in enumerate(BACK_DISTANCES):
        head = member ^ distance
        arriving.append([pltpu.make_async_copy(pieces[item], buffer.at[item], arrived.at[item])])
        pairs = [
            (buffer.at[item, :, pl.ds(0, width)], columns_of(left_ref, head, width)),
            (buffer.at[item, :, pl.ds(width, width)], columns_of(right_ref, head, width)),
        ]
        leaving.append(copies_of(pairs, sent.at[item]))
    staged(arriving, leaving)


def unpack(pieces):
    rows, columns = pieces[0].shape
    whole = jax.ShapeDtypeStruct((rows, MEMBERS * columns // 2), pieces[0].dtype)
    return pl.pallas_call(
        unpack_kernel,
        in_specs=[IN_HBM] * MEMBERS,
        out_specs=[IN_HBM] * 2,
        out_shape=[whole] * 2,
        scratch_shapes=[
            pltpu.VMEM((MEMBERS, rows, columns), pieces[0].dtype),
            pltpu.SemaphoreType.DMA((MEMBERS,)),
            pltpu.SemaphoreType.DMA((MEMBERS, 2)),
        ],
        compiler_params=VMEM_LIMIT,
        cost_estimate=pl.CostEstimate(
            flops=0, bytes_accessed=4 * MEMBERS * rows * columns, transcendentals=0
        ),
    )(*pieces)


def attention_kernel(lengths_ref, rows_ref, *refs):
    own_halves, earlier_halves, out_ref, refs = refs[:2], refs[2:4], refs[4], refs[5:]
    own_grads, earlier_grads, refs = refs[:2], refs[2:4], refs[4:]
    kv, kv_turned, sums, low_sums, weights, grad_weights, refs = *refs[:6], refs[6:]
    scores, grads, (arrived, sent) = refs[:2], refs[2:4], refs[4:]
    step = pl.program_id(0)
    width = HEAD_WIDTH
    member = lax.axis_index("member")

    def arrivals():
        pairs = []
        for item, distance in enumerate(DISTANCES):
            half, part, chunk = item // HALF, item % HALF, member ^ distance
            pairs.append((earlier_halves[half].at[part], kv.at[chunk], arrived.at[chunk]))
            place = MEMBERS + chunk
            pairs.append((own_halves[half].at[part], kv.at[place], arrived.at[place]))
        return [pltpu.make_async_copy(*pair) for pair in pairs]

    def await_chunk(place):
        pltpu.make_async_copy(own_halves[0].at[0], kv.at[place], arrived.at[place]).wait()

    def turn(tile):
        part = kv[pl.ds(tile * CHUNKS, CHUNKS)].reshape(TILE, 2 * width)
        kv_turned[:, pl.ds(pl.multiple_of(tile * TILE, TILE), TILE)] = part.T

    @pl.when(step == 0)
    def _():
        for copy in arrivals():
            copy.start()
        sums[:MEMBERS] = jnp.zeros((MEMBERS, ROWS, 2 * width), jnp.float32)
        for chunk in range(MEMBERS):
            await_chunk(chunk)
        for tile in range(TILES):
            turn(tile)

    for part in range(CHUNKS):
        await_chunk(MEMBERS + step * CHUNKS + part)
    turn(TILES + step)

    def key_tile(item, first):
        tile = pl.ds((step + item) * CHUNKS, CHUNKS)
        return kv[tile, :, first : first + width].reshape(TILE, width)

    def turned_window(first):
        place = pl.ds(pl.multiple_of(step * TILE, TILE), KEYS)
        return kv_turned[first : first + width, place]

    def add(item, first, part):
        tile = pl.ds((step + item) * CHUNKS, CHUNKS)
        part = part.reshape(CHUNKS, ROWS, width)
        if item < TILES:
            part = sums[tile, :, first : first + width] + part
        sums[tile, :, first : first + width] = part

    queries = [rows_ref[:, head * width : (head + 1) * width] for head in range(2)]
    cotangents = [rows_ref[:, (2 + head) * width : (3 + head) * width] for head in range(2)]
    queries_turned = [part.T for part in queries]
    cotangents_turned = [part.T for part in cotangents]
    columns = [slice(head * TILE, (head + 1) * TILE) for head in range(2)]
    tiles = [slice(item * TILE, (item + 1) * TILE) for item in range(SPAN)]

    first_row = lax.axis_index("stretch") * WINDOW_LENGTH + step * TILE
    row = lax.broadcasted_iota(jnp.int32, (1, TILE), 1)
    oldest = row - (WINDOW_LENGTH - 1)

    def passed(item, carried):
        begin, oldest = carried
        near = begin - first_row
        oldest = jnp.where(near <= row, jnp.maximum(oldest, near), oldest)
        return begin + lengths_ref[item], oldest

    _, oldest = lax.fori_loop(0, lengths_ref.shape[0], passed, (jnp.int32(0), oldest))
    key_row = lax.broadcasted_iota(jnp.int32, (TILE, TILE), 0)

    tops = [jnp.full((1, TILE), -jnp.inf, jnp.float32)] * 2
    totals = [jnp.zeros((1, TILE), jnp.float32)] * 2

    def score(head, item):
        part = dot(key_tile(item, 0), queries_turned[head], (1, 0))
        seen = key_row >= oldest - (item - TILES) * TILE
        if item == TILES:
            seen = seen & (key_row <= row)
        part = jnp.where(seen, part, -jnp.inf)
        tops[head] = jnp.maximum(tops[head], jnp.max(part, axis=0, keepdims=True))
        scores[head][item] = part

    def weigh(head, item):
        part = jnp.exp2((scores[head][item] - tops[head]) * (SCORE_SCALE * LOG2_E))
        totals[head] = totals[head] + jnp.sum(part, axis=0, keepdims=True)
        weights[tiles[item], columns[head]] = part.astype(jnp.bfloat16)

    def grade(head, item):
        grads[head][item] = dot(key_tile(item, width), cotangents_turned[head], (1, 0))

    def put(head, first, part):
        place = slice((first + head) * width, (first + head + 1) * width)
        out_ref[:, place] = part.astype(jnp.bfloat16).T

    def attend(head, share):
        attended = dot(turned_window(width), weights[:, columns[head]], (1, 0))
        attended = (attended * share).astype(jnp.bfloat16)
        put(head, 0, attended)
        products = attended.astype(jnp.float32) * cotangents_turned[head].astype(jnp.float32)
        return jnp.sum(products, axis=0, keepdims=True)

    def weigh_grad(head, item, row_delta):
        part = weights[tiles[item], columns[head]].astype(jnp.float32)
        part = (part * (grads[head][item] - row_delta)).astype(jnp.bfloat16)
        grad_weights[tiles[item], columns[head]] = part

    def make_query_grad(head, share):
        query_grad = dot(turned_window(0), grad_weights[:, columns[head]], (1, 0))
        put(head, 2, query_grad * (share * SCORE_SCALE))

    def scaled(parts, shares):
        scaled_parts = []
        for part, share in zip(parts, shares):
            down = jnp.broadcast_to(share, (8, TILE)).T[:, :1]
            scaled_parts.append((part.astype(jnp.float32) * down).astype(jnp.bfloat16))
        return jnp.concatenate(scaled_parts, axis=0)

    for item in range(SPAN):
        score(0, item)
    for item in range(SPAN):
        score(1, item)
        weigh(0, item)
    for item in range(SPAN):
        grade(0, item)
        weigh(1, item)
    shares = [1.0 / total for total in totals]
    delta = attend(0, shares[0])
    for item in range(SPAN):
        grade(1, item)
        weigh_grad(0, item, delta)
    delta = attend(1, shares[1])
    cotangents_scaled = scaled(cotangents, shares)
    queries_scaled = scaled(queries, shares)
    for item in range(SPAN):
        add(item, width, dot(weights[tiles[item]], cotangents_scaled, (1, 0)))
        weigh_grad(1, item, delta)
    make_query_grad(0, shares[0])
    make_query_grad(1, shares[1])
    for item in range(SPAN):
        add(item, 0, dot(grad_weights[tiles[item]], queries_scaled, (1, 0)))

    def send(chunk):
        low_sums[chunk, :, :width] = (sums[chunk, :, :width] * SCORE_SCALE).astype(jnp.bfloat16)
        low_sums[chunk, :, width:] = sums[chunk, :, width:].astype(jnp.bfloat16)

    def departure(item, own):
        half, part, chunk = item // HALF, item % HALF, member ^ BACK_DISTANCES[item]
        place = MEMBERS + chunk if own else chunk
        halves = own_grads if own else earlier_grads
        return pltpu.make_async_copy(low_sums.at[place], halves[half].at[part], sent.at[place])

    for part in range(CHUNKS):
        send(step * CHUNKS + part)
    for item, distance in enumerate(BACK_DISTANCES):
        pl.when((member ^ distance) // CHUNKS == step)(departure(item, False).start)

    @pl.when(step == TILES - 1)
    def _():
        for chunk in range(MEMBERS, 2 * MEMBERS):
            send(chunk)
        for item in range(MEMBERS):
            departure(item, True).start()
        for item in range(MEMBERS):
            departure(item, False).wait()
            departure(item, True).wait()


def attention(doc_lengths, rows, own, earlier):
    width = HEAD_WIDTH
    products = 6 * 2 * WINDOW_LENGTH * 2 * KEYS * width
    half = jax.ShapeDtypeStruct((HALF, ROWS, 2 * width), jnp.bfloat16)
    rows_block = pl.BlockSpec((TILE, 4 * width), lambda i: (i, 0))
    outputs = pl.pallas_call(
        attention_kernel,
        grid=(TILES,),
        in_specs=[SCALARS, rows_block] + [IN_HBM] * 4,
        out_specs=[rows_block] + [IN_HBM] * 4,
        out_shape=[jax.ShapeDtypeStruct(rows.shape, jnp.bfloat16)] + [half] * 4,
        scratch_shapes=[
            pltpu.VMEM((2 * MEMBERS, ROWS, 2 * width), jnp.bfloat16),
            pltpu.VMEM((2 * width, 2 * WINDOW_LENGTH), jnp.bfloat16),
            pltpu.VMEM((2 * MEMBERS, ROWS, 2 * width), jnp.float32),
            pltpu.VMEM((2 * MEMBERS, ROWS, 2 * width), jnp.bfloat16),
            pltpu.VMEM((KEYS, COLUMNS), jnp.bfloat16),
            pltpu.VMEM((KEYS, COLUMNS), jnp.bfloat16),
        ]
        + [pltpu.VMEM((SPAN, TILE, TILE), jnp.float32)] * 4
        + [pltpu.SemaphoreType.DMA((2 * MEMBERS,))] * 2,
        compiler_params=VMEM_LIMIT,
        cost_estimate=pl.CostEstimate(
            flops=2 * products, bytes_accessed=WINDOW_LENGTH * width * 30, transcendentals=0
        ),
    )(doc_lengths, rows, *own, *earlier)
    return outputs[0], outputs[1:3], outputs[3:]


def by_head(block):
    return block.reshape(ROWS, MEMBERS, block.shape[1] // MEMBERS).transpose(1, 0, 2)


def by_token(blocks):
    return blocks.transpose(1, 0, 2).reshape(ROWS, MEMBERS * blocks.shape[2])


def exchanged(blocks):
    return lax.all_to_all(blocks, "member", split_axis=0, concat_axis=0, tiled=True)


def swapped(pieces, distances):
    moved = []
    for piece, distance in zip(pieces, distances):
        route = [(i, i ^ distance) for i in range(MEMBERS)]
        moved.append(lax.ppermute(piece, "member", route) if distance else piece)
    return moved


def onward(block, direction):
    lower = [(i, i + 1) for i in range(lax.axis_size("stretch") - 1)]
    route = lower if direction > 0 else [(j, i) for i, j in lower]
    return lax.ppermute(block, "stretch", route)


def shards(rotated_query_rows, rotated_key_rows, value_matrix, output_gradient, doc_lengths):
    pieces = swapped(pack(rotated_key_rows, value_matrix), DISTANCES)
    rows = jnp.concatenate([by_head(rotated_query_rows), by_head(output_gradient)], axis=2)
    pieces, rows = lax.optimization_barrier((pieces, rows))
    own = [jnp.stack(pieces[:HALF]), jnp.stack(pieces[HALF:])]
    earlier = [onward(half, 1) for half in own]
    rows = exchanged(rows).reshape(WINDOW_LENGTH, 4 * HEAD_WIDTH)
    results, own_grads, earlier_grads = attention(doc_lengths, rows, own, earlier)
    later = [onward(half, -1) for half in earlier_grads]
    results = exchanged(results.reshape(MEMBERS, ROWS, 4 * HEAD_WIDTH))
    attended = by_token(results[:, :, : 2 * HEAD_WIDTH])
    query_grad = by_token(results[:, :, 2 * HEAD_WIDTH :])
    sums = [
        (own_grads[half].astype(jnp.float32) + later[half].astype(jnp.float32)).astype(
            jnp.bfloat16
        )
        for half in range(2)
    ]
    pieces = [sums[item // HALF][item % HALF] for item in range(MEMBERS)]
    pieces = swapped(pieces, BACK_DISTANCES)
    attended, query_grad, pieces = lax.optimization_barrier((attended, query_grad, pieces))
    return (attended, query_grad, *unpack(pieces))


def solution(mesh):
    grouped = Mesh(mesh.devices.reshape(-1, MEMBERS), ("stretch", "member"))
    spread = P(("stretch", "member"), None)
    return jax.shard_map(
        shards,
        mesh=grouped,
        in_specs=(spread, spread, spread, spread, P()),
        out_specs=(spread, spread, spread, spread),
        check_vma=False,
    )
```

```python
import jax
import jax.numpy as jnp
from jax import lax
from jax.experimental import pallas as pl
from jax.experimental.pallas import tpu as pltpu
from jax.sharding import Mesh
from jax.sharding import PartitionSpec as P

HEAD_WIDTH = 256
WINDOW_LENGTH = 1024
MEMBERS = 8
HALF = MEMBERS // 2
DISTANCES = (7, 6, 5, 4, 3, 2, 1, 0)
BACK_DISTANCES = (7, 6, 5, 4, 0, 1, 2, 3)

TILE = 256
TILES = WINDOW_LENGTH // TILE
SPAN = TILES + 1
KEYS = SPAN * TILE
ROWS = WINDOW_LENGTH // MEMBERS
CHUNKS = TILE // ROWS
COLUMNS = 2 * TILE
SCORE_SCALE = HEAD_WIDTH ** (-0.5)
LOG2_E = 1.4426950408889634

ANYWHERE = pl.BlockSpec(memory_space=pl.ANY)
SCALARS = pl.BlockSpec(memory_space=pltpu.SMEM)
SMALL_LIMIT = pltpu.CompilerParams(vmem_limit_bytes=4 * 1024 * 1024)
LIMIT = pltpu.CompilerParams(vmem_limit_bytes=28 * 1024 * 1024)


def dot(left, right, contract):
    return lax.dot_general(
        left, right, ((contract[:1], contract[1:]), ((), ())), preferred_element_type=jnp.float32
    )


def copies_of(pairs, semaphores):
    return [
        pltpu.make_async_copy(source, target, semaphores.at[item])
        for item, (source, target) in enumerate(pairs)
    ]


def columns_of(ref, head, width):
    return ref.at[:, pl.ds(pl.multiple_of(head * width, width), width)]


def staged(arriving, leaving):
    for copies in arriving:
        for copy in copies:
            copy.start()
    for copies, onward in zip(arriving, leaving):
        for copy in copies:
            copy.wait()
        for copy in onward:
            copy.start()
    for onward in leaving:
        for copy in onward:
            copy.wait()


def pack_kernel(left_ref, right_ref, *refs):
    pieces, (buffer, arrived, sent) = refs[:MEMBERS], refs[MEMBERS:]
    member = lax.axis_index("member")
    width = left_ref.shape[1] // MEMBERS
    arriving, leaving = [], []
    for item, distance in enumerate(DISTANCES):
        head = member ^ distance
        pairs = [
            (columns_of(left_ref, head, width), buffer.at[item, :, pl.ds(0, width)]),
            (columns_of(right_ref, head, width), buffer.at[item, :, pl.ds(width, width)]),
        ]
        arriving.append(copies_of(pairs, arrived.at[item]))
        leaving.append([pltpu.make_async_copy(buffer.at[item], pieces[item], sent.at[item])])
    staged(arriving, leaving)


def pack(left, right):
    rows, columns = left.shape
    shape = (rows, 2 * columns // MEMBERS)
    return pl.pallas_call(
        pack_kernel,
        in_specs=[ANYWHERE] * 2,
        out_specs=[ANYWHERE] * MEMBERS,
        out_shape=[jax.ShapeDtypeStruct(shape, left.dtype)] * MEMBERS,
        scratch_shapes=[
            pltpu.VMEM((MEMBERS, *shape), left.dtype),
            pltpu.SemaphoreType.DMA((MEMBERS, 2)),
            pltpu.SemaphoreType.DMA((MEMBERS,)),
        ],
        compiler_params=SMALL_LIMIT,
        cost_estimate=pl.CostEstimate(
            flops=0, bytes_accessed=8 * rows * columns, transcendentals=0
        ),
    )(left, right)


def unpack_kernel(*refs):
    pieces, refs = refs[:MEMBERS], refs[MEMBERS:]
    left_ref, right_ref, buffer, arrived, sent = refs
    member = lax.axis_index("member")
    width = left_ref.shape[1] // MEMBERS
    arriving, leaving = [], []
    for item, distance in enumerate(BACK_DISTANCES):
        head = member ^ distance
        arriving.append([pltpu.make_async_copy(pieces[item], buffer.at[item], arrived.at[item])])
        pairs = [
            (buffer.at[item, :, pl.ds(0, width)], columns_of(left_ref, head, width)),
            (buffer.at[item, :, pl.ds(width, width)], columns_of(right_ref, head, width)),
        ]
        leaving.append(copies_of(pairs, sent.at[item]))
    staged(arriving, leaving)


def unpack(pieces):
    rows, columns = pieces[0].shape
    whole = jax.ShapeDtypeStruct((rows, MEMBERS * columns // 2), pieces[0].dtype)
    return pl.pallas_call(
        unpack_kernel,
        in_specs=[ANYWHERE] * MEMBERS,
        out_specs=[ANYWHERE] * 2,
        out_shape=[whole] * 2,
        scratch_shapes=[
            pltpu.VMEM((MEMBERS, rows, columns), pieces[0].dtype),
            pltpu.SemaphoreType.DMA((MEMBERS,)),
            pltpu.SemaphoreType.DMA((MEMBERS, 2)),
        ],
        compiler_params=SMALL_LIMIT,
        cost_estimate=pl.CostEstimate(
            flops=0, bytes_accessed=4 * MEMBERS * rows * columns, transcendentals=0
        ),
    )(*pieces)


def attention_kernel(lengths_ref, rows_ref, *refs):
    own_halves, earlier_halves, out_ref, refs = refs[:2], refs[2:4], refs[4], refs[5:]
    own_grads, earlier_grads, refs = refs[:2], refs[2:4], refs[4:]
    kv, kv_turned, sums, low_sums, weights, grad_weights, refs = *refs[:6], refs[6:]
    scores, grads, (arrived, sent) = refs[:2], refs[2:4], refs[4:]
    step = pl.program_id(0)
    width = HEAD_WIDTH
    member = lax.axis_index("member")

    def arrivals():
        pairs = []
        for item, distance in enumerate(DISTANCES):
            half, part, chunk = item // HALF, item % HALF, member ^ distance
            pairs.append((earlier_halves[half].at[part], kv.at[chunk], arrived.at[chunk]))
            place = MEMBERS + chunk
            pairs.append((own_halves[half].at[part], kv.at[place], arrived.at[place]))
        return [pltpu.make_async_copy(*pair) for pair in pairs]

    def await_chunk(place):
        pltpu.make_async_copy(own_halves[0].at[0], kv.at[place], arrived.at[place]).wait()

    def turn(tile):
        part = kv[pl.ds(tile * CHUNKS, CHUNKS)].reshape(TILE, 2 * width)
        kv_turned[:, pl.ds(pl.multiple_of(tile * TILE, TILE), TILE)] = part.T

    @pl.when(step == 0)
    def _():
        for copy in arrivals():
            copy.start()
        sums[:MEMBERS] = jnp.zeros((MEMBERS, ROWS, 2 * width), jnp.float32)
        for chunk in range(MEMBERS):
            await_chunk(chunk)
        for tile in range(TILES):
            turn(tile)

    for part in range(CHUNKS):
        await_chunk(MEMBERS + step * CHUNKS + part)
    turn(TILES + step)

    def key_tile(item, first):
        tile = pl.ds((step + item) * CHUNKS, CHUNKS)
        return kv[tile, :, first : first + width].reshape(TILE, width)

    def turned_window(first):
        place = pl.ds(pl.multiple_of(step * TILE, TILE), KEYS)
        return kv_turned[first : first + width, place]

    def add(item, first, part):
        tile = pl.ds((step + item) * CHUNKS, CHUNKS)
        part = part.reshape(CHUNKS, ROWS, width)
        if item < TILES:
            part = sums[tile, :, first : first + width] + part
        sums[tile, :, first : first + width] = part

    queries = [rows_ref[:, head * width : (head + 1) * width] for head in range(2)]
    cotangents = [rows_ref[:, (2 + head) * width : (3 + head) * width] for head in range(2)]
    queries_turned = [part.T for part in queries]
    cotangents_turned = [part.T for part in cotangents]
    columns = [slice(head * TILE, (head + 1) * TILE) for head in range(2)]
    tiles = [slice(item * TILE, (item + 1) * TILE) for item in range(SPAN)]

    first_row = lax.axis_index("stretch") * WINDOW_LENGTH + step * TILE
    row = lax.broadcasted_iota(jnp.int32, (1, TILE), 1)
    oldest = row - (WINDOW_LENGTH - 1)

    def passed(item, carried):
        begin, oldest = carried
        near = begin - first_row
        oldest = jnp.where(near <= row, jnp.maximum(oldest, near), oldest)
        return begin + lengths_ref[item], oldest

    _, oldest = lax.fori_loop(0, lengths_ref.shape[0], passed, (jnp.int32(0), oldest))
    key_row = lax.broadcasted_iota(jnp.int32, (TILE, TILE), 0)

    tops = [jnp.full((1, TILE), -jnp.inf, jnp.float32)] * 2
    totals = [jnp.zeros((1, TILE), jnp.float32)] * 2

    def score(head, item):
        part = dot(key_tile(item, 0), queries_turned[head], (1, 0))
        seen = key_row >= oldest - (item - TILES) * TILE
        if item == TILES:
            seen = seen & (key_row <= row)
        part = jnp.where(seen, part, -jnp.inf)
        tops[head] = jnp.maximum(tops[head], jnp.max(part, axis=0, keepdims=True))
        scores[head][item] = part

    def weigh(head, item):
        part = jnp.exp2((scores[head][item] - tops[head]) * (SCORE_SCALE * LOG2_E))
        totals[head] = totals[head] + jnp.sum(part, axis=0, keepdims=True)
        weights[tiles[item], columns[head]] = part.astype(jnp.bfloat16)

    def grade(head, item):
        grads[head][item] = dot(key_tile(item, width), cotangents_turned[head], (1, 0))

    def put(head, first, part):
        place = slice((first + head) * width, (first + head + 1) * width)
        out_ref[:, place] = part.astype(jnp.bfloat16).T

    def attend(head, share):
        attended = dot(turned_window(width), weights[:, columns[head]], (1, 0))
        attended = (attended * share).astype(jnp.bfloat16)
        put(head, 0, attended)
        products = attended.astype(jnp.float32) * cotangents_turned[head].astype(jnp.float32)
        return jnp.sum(products, axis=0, keepdims=True)

    def weigh_grad(head, item, row_delta):
        part = weights[tiles[item], columns[head]].astype(jnp.float32)
        part = (part * (grads[head][item] - row_delta)).astype(jnp.bfloat16)
        grad_weights[tiles[item], columns[head]] = part

    def make_query_grad(head, share):
        query_grad = dot(turned_window(0), grad_weights[:, columns[head]], (1, 0))
        put(head, 2, query_grad * (share * SCORE_SCALE))

    def scaled(parts, shares):
        scaled_parts = []
        for part, share in zip(parts, shares):
            down = jnp.broadcast_to(share, (8, TILE)).T[:, :1]
            scaled_parts.append((part.astype(jnp.float32) * down).astype(jnp.bfloat16))
        return jnp.concatenate(scaled_parts, axis=0)

    for item in range(SPAN):
        score(0, item)
    for item in range(SPAN):
        score(1, item)
        weigh(0, item)
    for item in range(SPAN):
        grade(0, item)
        weigh(1, item)
    shares = [1.0 / total for total in totals]
    delta = attend(0, shares[0])
    for item in range(SPAN):
        grade(1, item)
        weigh_grad(0, item, delta)
    delta = attend(1, shares[1])
    cotangents_scaled = scaled(cotangents, shares)
    queries_scaled = scaled(queries, shares)
    for item in range(SPAN):
        add(item, width, dot(weights[tiles[item]], cotangents_scaled, (1, 0)))
        weigh_grad(1, item, delta)
    make_query_grad(0, shares[0])
    make_query_grad(1, shares[1])
    for item in range(SPAN):
        add(item, 0, dot(grad_weights[tiles[item]], queries_scaled, (1, 0)))

    def send(chunk):
        low_sums[chunk, :, :width] = (sums[chunk, :, :width] * SCORE_SCALE).astype(jnp.bfloat16)
        low_sums[chunk, :, width:] = sums[chunk, :, width:].astype(jnp.bfloat16)

    def departure(item, own):
        half, part, chunk = item // HALF, item % HALF, member ^ BACK_DISTANCES[item]
        place = MEMBERS + chunk if own else chunk
        halves = own_grads if own else earlier_grads
        return pltpu.make_async_copy(low_sums.at[place], halves[half].at[part], sent.at[place])

    for part in range(CHUNKS):
        send(step * CHUNKS + part)
    for item, distance in enumerate(BACK_DISTANCES):
        pl.when((member ^ distance) // CHUNKS == step)(departure(item, False).start)

    @pl.when(step == TILES - 1)
    def _():
        for chunk in range(MEMBERS, 2 * MEMBERS):
            send(chunk)
        for item in range(MEMBERS):
            departure(item, True).start()
        for item in range(MEMBERS):
            departure(item, False).wait()
            departure(item, True).wait()


def attention(doc_lengths, rows, own, earlier):
    width = HEAD_WIDTH
    products = 6 * 2 * WINDOW_LENGTH * 2 * KEYS * width
    half = jax.ShapeDtypeStruct((HALF, ROWS, 2 * width), jnp.bfloat16)
    rows_block = pl.BlockSpec((TILE, 4 * width), lambda i: (i, 0))
    outputs = pl.pallas_call(
        attention_kernel,
        grid=(TILES,),
        in_specs=[SCALARS, rows_block] + [ANYWHERE] * 4,
        out_specs=[rows_block] + [ANYWHERE] * 4,
        out_shape=[jax.ShapeDtypeStruct(rows.shape, jnp.bfloat16)] + [half] * 4,
        scratch_shapes=[
            pltpu.VMEM((2 * MEMBERS, ROWS, 2 * width), jnp.bfloat16),
            pltpu.VMEM((2 * width, 2 * WINDOW_LENGTH), jnp.bfloat16),
            pltpu.VMEM((2 * MEMBERS, ROWS, 2 * width), jnp.float32),
            pltpu.VMEM((2 * MEMBERS, ROWS, 2 * width), jnp.bfloat16),
            pltpu.VMEM((KEYS, COLUMNS), jnp.bfloat16),
            pltpu.VMEM((KEYS, COLUMNS), jnp.bfloat16),
        ]
        + [pltpu.VMEM((SPAN, TILE, TILE), jnp.float32)] * 4
        + [pltpu.SemaphoreType.DMA((2 * MEMBERS,))] * 2,
        compiler_params=LIMIT,
        cost_estimate=pl.CostEstimate(
            flops=2 * products, bytes_accessed=WINDOW_LENGTH * width * 30, transcendentals=0
        ),
    )(doc_lengths, rows, *own, *earlier)
    return outputs[0], outputs[1:3], outputs[3:]


def by_head(block):
    return block.reshape(ROWS, MEMBERS, block.shape[1] // MEMBERS).transpose(1, 0, 2)


def by_token(blocks):
    return blocks.transpose(1, 0, 2).reshape(ROWS, MEMBERS * blocks.shape[2])


def exchanged(blocks):
    return lax.all_to_all(blocks, "member", split_axis=0, concat_axis=0, tiled=True)


def swapped(pieces, distances):
    moved = []
    for piece, distance in zip(pieces, distances):
        route = [(i, i ^ distance) for i in range(MEMBERS)]
        moved.append(lax.ppermute(piece, "member", route) if distance else piece)
    return moved


def onward(block, direction):
    lower = [(i, i + 1) for i in range(lax.axis_size("stretch") - 1)]
    route = lower if direction > 0 else [(j, i) for i, j in lower]
    return lax.ppermute(block, "stretch", route)


def shards(rotated_query_rows, rotated_key_rows, value_matrix, output_gradient, doc_lengths):
    pieces = swapped(pack(rotated_key_rows, value_matrix), DISTANCES)
    rows = jnp.concatenate([by_head(rotated_query_rows), by_head(output_gradient)], axis=2)
    pieces, rows = lax.optimization_barrier((pieces, rows))
    own = [jnp.stack(pieces[:HALF]), jnp.stack(pieces[HALF:])]
    earlier = [onward(half, 1) for half in own]
    rows = exchanged(rows).reshape(WINDOW_LENGTH, 4 * HEAD_WIDTH)
    results, own_grads, earlier_grads = attention(doc_lengths, rows, own, earlier)
    later = [onward(half, -1) for half in earlier_grads]
    results = exchanged(results.reshape(MEMBERS, ROWS, 4 * HEAD_WIDTH))
    attended = by_token(results[:, :, : 2 * HEAD_WIDTH])
    query_grad = by_token(results[:, :, 2 * HEAD_WIDTH :])
    sums = [
        (own_grads[half].astype(jnp.float32) + later[half].astype(jnp.float32)).astype(
            jnp.bfloat16
        )
        for half in range(2)
    ]
    pieces = [sums[item // HALF][item % HALF] for item in range(MEMBERS)]
    pieces = swapped(pieces, BACK_DISTANCES)
    attended, query_grad, pieces = lax.optimization_barrier((attended, query_grad, pieces))
    return (attended, query_grad, *unpack(pieces))


def solution(mesh):
    grouped = Mesh(mesh.devices.reshape(-1, MEMBERS), ("stretch", "member"))
    spread = P(("stretch", "member"), None)
    return jax.shard_map(
        shards,
        mesh=grouped,
        in_specs=(spread, spread, spread, spread, P()),
        out_specs=(spread, spread, spread, spread),
        check_vma=False,
    )
```

```python
import jax
import jax.numpy as jnp
from jax import lax
from jax.experimental import pallas as pl
from jax.experimental.pallas import tpu as pltpu
from jax.sharding import Mesh
from jax.sharding import PartitionSpec as P

HEAD_WIDTH = 256
WINDOW_LENGTH = 1024
MEMBERS = 8
HALF = MEMBERS // 2
DISTANCES = (7, 6, 5, 4, 3, 2, 1, 0)
BACK_DISTANCES = (7, 6, 5, 4, 0, 1, 2, 3)

TILE = 256
TILES = WINDOW_LENGTH // TILE
SPAN = TILES + 1
KEYS = SPAN * TILE
ROWS = WINDOW_LENGTH // MEMBERS
CHUNKS = TILE // ROWS
COLUMNS = 2 * TILE
SCORE_SCALE = HEAD_WIDTH ** (-0.5)
LOG2_E = 1.4426950408889634

ANYWHERE = pl.BlockSpec(memory_space=pl.ANY)
IN_HBM = pl.BlockSpec(memory_space=pltpu.HBM)
SCALARS = pl.BlockSpec(memory_space=pltpu.SMEM)
SMALL_LIMIT = pltpu.CompilerParams(vmem_limit_bytes=4 * 1024 * 1024)
WHOLE_LIMIT = pltpu.CompilerParams(vmem_limit_bytes=64 * 1024 * 1024)
LIMIT = pltpu.CompilerParams(vmem_limit_bytes=48 * 1024 * 1024)


def dot(left, right, contract):
    return lax.dot_general(
        left, right, ((contract[:1], contract[1:]), ((), ())), preferred_element_type=jnp.float32
    )


def copies_of(pairs, semaphores):
    return [
        pltpu.make_async_copy(source, target, semaphores.at[item])
        for item, (source, target) in enumerate(pairs)
    ]


def columns_of(ref, head, width):
    return ref.at[:, pl.ds(pl.multiple_of(head * width, width), width)]


def staged(arriving, leaving):
    for copies in arriving:
        for copy in copies:
            copy.start()
    for copies, onward in zip(arriving, leaving):
        for copy in copies:
            copy.wait()
        for copy in onward:
            copy.start()
    for onward in leaving:
        for copy in onward:
            copy.wait()


def pack_kernel(left_ref, right_ref, *refs):
    pieces, (buffer, arrived, sent) = refs[:MEMBERS], refs[MEMBERS:]
    member = lax.axis_index("member")
    width = left_ref.shape[1] // MEMBERS
    arriving, leaving = [], []
    for item, distance in enumerate(DISTANCES):
        head = member ^ distance
        pairs = [
            (columns_of(left_ref, head, width), buffer.at[item, :, pl.ds(0, width)]),
            (columns_of(right_ref, head, width), buffer.at[item, :, pl.ds(width, width)]),
        ]
        arriving.append(copies_of(pairs, arrived.at[item]))
        leaving.append([pltpu.make_async_copy(buffer.at[item], pieces[item], sent.at[item])])
    staged(arriving, leaving)


def pack(left, right):
    rows, columns = left.shape
    shape = (rows, 2 * columns // MEMBERS)
    return pl.pallas_call(
        pack_kernel,
        in_specs=[IN_HBM] * 2,
        out_specs=[IN_HBM] * MEMBERS,
        out_shape=[jax.ShapeDtypeStruct(shape, left.dtype)] * MEMBERS,
        scratch_shapes=[
            pltpu.VMEM((MEMBERS, *shape), left.dtype),
            pltpu.SemaphoreType.DMA((MEMBERS, 2)),
            pltpu.SemaphoreType.DMA((MEMBERS,)),
        ],
        compiler_params=WHOLE_LIMIT,
        cost_estimate=pl.CostEstimate(
            flops=0, bytes_accessed=8 * rows * columns, transcendentals=0
        ),
    )(left, right)


def unpack_kernel(*refs):
    pieces, refs = refs[:MEMBERS], refs[MEMBERS:]
    left_ref, right_ref, buffer, arrived, sent = refs
    member = lax.axis_index("member")
    width = left_ref.shape[1] // MEMBERS
    arriving, leaving = [], []
    for item, distance in enumerate(BACK_DISTANCES):
        head = member ^ distance
        arriving.append([pltpu.make_async_copy(pieces[item], buffer.at[item], arrived.at[item])])
        pairs = [
            (buffer.at[item, :, pl.ds(0, width)], columns_of(left_ref, head, width)),
            (buffer.at[item, :, pl.ds(width, width)], columns_of(right_ref, head, width)),
        ]
        leaving.append(copies_of(pairs, sent.at[item]))
    staged(arriving, leaving)


def unpack(pieces):
    rows, columns = pieces[0].shape
    whole = jax.ShapeDtypeStruct((rows, MEMBERS * columns // 2), pieces[0].dtype)
    return pl.pallas_call(
        unpack_kernel,
        in_specs=[ANYWHERE] * MEMBERS,
        out_specs=[ANYWHERE] * 2,
        out_shape=[whole] * 2,
        scratch_shapes=[
            pltpu.VMEM((MEMBERS, rows, columns), pieces[0].dtype),
            pltpu.SemaphoreType.DMA((MEMBERS,)),
            pltpu.SemaphoreType.DMA((MEMBERS, 2)),
        ],
        compiler_params=SMALL_LIMIT,
        cost_estimate=pl.CostEstimate(
            flops=0, bytes_accessed=4 * MEMBERS * rows * columns, transcendentals=0
        ),
    )(*pieces)


def attention_kernel(lengths_ref, rows_ref, *refs):
    own_halves, earlier_halves, out_ref, refs = refs[:2], refs[2:4], refs[4], refs[5:]
    own_grads, earlier_grads, refs = refs[:2], refs[2:4], refs[4:]
    kv, kv_turned, sums, weights, grad_weights, refs = *refs[:5], refs[5:]
    scores, grads = refs[:2], refs[2:4]
    step = pl.program_id(0)
    width = HEAD_WIDTH
    member = lax.axis_index("member")

    def turn(tile):
        part = kv[pl.ds(tile * CHUNKS, CHUNKS)].reshape(TILE, 2 * width)
        kv_turned[:, pl.ds(pl.multiple_of(tile * TILE, TILE), TILE)] = part.T

    @pl.when(step == 0)
    def _():
        for item, distance in enumerate(DISTANCES):
            half, part, chunk = item // HALF, item % HALF, member ^ distance
            kv[chunk] = earlier_halves[half][part]
            kv[MEMBERS + chunk] = own_halves[half][part]
        sums[:MEMBERS] = jnp.zeros((MEMBERS, ROWS, 2 * width), jnp.float32)
        for tile in range(TILES):
            turn(tile)

    turn(TILES + step)

    def key_tile(item, first):
        tile = pl.ds((step + item) * CHUNKS, CHUNKS)
        return kv[tile, :, first : first + width].reshape(TILE, width)

    def turned_window(first):
        place = pl.ds(pl.multiple_of(step * TILE, TILE), KEYS)
        return kv_turned[first : first + width, place]

    def add(item, first, part):
        tile = pl.ds((step + item) * CHUNKS, CHUNKS)
        part = part.reshape(CHUNKS, ROWS, width)
        if item < TILES:
            part = sums[tile, :, first : first + width] + part
        sums[tile, :, first : first + width] = part

    queries = [rows_ref[:, head * width : (head + 1) * width] for head in range(2)]
    cotangents = [rows_ref[:, (2 + head) * width : (3 + head) * width] for head in range(2)]
    queries_turned = [part.T for part in queries]
    cotangents_turned = [part.T for part in cotangents]
    columns = [slice(head * TILE, (head + 1) * TILE) for head in range(2)]
    tiles = [slice(item * TILE, (item + 1) * TILE) for item in range(SPAN)]

    first_row = lax.axis_index("stretch") * WINDOW_LENGTH + step * TILE
    row = lax.broadcasted_iota(jnp.int32, (1, TILE), 1)
    oldest = row - (WINDOW_LENGTH - 1)

    def passed(item, carried):
        begin, oldest = carried
        near = begin - first_row
        oldest = jnp.where(near <= row, jnp.maximum(oldest, near), oldest)
        return begin + lengths_ref[item], oldest

    _, oldest = lax.fori_loop(0, lengths_ref.shape[0], passed, (jnp.int32(0), oldest))
    key_row = lax.broadcasted_iota(jnp.int32, (TILE, TILE), 0)

    tops = [jnp.full((1, TILE), -jnp.inf, jnp.float32)] * 2
    totals = [jnp.zeros((1, TILE), jnp.float32)] * 2

    def score(head, item):
        part = dot(key_tile(item, 0), queries_turned[head], (1, 0))
        seen = key_row >= oldest - (item - TILES) * TILE
        if item == TILES:
            seen = seen & (key_row <= row)
        part = jnp.where(seen, part, -jnp.inf)
        tops[head] = jnp.maximum(tops[head], jnp.max(part, axis=0, keepdims=True))
        scores[head][item] = part

    def weigh(head, item):
        part = jnp.exp2((scores[head][item] - tops[head]) * (SCORE_SCALE * LOG2_E))
        totals[head] = totals[head] + jnp.sum(part, axis=0, keepdims=True)
        weights[tiles[item], columns[head]] = part.astype(jnp.bfloat16)

    def grade(head, item):
        grads[head][item] = dot(key_tile(item, width), cotangents_turned[head], (1, 0))

    def put(head, first, part):
        place = slice((first + head) * width, (first + head + 1) * width)
        out_ref[:, place] = part.astype(jnp.bfloat16).T

    def attend(head, share):
        attended = dot(turned_window(width), weights[:, columns[head]], (1, 0))
        attended = (attended * share).astype(jnp.bfloat16)
        put(head, 0, attended)
        products = attended.astype(jnp.float32) * cotangents_turned[head].astype(jnp.float32)
        return jnp.sum(products, axis=0, keepdims=True)

    def weigh_grad(head, item, row_delta):
        part = weights[tiles[item], columns[head]].astype(jnp.float32)
        part = (part * (grads[head][item] - row_delta)).astype(jnp.bfloat16)
        grad_weights[tiles[item], columns[head]] = part

    def make_query_grad(head, share):
        query_grad = dot(turned_window(0), grad_weights[:, columns[head]], (1, 0))
        put(head, 2, query_grad * (share * SCORE_SCALE))

    def scaled(parts, shares):
        scaled_parts = []
        for part, share in zip(parts, shares):
            down = jnp.broadcast_to(share, (8, TILE)).T[:, :1]
            scaled_parts.append((part.astype(jnp.float32) * down).astype(jnp.bfloat16))
        return jnp.concatenate(scaled_parts, axis=0)

    for item in range(SPAN):
        score(0, item)
    for item in range(SPAN):
        score(1, item)
        weigh(0, item)
    for item in range(SPAN):
        grade(0, item)
        weigh(1, item)
    shares = [1.0 / total for total in totals]
    delta = attend(0, shares[0])
    for item in range(SPAN):
        grade(1, item)
        weigh_grad(0, item, delta)
    delta = attend(1, shares[1])
    cotangents_scaled = scaled(cotangents, shares)
    queries_scaled = scaled(queries, shares)
    for item in range(SPAN):
        add(item, width, dot(weights[tiles[item]], cotangents_scaled, (1, 0)))
        weigh_grad(1, item, delta)
    make_query_grad(0, shares[0])
    make_query_grad(1, shares[1])
    for item in range(SPAN):
        add(item, 0, dot(grad_weights[tiles[item]], queries_scaled, (1, 0)))

    @pl.when(step == TILES - 1)
    def _():
        for item, distance in enumerate(BACK_DISTANCES):
            half, part, chunk = item // HALF, item % HALF, member ^ distance
            for halves, place in ((earlier_grads, chunk), (own_grads, MEMBERS + chunk)):
                target = halves[half]
                target[part, :, :width] = (sums[place, :, :width] * SCORE_SCALE).astype(
                    jnp.bfloat16
                )
                target[part, :, width:] = sums[place, :, width:].astype(jnp.bfloat16)


def attention(doc_lengths, rows, own, earlier):
    width = HEAD_WIDTH
    products = 6 * 2 * WINDOW_LENGTH * 2 * KEYS * width
    half = jax.ShapeDtypeStruct((HALF, ROWS, 2 * width), jnp.bfloat16)
    rows_block = pl.BlockSpec((TILE, 4 * width), lambda i: (i, 0))
    half_block = pl.BlockSpec(half.shape, lambda i: (0, 0, 0))
    outputs = pl.pallas_call(
        attention_kernel,
        grid=(TILES,),
        in_specs=[SCALARS, rows_block] + [half_block] * 4,
        out_specs=[rows_block] + [half_block] * 4,
        out_shape=[jax.ShapeDtypeStruct(rows.shape, jnp.bfloat16)] + [half] * 4,
        scratch_shapes=[
            pltpu.VMEM((2 * MEMBERS, ROWS, 2 * width), jnp.bfloat16),
            pltpu.VMEM((2 * width, 2 * WINDOW_LENGTH), jnp.bfloat16),
            pltpu.VMEM((2 * MEMBERS, ROWS, 2 * width), jnp.float32),
            pltpu.VMEM((KEYS, COLUMNS), jnp.bfloat16),
            pltpu.VMEM((KEYS, COLUMNS), jnp.bfloat16),
        ]
        + [pltpu.VMEM((SPAN, TILE, TILE), jnp.float32)] * 4,
        compiler_params=LIMIT,
        cost_estimate=pl.CostEstimate(
            flops=2 * products, bytes_accessed=WINDOW_LENGTH * width * 30, transcendentals=0
        ),
    )(doc_lengths, rows, *own, *earlier)
    return outputs[0], outputs[1:3], outputs[3:]


def by_head(block):
    return block.reshape(ROWS, MEMBERS, block.shape[1] // MEMBERS).transpose(1, 0, 2)


def by_token(blocks):
    return blocks.transpose(1, 0, 2).reshape(ROWS, MEMBERS * blocks.shape[2])


def exchanged(blocks):
    return lax.all_to_all(blocks, "member", split_axis=0, concat_axis=0, tiled=True)


def swapped(pieces, distances):
    moved = []
    for piece, distance in zip(pieces, distances):
        route = [(i, i ^ distance) for i in range(MEMBERS)]
        moved.append(lax.ppermute(piece, "member", route) if distance else piece)
    return moved


def onward(block, direction):
    lower = [(i, i + 1) for i in range(lax.axis_size("stretch") - 1)]
    route = lower if direction > 0 else [(j, i) for i, j in lower]
    return lax.ppermute(block, "stretch", route)


def shards(rotated_query_rows, rotated_key_rows, value_matrix, output_gradient, doc_lengths):
    pieces = swapped(pack(rotated_key_rows, value_matrix), DISTANCES)
    rows = jnp.concatenate([by_head(rotated_query_rows), by_head(output_gradient)], axis=2)
    pieces, rows = lax.optimization_barrier((pieces, rows))
    own = [jnp.stack(pieces[:HALF]), jnp.stack(pieces[HALF:])]
    earlier = [onward(half, 1) for half in own]
    rows = exchanged(rows).reshape(WINDOW_LENGTH, 4 * HEAD_WIDTH)
    results, own_grads, earlier_grads = attention(doc_lengths, rows, own, earlier)
    later = [onward(half, -1) for half in earlier_grads]
    results = exchanged(results.reshape(MEMBERS, ROWS, 4 * HEAD_WIDTH))
    attended = by_token(results[:, :, : 2 * HEAD_WIDTH])
    query_grad = by_token(results[:, :, 2 * HEAD_WIDTH :])
    sums = [
        (own_grads[half].astype(jnp.float32) + later[half].astype(jnp.float32)).astype(
            jnp.bfloat16
        )
        for half in range(2)
    ]
    pieces = [sums[item // HALF][item % HALF] for item in range(MEMBERS)]
    pieces = swapped(pieces, BACK_DISTANCES)
    attended, query_grad, pieces = lax.optimization_barrier((attended, query_grad, pieces))
    return (attended, query_grad, *unpack(pieces))


def solution(mesh):
    grouped = Mesh(mesh.devices.reshape(-1, MEMBERS), ("stretch", "member"))
    spread = P(("stretch", "member"), None)
    return jax.shard_map(
        shards,
        mesh=grouped,
        in_specs=(spread, spread, spread, spread, P()),
        out_specs=(spread, spread, spread, spread),
        check_vma=False,
    )
```

```python
import jax
import jax.numpy as jnp
from jax import lax
from jax.experimental import pallas as pl
from jax.experimental.pallas import tpu as pltpu
from jax.sharding import Mesh
from jax.sharding import PartitionSpec as P

HEAD_WIDTH = 256
WINDOW_LENGTH = 1024
MEMBERS = 8
HALF = MEMBERS // 2
DISTANCES = (7, 6, 5, 4, 3, 2, 1, 0)
BACK_DISTANCES = (7, 6, 5, 4, 0, 1, 2, 3)

TILE = 256
TILES = WINDOW_LENGTH // TILE
SPAN = TILES + 1
KEYS = SPAN * TILE
ROWS = WINDOW_LENGTH // MEMBERS
CHUNKS = TILE // ROWS
COLUMNS = 2 * TILE
SCORE_SCALE = HEAD_WIDTH ** (-0.5)
LOG2_E = 1.4426950408889634

ANYWHERE = pl.BlockSpec(memory_space=pl.ANY)
IN_HBM = pl.BlockSpec(memory_space=pltpu.HBM)
SCALARS = pl.BlockSpec(memory_space=pltpu.SMEM)
SMALL_LIMIT = pltpu.CompilerParams(vmem_limit_bytes=4 * 1024 * 1024)
WHOLE_LIMIT = pltpu.CompilerParams(vmem_limit_bytes=64 * 1024 * 1024)
LIMIT = pltpu.CompilerParams(vmem_limit_bytes=40 * 1024 * 1024)


def dot(left, right, contract):
    return lax.dot_general(
        left, right, ((contract[:1], contract[1:]), ((), ())), preferred_element_type=jnp.float32
    )


def copies_of(pairs, semaphores):
    return [
        pltpu.make_async_copy(source, target, semaphores.at[item])
        for item, (source, target) in enumerate(pairs)
    ]


def columns_of(ref, head, width):
    return ref.at[:, pl.ds(pl.multiple_of(head * width, width), width)]


def staged(arriving, leaving):
    for copies in arriving:
        for copy in copies:
            copy.start()
    for copies, onward in zip(arriving, leaving):
        for copy in copies:
            copy.wait()
        for copy in onward:
            copy.start()
    for onward in leaving:
        for copy in onward:
            copy.wait()


def pack_kernel(left_ref, right_ref, *refs):
    pieces, (buffer, arrived, sent) = refs[:MEMBERS], refs[MEMBERS:]
    member = lax.axis_index("member")
    width = left_ref.shape[1] // MEMBERS
    arriving, leaving = [], []
    for item, distance in enumerate(DISTANCES):
        head = member ^ distance
        pairs = [
            (columns_of(left_ref, head, width), buffer.at[item, :, pl.ds(0, width)]),
            (columns_of(right_ref, head, width), buffer.at[item, :, pl.ds(width, width)]),
        ]
        arriving.append(copies_of(pairs, arrived.at[item]))
        leaving.append([pltpu.make_async_copy(buffer.at[item], pieces[item], sent.at[item])])
    staged(arriving, leaving)


def pack(left, right):
    rows, columns = left.shape
    shape = (rows, 2 * columns // MEMBERS)
    return pl.pallas_call(
        pack_kernel,
        in_specs=[IN_HBM] * 2,
        out_specs=[IN_HBM] * MEMBERS,
        out_shape=[jax.ShapeDtypeStruct(shape, left.dtype)] * MEMBERS,
        scratch_shapes=[
            pltpu.VMEM((MEMBERS, *shape), left.dtype),
            pltpu.SemaphoreType.DMA((MEMBERS, 2)),
            pltpu.SemaphoreType.DMA((MEMBERS,)),
        ],
        compiler_params=WHOLE_LIMIT,
        cost_estimate=pl.CostEstimate(
            flops=0, bytes_accessed=8 * rows * columns, transcendentals=0
        ),
    )(left, right)


def unpack_kernel(*refs):
    pieces, refs = refs[:MEMBERS], refs[MEMBERS:]
    left_ref, right_ref, buffer, arrived, sent = refs
    member = lax.axis_index("member")
    width = left_ref.shape[1] // MEMBERS
    arriving, leaving = [], []
    for item, distance in enumerate(BACK_DISTANCES):
        head = member ^ distance
        arriving.append([pltpu.make_async_copy(pieces[item], buffer.at[item], arrived.at[item])])
        pairs = [
            (buffer.at[item, :, pl.ds(0, width)], columns_of(left_ref, head, width)),
            (buffer.at[item, :, pl.ds(width, width)], columns_of(right_ref, head, width)),
        ]
        leaving.append(copies_of(pairs, sent.at[item]))
    staged(arriving, leaving)


def unpack(pieces):
    rows, columns = pieces[0].shape
    whole = jax.ShapeDtypeStruct((rows, MEMBERS * columns // 2), pieces[0].dtype)
    return pl.pallas_call(
        unpack_kernel,
        in_specs=[ANYWHERE] * MEMBERS,
        out_specs=[ANYWHERE] * 2,
        out_shape=[whole] * 2,
        scratch_shapes=[
            pltpu.VMEM((MEMBERS, rows, columns), pieces[0].dtype),
            pltpu.SemaphoreType.DMA((MEMBERS,)),
            pltpu.SemaphoreType.DMA((MEMBERS, 2)),
        ],
        compiler_params=SMALL_LIMIT,
        cost_estimate=pl.CostEstimate(
            flops=0, bytes_accessed=4 * MEMBERS * rows * columns, transcendentals=0
        ),
    )(*pieces)


def attention_kernel(lengths_ref, rows_ref, *refs):
    own_halves, earlier_halves, out_ref, refs = refs[:2], refs[2:4], refs[4], refs[5:]
    own_grads, earlier_grads, refs = refs[:2], refs[2:4], refs[4:]
    kv, kv_turned, sums, weights, grad_weights, refs = *refs[:5], refs[5:]
    scores, grads = refs[:2], refs[2:4]
    step = pl.program_id(0)
    width = HEAD_WIDTH
    member = lax.axis_index("member")

    def turn(tile):
        part = kv[pl.ds(tile * CHUNKS, CHUNKS)].reshape(TILE, 2 * width)
        kv_turned[:, pl.ds(pl.multiple_of(tile * TILE, TILE), TILE)] = part.T

    @pl.when(step == 0)
    def _():
        for item, distance in enumerate(DISTANCES):
            half, part, chunk = item // HALF, item % HALF, member ^ distance
            kv[chunk] = earlier_halves[half][part]
            kv[MEMBERS + chunk] = own_halves[half][part]
        sums[:MEMBERS] = jnp.zeros((MEMBERS, ROWS, 2 * width), jnp.float32)
        for tile in range(TILES):
            turn(tile)

    turn(TILES + step)

    def key_tile(item, first):
        tile = pl.ds((step + item) * CHUNKS, CHUNKS)
        return kv[tile, :, first : first + width].reshape(TILE, width)

    def turned_window(first):
        place = pl.ds(pl.multiple_of(step * TILE, TILE), KEYS)
        return kv_turned[first : first + width, place]

    def add(item, first, part):
        tile = pl.ds((step + item) * CHUNKS, CHUNKS)
        part = part.reshape(CHUNKS, ROWS, width)
        if item < TILES:
            part = sums[tile, :, first : first + width] + part
        sums[tile, :, first : first + width] = part

    queries = [rows_ref[:, head * width : (head + 1) * width] for head in range(2)]
    cotangents = [rows_ref[:, (2 + head) * width : (3 + head) * width] for head in range(2)]
    queries_turned = [part.T for part in queries]
    cotangents_turned = [part.T for part in cotangents]
    columns = [slice(head * TILE, (head + 1) * TILE) for head in range(2)]
    tiles = [slice(item * TILE, (item + 1) * TILE) for item in range(SPAN)]

    first_row = lax.axis_index("stretch") * WINDOW_LENGTH + step * TILE
    row = lax.broadcasted_iota(jnp.int32, (1, TILE), 1)
    oldest = row - (WINDOW_LENGTH - 1)

    def passed(item, carried):
        begin, oldest = carried
        near = begin - first_row
        oldest = jnp.where(near <= row, jnp.maximum(oldest, near), oldest)
        return begin + lengths_ref[item], oldest

    _, oldest = lax.fori_loop(0, lengths_ref.shape[0], passed, (jnp.int32(0), oldest))
    key_row = lax.broadcasted_iota(jnp.int32, (TILE, TILE), 0)

    tops = [jnp.full((1, TILE), -jnp.inf, jnp.float32)] * 2
    totals = [jnp.zeros((1, TILE), jnp.float32)] * 2

    def score(head, item):
        part = dot(key_tile(item, 0), queries_turned[head], (1, 0))
        seen = key_row >= oldest - (item - TILES) * TILE
        if item == TILES:
            seen = seen & (key_row <= row)
        part = jnp.where(seen, part, -jnp.inf)
        tops[head] = jnp.maximum(tops[head], jnp.max(part, axis=0, keepdims=True))
        scores[head][item] = part

    def weigh(head, item):
        part = jnp.exp2((scores[head][item] - tops[head]) * (SCORE_SCALE * LOG2_E))
        totals[head] = totals[head] + jnp.sum(part, axis=0, keepdims=True)
        weights[tiles[item], columns[head]] = part.astype(jnp.bfloat16)

    def grade(head, item):
        grads[head][item] = dot(key_tile(item, width), cotangents_turned[head], (1, 0))

    def put(head, first, part):
        place = slice((first + head) * width, (first + head + 1) * width)
        out_ref[:, place] = part.astype(jnp.bfloat16).T

    def attend(head, share):
        attended = dot(turned_window(width), weights[:, columns[head]], (1, 0))
        attended = (attended * share).astype(jnp.bfloat16)
        put(head, 0, attended)
        products = attended.astype(jnp.float32) * cotangents_turned[head].astype(jnp.float32)
        return jnp.sum(products, axis=0, keepdims=True)

    def weigh_grad(head, item, row_delta):
        part = weights[tiles[item], columns[head]].astype(jnp.float32)
        part = (part * (grads[head][item] - row_delta)).astype(jnp.bfloat16)
        grad_weights[tiles[item], columns[head]] = part

    def make_query_grad(head, share):
        query_grad = dot(turned_window(0), grad_weights[:, columns[head]], (1, 0))
        put(head, 2, query_grad * (share * SCORE_SCALE))

    def scaled(parts, shares):
        scaled_parts = []
        for part, share in zip(parts, shares):
            down = jnp.broadcast_to(share, (8, TILE)).T[:, :1]
            scaled_parts.append((part.astype(jnp.float32) * down).astype(jnp.bfloat16))
        return jnp.concatenate(scaled_parts, axis=0)

    for item in range(SPAN):
        score(0, item)
    for item in range(SPAN):
        score(1, item)
        weigh(0, item)
    for item in range(SPAN):
        grade(0, item)
        weigh(1, item)
    shares = [1.0 / total for total in totals]
    delta = attend(0, shares[0])
    for item in range(SPAN):
        grade(1, item)
        weigh_grad(0, item, delta)
    delta = attend(1, shares[1])
    cotangents_scaled = scaled(cotangents, shares)
    queries_scaled = scaled(queries, shares)
    for item in range(SPAN):
        add(item, width, dot(weights[tiles[item]], cotangents_scaled, (1, 0)))
        weigh_grad(1, item, delta)
    make_query_grad(0, shares[0])
    make_query_grad(1, shares[1])
    for item in range(SPAN):
        add(item, 0, dot(grad_weights[tiles[item]], queries_scaled, (1, 0)))

    @pl.when(step == TILES - 1)
    def _():
        for item, distance in enumerate(BACK_DISTANCES):
            half, part, chunk = item // HALF, item % HALF, member ^ distance
            for halves, place in ((earlier_grads, chunk), (own_grads, MEMBERS + chunk)):
                target = halves[half]
                target[part, :, :width] = (sums[place, :, :width] * SCORE_SCALE).astype(
                    jnp.bfloat16
                )
                target[part, :, width:] = sums[place, :, width:].astype(jnp.bfloat16)


def attention(doc_lengths, rows, own, earlier):
    width = HEAD_WIDTH
    products = 6 * 2 * WINDOW_LENGTH * 2 * KEYS * width
    half = jax.ShapeDtypeStruct((HALF, ROWS, 2 * width), jnp.bfloat16)
    rows_block = pl.BlockSpec((TILE, 4 * width), lambda i: (i, 0))
    half_block = pl.BlockSpec(half.shape, lambda i: (0, 0, 0))
    outputs = pl.pallas_call(
        attention_kernel,
        grid=(TILES,),
        in_specs=[SCALARS, rows_block] + [half_block] * 4,
        out_specs=[rows_block] + [half_block] * 4,
        out_shape=[jax.ShapeDtypeStruct(rows.shape, jnp.bfloat16)] + [half] * 4,
        scratch_shapes=[
            pltpu.VMEM((2 * MEMBERS, ROWS, 2 * width), jnp.bfloat16),
            pltpu.VMEM((2 * width, 2 * WINDOW_LENGTH), jnp.bfloat16),
            pltpu.VMEM((2 * MEMBERS, ROWS, 2 * width), jnp.float32),
            pltpu.VMEM((KEYS, COLUMNS), jnp.bfloat16),
            pltpu.VMEM((KEYS, COLUMNS), jnp.bfloat16),
        ]
        + [pltpu.VMEM((SPAN, TILE, TILE), jnp.float32)] * 4,
        compiler_params=LIMIT,
        cost_estimate=pl.CostEstimate(
            flops=2 * products, bytes_accessed=WINDOW_LENGTH * width * 30, transcendentals=0
        ),
    )(doc_lengths, rows, *own, *earlier)
    return outputs[0], outputs[1:3], outputs[3:]


def by_head(block):
    return block.reshape(ROWS, MEMBERS, block.shape[1] // MEMBERS).transpose(1, 0, 2)


def by_token(blocks):
    return blocks.transpose(1, 0, 2).reshape(ROWS, MEMBERS * blocks.shape[2])


def exchanged(blocks):
    return lax.all_to_all(blocks, "member", split_axis=0, concat_axis=0, tiled=True)


def swapped(pieces, distances):
    moved = []
    for piece, distance in zip(pieces, distances):
        route = [(i, i ^ distance) for i in range(MEMBERS)]
        moved.append(lax.ppermute(piece, "member", route) if distance else piece)
    return moved


def onward(block, direction):
    lower = [(i, i + 1) for i in range(lax.axis_size("stretch") - 1)]
    route = lower if direction > 0 else [(j, i) for i, j in lower]
    return lax.ppermute(block, "stretch", route)


def shards(rotated_query_rows, rotated_key_rows, value_matrix, output_gradient, doc_lengths):
    pieces = swapped(pack(rotated_key_rows, value_matrix), DISTANCES)
    rows = jnp.concatenate([by_head(rotated_query_rows), by_head(output_gradient)], axis=2)
    pieces, rows = lax.optimization_barrier((pieces, rows))
    own = [jnp.stack(pieces[:HALF]), jnp.stack(pieces[HALF:])]
    earlier = [onward(half, 1) for half in own]
    rows = exchanged(rows).reshape(WINDOW_LENGTH, 4 * HEAD_WIDTH)
    results, own_grads, earlier_grads = attention(doc_lengths, rows, own, earlier)
    later = [onward(half, -1) for half in earlier_grads]
    results = exchanged(results.reshape(MEMBERS, ROWS, 4 * HEAD_WIDTH))
    attended = by_token(results[:, :, : 2 * HEAD_WIDTH])
    query_grad = by_token(results[:, :, 2 * HEAD_WIDTH :])
    sums = [
        (own_grads[half].astype(jnp.float32) + later[half].astype(jnp.float32)).astype(
            jnp.bfloat16
        )
        for half in range(2)
    ]
    pieces = [sums[item // HALF][item % HALF] for item in range(MEMBERS)]
    pieces = swapped(pieces, BACK_DISTANCES)
    attended, query_grad, pieces = lax.optimization_barrier((attended, query_grad, pieces))
    return (attended, query_grad, *unpack(pieces))


def solution(mesh):
    grouped = Mesh(mesh.devices.reshape(-1, MEMBERS), ("stretch", "member"))
    spread = P(("stretch", "member"), None)
    return jax.shard_map(
        shards,
        mesh=grouped,
        in_specs=(spread, spread, spread, spread, P()),
        out_specs=(spread, spread, spread, spread),
        check_vma=False,
    )
```

```python
import jax
import jax.numpy as jnp
from jax import lax
from jax.experimental import pallas as pl
from jax.experimental.pallas import tpu as pltpu
from jax.sharding import Mesh
from jax.sharding import PartitionSpec as P

HEAD_WIDTH = 256
WINDOW_LENGTH = 1024
MEMBERS = 8
HALF = MEMBERS // 2
DISTANCES = (7, 6, 5, 4, 3, 2, 1, 0)
BACK_DISTANCES = (7, 6, 5, 4, 0, 1, 2, 3)

TILE = 256
TILES = WINDOW_LENGTH // TILE
SPAN = TILES + 1
KEYS = SPAN * TILE
ROWS = WINDOW_LENGTH // MEMBERS
CHUNKS = TILE // ROWS
COLUMNS = 2 * TILE
SCORE_SCALE = HEAD_WIDTH ** (-0.5)
LOG2_E = 1.4426950408889634

ANYWHERE = pl.BlockSpec(memory_space=pl.ANY)
IN_HBM = pl.BlockSpec(memory_space=pltpu.HBM)
SCALARS = pl.BlockSpec(memory_space=pltpu.SMEM)
SMALL_LIMIT = pltpu.CompilerParams(vmem_limit_bytes=4 * 1024 * 1024)
WHOLE_LIMIT = pltpu.CompilerParams(vmem_limit_bytes=64 * 1024 * 1024)
LIMIT = pltpu.CompilerParams(vmem_limit_bytes=62 * 1024 * 1024)


def dot(left, right, contract):
    return lax.dot_general(
        left, right, ((contract[:1], contract[1:]), ((), ())), preferred_element_type=jnp.float32
    )


def copies_of(pairs, semaphores):
    return [
        pltpu.make_async_copy(source, target, semaphores.at[item])
        for item, (source, target) in enumerate(pairs)
    ]


def columns_of(ref, head, width):
    return ref.at[:, pl.ds(pl.multiple_of(head * width, width), width)]


def staged(arriving, leaving):
    for copies in arriving:
        for copy in copies:
            copy.start()
    for copies, onward in zip(arriving, leaving):
        for copy in copies:
            copy.wait()
        for copy in onward:
            copy.start()
    for onward in leaving:
        for copy in onward:
            copy.wait()


def pack_kernel(left_ref, right_ref, *refs):
    pieces, (buffer, arrived, sent) = refs[:MEMBERS], refs[MEMBERS:]
    member = lax.axis_index("member")
    width = left_ref.shape[1] // MEMBERS
    arriving, leaving = [], []
    for item, distance in enumerate(DISTANCES):
        head = member ^ distance
        pairs = [
            (columns_of(left_ref, head, width), buffer.at[item, :, pl.ds(0, width)]),
            (columns_of(right_ref, head, width), buffer.at[item, :, pl.ds(width, width)]),
        ]
        arriving.append(copies_of(pairs, arrived.at[item]))
        leaving.append([pltpu.make_async_copy(buffer.at[item], pieces[item], sent.at[item])])
    staged(arriving, leaving)


def pack(left, right):
    rows, columns = left.shape
    shape = (rows, 2 * columns // MEMBERS)
    return pl.pallas_call(
        pack_kernel,
        in_specs=[IN_HBM] * 2,
        out_specs=[IN_HBM] * MEMBERS,
        out_shape=[jax.ShapeDtypeStruct(shape, left.dtype)] * MEMBERS,
        scratch_shapes=[
            pltpu.VMEM((MEMBERS, *shape), left.dtype),
            pltpu.SemaphoreType.DMA((MEMBERS, 2)),
            pltpu.SemaphoreType.DMA((MEMBERS,)),
        ],
        compiler_params=WHOLE_LIMIT,
        cost_estimate=pl.CostEstimate(
            flops=0, bytes_accessed=8 * rows * columns, transcendentals=0
        ),
    )(left, right)


def unpack_kernel(*refs):
    pieces, refs = refs[:MEMBERS], refs[MEMBERS:]
    left_ref, right_ref, buffer, arrived, sent = refs
    member = lax.axis_index("member")
    width = left_ref.shape[1] // MEMBERS
    arriving, leaving = [], []
    for item, distance in enumerate(BACK_DISTANCES):
        head = member ^ distance
        arriving.append([pltpu.make_async_copy(pieces[item], buffer.at[item], arrived.at[item])])
        pairs = [
            (buffer.at[item, :, pl.ds(0, width)], columns_of(left_ref, head, width)),
            (buffer.at[item, :, pl.ds(width, width)], columns_of(right_ref, head, width)),
        ]
        leaving.append(copies_of(pairs, sent.at[item]))
    staged(arriving, leaving)


def unpack(pieces):
    rows, columns = pieces[0].shape
    whole = jax.ShapeDtypeStruct((rows, MEMBERS * columns // 2), pieces[0].dtype)
    return pl.pallas_call(
        unpack_kernel,
        in_specs=[ANYWHERE] * MEMBERS,
        out_specs=[ANYWHERE] * 2,
        out_shape=[whole] * 2,
        scratch_shapes=[
            pltpu.VMEM((MEMBERS, rows, columns), pieces[0].dtype),
            pltpu.SemaphoreType.DMA((MEMBERS,)),
            pltpu.SemaphoreType.DMA((MEMBERS, 2)),
        ],
        compiler_params=SMALL_LIMIT,
        cost_estimate=pl.CostEstimate(
            flops=0, bytes_accessed=4 * MEMBERS * rows * columns, transcendentals=0
        ),
    )(*pieces)


def attention_kernel(lengths_ref, rows_ref, *refs):
    own_halves, earlier_halves, out_ref, refs = refs[:2], refs[2:4], refs[4], refs[5:]
    own_grads, earlier_grads, refs = refs[:2], refs[2:4], refs[4:]
    kv, kv_turned, sums, weights, grad_weights, refs = *refs[:5], refs[5:]
    scores, grads = refs[:2], refs[2:4]
    step = pl.program_id(0)
    width = HEAD_WIDTH
    member = lax.axis_index("member")

    def turn(tile):
        part = kv[pl.ds(tile * CHUNKS, CHUNKS)].reshape(TILE, 2 * width)
        kv_turned[:, pl.ds(pl.multiple_of(tile * TILE, TILE), TILE)] = part.T

    @pl.when(step == 0)
    def _():
        for item, distance in enumerate(DISTANCES):
            half, part, chunk = item // HALF, item % HALF, member ^ distance
            kv[chunk] = earlier_halves[half][part]
            kv[MEMBERS + chunk] = own_halves[half][part]
        sums[:MEMBERS] = jnp.zeros((MEMBERS, ROWS, 2 * width), jnp.float32)
        for tile in range(TILES):
            turn(tile)

    turn(TILES + step)

    def key_tile(item, first):
        tile = pl.ds((step + item) * CHUNKS, CHUNKS)
        return kv[tile, :, first : first + width].reshape(TILE, width)

    def turned_window(first):
        place = pl.ds(pl.multiple_of(step * TILE, TILE), KEYS)
        return kv_turned[first : first + width, place]

    def add(item, first, part):
        tile = pl.ds((step + item) * CHUNKS, CHUNKS)
        part = part.reshape(CHUNKS, ROWS, width)
        if item < TILES:
            part = sums[tile, :, first : first + width] + part
        sums[tile, :, first : first + width] = part

    queries = [rows_ref[:, head * width : (head + 1) * width] for head in range(2)]
    cotangents = [rows_ref[:, (2 + head) * width : (3 + head) * width] for head in range(2)]
    queries_turned = [part.T for part in queries]
    cotangents_turned = [part.T for part in cotangents]
    columns = [slice(head * TILE, (head + 1) * TILE) for head in range(2)]
    tiles = [slice(item * TILE, (item + 1) * TILE) for item in range(SPAN)]

    first_row = lax.axis_index("stretch") * WINDOW_LENGTH + step * TILE
    row = lax.broadcasted_iota(jnp.int32, (1, TILE), 1)
    oldest = row - (WINDOW_LENGTH - 1)

    def passed(item, carried):
        begin, oldest = carried
        near = begin - first_row
        oldest = jnp.where(near <= row, jnp.maximum(oldest, near), oldest)
        return begin + lengths_ref[item], oldest

    _, oldest = lax.fori_loop(0, lengths_ref.shape[0], passed, (jnp.int32(0), oldest))
    key_row = lax.broadcasted_iota(jnp.int32, (TILE, TILE), 0)

    tops = [jnp.full((1, TILE), -jnp.inf, jnp.float32)] * 2
    totals = [jnp.zeros((1, TILE), jnp.float32)] * 2

    def score(head, item):
        part = dot(key_tile(item, 0), queries_turned[head], (1, 0))
        seen = key_row >= oldest - (item - TILES) * TILE
        if item == TILES:
            seen = seen & (key_row <= row)
        part = jnp.where(seen, part, -jnp.inf)
        tops[head] = jnp.maximum(tops[head], jnp.max(part, axis=0, keepdims=True))
        scores[head][item] = part

    def weigh(head, item):
        part = jnp.exp2((scores[head][item] - tops[head]) * (SCORE_SCALE * LOG2_E))
        totals[head] = totals[head] + jnp.sum(part, axis=0, keepdims=True)
        weights[tiles[item], columns[head]] = part.astype(jnp.bfloat16)

    def grade(head, item):
        grads[head][item] = dot(key_tile(item, width), cotangents_turned[head], (1, 0))

    def put(head, first, part):
        place = slice((first + head) * width, (first + head + 1) * width)
        out_ref[:, place] = part.astype(jnp.bfloat16).T

    def attend(head, share):
        attended = dot(turned_window(width), weights[:, columns[head]], (1, 0))
        attended = (attended * share).astype(jnp.bfloat16)
        put(head, 0, attended)
        products = attended.astype(jnp.float32) * cotangents_turned[head].astype(jnp.float32)
        return jnp.sum(products, axis=0, keepdims=True)

    def weigh_grad(head, item, row_delta):
        part = weights[tiles[item], columns[head]].astype(jnp.float32)
        part = (part * (grads[head][item] - row_delta)).astype(jnp.bfloat16)
        grad_weights[tiles[item], columns[head]] = part

    def make_query_grad(head, share):
        query_grad = dot(turned_window(0), grad_weights[:, columns[head]], (1, 0))
        put(head, 2, query_grad * (share * SCORE_SCALE))

    def scaled(parts, shares):
        scaled_parts = []
        for part, share in zip(parts, shares):
            down = jnp.broadcast_to(share, (8, TILE)).T[:, :1]
            scaled_parts.append((part.astype(jnp.float32) * down).astype(jnp.bfloat16))
        return jnp.concatenate(scaled_parts, axis=0)

    for item in range(SPAN):
        score(0, item)
    for item in range(SPAN):
        score(1, item)
        weigh(0, item)
    for item in range(SPAN):
        grade(0, item)
        weigh(1, item)
    shares = [1.0 / total for total in totals]
    delta = attend(0, shares[0])
    for item in range(SPAN):
        grade(1, item)
        weigh_grad(0, item, delta)
    delta = attend(1, shares[1])
    cotangents_scaled = scaled(cotangents, shares)
    queries_scaled = scaled(queries, shares)
    for item in range(SPAN):
        add(item, width, dot(weights[tiles[item]], cotangents_scaled, (1, 0)))
        weigh_grad(1, item, delta)
    make_query_grad(0, shares[0])
    make_query_grad(1, shares[1])
    for item in range(SPAN):
        add(item, 0, dot(grad_weights[tiles[item]], queries_scaled, (1, 0)))

    @pl.when(step == TILES - 1)
    def _():
        for item, distance in enumerate(BACK_DISTANCES):
            half, part, chunk = item // HALF, item % HALF, member ^ distance
            for halves, place in ((earlier_grads, chunk), (own_grads, MEMBERS + chunk)):
                target = halves[half]
                target[part, :, :width] = (sums[place, :, :width] * SCORE_SCALE).astype(
                    jnp.bfloat16
                )
                target[part, :, width:] = sums[place, :, width:].astype(jnp.bfloat16)


def attention(doc_lengths, rows, own, earlier):
    width = HEAD_WIDTH
    products = 6 * 2 * WINDOW_LENGTH * 2 * KEYS * width
    half = jax.ShapeDtypeStruct((HALF, ROWS, 2 * width), jnp.bfloat16)
    rows_block = pl.BlockSpec((TILE, 4 * width), lambda i: (i, 0))
    half_block = pl.BlockSpec(half.shape, lambda i: (0, 0, 0))
    outputs = pl.pallas_call(
        attention_kernel,
        grid=(TILES,),
        in_specs=[SCALARS, rows_block] + [half_block] * 4,
        out_specs=[rows_block] + [half_block] * 4,
        out_shape=[jax.ShapeDtypeStruct(rows.shape, jnp.bfloat16)] + [half] * 4,
        scratch_shapes=[
            pltpu.VMEM((2 * MEMBERS, ROWS, 2 * width), jnp.bfloat16),
            pltpu.VMEM((2 * width, 2 * WINDOW_LENGTH), jnp.bfloat16),
            pltpu.VMEM((2 * MEMBERS, ROWS, 2 * width), jnp.float32),
            pltpu.VMEM((KEYS, COLUMNS), jnp.bfloat16),
            pltpu.VMEM((KEYS, COLUMNS), jnp.bfloat16),
        ]
        + [pltpu.VMEM((SPAN, TILE, TILE), jnp.float32)] * 4,
        compiler_params=LIMIT,
        cost_estimate=pl.CostEstimate(
            flops=2 * products, bytes_accessed=WINDOW_LENGTH * width * 30, transcendentals=0
        ),
    )(doc_lengths, rows, *own, *earlier)
    return outputs[0], outputs[1:3], outputs[3:]


def by_head(block):
    return block.reshape(ROWS, MEMBERS, block.shape[1] // MEMBERS).transpose(1, 0, 2)


def by_token(blocks):
    return blocks.transpose(1, 0, 2).reshape(ROWS, MEMBERS * blocks.shape[2])


def exchanged(blocks):
    return lax.all_to_all(blocks, "member", split_axis=0, concat_axis=0, tiled=True)


def swapped(pieces, distances):
    moved = []
    for piece, distance in zip(pieces, distances):
        route = [(i, i ^ distance) for i in range(MEMBERS)]
        moved.append(lax.ppermute(piece, "member", route) if distance else piece)
    return moved


def onward(block, direction):
    lower = [(i, i + 1) for i in range(lax.axis_size("stretch") - 1)]
    route = lower if direction > 0 else [(j, i) for i, j in lower]
    return lax.ppermute(block, "stretch", route)


def shards(rotated_query_rows, rotated_key_rows, value_matrix, output_gradient, doc_lengths):
    pieces = swapped(pack(rotated_key_rows, value_matrix), DISTANCES)
    rows = jnp.concatenate([by_head(rotated_query_rows), by_head(output_gradient)], axis=2)
    pieces, rows = lax.optimization_barrier((pieces, rows))
    own = [jnp.stack(pieces[:HALF]), jnp.stack(pieces[HALF:])]
    earlier = [onward(half, 1) for half in own]
    rows = exchanged(rows).reshape(WINDOW_LENGTH, 4 * HEAD_WIDTH)
    results, own_grads, earlier_grads = attention(doc_lengths, rows, own, earlier)
    later = [onward(half, -1) for half in earlier_grads]
    results = exchanged(results.reshape(MEMBERS, ROWS, 4 * HEAD_WIDTH))
    attended = by_token(results[:, :, : 2 * HEAD_WIDTH])
    query_grad = by_token(results[:, :, 2 * HEAD_WIDTH :])
    sums = [
        (own_grads[half].astype(jnp.float32) + later[half].astype(jnp.float32)).astype(
            jnp.bfloat16
        )
        for half in range(2)
    ]
    pieces = [sums[item // HALF][item % HALF] for item in range(MEMBERS)]
    pieces = swapped(pieces, BACK_DISTANCES)
    attended, query_grad, pieces = lax.optimization_barrier((attended, query_grad, pieces))
    return (attended, query_grad, *unpack(pieces))


def solution(mesh):
    grouped = Mesh(mesh.devices.reshape(-1, MEMBERS), ("stretch", "member"))
    spread = P(("stretch", "member"), None)
    return jax.shard_map(
        shards,
        mesh=grouped,
        in_specs=(spread, spread, spread, spread, P()),
        out_specs=(spread, spread, spread, spread),
        check_vma=False,
    )
```

```python
import jax
import jax.numpy as jnp
from jax import lax
from jax.experimental import pallas as pl
from jax.experimental.pallas import tpu as pltpu
from jax.sharding import Mesh
from jax.sharding import PartitionSpec as P

HEAD_WIDTH = 256
WINDOW_LENGTH = 1024
MEMBERS = 8
HALF = MEMBERS // 2
DISTANCES = (7, 6, 5, 4, 3, 2, 1, 0)
BACK_DISTANCES = (7, 6, 5, 4, 0, 1, 2, 3)

TILE = 256
TILES = WINDOW_LENGTH // TILE
SPAN = TILES + 1
KEYS = SPAN * TILE
ROWS = WINDOW_LENGTH // MEMBERS
CHUNKS = TILE // ROWS
COLUMNS = 2 * TILE
SCORE_SCALE = HEAD_WIDTH ** (-0.5)
LOG2_E = 1.4426950408889634

IN_HBM = pl.BlockSpec(memory_space=pltpu.HBM)
SCALARS = pl.BlockSpec(memory_space=pltpu.SMEM)
SMALL_LIMIT = pltpu.CompilerParams(vmem_limit_bytes=4 * 1024 * 1024)
WHOLE_LIMIT = pltpu.CompilerParams(vmem_limit_bytes=64 * 1024 * 1024)
LIMIT = pltpu.CompilerParams(vmem_limit_bytes=62 * 1024 * 1024)


def dot(left, right, contract):
    return lax.dot_general(
        left, right, ((contract[:1], contract[1:]), ((), ())), preferred_element_type=jnp.float32
    )


def copies_of(pairs, semaphores):
    return [
        pltpu.make_async_copy(source, target, semaphores.at[item])
        for item, (source, target) in enumerate(pairs)
    ]


def columns_of(ref, head, width):
    return ref.at[:, pl.ds(pl.multiple_of(head * width, width), width)]


def staged(arriving, leaving):
    for copies in arriving:
        for copy in copies:
            copy.start()
    for copies, onward in zip(arriving, leaving):
        for copy in copies:
            copy.wait()
        for copy in onward:
            copy.start()
    for onward in leaving:
        for copy in onward:
            copy.wait()


def pack_kernel(left_ref, right_ref, *refs):
    pieces, (buffer, arrived, sent) = refs[:MEMBERS], refs[MEMBERS:]
    member = lax.axis_index("member")
    width = left_ref.shape[1] // MEMBERS
    arriving, leaving = [], []
    for item, distance in enumerate(DISTANCES):
        head = member ^ distance
        pairs = [
            (columns_of(left_ref, head, width), buffer.at[item, :, pl.ds(0, width)]),
            (columns_of(right_ref, head, width), buffer.at[item, :, pl.ds(width, width)]),
        ]
        arriving.append(copies_of(pairs, arrived.at[item]))
        leaving.append([pltpu.make_async_copy(buffer.at[item], pieces[item], sent.at[item])])
    staged(arriving, leaving)


def pack(left, right):
    rows, columns = left.shape
    shape = (rows, 2 * columns // MEMBERS)
    return pl.pallas_call(
        pack_kernel,
        in_specs=[IN_HBM] * 2,
        out_specs=[IN_HBM] * MEMBERS,
        out_shape=[jax.ShapeDtypeStruct(shape, left.dtype)] * MEMBERS,
        scratch_shapes=[
            pltpu.VMEM((MEMBERS, *shape), left.dtype),
            pltpu.SemaphoreType.DMA((MEMBERS, 2)),
            pltpu.SemaphoreType.DMA((MEMBERS,)),
        ],
        compiler_params=WHOLE_LIMIT,
        cost_estimate=pl.CostEstimate(
            flops=0, bytes_accessed=8 * rows * columns, transcendentals=0
        ),
    )(left, right)


def unpack_kernel(*refs):
    pieces, (left_ref, right_ref, sent) = refs[:MEMBERS], refs[MEMBERS:]
    member = lax.axis_index("member")
    width = left_ref.shape[1] // MEMBERS
    copies = []
    for item, distance in enumerate(BACK_DISTANCES):
        head = member ^ distance
        pairs = [
            (pieces[item].at[:, pl.ds(0, width)], columns_of(left_ref, head, width)),
            (pieces[item].at[:, pl.ds(width, width)], columns_of(right_ref, head, width)),
        ]
        copies += copies_of(pairs, sent.at[item])
    for copy in copies:
        copy.start()
    for copy in copies:
        copy.wait()


def unpack(pieces):
    rows, columns = pieces[0].shape
    whole = jax.ShapeDtypeStruct((rows, MEMBERS * columns // 2), pieces[0].dtype)
    return pl.pallas_call(
        unpack_kernel,
        in_specs=[pl.BlockSpec(memory_space=pltpu.VMEM)] * MEMBERS,
        out_specs=[IN_HBM] * 2,
        out_shape=[whole] * 2,
        scratch_shapes=[pltpu.SemaphoreType.DMA((MEMBERS, 2))],
        compiler_params=SMALL_LIMIT,
        cost_estimate=pl.CostEstimate(
            flops=0, bytes_accessed=4 * MEMBERS * rows * columns, transcendentals=0
        ),
    )(*pieces)


def attention_kernel(lengths_ref, rows_ref, *refs):
    own_halves, earlier_halves, out_ref, refs = refs[:2], refs[2:4], refs[4], refs[5:]
    own_grads, earlier_grads, refs = refs[:2], refs[2:4], refs[4:]
    kv, kv_turned, sums, weights, grad_weights, refs = *refs[:5], refs[5:]
    scores = refs
    step = pl.program_id(0)
    width = HEAD_WIDTH
    member = lax.axis_index("member")

    def turn(tile):
        part = kv[pl.ds(tile * CHUNKS, CHUNKS)].reshape(TILE, 2 * width)
        kv_turned[:, pl.ds(pl.multiple_of(tile * TILE, TILE), TILE)] = part.T

    @pl.when(step == 0)
    def _():
        for item, distance in enumerate(DISTANCES):
            half, part, chunk = item // HALF, item % HALF, member ^ distance
            kv[chunk] = earlier_halves[half][part]
            kv[MEMBERS + chunk] = own_halves[half][part]
        sums[:MEMBERS] = jnp.zeros((MEMBERS, ROWS, 2 * width), jnp.float32)
        for tile in range(TILES):
            turn(tile)

    turn(TILES + step)

    def key_tile(item, first):
        tile = pl.ds((step + item) * CHUNKS, CHUNKS)
        return kv[tile, :, first : first + width].reshape(TILE, width)

    def turned_window(first):
        place = pl.ds(pl.multiple_of(step * TILE, TILE), KEYS)
        return kv_turned[first : first + width, place]

    def add(item, first, part):
        tile = pl.ds((step + item) * CHUNKS, CHUNKS)
        part = part.reshape(CHUNKS, ROWS, width)
        if item < TILES:
            part = sums[tile, :, first : first + width] + part
        sums[tile, :, first : first + width] = part

    queries = [rows_ref[:, head * width : (head + 1) * width] for head in range(2)]
    cotangents = [rows_ref[:, (2 + head) * width : (3 + head) * width] for head in range(2)]
    queries_turned = [part.T for part in queries]
    cotangents_turned = [part.T for part in cotangents]
    columns = [slice(head * TILE, (head + 1) * TILE) for head in range(2)]
    tiles = [slice(item * TILE, (item + 1) * TILE) for item in range(SPAN)]

    first_row = lax.axis_index("stretch") * WINDOW_LENGTH + step * TILE
    row = lax.broadcasted_iota(jnp.int32, (1, TILE), 1)
    oldest = row - (WINDOW_LENGTH - 1)

    def passed(item, carried):
        begin, oldest = carried
        near = begin - first_row
        oldest = jnp.where(near <= row, jnp.maximum(oldest, near), oldest)
        return begin + lengths_ref[item], oldest

    _, oldest = lax.fori_loop(0, lengths_ref.shape[0], passed, (jnp.int32(0), oldest))
    key_row = lax.broadcasted_iota(jnp.int32, (TILE, TILE), 0)

    tops = [jnp.full((1, TILE), -jnp.inf, jnp.float32)] * 2
    totals = [jnp.zeros((1, TILE), jnp.float32)] * 2

    def score(head, item):
        part = dot(key_tile(item, 0), queries_turned[head], (1, 0))
        seen = key_row >= oldest - (item - TILES) * TILE
        if item == TILES:
            seen = seen & (key_row <= row)
        part = jnp.where(seen, part, -jnp.inf)
        tops[head] = jnp.maximum(tops[head], jnp.max(part, axis=0, keepdims=True))
        scores[head][item] = part

    def weigh(head, item):
        part = jnp.exp2((scores[head][item] - tops[head]) * (SCORE_SCALE * LOG2_E))
        totals[head] = totals[head] + jnp.sum(part, axis=0, keepdims=True)
        weights[tiles[item], columns[head]] = part.astype(jnp.bfloat16)

    def put(head, first, part):
        place = slice((first + head) * width, (first + head + 1) * width)
        out_ref[:, place] = part.astype(jnp.bfloat16).T

    def attend(head, share):
        attended = dot(turned_window(width), weights[:, columns[head]], (1, 0))
        attended = (attended * share).astype(jnp.bfloat16)
        put(head, 0, attended)
        products = attended.astype(jnp.float32) * cotangents_turned[head].astype(jnp.float32)
        return jnp.sum(products, axis=0, keepdims=True)

    def weigh_grad(head, item, row_delta):
        grad = dot(key_tile(item, width), cotangents_turned[head], (1, 0)) - row_delta
        part = weights[tiles[item], columns[head]].astype(jnp.float32)
        part = (part * grad).astype(jnp.bfloat16)
        grad_weights[tiles[item], columns[head]] = part

    def make_query_grad(head, share):
        query_grad = dot(turned_window(0), grad_weights[:, columns[head]], (1, 0))
        put(head, 2, query_grad * (share * SCORE_SCALE))

    def scaled(parts, shares):
        scaled_parts = []
        for part, share in zip(parts, shares):
            down = jnp.broadcast_to(share, (8, TILE)).T[:, :1]
            scaled_parts.append((part.astype(jnp.float32) * down).astype(jnp.bfloat16))
        return jnp.concatenate(scaled_parts, axis=0)

    for item in range(SPAN):
        score(0, item)
    for item in range(SPAN):
        score(1, item)
        weigh(0, item)
    for item in range(SPAN):
        weigh(1, item)
    shares = [1.0 / total for total in totals]
    deltas = [attend(head, shares[head]) for head in range(2)]
    cotangents_scaled = scaled(cotangents, shares)
    queries_scaled = scaled(queries, shares)
    for item in range(SPAN):
        weigh_grad(0, item, deltas[0])
        weigh_grad(1, item, deltas[1])
        add(item, width, dot(weights[tiles[item]], cotangents_scaled, (1, 0)))
        add(item, 0, dot(grad_weights[tiles[item]], queries_scaled, (1, 0)))
    make_query_grad(0, shares[0])
    make_query_grad(1, shares[1])

    @pl.when(step == TILES - 1)
    def _():
        for item, distance in enumerate(BACK_DISTANCES):
            half, part, chunk = item // HALF, item % HALF, member ^ distance
            for halves, place in ((earlier_grads, chunk), (own_grads, MEMBERS + chunk)):
                target = halves[half]
                target[part, :, :width] = (sums[place, :, :width] * SCORE_SCALE).astype(
                    jnp.bfloat16
                )
                target[part, :, width:] = sums[place, :, width:].astype(jnp.bfloat16)


def attention(doc_lengths, rows, own, earlier):
    width = HEAD_WIDTH
    products = 6 * 2 * WINDOW_LENGTH * 2 * KEYS * width
    half = jax.ShapeDtypeStruct((HALF, ROWS, 2 * width), jnp.bfloat16)
    rows_block = pl.BlockSpec((TILE, 4 * width), lambda i: (i, 0))
    half_block = pl.BlockSpec(half.shape, lambda i: (0, 0, 0))
    outputs = pl.pallas_call(
        attention_kernel,
        grid=(TILES,),
        in_specs=[SCALARS, rows_block] + [half_block] * 4,
        out_specs=[rows_block] + [half_block] * 4,
        out_shape=[jax.ShapeDtypeStruct(rows.shape, jnp.bfloat16)] + [half] * 4,
        scratch_shapes=[
            pltpu.VMEM((2 * MEMBERS, ROWS, 2 * width), jnp.bfloat16),
            pltpu.VMEM((2 * width, 2 * WINDOW_LENGTH), jnp.bfloat16),
            pltpu.VMEM((2 * MEMBERS, ROWS, 2 * width), jnp.float32),
            pltpu.VMEM((KEYS, COLUMNS), jnp.bfloat16),
            pltpu.VMEM((KEYS, COLUMNS), jnp.bfloat16),
        ]
        + [pltpu.VMEM((SPAN, TILE, TILE), jnp.float32)] * 2,
        compiler_params=LIMIT,
        cost_estimate=pl.CostEstimate(
            flops=2 * products, bytes_accessed=WINDOW_LENGTH * width * 30, transcendentals=0
        ),
    )(doc_lengths, rows, *own, *earlier)
    return outputs[0], outputs[1:3], outputs[3:]


def by_head(block):
    return block.reshape(ROWS, MEMBERS, block.shape[1] // MEMBERS).transpose(1, 0, 2)


def by_token(blocks):
    return blocks.transpose(1, 0, 2).reshape(ROWS, MEMBERS * blocks.shape[2])


def exchanged(blocks):
    return lax.all_to_all(blocks, "member", split_axis=0, concat_axis=0, tiled=True)


def swapped(pieces, distances):
    moved = []
    for piece, distance in zip(pieces, distances):
        route = [(i, i ^ distance) for i in range(MEMBERS)]
        moved.append(lax.ppermute(piece, "member", route) if distance else piece)
    return moved


def onward(block, direction):
    lower = [(i, i + 1) for i in range(lax.axis_size("stretch") - 1)]
    route = lower if direction > 0 else [(j, i) for i, j in lower]
    return lax.ppermute(block, "stretch", route)


def shards(rotated_query_rows, rotated_key_rows, value_matrix, output_gradient, doc_lengths):
    pieces = swapped(pack(rotated_key_rows, value_matrix), DISTANCES)
    rows = jnp.concatenate([by_head(rotated_query_rows), by_head(output_gradient)], axis=2)
    pieces, rows = lax.optimization_barrier((pieces, rows))
    own = [jnp.stack(pieces[:HALF]), jnp.stack(pieces[HALF:])]
    earlier = [onward(half, 1) for half in own]
    rows = exchanged(rows).reshape(WINDOW_LENGTH, 4 * HEAD_WIDTH)
    results, own_grads, earlier_grads = attention(doc_lengths, rows, own, earlier)
    later = [onward(half, -1) for half in earlier_grads]
    results = exchanged(results.reshape(MEMBERS, ROWS, 4 * HEAD_WIDTH))
    attended = by_token(results[:, :, : 2 * HEAD_WIDTH])
    query_grad = by_token(results[:, :, 2 * HEAD_WIDTH :])
    sums = [
        (own_grads[half].astype(jnp.float32) + later[half].astype(jnp.float32)).astype(
            jnp.bfloat16
        )
        for half in range(2)
    ]
    pieces = [sums[item // HALF][item % HALF] for item in range(MEMBERS)]
    pieces = swapped(pieces, BACK_DISTANCES)
    attended, query_grad, pieces = lax.optimization_barrier((attended, query_grad, pieces))
    return (attended, query_grad, *unpack(pieces))


def solution(mesh):
    grouped = Mesh(mesh.devices.reshape(-1, MEMBERS), ("stretch", "member"))
    spread = P(("stretch", "member"), None)
    return jax.shard_map(
        shards,
        mesh=grouped,
        in_specs=(spread, spread, spread, spread, P()),
        out_specs=(spread, spread, spread, spread),
        check_vma=False,
    )
```

```python
import functools

import jax
import jax.numpy as jnp
from jax import lax
from jax.experimental import pallas as pl
from jax.experimental.pallas import tpu as pltpu
from jax.sharding import Mesh
from jax.sharding import PartitionSpec as P

HEAD_WIDTH = 256
WINDOW_LENGTH = 1024
MEMBERS = 8
HALF = MEMBERS // 2
DISTANCES = (7, 6, 5, 4, 3, 2, 1, 0)
BACK_DISTANCES = (7, 6, 5, 4, 0, 1, 2, 3)

TILE = 256
TILES = WINDOW_LENGTH // TILE
SPAN = TILES + 1
KEYS = SPAN * TILE
ROWS = WINDOW_LENGTH // MEMBERS
CHUNKS = TILE // ROWS
COLUMNS = 2 * TILE
SCORE_SCALE = HEAD_WIDTH ** (-0.5)
LOG2_E = 1.4426950408889634

IN_HBM = pl.BlockSpec(memory_space=pltpu.HBM)
SCALARS = pl.BlockSpec(memory_space=pltpu.SMEM)
SMALL_LIMIT = pltpu.CompilerParams(vmem_limit_bytes=4 * 1024 * 1024)
WHOLE_LIMIT = pltpu.CompilerParams(vmem_limit_bytes=64 * 1024 * 1024)
LIMIT = pltpu.CompilerParams(vmem_limit_bytes=62 * 1024 * 1024)


def dot(left, right, contract):
    return lax.dot_general(
        left, right, ((contract[:1], contract[1:]), ((), ())), preferred_element_type=jnp.float32
    )


def copies_of(pairs, semaphores):
    return [
        pltpu.make_async_copy(source, target, semaphores.at[item])
        for item, (source, target) in enumerate(pairs)
    ]


def columns_of(ref, head, width):
    return ref.at[:, pl.ds(pl.multiple_of(head * width, width), width)]


def staged(arriving, leaving):
    for copies in arriving:
        for copy in copies:
            copy.start()
    for copies, onward in zip(arriving, leaving):
        for copy in copies:
            copy.wait()
        for copy in onward:
            copy.start()
    for onward in leaving:
        for copy in onward:
            copy.wait()


def pack_kernel(distances, left_ref, right_ref, *refs):
    pieces, (buffer, arrived, sent) = refs[:HALF], refs[HALF:]
    member = lax.axis_index("member")
    width = left_ref.shape[1] // MEMBERS
    arriving, leaving = [], []
    for item, distance in enumerate(distances):
        head = member ^ distance
        pairs = [
            (columns_of(left_ref, head, width), buffer.at[item, :, pl.ds(0, width)]),
            (columns_of(right_ref, head, width), buffer.at[item, :, pl.ds(width, width)]),
        ]
        arriving.append(copies_of(pairs, arrived.at[item]))
        leaving.append([pltpu.make_async_copy(buffer.at[item], pieces[item], sent.at[item])])
    staged(arriving, leaving)


def pack(left, right, distances):
    rows, columns = left.shape
    shape = (rows, 2 * columns // MEMBERS)
    return pl.pallas_call(
        functools.partial(pack_kernel, distances),
        in_specs=[IN_HBM] * 2,
        out_specs=[IN_HBM] * HALF,
        out_shape=[jax.ShapeDtypeStruct(shape, left.dtype)] * HALF,
        scratch_shapes=[
            pltpu.VMEM((HALF, *shape), left.dtype),
            pltpu.SemaphoreType.DMA((HALF, 2)),
            pltpu.SemaphoreType.DMA((HALF,)),
        ],
        compiler_params=WHOLE_LIMIT,
        cost_estimate=pl.CostEstimate(
            flops=0, bytes_accessed=4 * rows * columns, transcendentals=0
        ),
    )(left, right)


def unpack_kernel(*refs):
    pieces, (left_ref, right_ref, sent) = refs[:MEMBERS], refs[MEMBERS:]
    member = lax.axis_index("member")
    width = left_ref.shape[1] // MEMBERS
    copies = []
    for item, distance in enumerate(BACK_DISTANCES):
        head = member ^ distance
        pairs = [
            (pieces[item].at[:, pl.ds(0, width)], columns_of(left_ref, head, width)),
            (pieces[item].at[:, pl.ds(width, width)], columns_of(right_ref, head, width)),
        ]
        copies += copies_of(pairs, sent.at[item])
    for copy in copies:
        copy.start()
    for copy in copies:
        copy.wait()


def unpack(pieces):
    rows, columns = pieces[0].shape
    whole = jax.ShapeDtypeStruct((rows, MEMBERS * columns // 2), pieces[0].dtype)
    return pl.pallas_call(
        unpack_kernel,
        in_specs=[pl.BlockSpec(memory_space=pltpu.VMEM)] * MEMBERS,
        out_specs=[IN_HBM] * 2,
        out_shape=[whole] * 2,
        scratch_shapes=[pltpu.SemaphoreType.DMA((MEMBERS, 2))],
        compiler_params=SMALL_LIMIT,
        cost_estimate=pl.CostEstimate(
            flops=0, bytes_accessed=4 * MEMBERS * rows * columns, transcendentals=0
        ),
    )(*pieces)


def attention_kernel(lengths_ref, rows_ref, *refs):
    own_halves, earlier_halves, out_ref, refs = refs[:2], refs[2:4], refs[4], refs[5:]
    own_grads, earlier_grads, refs = refs[:2], refs[2:4], refs[4:]
    kv, kv_turned, sums, weights, grad_weights, refs = *refs[:5], refs[5:]
    scores = refs
    step = pl.program_id(0)
    width = HEAD_WIDTH
    member = lax.axis_index("member")

    def turn(tile):
        part = kv[pl.ds(tile * CHUNKS, CHUNKS)].reshape(TILE, 2 * width)
        kv_turned[:, pl.ds(pl.multiple_of(tile * TILE, TILE), TILE)] = part.T

    @pl.when(step == 0)
    def _():
        for item, distance in enumerate(DISTANCES):
            half, part, chunk = item // HALF, item % HALF, member ^ distance
            kv[chunk] = earlier_halves[half][part]
            kv[MEMBERS + chunk] = own_halves[half][part]
        sums[:MEMBERS] = jnp.zeros((MEMBERS, ROWS, 2 * width), jnp.float32)
        for tile in range(TILES):
            turn(tile)

    turn(TILES + step)

    def key_tile(item, first):
        tile = pl.ds((step + item) * CHUNKS, CHUNKS)
        return kv[tile, :, first : first + width].reshape(TILE, width)

    def turned_window(first):
        place = pl.ds(pl.multiple_of(step * TILE, TILE), KEYS)
        return kv_turned[first : first + width, place]

    def add(item, first, part):
        tile = pl.ds((step + item) * CHUNKS, CHUNKS)
        part = part.reshape(CHUNKS, ROWS, width)
        if item < TILES:
            part = sums[tile, :, first : first + width] + part
        sums[tile, :, first : first + width] = part

    queries = [rows_ref[:, head * width : (head + 1) * width] for head in range(2)]
    cotangents = [rows_ref[:, (2 + head) * width : (3 + head) * width] for head in range(2)]
    queries_turned = [part.T for part in queries]
    cotangents_turned = [part.T for part in cotangents]
    columns = [slice(head * TILE, (head + 1) * TILE) for head in range(2)]
    tiles = [slice(item * TILE, (item + 1) * TILE) for item in range(SPAN)]

    first_row = lax.axis_index("stretch") * WINDOW_LENGTH + step * TILE
    row = lax.broadcasted_iota(jnp.int32, (1, TILE), 1)
    oldest = row - (WINDOW_LENGTH - 1)

    def passed(item, carried):
        begin, oldest = carried
        near = begin - first_row
        oldest = jnp.where(near <= row, jnp.maximum(oldest, near), oldest)
        return begin + lengths_ref[item], oldest

    _, oldest = lax.fori_loop(0, lengths_ref.shape[0], passed, (jnp.int32(0), oldest))
    key_row = lax.broadcasted_iota(jnp.int32, (TILE, TILE), 0)

    tops = [jnp.full((1, TILE), -jnp.inf, jnp.float32)] * 2
    totals = [jnp.zeros((1, TILE), jnp.float32)] * 2

    def score(head, item):
        part = dot(key_tile(item, 0), queries_turned[head], (1, 0))
        seen = key_row >= oldest - (item - TILES) * TILE
        if item == TILES:
            seen = seen & (key_row <= row)
        part = jnp.where(seen, part, -jnp.inf)
        tops[head] = jnp.maximum(tops[head], jnp.max(part, axis=0, keepdims=True))
        scores[head][item] = part

    def weigh(head, item):
        part = jnp.exp2((scores[head][item] - tops[head]) * (SCORE_SCALE * LOG2_E))
        totals[head] = totals[head] + jnp.sum(part, axis=0, keepdims=True)
        weights[tiles[item], columns[head]] = part.astype(jnp.bfloat16)

    def put(head, first, part):
        place = slice((first + head) * width, (first + head + 1) * width)
        out_ref[:, place] = part.astype(jnp.bfloat16).T

    def attend(head, share):
        attended = dot(turned_window(width), weights[:, columns[head]], (1, 0))
        attended = (attended * share).astype(jnp.bfloat16)
        put(head, 0, attended)
        products = attended.astype(jnp.float32) * cotangents_turned[head].astype(jnp.float32)
        return jnp.sum(products, axis=0, keepdims=True)

    def weigh_grad(head, item, row_delta):
        grad = dot(key_tile(item, width), cotangents_turned[head], (1, 0)) - row_delta
        part = weights[tiles[item], columns[head]].astype(jnp.float32)
        part = (part * grad).astype(jnp.bfloat16)
        grad_weights[tiles[item], columns[head]] = part

    def make_query_grad(head, share):
        query_grad = dot(turned_window(0), grad_weights[:, columns[head]], (1, 0))
        put(head, 2, query_grad * (share * SCORE_SCALE))

    def scaled(parts, shares):
        scaled_parts = []
        for part, share in zip(parts, shares):
            down = jnp.broadcast_to(share, (8, TILE)).T[:, :1]
            scaled_parts.append((part.astype(jnp.float32) * down).astype(jnp.bfloat16))
        return jnp.concatenate(scaled_parts, axis=0)

    for item in range(SPAN):
        score(0, item)
    for item in range(SPAN):
        score(1, item)
        weigh(0, item)
    shares = [1.0 / totals[0]]
    deltas = [attend(0, shares[0])]
    for item in range(SPAN):
        weigh(1, item)
    shares.append(1.0 / totals[1])
    deltas.append(attend(1, shares[1]))
    cotangents_scaled = scaled(cotangents, shares)
    queries_scaled = scaled(queries, shares)
    for item in range(SPAN):
        weigh_grad(0, item, deltas[0])
        weigh_grad(1, item, deltas[1])
        add(item, width, dot(weights[tiles[item]], cotangents_scaled, (1, 0)))
        add(item, 0, dot(grad_weights[tiles[item]], queries_scaled, (1, 0)))
    make_query_grad(0, shares[0])
    make_query_grad(1, shares[1])

    @pl.when(step == TILES - 1)
    def _():
        for item, distance in enumerate(BACK_DISTANCES):
            half, part, chunk = item // HALF, item % HALF, member ^ distance
            for halves, place in ((earlier_grads, chunk), (own_grads, MEMBERS + chunk)):
                target = halves[half]
                target[part, :, :width] = (sums[place, :, :width] * SCORE_SCALE).astype(
                    jnp.bfloat16
                )
                target[part, :, width:] = sums[place, :, width:].astype(jnp.bfloat16)


def attention(doc_lengths, rows, own, earlier):
    width = HEAD_WIDTH
    products = 6 * 2 * WINDOW_LENGTH * 2 * KEYS * width
    half = jax.ShapeDtypeStruct((HALF, ROWS, 2 * width), jnp.bfloat16)
    rows_block = pl.BlockSpec((TILE, 4 * width), lambda i: (i, 0))
    half_block = pl.BlockSpec(half.shape, lambda i: (0, 0, 0))
    outputs = pl.pallas_call(
        attention_kernel,
        grid=(TILES,),
        in_specs=[SCALARS, rows_block] + [half_block] * 4,
        out_specs=[rows_block] + [half_block] * 4,
        out_shape=[jax.ShapeDtypeStruct(rows.shape, jnp.bfloat16)] + [half] * 4,
        scratch_shapes=[
            pltpu.VMEM((2 * MEMBERS, ROWS, 2 * width), jnp.bfloat16),
            pltpu.VMEM((2 * width, 2 * WINDOW_LENGTH), jnp.bfloat16),
            pltpu.VMEM((2 * MEMBERS, ROWS, 2 * width), jnp.float32),
            pltpu.VMEM((KEYS, COLUMNS), jnp.bfloat16),
            pltpu.VMEM((KEYS, COLUMNS), jnp.bfloat16),
        ]
        + [pltpu.VMEM((SPAN, TILE, TILE), jnp.float32)] * 2,
        compiler_params=LIMIT,
        cost_estimate=pl.CostEstimate(
            flops=2 * products, bytes_accessed=WINDOW_LENGTH * width * 30, transcendentals=0
        ),
    )(doc_lengths, rows, *own, *earlier)
    return outputs[0], outputs[1:3], outputs[3:]


def by_head(block):
    return block.reshape(ROWS, MEMBERS, block.shape[1] // MEMBERS).transpose(1, 0, 2)


def by_token(blocks):
    return blocks.transpose(1, 0, 2).reshape(ROWS, MEMBERS * blocks.shape[2])


def exchanged(blocks):
    return lax.all_to_all(blocks, "member", split_axis=0, concat_axis=0, tiled=True)


def swapped(pieces, distances):
    moved = []
    for piece, distance in zip(pieces, distances):
        route = [(i, i ^ distance) for i in range(MEMBERS)]
        moved.append(lax.ppermute(piece, "member", route) if distance else piece)
    return moved


def onward(block, direction):
    lower = [(i, i + 1) for i in range(lax.axis_size("stretch") - 1)]
    route = lower if direction > 0 else [(j, i) for i, j in lower]
    return lax.ppermute(block, "stretch", route)


def shards(rotated_query_rows, rotated_key_rows, value_matrix, output_gradient, doc_lengths):
    heavy, light = DISTANCES[:HALF], DISTANCES[HALF:]
    pieces = pack(rotated_key_rows, value_matrix, heavy)
    pieces, rotated_key_rows, value_matrix = lax.optimization_barrier(
        (pieces, rotated_key_rows, value_matrix)
    )
    pieces = swapped(pieces, heavy)
    pieces += swapped(pack(rotated_key_rows, value_matrix, light), light)
    rows = jnp.concatenate([by_head(rotated_query_rows), by_head(output_gradient)], axis=2)
    pieces, rows = lax.optimization_barrier((pieces, rows))
    own = [jnp.stack(pieces[:HALF]), jnp.stack(pieces[HALF:])]
    earlier = [onward(half, 1) for half in own]
    rows = exchanged(rows).reshape(WINDOW_LENGTH, 4 * HEAD_WIDTH)
    results, own_grads, earlier_grads = attention(doc_lengths, rows, own, earlier)
    later = [onward(half, -1) for half in earlier_grads]
    results = exchanged(results.reshape(MEMBERS, ROWS, 4 * HEAD_WIDTH))
    attended = by_token(results[:, :, : 2 * HEAD_WIDTH])
    query_grad = by_token(results[:, :, 2 * HEAD_WIDTH :])
    sums = [
        (own_grads[half].astype(jnp.float32) + later[half].astype(jnp.float32)).astype(
            jnp.bfloat16
        )
        for half in range(2)
    ]
    pieces = [sums[item // HALF][item % HALF] for item in range(MEMBERS)]
    pieces = swapped(pieces, BACK_DISTANCES)
    attended, query_grad, pieces = lax.optimization_barrier((attended, query_grad, pieces))
    return (attended, query_grad, *unpack(pieces))


def solution(mesh):
    grouped = Mesh(mesh.devices.reshape(-1, MEMBERS), ("stretch", "member"))
    spread = P(("stretch", "member"), None)
    return jax.shard_map(
        shards,
        mesh=grouped,
        in_specs=(spread, spread, spread, spread, P()),
        out_specs=(spread, spread, spread, spread),
        check_vma=False,
    )
```

```python
import functools

import jax
import jax.numpy as jnp
from jax import lax
from jax.experimental import pallas as pl
from jax.experimental.pallas import tpu as pltpu
from jax.sharding import Mesh
from jax.sharding import PartitionSpec as P

HEAD_WIDTH = 256
WINDOW_LENGTH = 1024
MEMBERS = 8
HALF = MEMBERS // 2
DISTANCES = (7, 6, 5, 4, 3, 2, 1, 0)
BACK_DISTANCES = (7, 6, 5, 4, 0, 1, 2, 3)

TILE = 256
TILES = WINDOW_LENGTH // TILE
SPAN = TILES + 1
KEYS = SPAN * TILE
ROWS = WINDOW_LENGTH // MEMBERS
CHUNKS = TILE // ROWS
COLUMNS = 2 * TILE
SCORE_SCALE = HEAD_WIDTH ** (-0.5)
LOG2_E = 1.4426950408889634

IN_HBM = pl.BlockSpec(memory_space=pltpu.HBM)
SCALARS = pl.BlockSpec(memory_space=pltpu.SMEM)
SMALL_LIMIT = pltpu.CompilerParams(vmem_limit_bytes=4 * 1024 * 1024)
WHOLE_LIMIT = pltpu.CompilerParams(vmem_limit_bytes=64 * 1024 * 1024)
LIMIT = pltpu.CompilerParams(vmem_limit_bytes=62 * 1024 * 1024)


def dot(left, right, contract):
    return lax.dot_general(
        left, right, ((contract[:1], contract[1:]), ((), ())), preferred_element_type=jnp.float32
    )


def copies_of(pairs, semaphores):
    return [
        pltpu.make_async_copy(source, target, semaphores.at[item])
        for item, (source, target) in enumerate(pairs)
    ]


def columns_of(ref, head, width):
    return ref.at[:, pl.ds(pl.multiple_of(head * width, width), width)]


def staged(arriving, leaving):
    for copies in arriving:
        for copy in copies:
            copy.start()
    for copies, onward in zip(arriving, leaving):
        for copy in copies:
            copy.wait()
        for copy in onward:
            copy.start()
    for onward in leaving:
        for copy in onward:
            copy.wait()


def pack_kernel(distances, left_ref, right_ref, *refs):
    pieces, (buffer, arrived, sent) = refs[:HALF], refs[HALF:]
    member = lax.axis_index("member")
    width = left_ref.shape[1] // MEMBERS
    arriving, leaving = [], []
    for item, distance in enumerate(distances):
        head = member ^ distance
        pairs = [
            (columns_of(left_ref, head, width), buffer.at[item, :, pl.ds(0, width)]),
            (columns_of(right_ref, head, width), buffer.at[item, :, pl.ds(width, width)]),
        ]
        arriving.append(copies_of(pairs, arrived.at[item]))
        leaving.append([pltpu.make_async_copy(buffer.at[item], pieces[item], sent.at[item])])
    staged(arriving, leaving)


def pack(left, right, distances):
    rows, columns = left.shape
    shape = (rows, 2 * columns // MEMBERS)
    return pl.pallas_call(
        functools.partial(pack_kernel, distances),
        in_specs=[IN_HBM] * 2,
        out_specs=[IN_HBM] * HALF,
        out_shape=[jax.ShapeDtypeStruct(shape, left.dtype)] * HALF,
        scratch_shapes=[
            pltpu.VMEM((HALF, *shape), left.dtype),
            pltpu.SemaphoreType.DMA((HALF, 2)),
            pltpu.SemaphoreType.DMA((HALF,)),
        ],
        compiler_params=WHOLE_LIMIT,
        cost_estimate=pl.CostEstimate(
            flops=0, bytes_accessed=4 * rows * columns, transcendentals=0
        ),
    )(left, right)


def unpack_kernel(*refs):
    pieces, (left_ref, right_ref, sent) = refs[:MEMBERS], refs[MEMBERS:]
    member = lax.axis_index("member")
    width = left_ref.shape[1] // MEMBERS
    copies = []
    for item, distance in enumerate(BACK_DISTANCES):
        head = member ^ distance
        pairs = [
            (pieces[item].at[:, pl.ds(0, width)], columns_of(left_ref, head, width)),
            (pieces[item].at[:, pl.ds(width, width)], columns_of(right_ref, head, width)),
        ]
        copies += copies_of(pairs, sent.at[item])
    for copy in copies:
        copy.start()
    for copy in copies:
        copy.wait()


def unpack(pieces):
    rows, columns = pieces[0].shape
    whole = jax.ShapeDtypeStruct((rows, MEMBERS * columns // 2), pieces[0].dtype)
    return pl.pallas_call(
        unpack_kernel,
        in_specs=[pl.BlockSpec(memory_space=pltpu.VMEM)] * MEMBERS,
        out_specs=[IN_HBM] * 2,
        out_shape=[whole] * 2,
        scratch_shapes=[pltpu.SemaphoreType.DMA((MEMBERS, 2))],
        compiler_params=SMALL_LIMIT,
        cost_estimate=pl.CostEstimate(
            flops=0, bytes_accessed=4 * MEMBERS * rows * columns, transcendentals=0
        ),
    )(*pieces)


def attention_kernel(lengths_ref, rows_ref, *refs):
    own_halves, earlier_halves, out_ref, refs = refs[:2], refs[2:4], refs[4], refs[5:]
    own_grads, earlier_grads, refs = refs[:2], refs[2:4], refs[4:]
    kv, kv_turned, sums, weights, grad_weights, refs = *refs[:5], refs[5:]
    scores = refs
    step = pl.program_id(0)
    width = HEAD_WIDTH
    member = lax.axis_index("member")

    def turn(tile):
        part = kv[pl.ds(tile * CHUNKS, CHUNKS)].reshape(TILE, 2 * width)
        kv_turned[:, pl.ds(pl.multiple_of(tile * TILE, TILE), TILE)] = part.T

    @pl.when(step == 0)
    def _():
        for item, distance in enumerate(DISTANCES):
            half, part, chunk = item // HALF, item % HALF, member ^ distance
            kv[chunk] = earlier_halves[half][part]
            kv[MEMBERS + chunk] = own_halves[half][part]
        sums[:MEMBERS] = jnp.zeros((MEMBERS, ROWS, 2 * width), jnp.float32)
        for tile in range(TILES):
            turn(tile)

    turn(TILES + step)

    def key_tile(item, first):
        tile = pl.ds((step + item) * CHUNKS, CHUNKS)
        return kv[tile, :, first : first + width].reshape(TILE, width)

    def turned_window(first):
        place = pl.ds(pl.multiple_of(step * TILE, TILE), KEYS)
        return kv_turned[first : first + width, place]

    def add(item, first, part):
        tile = pl.ds((step + item) * CHUNKS, CHUNKS)
        part = part.reshape(CHUNKS, ROWS, width)
        if item < TILES:
            part = sums[tile, :, first : first + width] + part
        sums[tile, :, first : first + width] = part

    queries = [rows_ref[:, head * width : (head + 1) * width] for head in range(2)]
    cotangents = [rows_ref[:, (2 + head) * width : (3 + head) * width] for head in range(2)]
    cotangents_turned = [part.T for part in cotangents]
    columns = [slice(head * TILE, (head + 1) * TILE) for head in range(2)]
    tiles = [slice(item * TILE, (item + 1) * TILE) for item in range(SPAN)]

    first_row = lax.axis_index("stretch") * WINDOW_LENGTH + step * TILE
    row = lax.broadcasted_iota(jnp.int32, (1, TILE), 1)
    oldest = row - (WINDOW_LENGTH - 1)

    def passed(item, carried):
        begin, oldest = carried
        near = begin - first_row
        oldest = jnp.where(near <= row, jnp.maximum(oldest, near), oldest)
        return begin + lengths_ref[item], oldest

    _, oldest = lax.fori_loop(0, lengths_ref.shape[0], passed, (jnp.int32(0), oldest))
    key_row = lax.broadcasted_iota(jnp.int32, (TILE, TILE), 0)

    tops = [jnp.full((1, TILE), -jnp.inf, jnp.float32)] * 2
    totals = [jnp.zeros((1, TILE), jnp.float32)] * 2

    def score(head, item):
        part = dot(key_tile(item, 0), queries[head], (1, 1))
        seen = key_row >= oldest - (item - TILES) * TILE
        if item == TILES:
            seen = seen & (key_row <= row)
        part = jnp.where(seen, part, -jnp.inf)
        tops[head] = jnp.maximum(tops[head], jnp.max(part, axis=0, keepdims=True))
        scores[head][item] = part

    def weigh(head, item):
        part = jnp.exp2((scores[head][item] - tops[head]) * (SCORE_SCALE * LOG2_E))
        totals[head] = totals[head] + jnp.sum(part, axis=0, keepdims=True)
        weights[tiles[item], columns[head]] = part.astype(jnp.bfloat16)

    def put(head, first, part):
        place = slice((first + head) * width, (first + head + 1) * width)
        out_ref[:, place] = part.astype(jnp.bfloat16).T

    def attend(head, share):
        attended = dot(turned_window(width), weights[:, columns[head]], (1, 0))
        attended = (attended * share).astype(jnp.bfloat16)
        put(head, 0, attended)
        products = attended.astype(jnp.float32) * cotangents_turned[head].astype(jnp.float32)
        return jnp.sum(products, axis=0, keepdims=True)

    def weigh_grad(head, item, row_delta):
        grad = dot(key_tile(item, width), cotangents[head], (1, 1)) - row_delta
        part = weights[tiles[item], columns[head]].astype(jnp.float32)
        part = (part * grad).astype(jnp.bfloat16)
        grad_weights[tiles[item], columns[head]] = part

    def make_query_grad(head, share):
        query_grad = dot(turned_window(0), grad_weights[:, columns[head]], (1, 0))
        put(head, 2, query_grad * (share * SCORE_SCALE))

    def scaled(parts, shares):
        scaled_parts = []
        for part, share in zip(parts, shares):
            down = jnp.broadcast_to(share, (8, TILE)).T[:, :1]
            scaled_parts.append((part.astype(jnp.float32) * down).astype(jnp.bfloat16))
        return jnp.concatenate(scaled_parts, axis=0)

    for item in range(SPAN):
        score(0, item)
    for item in range(SPAN):
        score(1, item)
        weigh(0, item)
    shares = [1.0 / totals[0]]
    deltas = [attend(0, shares[0])]
    for item in range(SPAN):
        weigh(1, item)
    shares.append(1.0 / totals[1])
    deltas.append(attend(1, shares[1]))
    cotangents_scaled = scaled(cotangents, shares)
    queries_scaled = scaled(queries, shares)
    for item in range(SPAN):
        weigh_grad(0, item, deltas[0])
        weigh_grad(1, item, deltas[1])
        add(item, width, dot(weights[tiles[item]], cotangents_scaled, (1, 0)))
        add(item, 0, dot(grad_weights[tiles[item]], queries_scaled, (1, 0)))
    make_query_grad(0, shares[0])
    make_query_grad(1, shares[1])

    @pl.when(step == TILES - 1)
    def _():
        for item, distance in enumerate(BACK_DISTANCES):
            half, part, chunk = item // HALF, item % HALF, member ^ distance
            for halves, place in ((earlier_grads, chunk), (own_grads, MEMBERS + chunk)):
                target = halves[half]
                target[part, :, :width] = (sums[place, :, :width] * SCORE_SCALE).astype(
                    jnp.bfloat16
                )
                target[part, :, width:] = sums[place, :, width:].astype(jnp.bfloat16)


def attention(doc_lengths, rows, own, earlier):
    width = HEAD_WIDTH
    products = 6 * 2 * WINDOW_LENGTH * 2 * KEYS * width
    half = jax.ShapeDtypeStruct((HALF, ROWS, 2 * width), jnp.bfloat16)
    rows_block = pl.BlockSpec((TILE, 4 * width), lambda i: (i, 0))
    half_block = pl.BlockSpec(half.shape, lambda i: (0, 0, 0))
    outputs = pl.pallas_call(
        attention_kernel,
        grid=(TILES,),
        in_specs=[SCALARS, rows_block] + [half_block] * 4,
        out_specs=[rows_block] + [half_block] * 4,
        out_shape=[jax.ShapeDtypeStruct(rows.shape, jnp.bfloat16)] + [half] * 4,
        scratch_shapes=[
            pltpu.VMEM((2 * MEMBERS, ROWS, 2 * width), jnp.bfloat16),
            pltpu.VMEM((2 * width, 2 * WINDOW_LENGTH), jnp.bfloat16),
            pltpu.VMEM((2 * MEMBERS, ROWS, 2 * width), jnp.float32),
            pltpu.VMEM((KEYS, COLUMNS), jnp.bfloat16),
            pltpu.VMEM((KEYS, COLUMNS), jnp.bfloat16),
        ]
        + [pltpu.VMEM((SPAN, TILE, TILE), jnp.float32)] * 2,
        compiler_params=LIMIT,
        cost_estimate=pl.CostEstimate(
            flops=2 * products, bytes_accessed=WINDOW_LENGTH * width * 30, transcendentals=0
        ),
    )(doc_lengths, rows, *own, *earlier)
    return outputs[0], outputs[1:3], outputs[3:]


def by_head(block):
    return block.reshape(ROWS, MEMBERS, block.shape[1] // MEMBERS).transpose(1, 0, 2)


def by_token(blocks):
    return blocks.transpose(1, 0, 2).reshape(ROWS, MEMBERS * blocks.shape[2])


def exchanged(blocks):
    return lax.all_to_all(blocks, "member", split_axis=0, concat_axis=0, tiled=True)


def swapped(pieces, distances):
    moved = []
    for piece, distance in zip(pieces, distances):
        route = [(i, i ^ distance) for i in range(MEMBERS)]
        moved.append(lax.ppermute(piece, "member", route) if distance else piece)
    return moved


def onward(block, direction):
    lower = [(i, i + 1) for i in range(lax.axis_size("stretch") - 1)]
    route = lower if direction > 0 else [(j, i) for i, j in lower]
    return lax.ppermute(block, "stretch", route)


def shards(rotated_query_rows, rotated_key_rows, value_matrix, output_gradient, doc_lengths):
    heavy, light = DISTANCES[:HALF], DISTANCES[HALF:]
    pieces = pack(rotated_key_rows, value_matrix, heavy)
    pieces, rotated_key_rows, value_matrix = lax.optimization_barrier(
        (pieces, rotated_key_rows, value_matrix)
    )
    pieces = swapped(pieces, heavy)
    pieces += swapped(pack(rotated_key_rows, value_matrix, light), light)
    rows = jnp.concatenate([by_head(rotated_query_rows), by_head(output_gradient)], axis=2)
    pieces, rows = lax.optimization_barrier((pieces, rows))
    own = [jnp.stack(pieces[:HALF]), jnp.stack(pieces[HALF:])]
    earlier = [onward(half, 1) for half in own]
    rows = exchanged(rows).reshape(WINDOW_LENGTH, 4 * HEAD_WIDTH)
    results, own_grads, earlier_grads = attention(doc_lengths, rows, own, earlier)
    later = [onward(half, -1) for half in earlier_grads]
    results = exchanged(results.reshape(MEMBERS, ROWS, 4 * HEAD_WIDTH))
    attended = by_token(results[:, :, : 2 * HEAD_WIDTH])
    query_grad = by_token(results[:, :, 2 * HEAD_WIDTH :])
    sums = [
        (own_grads[half].astype(jnp.float32) + later[half].astype(jnp.float32)).astype(
            jnp.bfloat16
        )
        for half in range(2)
    ]
    pieces = [sums[item // HALF][item % HALF] for item in range(MEMBERS)]
    pieces = swapped(pieces, BACK_DISTANCES)
    attended, query_grad, pieces = lax.optimization_barrier((attended, query_grad, pieces))
    return (attended, query_grad, *unpack(pieces))


def solution(mesh):
    grouped = Mesh(mesh.devices.reshape(-1, MEMBERS), ("stretch", "member"))
    spread = P(("stretch", "member"), None)
    return jax.shard_map(
        shards,
        mesh=grouped,
        in_specs=(spread, spread, spread, spread, P()),
        out_specs=(spread, spread, spread, spread),
        check_vma=False,
    )
```

```python
import functools

import jax
import jax.numpy as jnp
from jax import lax
from jax.experimental import pallas as pl
from jax.experimental.pallas import tpu as pltpu
from jax.sharding import Mesh
from jax.sharding import PartitionSpec as P

HEAD_WIDTH = 256
WINDOW_LENGTH = 1024
MEMBERS = 8
HALF = MEMBERS // 2
GROUPS = ((7, 6, 5, 4), (3, 2), (1, 0))
BACK_DISTANCES = (7, 6, 5, 4, 0, 1, 2, 3)

TILE = 256
TILES = WINDOW_LENGTH // TILE
SPAN = TILES + 1
KEYS = SPAN * TILE
ROWS = WINDOW_LENGTH // MEMBERS
CHUNKS = TILE // ROWS
COLUMNS = 2 * TILE
SCORE_SCALE = HEAD_WIDTH ** (-0.5)
LOG2_E = 1.4426950408889634

IN_HBM = pl.BlockSpec(memory_space=pltpu.HBM)
SCALARS = pl.BlockSpec(memory_space=pltpu.SMEM)
SMALL_LIMIT = pltpu.CompilerParams(vmem_limit_bytes=4 * 1024 * 1024)
WHOLE_LIMIT = pltpu.CompilerParams(vmem_limit_bytes=64 * 1024 * 1024)
LIMIT = pltpu.CompilerParams(vmem_limit_bytes=62 * 1024 * 1024)


def dot(left, right, contract):
    return lax.dot_general(
        left, right, ((contract[:1], contract[1:]), ((), ())), preferred_element_type=jnp.float32
    )


def copies_of(pairs, semaphores):
    return [
        pltpu.make_async_copy(source, target, semaphores.at[item])
        for item, (source, target) in enumerate(pairs)
    ]


def columns_of(ref, head, width):
    return ref.at[:, pl.ds(pl.multiple_of(head * width, width), width)]


def staged(arriving, leaving):
    for copies in arriving:
        for copy in copies:
            copy.start()
    for copies, onward in zip(arriving, leaving):
        for copy in copies:
            copy.wait()
        for copy in onward:
            copy.start()
    for onward in leaving:
        for copy in onward:
            copy.wait()


def pack_kernel(distances, left_ref, right_ref, *refs):
    pieces, (buffer, arrived, sent) = refs[:HALF], refs[HALF:]
    member = lax.axis_index("member")
    width = left_ref.shape[1] // MEMBERS
    arriving, leaving = [], []
    for item, distance in enumerate(distances):
        head = member ^ distance
        pairs = [
            (columns_of(left_ref, head, width), buffer.at[item, :, pl.ds(0, width)]),
            (columns_of(right_ref, head, width), buffer.at[item, :, pl.ds(width, width)]),
        ]
        arriving.append(copies_of(pairs, arrived.at[item]))
        leaving.append([pltpu.make_async_copy(buffer.at[item], pieces[item], sent.at[item])])
    staged(arriving, leaving)


def pack(left, right, distances):
    rows, columns = left.shape
    shape = (rows, 2 * columns // MEMBERS)
    return pl.pallas_call(
        functools.partial(pack_kernel, distances),
        in_specs=[IN_HBM] * 2,
        out_specs=[IN_HBM] * HALF,
        out_shape=[jax.ShapeDtypeStruct(shape, left.dtype)] * HALF,
        scratch_shapes=[
            pltpu.VMEM((HALF, *shape), left.dtype),
            pltpu.SemaphoreType.DMA((HALF, 2)),
            pltpu.SemaphoreType.DMA((HALF,)),
        ],
        compiler_params=WHOLE_LIMIT,
        cost_estimate=pl.CostEstimate(
            flops=0, bytes_accessed=4 * rows * columns, transcendentals=0
        ),
    )(left, right)


def unpack_kernel(*refs):
    pieces, (left_ref, right_ref, sent) = refs[:MEMBERS], refs[MEMBERS:]
    member = lax.axis_index("member")
    width = left_ref.shape[1] // MEMBERS
    copies = []
    for item, distance in enumerate(BACK_DISTANCES):
        head = member ^ distance
        pairs = [
            (pieces[item].at[:, pl.ds(0, width)], columns_of(left_ref, head, width)),
            (pieces[item].at[:, pl.ds(width, width)], columns_of(right_ref, head, width)),
        ]
        copies += copies_of(pairs, sent.at[item])
    for copy in copies:
        copy.start()
    for copy in copies:
        copy.wait()


def unpack(pieces):
    rows, columns = pieces[0].shape
    whole = jax.ShapeDtypeStruct((rows, MEMBERS * columns // 2), pieces[0].dtype)
    return pl.pallas_call(
        unpack_kernel,
        in_specs=[pl.BlockSpec(memory_space=pltpu.VMEM)] * MEMBERS,
        out_specs=[IN_HBM] * 2,
        out_shape=[whole] * 2,
        scratch_shapes=[pltpu.SemaphoreType.DMA((MEMBERS, 2))],
        compiler_params=SMALL_LIMIT,
        cost_estimate=pl.CostEstimate(
            flops=0, bytes_accessed=4 * MEMBERS * rows * columns, transcendentals=0
        ),
    )(*pieces)


def attention_kernel(lengths_ref, rows_ref, *refs):
    own_parts, earlier_parts, out_ref, refs = refs[:3], refs[3:6], refs[6], refs[7:]
    own_grads, earlier_grads, refs = refs[:2], refs[2:4], refs[4:]
    kv, kv_turned, sums, weights, grad_weights, refs = *refs[:5], refs[5:]
    scores = refs
    step = pl.program_id(0)
    width = HEAD_WIDTH
    member = lax.axis_index("member")

    def turn(tile):
        part = kv[pl.ds(tile * CHUNKS, CHUNKS)].reshape(TILE, 2 * width)
        kv_turned[:, pl.ds(pl.multiple_of(tile * TILE, TILE), TILE)] = part.T

    @pl.when(step == 0)
    def _():
        for group, distances in enumerate(GROUPS):
            for part, distance in enumerate(distances):
                chunk = member ^ distance
                kv[chunk] = earlier_parts[group][part]
                kv[MEMBERS + chunk] = own_parts[group][part]
        sums[:MEMBERS] = jnp.zeros((MEMBERS, ROWS, 2 * width), jnp.float32)
        for tile in range(TILES):
            turn(tile)

    turn(TILES + step)

    def key_tile(item, first):
        tile = pl.ds((step + item) * CHUNKS, CHUNKS)
        return kv[tile, :, first : first + width].reshape(TILE, width)

    def turned_window(first):
        place = pl.ds(pl.multiple_of(step * TILE, TILE), KEYS)
        return kv_turned[first : first + width, place]

    def add(item, first, part):
        tile = pl.ds((step + item) * CHUNKS, CHUNKS)
        part = part.reshape(CHUNKS, ROWS, width)
        if item < TILES:
            part = sums[tile, :, first : first + width] + part
        sums[tile, :, first : first + width] = part

    queries = [rows_ref[:, head * width : (head + 1) * width] for head in range(2)]
    cotangents = [rows_ref[:, (2 + head) * width : (3 + head) * width] for head in range(2)]
    queries_turned = [part.T for part in queries]
    cotangents_turned = [part.T for part in cotangents]
    columns = [slice(head * TILE, (head + 1) * TILE) for head in range(2)]
    tiles = [slice(item * TILE, (item + 1) * TILE) for item in range(SPAN)]

    first_row = lax.axis_index("stretch") * WINDOW_LENGTH + step * TILE
    row = lax.broadcasted_iota(jnp.int32, (1, TILE), 1)
    oldest = row - (WINDOW_LENGTH - 1)

    def passed(item, carried):
        begin, oldest = carried
        near = begin - first_row
        oldest = jnp.where(near <= row, jnp.maximum(oldest, near), oldest)
        return begin + lengths_ref[item], oldest

    _, oldest = lax.fori_loop(0, lengths_ref.shape[0], passed, (jnp.int32(0), oldest))
    key_row = lax.broadcasted_iota(jnp.int32, (TILE, TILE), 0)

    tops = [jnp.full((1, TILE), -jnp.inf, jnp.float32)] * 2
    totals = [jnp.zeros((1, TILE), jnp.float32)] * 2

    def score(head, item):
        part = dot(key_tile(item, 0), queries_turned[head], (1, 0))
        seen = key_row >= oldest - (item - TILES) * TILE
        if item == TILES:
            seen = seen & (key_row <= row)
        part = jnp.where(seen, part, -jnp.inf)
        tops[head] = jnp.maximum(tops[head], jnp.max(part, axis=0, keepdims=True))
        scores[head][item] = part

    def weigh(head, item):
        part = jnp.exp2((scores[head][item] - tops[head]) * (SCORE_SCALE * LOG2_E))
        totals[head] = totals[head] + jnp.sum(part, axis=0, keepdims=True)
        weights[tiles[item], columns[head]] = part.astype(jnp.bfloat16)

    def put(head, first, part):
        place = slice((first + head) * width, (first + head + 1) * width)
        out_ref[:, place] = part.astype(jnp.bfloat16).T

    def attend(head, share):
        attended = dot(turned_window(width), weights[:, columns[head]], (1, 0))
        attended = (attended * share).astype(jnp.bfloat16)
        put(head, 0, attended)
        products = attended.astype(jnp.float32) * cotangents_turned[head].astype(jnp.float32)
        return jnp.sum(products, axis=0, keepdims=True)

    def weigh_grad(head, item, row_delta):
        grad = dot(key_tile(item, width), cotangents_turned[head], (1, 0)) - row_delta
        part = weights[tiles[item], columns[head]].astype(jnp.float32)
        part = (part * grad).astype(jnp.bfloat16)
        grad_weights[tiles[item], columns[head]] = part

    def make_query_grad(head, share):
        query_grad = dot(turned_window(0), grad_weights[:, columns[head]], (1, 0))
        put(head, 2, query_grad * (share * SCORE_SCALE))

    def scaled(parts, shares):
        scaled_parts = []
        for part, share in zip(parts, shares):
            down = jnp.broadcast_to(share, (8, TILE)).T[:, :1]
            scaled_parts.append((part.astype(jnp.float32) * down).astype(jnp.bfloat16))
        return jnp.concatenate(scaled_parts, axis=0)

    for item in range(SPAN):
        score(0, item)
    for item in range(SPAN):
        score(1, item)
        weigh(0, item)
    shares = [1.0 / totals[0]]
    deltas = [attend(0, shares[0])]
    for item in range(SPAN):
        weigh(1, item)
    shares.append(1.0 / totals[1])
    deltas.append(attend(1, shares[1]))
    cotangents_scaled = scaled(cotangents, shares)
    queries_scaled = scaled(queries, shares)
    for item in range(SPAN):
        weigh_grad(0, item, deltas[0])
        weigh_grad(1, item, deltas[1])
        add(item, width, dot(weights[tiles[item]], cotangents_scaled, (1, 0)))
        add(item, 0, dot(grad_weights[tiles[item]], queries_scaled, (1, 0)))
    make_query_grad(0, shares[0])
    make_query_grad(1, shares[1])

    @pl.when(step == TILES - 1)
    def _():
        for item, distance in enumerate(BACK_DISTANCES):
            half, part, chunk = item // HALF, item % HALF, member ^ distance
            for halves, place in ((earlier_grads, chunk), (own_grads, MEMBERS + chunk)):
                target = halves[half]
                target[part, :, :width] = (sums[place, :, :width] * SCORE_SCALE).astype(
                    jnp.bfloat16
                )
                target[part, :, width:] = sums[place, :, width:].astype(jnp.bfloat16)


def attention(doc_lengths, rows, own, earlier):
    width = HEAD_WIDTH
    products = 6 * 2 * WINDOW_LENGTH * 2 * KEYS * width
    half = jax.ShapeDtypeStruct((HALF, ROWS, 2 * width), jnp.bfloat16)
    rows_block = pl.BlockSpec((TILE, 4 * width), lambda i: (i, 0))
    half_block = pl.BlockSpec(half.shape, lambda i: (0, 0, 0))
    group_blocks = [
        pl.BlockSpec((len(group), ROWS, 2 * width), lambda i: (0, 0, 0)) for group in GROUPS
    ]
    outputs = pl.pallas_call(
        attention_kernel,
        grid=(TILES,),
        in_specs=[SCALARS, rows_block] + group_blocks * 2,
        out_specs=[rows_block] + [half_block] * 4,
        out_shape=[jax.ShapeDtypeStruct(rows.shape, jnp.bfloat16)] + [half] * 4,
        scratch_shapes=[
            pltpu.VMEM((2 * MEMBERS, ROWS, 2 * width), jnp.bfloat16),
            pltpu.VMEM((2 * width, 2 * WINDOW_LENGTH), jnp.bfloat16),
            pltpu.VMEM((2 * MEMBERS, ROWS, 2 * width), jnp.float32),
            pltpu.VMEM((KEYS, COLUMNS), jnp.bfloat16),
            pltpu.VMEM((KEYS, COLUMNS), jnp.bfloat16),
        ]
        + [pltpu.VMEM((SPAN, TILE, TILE), jnp.float32)] * 2,
        compiler_params=LIMIT,
        cost_estimate=pl.CostEstimate(
            flops=2 * products, bytes_accessed=WINDOW_LENGTH * width * 30, transcendentals=0
        ),
    )(doc_lengths, rows, *own, *earlier)
    return outputs[0], outputs[1:3], outputs[3:]


def by_head(block):
    return block.reshape(ROWS, MEMBERS, block.shape[1] // MEMBERS).transpose(1, 0, 2)


def by_token(blocks):
    return blocks.transpose(1, 0, 2).reshape(ROWS, MEMBERS * blocks.shape[2])


def exchanged(blocks):
    return lax.all_to_all(blocks, "member", split_axis=0, concat_axis=0, tiled=True)


def swapped(pieces, distances):
    moved = []
    for piece, distance in zip(pieces, distances):
        route = [(i, i ^ distance) for i in range(MEMBERS)]
        moved.append(lax.ppermute(piece, "member", route) if distance else piece)
    return moved


def onward(block, direction):
    lower = [(i, i + 1) for i in range(lax.axis_size("stretch") - 1)]
    route = lower if direction > 0 else [(j, i) for i, j in lower]
    return lax.ppermute(block, "stretch", route)


def shards(rotated_query_rows, rotated_key_rows, value_matrix, output_gradient, doc_lengths):
    heavy, light = GROUPS[0], GROUPS[1] + GROUPS[2]
    pieces = pack(rotated_key_rows, value_matrix, heavy)
    pieces, rotated_key_rows, value_matrix = lax.optimization_barrier(
        (pieces, rotated_key_rows, value_matrix)
    )
    pieces = swapped(pieces, heavy)
    pieces += swapped(pack(rotated_key_rows, value_matrix, light), light)
    near = jnp.stack(pieces[6:])
    earlier_near = onward(near, 1)
    rows = jnp.concatenate([by_head(rotated_query_rows), by_head(output_gradient)], axis=2)
    pieces, earlier_near, rows = lax.optimization_barrier((pieces[:6], earlier_near, rows))
    own = [jnp.stack(pieces[:4]), jnp.stack(pieces[4:])]
    earlier = [onward(part, 1) for part in own] + [earlier_near]
    own.append(near)
    rows = exchanged(rows).reshape(WINDOW_LENGTH, 4 * HEAD_WIDTH)
    results, own_grads, earlier_grads = attention(doc_lengths, rows, own, earlier)
    later = [onward(half, -1) for half in earlier_grads]
    results = exchanged(results.reshape(MEMBERS, ROWS, 4 * HEAD_WIDTH))
    attended = by_token(results[:, :, : 2 * HEAD_WIDTH])
    query_grad = by_token(results[:, :, 2 * HEAD_WIDTH :])
    sums = [
        (own_grads[half].astype(jnp.float32) + later[half].astype(jnp.float32)).astype(
            jnp.bfloat16
        )
        for half in range(2)
    ]
    pieces = [sums[item // HALF][item % HALF] for item in range(MEMBERS)]
    pieces = swapped(pieces, BACK_DISTANCES)
    attended, query_grad, pieces = lax.optimization_barrier((attended, query_grad, pieces))
    return (attended, query_grad, *unpack(pieces))


def solution(mesh):
    grouped = Mesh(mesh.devices.reshape(-1, MEMBERS), ("stretch", "member"))
    spread = P(("stretch", "member"), None)
    return jax.shard_map(
        shards,
        mesh=grouped,
        in_specs=(spread, spread, spread, spread, P()),
        out_specs=(spread, spread, spread, spread),
        check_vma=False,
    )
```

```python
import functools

import jax
import jax.numpy as jnp
from jax import lax
from jax.experimental import pallas as pl
from jax.experimental.pallas import tpu as pltpu
from jax.sharding import Mesh
from jax.sharding import PartitionSpec as P

HEAD_WIDTH = 256
WINDOW_LENGTH = 1024
MEMBERS = 8
HALF = MEMBERS // 2
DISTANCES = (7, 6, 5, 4, 3, 2, 1, 0)
BACK_DISTANCES = (7, 6, 5, 4, 0, 1, 2, 3)

TILE = 256
TILES = WINDOW_LENGTH // TILE
SPAN = TILES + 1
KEYS = SPAN * TILE
ROWS = WINDOW_LENGTH // MEMBERS
CHUNKS = TILE // ROWS
COLUMNS = 2 * TILE
SCORE_SCALE = HEAD_WIDTH ** (-0.5)
LOG2_E = 1.4426950408889634

IN_HBM = pl.BlockSpec(memory_space=pltpu.HBM)
SCALARS = pl.BlockSpec(memory_space=pltpu.SMEM)
SMALL_LIMIT = pltpu.CompilerParams(vmem_limit_bytes=4 * 1024 * 1024)
WHOLE_LIMIT = pltpu.CompilerParams(vmem_limit_bytes=64 * 1024 * 1024)
LIMIT = pltpu.CompilerParams(vmem_limit_bytes=62 * 1024 * 1024)


def dot(left, right, contract):
    return lax.dot_general(
        left, right, ((contract[:1], contract[1:]), ((), ())), preferred_element_type=jnp.float32
    )


def copies_of(pairs, semaphores):
    return [
        pltpu.make_async_copy(source, target, semaphores.at[item])
        for item, (source, target) in enumerate(pairs)
    ]


def columns_of(ref, head, width):
    return ref.at[:, pl.ds(pl.multiple_of(head * width, width), width)]


def staged(arriving, leaving):
    for copies in arriving:
        for copy in copies:
            copy.start()
    for copies, onward in zip(arriving, leaving):
        for copy in copies:
            copy.wait()
        for copy in onward:
            copy.start()
    for onward in leaving:
        for copy in onward:
            copy.wait()


def pack_kernel(distances, left_ref, right_ref, *refs):
    pieces, (buffer, arrived, sent) = refs[:HALF], refs[HALF:]
    member = lax.axis_index("member")
    width = left_ref.shape[1] // MEMBERS
    arriving, leaving = [], []
    for item, distance in enumerate(distances):
        head = member ^ distance
        pairs = [
            (columns_of(left_ref, head, width), buffer.at[item, :, pl.ds(0, width)]),
            (columns_of(right_ref, head, width), buffer.at[item, :, pl.ds(width, width)]),
        ]
        arriving.append(copies_of(pairs, arrived.at[item]))
        leaving.append([pltpu.make_async_copy(buffer.at[item], pieces[item], sent.at[item])])
    staged(arriving, leaving)


def pack(left, right, distances):
    rows, columns = left.shape
    shape = (rows, 2 * columns // MEMBERS)
    return pl.pallas_call(
        functools.partial(pack_kernel, distances),
        in_specs=[IN_HBM] * 2,
        out_specs=[IN_HBM] * HALF,
        out_shape=[jax.ShapeDtypeStruct(shape, left.dtype)] * HALF,
        scratch_shapes=[
            pltpu.VMEM((HALF, *shape), left.dtype),
            pltpu.SemaphoreType.DMA((HALF, 2)),
            pltpu.SemaphoreType.DMA((HALF,)),
        ],
        compiler_params=WHOLE_LIMIT,
        cost_estimate=pl.CostEstimate(
            flops=0, bytes_accessed=4 * rows * columns, transcendentals=0
        ),
    )(left, right)


def unpack_kernel(*refs):
    pieces, (left_ref, right_ref, sent) = refs[:MEMBERS], refs[MEMBERS:]
    member = lax.axis_index("member")
    width = left_ref.shape[1] // MEMBERS
    copies = []
    for item, distance in enumerate(BACK_DISTANCES):
        head = member ^ distance
        pairs = [
            (pieces[item].at[:, pl.ds(0, width)], columns_of(left_ref, head, width)),
            (pieces[item].at[:, pl.ds(width, width)], columns_of(right_ref, head, width)),
        ]
        copies += copies_of(pairs, sent.at[item])
    for copy in copies:
        copy.start()
    for copy in copies:
        copy.wait()


def unpack(pieces):
    rows, columns = pieces[0].shape
    whole = jax.ShapeDtypeStruct((rows, MEMBERS * columns // 2), pieces[0].dtype)
    return pl.pallas_call(
        unpack_kernel,
        in_specs=[pl.BlockSpec(memory_space=pltpu.VMEM)] * MEMBERS,
        out_specs=[IN_HBM] * 2,
        out_shape=[whole] * 2,
        scratch_shapes=[pltpu.SemaphoreType.DMA((MEMBERS, 2))],
        compiler_params=SMALL_LIMIT,
        cost_estimate=pl.CostEstimate(
            flops=0, bytes_accessed=4 * MEMBERS * rows * columns, transcendentals=0
        ),
    )(*pieces)


def attention_kernel(lengths_ref, rows_ref, *refs):
    own_halves, earlier_halves, out_ref, refs = refs[:2], refs[2:4], refs[4], refs[5:]
    own_grads, earlier_grads, refs = refs[:2], refs[2:4], refs[4:]
    kv, kv_turned, sums, weights, grad_weights, refs = *refs[:5], refs[5:]
    scores = refs
    step = pl.program_id(0)
    width = HEAD_WIDTH
    member = lax.axis_index("member")

    def turn(tile):
        part = kv[pl.ds(tile * CHUNKS, CHUNKS)].reshape(TILE, 2 * width)
        kv_turned[:, pl.ds(pl.multiple_of(tile * TILE, TILE), TILE)] = part.T

    @pl.when(step == 0)
    def _():
        for item, distance in enumerate(DISTANCES):
            half, part, chunk = item // HALF, item % HALF, member ^ distance
            kv[chunk] = earlier_halves[half][part]
            kv[MEMBERS + chunk] = own_halves[half][part]
        sums[:MEMBERS] = jnp.zeros((MEMBERS, ROWS, 2 * width), jnp.float32)
        for tile in range(TILES):
            turn(tile)

    turn(TILES + step)

    def key_tile(item, first):
        tile = pl.ds((step + item) * CHUNKS, CHUNKS)
        return kv[tile, :, first : first + width].reshape(TILE, width)

    def turned_window(first):
        place = pl.ds(pl.multiple_of(step * TILE, TILE), KEYS)
        return kv_turned[first : first + width, place]

    def add(item, first, part):
        tile = pl.ds((step + item) * CHUNKS, CHUNKS)
        part = part.reshape(CHUNKS, ROWS, width)
        if item < TILES:
            part = sums[tile, :, first : first + width] + part
        sums[tile, :, first : first + width] = part

    queries = [rows_ref[:, head * width : (head + 1) * width] for head in range(2)]
    cotangents = [rows_ref[:, (2 + head) * width : (3 + head) * width] for head in range(2)]
    queries_turned = [part.T for part in queries]
    cotangents_turned = [part.T for part in cotangents]
    columns = [slice(head * TILE, (head + 1) * TILE) for head in range(2)]
    tiles = [slice(item * TILE, (item + 1) * TILE) for item in range(SPAN)]

    first_row = lax.axis_index("stretch") * WINDOW_LENGTH + step * TILE
    row = lax.broadcasted_iota(jnp.int32, (1, TILE), 1)
    oldest = row - (WINDOW_LENGTH - 1)

    def passed(item, carried):
        begin, oldest = carried
        near = begin - first_row
        oldest = jnp.where(near <= row, jnp.maximum(oldest, near), oldest)
        return begin + lengths_ref[item], oldest

    _, oldest = lax.fori_loop(0, lengths_ref.shape[0], passed, (jnp.int32(0), oldest))
    key_row = lax.broadcasted_iota(jnp.int32, (TILE, TILE), 0)

    tops = [jnp.full((1, TILE), -jnp.inf, jnp.float32)] * 2
    totals = [jnp.zeros((1, TILE), jnp.float32)] * 2

    causal = key_row <= row
    edge_oldest = jnp.where(causal, oldest, oldest + WINDOW_LENGTH)

    def score(head, item):
        part = dot(key_tile(item, 0), queries_turned[head], (1, 0))
        if item:
            seen = key_row >= oldest - (item - TILES) * TILE
        else:
            last = dot(key_tile(TILES, 0), queries_turned[head], (1, 0))
            part = jnp.where(causal, last, part)
            seen = key_row >= edge_oldest
        part = jnp.where(seen, part, -jnp.inf)
        tops[head] = jnp.maximum(tops[head], jnp.max(part, axis=0, keepdims=True))
        scores[head][item] = part

    def weigh(head, item):
        part = jnp.exp2((scores[head][item] - tops[head]) * (SCORE_SCALE * LOG2_E))
        totals[head] = totals[head] + jnp.sum(part, axis=0, keepdims=True)
        if item == 0:
            last = jnp.where(causal, part, 0.0)
            weights[tiles[TILES], columns[head]] = last.astype(jnp.bfloat16)
            part = jnp.where(causal, 0.0, part)
        weights[tiles[item], columns[head]] = part.astype(jnp.bfloat16)

    def put(head, first, part):
        place = slice((first + head) * width, (first + head + 1) * width)
        out_ref[:, place] = part.astype(jnp.bfloat16).T

    def attend(head, share):
        attended = dot(turned_window(width), weights[:, columns[head]], (1, 0))
        attended = (attended * share).astype(jnp.bfloat16)
        put(head, 0, attended)
        products = attended.astype(jnp.float32) * cotangents_turned[head].astype(jnp.float32)
        return jnp.sum(products, axis=0, keepdims=True)

    def weigh_grad(head, item, row_delta):
        grad = dot(key_tile(item, width), cotangents_turned[head], (1, 0)) - row_delta
        part = weights[tiles[item], columns[head]].astype(jnp.float32)
        part = (part * grad).astype(jnp.bfloat16)
        grad_weights[tiles[item], columns[head]] = part

    def make_query_grad(head, share):
        query_grad = dot(turned_window(0), grad_weights[:, columns[head]], (1, 0))
        put(head, 2, query_grad * (share * SCORE_SCALE))

    def scaled(parts, shares):
        scaled_parts = []
        for part, share in zip(parts, shares):
            down = jnp.broadcast_to(share, (8, TILE)).T[:, :1]
            scaled_parts.append((part.astype(jnp.float32) * down).astype(jnp.bfloat16))
        return jnp.concatenate(scaled_parts, axis=0)

    for item in range(TILES):
        score(0, item)
    for item in range(TILES):
        score(1, item)
        weigh(0, item)
    shares = [1.0 / totals[0]]
    deltas = [attend(0, shares[0])]
    for item in range(TILES):
        weigh(1, item)
    shares.append(1.0 / totals[1])
    deltas.append(attend(1, shares[1]))
    cotangents_scaled = scaled(cotangents, shares)
    queries_scaled = scaled(queries, shares)
    for item in range(SPAN):
        weigh_grad(0, item, deltas[0])
        weigh_grad(1, item, deltas[1])
        add(item, width, dot(weights[tiles[item]], cotangents_scaled, (1, 0)))
        add(item, 0, dot(grad_weights[tiles[item]], queries_scaled, (1, 0)))
    make_query_grad(0, shares[0])
    make_query_grad(1, shares[1])

    @pl.when(step == TILES - 1)
    def _():
        for item, distance in enumerate(BACK_DISTANCES):
            half, part, chunk = item // HALF, item % HALF, member ^ distance
            for halves, place in ((earlier_grads, chunk), (own_grads, MEMBERS + chunk)):
                target = halves[half]
                target[part, :, :width] = (sums[place, :, :width] * SCORE_SCALE).astype(
                    jnp.bfloat16
                )
                target[part, :, width:] = sums[place, :, width:].astype(jnp.bfloat16)


def attention(doc_lengths, rows, own, earlier):
    width = HEAD_WIDTH
    products = 6 * 2 * WINDOW_LENGTH * 2 * KEYS * width
    half = jax.ShapeDtypeStruct((HALF, ROWS, 2 * width), jnp.bfloat16)
    rows_block = pl.BlockSpec((TILE, 4 * width), lambda i: (i, 0))
    half_block = pl.BlockSpec(half.shape, lambda i: (0, 0, 0))
    outputs = pl.pallas_call(
        attention_kernel,
        grid=(TILES,),
        in_specs=[SCALARS, rows_block] + [half_block] * 4,
        out_specs=[rows_block] + [half_block] * 4,
        out_shape=[jax.ShapeDtypeStruct(rows.shape, jnp.bfloat16)] + [half] * 4,
        scratch_shapes=[
            pltpu.VMEM((2 * MEMBERS, ROWS, 2 * width), jnp.bfloat16),
            pltpu.VMEM((2 * width, 2 * WINDOW_LENGTH), jnp.bfloat16),
            pltpu.VMEM((2 * MEMBERS, ROWS, 2 * width), jnp.float32),
            pltpu.VMEM((KEYS, COLUMNS), jnp.bfloat16),
            pltpu.VMEM((KEYS, COLUMNS), jnp.bfloat16),
        ]
        + [pltpu.VMEM((TILES, TILE, TILE), jnp.float32)] * 2,
        compiler_params=LIMIT,
        cost_estimate=pl.CostEstimate(
            flops=2 * products, bytes_accessed=WINDOW_LENGTH * width * 30, transcendentals=0
        ),
    )(doc_lengths, rows, *own, *earlier)
    return outputs[0], outputs[1:3], outputs[3:]


def by_head(block):
    return block.reshape(ROWS, MEMBERS, block.shape[1] // MEMBERS).transpose(1, 0, 2)


def by_token(blocks):
    return blocks.transpose(1, 0, 2).reshape(ROWS, MEMBERS * blocks.shape[2])


def exchanged(blocks):
    return lax.all_to_all(blocks, "member", split_axis=0, concat_axis=0, tiled=True)


def swapped(pieces, distances):
    moved = []
    for piece, distance in zip(pieces, distances):
        route = [(i, i ^ distance) for i in range(MEMBERS)]
        moved.append(lax.ppermute(piece, "member", route) if distance else piece)
    return moved


def onward(block, direction):
    lower = [(i, i + 1) for i in range(lax.axis_size("stretch") - 1)]
    route = lower if direction > 0 else [(j, i) for i, j in lower]
    return lax.ppermute(block, "stretch", route)


def shards(rotated_query_rows, rotated_key_rows, value_matrix, output_gradient, doc_lengths):
    heavy, light = DISTANCES[:HALF], DISTANCES[HALF:]
    pieces = pack(rotated_key_rows, value_matrix, heavy)
    pieces, rotated_key_rows, value_matrix = lax.optimization_barrier(
        (pieces, rotated_key_rows, value_matrix)
    )
    pieces = swapped(pieces, heavy)
    pieces += swapped(pack(rotated_key_rows, value_matrix, light), light)
    rows = jnp.concatenate([by_head(rotated_query_rows), by_head(output_gradient)], axis=2)
    pieces, rows = lax.optimization_barrier((pieces, rows))
    own = [jnp.stack(pieces[:HALF]), jnp.stack(pieces[HALF:])]
    earlier = [onward(half, 1) for half in own]
    rows = exchanged(rows).reshape(WINDOW_LENGTH, 4 * HEAD_WIDTH)
    results, own_grads, earlier_grads = attention(doc_lengths, rows, own, earlier)
    later = [onward(half, -1) for half in earlier_grads]
    results = exchanged(results.reshape(MEMBERS, ROWS, 4 * HEAD_WIDTH))
    attended = by_token(results[:, :, : 2 * HEAD_WIDTH])
    query_grad = by_token(results[:, :, 2 * HEAD_WIDTH :])
    sums = [
        (own_grads[half].astype(jnp.float32) + later[half].astype(jnp.float32)).astype(
            jnp.bfloat16
        )
        for half in range(2)
    ]
    pieces = [sums[item // HALF][item % HALF] for item in range(MEMBERS)]
    pieces = swapped(pieces, BACK_DISTANCES)
    attended, query_grad, pieces = lax.optimization_barrier((attended, query_grad, pieces))
    return (attended, query_grad, *unpack(pieces))


def solution(mesh):
    grouped = Mesh(mesh.devices.reshape(-1, MEMBERS), ("stretch", "member"))
    spread = P(("stretch", "member"), None)
    return jax.shard_map(
        shards,
        mesh=grouped,
        in_specs=(spread, spread, spread, spread, P()),
        out_specs=(spread, spread, spread, spread),
        check_vma=False,
    )
```

```python
import functools

import jax
import jax.numpy as jnp
from jax import lax
from jax.experimental import pallas as pl
from jax.experimental.pallas import tpu as pltpu
from jax.sharding import Mesh
from jax.sharding import PartitionSpec as P

HEAD_WIDTH = 256
WINDOW_LENGTH = 1024
MEMBERS = 8
HALF = MEMBERS // 2
DISTANCES = (7, 6, 5, 4, 3, 2, 1, 0)
BACK_DISTANCES = (7, 6, 5, 4, 0, 1, 2, 3)

TILE = 256
TILES = WINDOW_LENGTH // TILE
SPAN = TILES + 1
KEYS = SPAN * TILE
ROWS = WINDOW_LENGTH // MEMBERS
CHUNKS = TILE // ROWS
ONES = 16
COLUMNS = 2 * TILE
SCORE_SCALE = HEAD_WIDTH ** (-0.5)
LOG2_E = 1.4426950408889634

IN_HBM = pl.BlockSpec(memory_space=pltpu.HBM)
SCALARS = pl.BlockSpec(memory_space=pltpu.SMEM)
SMALL_LIMIT = pltpu.CompilerParams(vmem_limit_bytes=4 * 1024 * 1024)
WHOLE_LIMIT = pltpu.CompilerParams(vmem_limit_bytes=64 * 1024 * 1024)
LIMIT = pltpu.CompilerParams(vmem_limit_bytes=62 * 1024 * 1024)


def dot(left, right, contract):
    return lax.dot_general(
        left, right, ((contract[:1], contract[1:]), ((), ())), preferred_element_type=jnp.float32
    )


def copies_of(pairs, semaphores):
    return [
        pltpu.make_async_copy(source, target, semaphores.at[item])
        for item, (source, target) in enumerate(pairs)
    ]


def columns_of(ref, head, width):
    return ref.at[:, pl.ds(pl.multiple_of(head * width, width), width)]


def staged(arriving, leaving):
    for copies in arriving:
        for copy in copies:
            copy.start()
    for copies, onward in zip(arriving, leaving):
        for copy in copies:
            copy.wait()
        for copy in onward:
            copy.start()
    for onward in leaving:
        for copy in onward:
            copy.wait()


def pack_kernel(distances, left_ref, right_ref, *refs):
    pieces, (buffer, arrived, sent) = refs[:HALF], refs[HALF:]
    member = lax.axis_index("member")
    width = left_ref.shape[1] // MEMBERS
    arriving, leaving = [], []
    for item, distance in enumerate(distances):
        head = member ^ distance
        pairs = [
            (columns_of(left_ref, head, width), buffer.at[item, :, pl.ds(0, width)]),
            (columns_of(right_ref, head, width), buffer.at[item, :, pl.ds(width, width)]),
        ]
        arriving.append(copies_of(pairs, arrived.at[item]))
        leaving.append([pltpu.make_async_copy(buffer.at[item], pieces[item], sent.at[item])])
    staged(arriving, leaving)


def pack(left, right, distances):
    rows, columns = left.shape
    shape = (rows, 2 * columns // MEMBERS)
    return pl.pallas_call(
        functools.partial(pack_kernel, distances),
        in_specs=[IN_HBM] * 2,
        out_specs=[IN_HBM] * HALF,
        out_shape=[jax.ShapeDtypeStruct(shape, left.dtype)] * HALF,
        scratch_shapes=[
            pltpu.VMEM((HALF, *shape), left.dtype),
            pltpu.SemaphoreType.DMA((HALF, 2)),
            pltpu.SemaphoreType.DMA((HALF,)),
        ],
        compiler_params=WHOLE_LIMIT,
        cost_estimate=pl.CostEstimate(
            flops=0, bytes_accessed=4 * rows * columns, transcendentals=0
        ),
    )(left, right)


def unpack_kernel(*refs):
    pieces, (left_ref, right_ref, sent) = refs[:MEMBERS], refs[MEMBERS:]
    member = lax.axis_index("member")
    width = left_ref.shape[1] // MEMBERS
    copies = []
    for item, distance in enumerate(BACK_DISTANCES):
        head = member ^ distance
        pairs = [
            (pieces[item].at[:, pl.ds(0, width)], columns_of(left_ref, head, width)),
            (pieces[item].at[:, pl.ds(width, width)], columns_of(right_ref, head, width)),
        ]
        copies += copies_of(pairs, sent.at[item])
    for copy in copies:
        copy.start()
    for copy in copies:
        copy.wait()


def unpack(pieces):
    rows, columns = pieces[0].shape
    whole = jax.ShapeDtypeStruct((rows, MEMBERS * columns // 2), pieces[0].dtype)
    return pl.pallas_call(
        unpack_kernel,
        in_specs=[pl.BlockSpec(memory_space=pltpu.VMEM)] * MEMBERS,
        out_specs=[IN_HBM] * 2,
        out_shape=[whole] * 2,
        scratch_shapes=[pltpu.SemaphoreType.DMA((MEMBERS, 2))],
        compiler_params=SMALL_LIMIT,
        cost_estimate=pl.CostEstimate(
            flops=0, bytes_accessed=4 * MEMBERS * rows * columns, transcendentals=0
        ),
    )(*pieces)


def attention_kernel(lengths_ref, rows_ref, *refs):
    own_halves, earlier_halves, out_ref, refs = refs[:2], refs[2:4], refs[4], refs[5:]
    own_grads, earlier_grads, refs = refs[:2], refs[2:4], refs[4:]
    kv, kv_turned, sums, weights, grad_weights, refs = *refs[:5], refs[5:]
    scores = refs
    step = pl.program_id(0)
    width = HEAD_WIDTH
    member = lax.axis_index("member")

    def turn(tile):
        part = kv[pl.ds(tile * CHUNKS, CHUNKS)].reshape(TILE, 2 * width)
        kv_turned[: 2 * width, pl.ds(pl.multiple_of(tile * TILE, TILE), TILE)] = part.T

    @pl.when(step == 0)
    def _():
        for item, distance in enumerate(DISTANCES):
            half, part, chunk = item // HALF, item % HALF, member ^ distance
            kv[chunk] = earlier_halves[half][part]
            kv[MEMBERS + chunk] = own_halves[half][part]
        sums[:MEMBERS] = jnp.zeros((MEMBERS, ROWS, 2 * width), jnp.float32)
        kv_turned[2 * width :] = jnp.ones((ONES, 2 * WINDOW_LENGTH), jnp.bfloat16)
        for tile in range(TILES):
            turn(tile)

    turn(TILES + step)

    def key_tile(item, first):
        tile = pl.ds((step + item) * CHUNKS, CHUNKS)
        return kv[tile, :, first : first + width].reshape(TILE, width)

    def turned_window(first, last):
        place = pl.ds(pl.multiple_of(step * TILE, TILE), KEYS)
        return kv_turned[first:last, place]

    def add(item, first, part):
        tile = pl.ds((step + item) * CHUNKS, CHUNKS)
        part = part.reshape(CHUNKS, ROWS, width)
        if item < TILES:
            part = sums[tile, :, first : first + width] + part
        sums[tile, :, first : first + width] = part

    queries = [rows_ref[:, head * width : (head + 1) * width] for head in range(2)]
    cotangents = [rows_ref[:, (2 + head) * width : (3 + head) * width] for head in range(2)]
    queries_turned = [part.T for part in queries]
    cotangents_turned = [part.T for part in cotangents]
    columns = [slice(head * TILE, (head + 1) * TILE) for head in range(2)]
    tiles = [slice(item * TILE, (item + 1) * TILE) for item in range(SPAN)]

    first_row = lax.axis_index("stretch") * WINDOW_LENGTH + step * TILE
    row = lax.broadcasted_iota(jnp.int32, (1, TILE), 1)
    oldest = row - (WINDOW_LENGTH - 1)

    def passed(item, carried):
        begin, oldest = carried
        near = begin - first_row
        oldest = jnp.where(near <= row, jnp.maximum(oldest, near), oldest)
        return begin + lengths_ref[item], oldest

    _, oldest = lax.fori_loop(0, lengths_ref.shape[0], passed, (jnp.int32(0), oldest))
    key_row = lax.broadcasted_iota(jnp.int32, (TILE, TILE), 0)

    tops = [jnp.full((1, TILE), -jnp.inf, jnp.float32)] * 2

    causal = key_row <= row
    edge_oldest = jnp.where(causal, oldest, oldest + WINDOW_LENGTH)

    def score(head, item):
        part = dot(key_tile(item, 0), queries_turned[head], (1, 0))
        if item:
            seen = key_row >= oldest - (item - TILES) * TILE
        else:
            last = dot(key_tile(TILES, 0), queries_turned[head], (1, 0))
            part = jnp.where(causal, last, part)
            seen = key_row >= edge_oldest
        part = jnp.where(seen, part, -jnp.inf)
        tops[head] = jnp.maximum(tops[head], jnp.max(part, axis=0, keepdims=True))
        scores[head][item] = part

    def weigh(head, item):
        part = jnp.exp2((scores[head][item] - tops[head]) * (SCORE_SCALE * LOG2_E))
        if item == 0:
            last = jnp.where(causal, part, 0.0)
            weights[tiles[TILES], columns[head]] = last.astype(jnp.bfloat16)
            part = jnp.where(causal, 0.0, part)
        weights[tiles[item], columns[head]] = part.astype(jnp.bfloat16)

    def put(head, first, part):
        place = slice((first + head) * width, (first + head + 1) * width)
        out_ref[:, place] = part.astype(jnp.bfloat16).T

    def attend(head):
        values = turned_window(width, 2 * width + ONES)
        attended = dot(values, weights[:, columns[head]], (1, 0))
        share = 1.0 / attended[width : width + 1]
        attended = (attended[:width] * share).astype(jnp.bfloat16)
        put(head, 0, attended)
        products = attended.astype(jnp.float32) * cotangents_turned[head].astype(jnp.float32)
        return share, jnp.sum(products, axis=0, keepdims=True)

    def weigh_grad(head, item, row_delta):
        grad = dot(key_tile(item, width), cotangents_turned[head], (1, 0)) - row_delta
        part = weights[tiles[item], columns[head]].astype(jnp.float32)
        part = (part * grad).astype(jnp.bfloat16)
        grad_weights[tiles[item], columns[head]] = part

    def make_query_grad(head, share):
        query_grad = dot(turned_window(0, width), grad_weights[:, columns[head]], (1, 0))
        put(head, 2, query_grad * (share * SCORE_SCALE))

    def scaled(parts, shares):
        scaled_parts = []
        for part, share in zip(parts, shares):
            down = jnp.broadcast_to(share, (8, TILE)).T[:, :1]
            scaled_parts.append((part.astype(jnp.float32) * down).astype(jnp.bfloat16))
        return jnp.concatenate(scaled_parts, axis=0)

    for item in range(TILES):
        score(0, item)
    for item in range(TILES):
        score(1, item)
        weigh(0, item)
    shares, deltas = [None] * 2, [None] * 2
    shares[0], deltas[0] = attend(0)
    for item in range(TILES):
        weigh(1, item)
    shares[1], deltas[1] = attend(1)
    cotangents_scaled = scaled(cotangents, shares)
    queries_scaled = scaled(queries, [share * SCORE_SCALE for share in shares])
    for item in range(SPAN):
        weigh_grad(0, item, deltas[0])
        weigh_grad(1, item, deltas[1])
        add(item, width, dot(weights[tiles[item]], cotangents_scaled, (1, 0)))
        add(item, 0, dot(grad_weights[tiles[item]], queries_scaled, (1, 0)))
    make_query_grad(0, shares[0])
    make_query_grad(1, shares[1])

    @pl.when(step == TILES - 1)
    def _():
        for item, distance in enumerate(BACK_DISTANCES):
            half, part, chunk = item // HALF, item % HALF, member ^ distance
            for halves, place in ((earlier_grads, chunk), (own_grads, MEMBERS + chunk)):
                target = halves[half]
                target[part] = sums[place].astype(jnp.bfloat16)


def attention(doc_lengths, rows, own, earlier):
    width = HEAD_WIDTH
    products = 6 * 2 * WINDOW_LENGTH * 2 * KEYS * width
    half = jax.ShapeDtypeStruct((HALF, ROWS, 2 * width), jnp.bfloat16)
    rows_block = pl.BlockSpec((TILE, 4 * width), lambda i: (i, 0))
    half_block = pl.BlockSpec(half.shape, lambda i: (0, 0, 0))
    outputs = pl.pallas_call(
        attention_kernel,
        grid=(TILES,),
        in_specs=[SCALARS, rows_block] + [half_block] * 4,
        out_specs=[rows_block] + [half_block] * 4,
        out_shape=[jax.ShapeDtypeStruct(rows.shape, jnp.bfloat16)] + [half] * 4,
        scratch_shapes=[
            pltpu.VMEM((2 * MEMBERS, ROWS, 2 * width), jnp.bfloat16),
            pltpu.VMEM((2 * width + ONES, 2 * WINDOW_LENGTH), jnp.bfloat16),
            pltpu.VMEM((2 * MEMBERS, ROWS, 2 * width), jnp.float32),
            pltpu.VMEM((KEYS, COLUMNS), jnp.bfloat16),
            pltpu.VMEM((KEYS, COLUMNS), jnp.bfloat16),
        ]
        + [pltpu.VMEM((TILES, TILE, TILE), jnp.float32)] * 2,
        compiler_params=LIMIT,
        cost_estimate=pl.CostEstimate(
            flops=2 * products, bytes_accessed=WINDOW_LENGTH * width * 30, transcendentals=0
        ),
    )(doc_lengths, rows, *own, *earlier)
    return outputs[0], outputs[1:3], outputs[3:]


def by_head(block):
    return block.reshape(ROWS, MEMBERS, block.shape[1] // MEMBERS).transpose(1, 0, 2)


def by_token(blocks):
    return blocks.transpose(1, 0, 2).reshape(ROWS, MEMBERS * blocks.shape[2])


def exchanged(blocks):
    return lax.all_to_all(blocks, "member", split_axis=0, concat_axis=0, tiled=True)


def swapped(pieces, distances):
    moved = []
    for piece, distance in zip(pieces, distances):
        route = [(i, i ^ distance) for i in range(MEMBERS)]
        moved.append(lax.ppermute(piece, "member", route) if distance else piece)
    return moved


def onward(block, direction):
    lower = [(i, i + 1) for i in range(lax.axis_size("stretch") - 1)]
    route = lower if direction > 0 else [(j, i) for i, j in lower]
    return lax.ppermute(block, "stretch", route)


def shards(rotated_query_rows, rotated_key_rows, value_matrix, output_gradient, doc_lengths):
    heavy, light = DISTANCES[:HALF], DISTANCES[HALF:]
    pieces = pack(rotated_key_rows, value_matrix, heavy)
    pieces, rotated_key_rows, value_matrix = lax.optimization_barrier(
        (pieces, rotated_key_rows, value_matrix)
    )
    pieces = swapped(pieces, heavy)
    pieces += swapped(pack(rotated_key_rows, value_matrix, light), light)
    rows = jnp.concatenate([by_head(rotated_query_rows), by_head(output_gradient)], axis=2)
    pieces, rows = lax.optimization_barrier((pieces, rows))
    own = [jnp.stack(pieces[:HALF]), jnp.stack(pieces[HALF:])]
    earlier = [onward(half, 1) for half in own]
    rows = exchanged(rows).reshape(WINDOW_LENGTH, 4 * HEAD_WIDTH)
    results, own_grads, earlier_grads = attention(doc_lengths, rows, own, earlier)
    later = [onward(half, -1) for half in earlier_grads]
    results = exchanged(results.reshape(MEMBERS, ROWS, 4 * HEAD_WIDTH))
    attended = by_token(results[:, :, : 2 * HEAD_WIDTH])
    query_grad = by_token(results[:, :, 2 * HEAD_WIDTH :])
    sums = [
        (own_grads[half].astype(jnp.float32) + later[half].astype(jnp.float32)).astype(
            jnp.bfloat16
        )
        for half in range(2)
    ]
    pieces = [sums[item // HALF][item % HALF] for item in range(MEMBERS)]
    pieces = swapped(pieces, BACK_DISTANCES)
    attended, query_grad, pieces = lax.optimization_barrier((attended, query_grad, pieces))
    return (attended, query_grad, *unpack(pieces))


def solution(mesh):
    grouped = Mesh(mesh.devices.reshape(-1, MEMBERS), ("stretch", "member"))
    spread = P(("stretch", "member"), None)
    return jax.shard_map(
        shards,
        mesh=grouped,
        in_specs=(spread, spread, spread, spread, P()),
        out_specs=(spread, spread, spread, spread),
        check_vma=False,
    )
```

```python
import functools

import jax
import jax.numpy as jnp
from jax import lax
from jax.experimental import pallas as pl
from jax.experimental.pallas import tpu as pltpu
from jax.sharding import Mesh
from jax.sharding import PartitionSpec as P

HEAD_WIDTH = 256
WINDOW_LENGTH = 1024
MEMBERS = 8
HALF = MEMBERS // 2
DISTANCES = (7, 6, 5, 4, 3, 2, 1, 0)
BACK_DISTANCES = (7, 6, 5, 4, 0, 1, 2, 3)

TILE = 256
TILES = WINDOW_LENGTH // TILE
SPAN = TILES + 1
KEYS = SPAN * TILE
ROWS = WINDOW_LENGTH // MEMBERS
CHUNKS = TILE // ROWS
COLUMNS = 2 * TILE
SCORE_SCALE = HEAD_WIDTH ** (-0.5)
LOG2_E = 1.4426950408889634

IN_HBM = pl.BlockSpec(memory_space=pltpu.HBM)
SCALARS = pl.BlockSpec(memory_space=pltpu.SMEM)
SMALL_LIMIT = pltpu.CompilerParams(vmem_limit_bytes=4 * 1024 * 1024)
WHOLE_LIMIT = pltpu.CompilerParams(vmem_limit_bytes=64 * 1024 * 1024)
LIMIT = pltpu.CompilerParams(vmem_limit_bytes=62 * 1024 * 1024)


def dot(left, right, contract):
    return lax.dot_general(
        left, right, ((contract[:1], contract[1:]), ((), ())), preferred_element_type=jnp.float32
    )


def copies_of(pairs, semaphores):
    return [
        pltpu.make_async_copy(source, target, semaphores.at[item])
        for item, (source, target) in enumerate(pairs)
    ]


def columns_of(ref, head, width):
    return ref.at[:, pl.ds(pl.multiple_of(head * width, width), width)]


def staged(arriving, leaving):
    for copies in arriving:
        for copy in copies:
            copy.start()
    for copies, onward in zip(arriving, leaving):
        for copy in copies:
            copy.wait()
        for copy in onward:
            copy.start()
    for onward in leaving:
        for copy in onward:
            copy.wait()


def pack_kernel(distances, left_ref, right_ref, *refs):
    pieces, (buffer, arrived, sent) = refs[:HALF], refs[HALF:]
    member = lax.axis_index("member")
    width = left_ref.shape[1] // MEMBERS
    arriving, leaving = [], []
    for item, distance in enumerate(distances):
        head = member ^ distance
        pairs = [
            (columns_of(left_ref, head, width), buffer.at[item, :, pl.ds(0, width)]),
            (columns_of(right_ref, head, width), buffer.at[item, :, pl.ds(width, width)]),
        ]
        arriving.append(copies_of(pairs, arrived.at[item]))
        leaving.append([pltpu.make_async_copy(buffer.at[item], pieces[item], sent.at[item])])
    staged(arriving, leaving)


def pack(left, right, distances):
    rows, columns = left.shape
    shape = (rows, 2 * columns // MEMBERS)
    return pl.pallas_call(
        functools.partial(pack_kernel, distances),
        in_specs=[IN_HBM] * 2,
        out_specs=[IN_HBM] * HALF,
        out_shape=[jax.ShapeDtypeStruct(shape, left.dtype)] * HALF,
        scratch_shapes=[
            pltpu.VMEM((HALF, *shape), left.dtype),
            pltpu.SemaphoreType.DMA((HALF, 2)),
            pltpu.SemaphoreType.DMA((HALF,)),
        ],
        compiler_params=WHOLE_LIMIT,
        cost_estimate=pl.CostEstimate(
            flops=0, bytes_accessed=4 * rows * columns, transcendentals=0
        ),
    )(left, right)


def unpack_kernel(*refs):
    pieces, (left_ref, right_ref, sent) = refs[:MEMBERS], refs[MEMBERS:]
    member = lax.axis_index("member")
    width = left_ref.shape[1] // MEMBERS
    copies = []
    for item, distance in enumerate(BACK_DISTANCES):
        head = member ^ distance
        pairs = [
            (pieces[item].at[:, pl.ds(0, width)], columns_of(left_ref, head, width)),
            (pieces[item].at[:, pl.ds(width, width)], columns_of(right_ref, head, width)),
        ]
        copies += copies_of(pairs, sent.at[item])
    for copy in copies:
        copy.start()
    for copy in copies:
        copy.wait()


def unpack(pieces):
    rows, columns = pieces[0].shape
    whole = jax.ShapeDtypeStruct((rows, MEMBERS * columns // 2), pieces[0].dtype)
    return pl.pallas_call(
        unpack_kernel,
        in_specs=[pl.BlockSpec(memory_space=pltpu.VMEM)] * MEMBERS,
        out_specs=[IN_HBM] * 2,
        out_shape=[whole] * 2,
        scratch_shapes=[pltpu.SemaphoreType.DMA((MEMBERS, 2))],
        compiler_params=SMALL_LIMIT,
        cost_estimate=pl.CostEstimate(
            flops=0, bytes_accessed=4 * MEMBERS * rows * columns, transcendentals=0
        ),
    )(*pieces)


def attention_kernel(lengths_ref, rows_ref, *refs):
    own_halves, earlier_halves, out_ref, refs = refs[:2], refs[2:4], refs[4], refs[5:]
    own_grads, earlier_grads, refs = refs[:2], refs[2:4], refs[4:]
    kv, kv_turned, sums, weights, grad_weights, refs = *refs[:5], refs[5:]
    scores = refs
    step = pl.program_id(0)
    width = HEAD_WIDTH
    member = lax.axis_index("member")

    def turn(tile):
        part = kv[pl.ds(tile * CHUNKS, CHUNKS)].reshape(TILE, 2 * width)
        kv_turned[:, pl.ds(pl.multiple_of(tile * TILE, TILE), TILE)] = part.T

    @pl.when(step == 0)
    def _():
        for item, distance in enumerate(DISTANCES):
            half, part, chunk = item // HALF, item % HALF, member ^ distance
            kv[chunk] = earlier_halves[half][part]
            kv[MEMBERS + chunk] = own_halves[half][part]
        sums[:MEMBERS] = jnp.zeros((MEMBERS, ROWS, 2 * width), jnp.float32)
        for tile in range(TILES):
            turn(tile)

    turn(TILES + step)

    def key_tile(item, first):
        tile = pl.ds((step + item) * CHUNKS, CHUNKS)
        return kv[tile, :, first : first + width].reshape(TILE, width)

    def turned_window(first):
        place = pl.ds(pl.multiple_of(step * TILE, TILE), KEYS)
        return kv_turned[first : first + width, place]

    def add(item, first, part):
        tile = pl.ds((step + item) * CHUNKS, CHUNKS)
        part = part.reshape(CHUNKS, ROWS, width)
        if item < TILES:
            part = sums[tile, :, first : first + width] + part
        sums[tile, :, first : first + width] = part

    queries = [rows_ref[:, head * width : (head + 1) * width] for head in range(2)]
    cotangents = [rows_ref[:, (2 + head) * width : (3 + head) * width] for head in range(2)]
    queries_turned = [part.T for part in queries]
    cotangents_turned = [part.T for part in cotangents]
    columns = [slice(head * TILE, (head + 1) * TILE) for head in range(2)]
    tiles = [slice(item * TILE, (item + 1) * TILE) for item in range(SPAN)]

    first_row = lax.axis_index("stretch") * WINDOW_LENGTH + step * TILE
    row = lax.broadcasted_iota(jnp.int32, (1, TILE), 1)
    oldest = row - (WINDOW_LENGTH - 1)

    def passed(item, carried):
        begin, oldest = carried
        near = begin - first_row
        oldest = jnp.where(near <= row, jnp.maximum(oldest, near), oldest)
        return begin + lengths_ref[item], oldest

    _, oldest = lax.fori_loop(0, lengths_ref.shape[0], passed, (jnp.int32(0), oldest))
    key_row = lax.broadcasted_iota(jnp.int32, (TILE, TILE), 0)

    tops = [jnp.full((1, TILE), -jnp.inf, jnp.float32)] * 2
    totals = [jnp.zeros((1, TILE), jnp.float32)] * 2

    causal = key_row <= row
    edge_oldest = jnp.where(causal, oldest, oldest + WINDOW_LENGTH)

    def score(head, item):
        part = dot(key_tile(item, 0), queries_turned[head], (1, 0))
        if item:
            seen = key_row >= oldest - (item - TILES) * TILE
        else:
            last = dot(key_tile(TILES, 0), queries_turned[head], (1, 0))
            part = jnp.where(causal, last, part)
            seen = key_row >= edge_oldest
        part = jnp.where(seen, part, -jnp.inf)
        tops[head] = jnp.maximum(tops[head], jnp.max(part, axis=0, keepdims=True))
        scores[head][item] = part

    def weigh(head, item):
        part = jnp.exp2((scores[head][item] - tops[head]) * (SCORE_SCALE * LOG2_E))
        totals[head] = totals[head] + jnp.sum(part, axis=0, keepdims=True)
        if item == 0:
            last = jnp.where(causal, part, 0.0)
            weights[tiles[TILES], columns[head]] = last.astype(jnp.bfloat16)
            part = jnp.where(causal, 0.0, part)
        weights[tiles[item], columns[head]] = part.astype(jnp.bfloat16)

    def put(head, first, part):
        place = slice((first + head) * width, (first + head + 1) * width)
        out_ref[:, place] = part.astype(jnp.bfloat16).T

    def attend(head, share):
        attended = dot(turned_window(width), weights[:, columns[head]], (1, 0))
        attended = (attended * share).astype(jnp.bfloat16)
        put(head, 0, attended)
        products = attended.astype(jnp.float32) * cotangents_turned[head].astype(jnp.float32)
        return jnp.sum(products, axis=0, keepdims=True)

    def weigh_grad(head, item, row_delta):
        grad = dot(key_tile(item, width), cotangents_turned[head], (1, 0)) - row_delta
        part = weights[tiles[item], columns[head]].astype(jnp.float32)
        part = (part * grad).astype(jnp.bfloat16)
        grad_weights[tiles[item], columns[head]] = part

    def make_query_grad(head, share):
        query_grad = dot(turned_window(0), grad_weights[:, columns[head]], (1, 0))
        put(head, 2, query_grad * (share * SCORE_SCALE))

    def scaled(parts, shares):
        scaled_parts = []
        for part, share in zip(parts, shares):
            down = jnp.broadcast_to(share, (8, TILE)).T[:, :1]
            scaled_parts.append((part.astype(jnp.float32) * down).astype(jnp.bfloat16))
        return jnp.concatenate(scaled_parts, axis=0)

    for item in range(TILES):
        score(0, item)
    for item in range(TILES):
        score(1, item)
        weigh(0, item)
    shares = [1.0 / totals[0]]
    deltas = [attend(0, shares[0])]
    for item in range(TILES):
        weigh(1, item)
    shares.append(1.0 / totals[1])
    deltas.append(attend(1, shares[1]))
    cotangents_scaled = scaled(cotangents, shares)
    queries_scaled = scaled(queries, shares)
    for item in range(SPAN):
        add(item, width, dot(weights[tiles[item]], cotangents_scaled, (1, 0)))
    for item in range(SPAN):
        weigh_grad(0, item, deltas[0])
        weigh_grad(1, item, deltas[1])
        add(item, 0, dot(grad_weights[tiles[item]], queries_scaled, (1, 0)))
    make_query_grad(0, shares[0])
    make_query_grad(1, shares[1])

    @pl.when(step == TILES - 1)
    def _():
        for item, distance in enumerate(BACK_DISTANCES):
            half, part, chunk = item // HALF, item % HALF, member ^ distance
            for halves, place in ((earlier_grads, chunk), (own_grads, MEMBERS + chunk)):
                target = halves[half]
                target[part, :, :width] = (sums[place, :, :width] * SCORE_SCALE).astype(
                    jnp.bfloat16
                )
                target[part, :, width:] = sums[place, :, width:].astype(jnp.bfloat16)


def attention(doc_lengths, rows, own, earlier):
    width = HEAD_WIDTH
    products = 6 * 2 * WINDOW_LENGTH * 2 * KEYS * width
    half = jax.ShapeDtypeStruct((HALF, ROWS, 2 * width), jnp.bfloat16)
    rows_block = pl.BlockSpec((TILE, 4 * width), lambda i: (i, 0))
    half_block = pl.BlockSpec(half.shape, lambda i: (0, 0, 0))
    outputs = pl.pallas_call(
        attention_kernel,
        grid=(TILES,),
        in_specs=[SCALARS, rows_block] + [half_block] * 4,
        out_specs=[rows_block] + [half_block] * 4,
        out_shape=[jax.ShapeDtypeStruct(rows.shape, jnp.bfloat16)] + [half] * 4,
        scratch_shapes=[
            pltpu.VMEM((2 * MEMBERS, ROWS, 2 * width), jnp.bfloat16),
            pltpu.VMEM((2 * width, 2 * WINDOW_LENGTH), jnp.bfloat16),
            pltpu.VMEM((2 * MEMBERS, ROWS, 2 * width), jnp.float32),
            pltpu.VMEM((KEYS, COLUMNS), jnp.bfloat16),
            pltpu.VMEM((KEYS, COLUMNS), jnp.bfloat16),
        ]
        + [pltpu.VMEM((TILES, TILE, TILE), jnp.float32)] * 2,
        compiler_params=LIMIT,
        cost_estimate=pl.CostEstimate(
            flops=2 * products, bytes_accessed=WINDOW_LENGTH * width * 30, transcendentals=0
        ),
    )(doc_lengths, rows, *own, *earlier)
    return outputs[0], outputs[1:3], outputs[3:]


def by_head(block):
    return block.reshape(ROWS, MEMBERS, block.shape[1] // MEMBERS).transpose(1, 0, 2)


def by_token(blocks):
    return blocks.transpose(1, 0, 2).reshape(ROWS, MEMBERS * blocks.shape[2])


def exchanged(blocks):
    return lax.all_to_all(blocks, "member", split_axis=0, concat_axis=0, tiled=True)


def swapped(pieces, distances):
    moved = []
    for piece, distance in zip(pieces, distances):
        route = [(i, i ^ distance) for i in range(MEMBERS)]
        moved.append(lax.ppermute(piece, "member", route) if distance else piece)
    return moved


def onward(block, direction):
    lower = [(i, i + 1) for i in range(lax.axis_size("stretch") - 1)]
    route = lower if direction > 0 else [(j, i) for i, j in lower]
    return lax.ppermute(block, "stretch", route)


def shards(rotated_query_rows, rotated_key_rows, value_matrix, output_gradient, doc_lengths):
    heavy, light = DISTANCES[:HALF], DISTANCES[HALF:]
    pieces = pack(rotated_key_rows, value_matrix, heavy)
    pieces, rotated_key_rows, value_matrix = lax.optimization_barrier(
        (pieces, rotated_key_rows, value_matrix)
    )
    pieces = swapped(pieces, heavy)
    pieces += swapped(pack(rotated_key_rows, value_matrix, light), light)
    rows = jnp.concatenate([by_head(rotated_query_rows), by_head(output_gradient)], axis=2)
    pieces, rows = lax.optimization_barrier((pieces, rows))
    own = [jnp.stack(pieces[:HALF]), jnp.stack(pieces[HALF:])]
    earlier = [onward(half, 1) for half in own]
    rows = exchanged(rows).reshape(WINDOW_LENGTH, 4 * HEAD_WIDTH)
    results, own_grads, earlier_grads = attention(doc_lengths, rows, own, earlier)
    later = [onward(half, -1) for half in earlier_grads]
    results = exchanged(results.reshape(MEMBERS, ROWS, 4 * HEAD_WIDTH))
    attended = by_token(results[:, :, : 2 * HEAD_WIDTH])
    query_grad = by_token(results[:, :, 2 * HEAD_WIDTH :])
    sums = [
        (own_grads[half].astype(jnp.float32) + later[half].astype(jnp.float32)).astype(
            jnp.bfloat16
        )
        for half in range(2)
    ]
    pieces = [sums[item // HALF][item % HALF] for item in range(MEMBERS)]
    pieces = swapped(pieces, BACK_DISTANCES)
    attended, query_grad, pieces = lax.optimization_barrier((attended, query_grad, pieces))
    return (attended, query_grad, *unpack(pieces))


def solution(mesh):
    grouped = Mesh(mesh.devices.reshape(-1, MEMBERS), ("stretch", "member"))
    spread = P(("stretch", "member"), None)
    return jax.shard_map(
        shards,
        mesh=grouped,
        in_specs=(spread, spread, spread, spread, P()),
        out_specs=(spread, spread, spread, spread),
        check_vma=False,
    )
```

```python
import functools

import jax
import jax.numpy as jnp
from jax import lax
from jax.experimental import pallas as pl
from jax.experimental.pallas import tpu as pltpu
from jax.sharding import Mesh
from jax.sharding import PartitionSpec as P

HEAD_WIDTH = 256
WINDOW_LENGTH = 1024
MEMBERS = 8
HALF = MEMBERS // 2
DISTANCES = (7, 6, 5, 4, 3, 2, 1, 0)
BACK_DISTANCES = (7, 6, 5, 4, 0, 1, 2, 3)

TILE = 256
TILES = WINDOW_LENGTH // TILE
SPAN = TILES + 1
KEYS = SPAN * TILE
ROWS = WINDOW_LENGTH // MEMBERS
CHUNKS = TILE // ROWS
COLUMNS = 2 * TILE
SCORE_SCALE = HEAD_WIDTH ** (-0.5)
LOG2_E = 1.4426950408889634

IN_HBM = pl.BlockSpec(memory_space=pltpu.HBM)
SCALARS = pl.BlockSpec(memory_space=pltpu.SMEM)
SMALL_LIMIT = pltpu.CompilerParams(vmem_limit_bytes=4 * 1024 * 1024)
WHOLE_LIMIT = pltpu.CompilerParams(vmem_limit_bytes=64 * 1024 * 1024)
LIMIT = pltpu.CompilerParams(vmem_limit_bytes=62 * 1024 * 1024)


def dot(left, right, contract):
    return lax.dot_general(
        left, right, ((contract[:1], contract[1:]), ((), ())), preferred_element_type=jnp.float32
    )


def copies_of(pairs, semaphores):
    return [
        pltpu.make_async_copy(source, target, semaphores.at[item])
        for item, (source, target) in enumerate(pairs)
    ]


def columns_of(ref, head, width):
    return ref.at[:, pl.ds(pl.multiple_of(head * width, width), width)]


def staged(arriving, leaving):
    for copies in arriving:
        for copy in copies:
            copy.start()
    for copies, onward in zip(arriving, leaving):
        for copy in copies:
            copy.wait()
        for copy in onward:
            copy.start()
    for onward in leaving:
        for copy in onward:
            copy.wait()


def pack_kernel(distances, left_ref, right_ref, *refs):
    pieces, (buffer, arrived, sent) = refs[:HALF], refs[HALF:]
    member = lax.axis_index("member")
    width = left_ref.shape[1] // MEMBERS
    arriving, leaving = [], []
    for item, distance in enumerate(distances):
        head = member ^ distance
        pairs = [
            (columns_of(left_ref, head, width), buffer.at[item, :, pl.ds(0, width)]),
            (columns_of(right_ref, head, width), buffer.at[item, :, pl.ds(width, width)]),
        ]
        arriving.append(copies_of(pairs, arrived.at[item]))
        leaving.append([pltpu.make_async_copy(buffer.at[item], pieces[item], sent.at[item])])
    staged(arriving, leaving)


def pack(left, right, distances):
    rows, columns = left.shape
    shape = (rows, 2 * columns // MEMBERS)
    return pl.pallas_call(
        functools.partial(pack_kernel, distances),
        in_specs=[IN_HBM] * 2,
        out_specs=[IN_HBM] * HALF,
        out_shape=[jax.ShapeDtypeStruct(shape, left.dtype)] * HALF,
        scratch_shapes=[
            pltpu.VMEM((HALF, *shape), left.dtype),
            pltpu.SemaphoreType.DMA((HALF, 2)),
            pltpu.SemaphoreType.DMA((HALF,)),
        ],
        compiler_params=WHOLE_LIMIT,
        cost_estimate=pl.CostEstimate(
            flops=0, bytes_accessed=4 * rows * columns, transcendentals=0
        ),
    )(left, right)


def unpack_kernel(*refs):
    pieces, (left_ref, right_ref, sent) = refs[:MEMBERS], refs[MEMBERS:]
    member = lax.axis_index("member")
    width = left_ref.shape[1] // MEMBERS
    copies = []
    for item, distance in enumerate(BACK_DISTANCES):
        head = member ^ distance
        pairs = [
            (pieces[item].at[:, pl.ds(0, width)], columns_of(left_ref, head, width)),
            (pieces[item].at[:, pl.ds(width, width)], columns_of(right_ref, head, width)),
        ]
        copies += copies_of(pairs, sent.at[item])
    for copy in copies:
        copy.start()
    for copy in copies:
        copy.wait()


def unpack(pieces):
    rows, columns = pieces[0].shape
    whole = jax.ShapeDtypeStruct((rows, MEMBERS * columns // 2), pieces[0].dtype)
    return pl.pallas_call(
        unpack_kernel,
        in_specs=[pl.BlockSpec(memory_space=pltpu.VMEM)] * MEMBERS,
        out_specs=[IN_HBM] * 2,
        out_shape=[whole] * 2,
        scratch_shapes=[pltpu.SemaphoreType.DMA((MEMBERS, 2))],
        compiler_params=SMALL_LIMIT,
        cost_estimate=pl.CostEstimate(
            flops=0, bytes_accessed=4 * MEMBERS * rows * columns, transcendentals=0
        ),
    )(*pieces)


def attention_kernel(lengths_ref, rows_ref, *refs):
    own_halves, earlier_halves, out_ref, refs = refs[:2], refs[2:4], refs[4], refs[5:]
    own_grads, earlier_grads, refs = refs[:2], refs[2:4], refs[4:]
    kv, kv_turned, sums, weights, grad_weights, refs = *refs[:5], refs[5:]
    scores = refs
    step = pl.program_id(0)
    width = HEAD_WIDTH
    member = lax.axis_index("member")

    def turn(tile):
        part = kv[pl.ds(tile * CHUNKS, CHUNKS)].reshape(TILE, 2 * width)
        kv_turned[:, pl.ds(pl.multiple_of(tile * TILE, TILE), TILE)] = part.T

    @pl.when(step == 0)
    def _():
        for item, distance in enumerate(DISTANCES):
            half, part, chunk = item // HALF, item % HALF, member ^ distance
            kv[chunk] = earlier_halves[half][part]
            kv[MEMBERS + chunk] = own_halves[half][part]
        sums[:MEMBERS] = jnp.zeros((MEMBERS, ROWS, 2 * width), jnp.float32)
        for tile in range(TILES):
            turn(tile)

    turn(TILES + step)

    def key_tile(item, first):
        tile = pl.ds((step + item) * CHUNKS, CHUNKS)
        return kv[tile, :, first : first + width].reshape(TILE, width)

    def turned_window(first):
        place = pl.ds(pl.multiple_of(step * TILE, TILE), KEYS)
        return kv_turned[first : first + width, place]

    def add(item, first, part):
        tile = pl.ds((step + item) * CHUNKS, CHUNKS)
        part = part.reshape(CHUNKS, ROWS, width)
        if item < TILES:
            part = sums[tile, :, first : first + width] + part
        sums[tile, :, first : first + width] = part

    queries = [rows_ref[:, head * width : (head + 1) * width] for head in range(2)]
    cotangents = [rows_ref[:, (2 + head) * width : (3 + head) * width] for head in range(2)]
    queries_turned = [part.T for part in queries]
    cotangents_turned = [part.T for part in cotangents]
    columns = [slice(head * TILE, (head + 1) * TILE) for head in range(2)]
    tiles = [slice(item * TILE, (item + 1) * TILE) for item in range(SPAN)]

    first_row = lax.axis_index("stretch") * WINDOW_LENGTH + step * TILE
    row = lax.broadcasted_iota(jnp.int32, (1, TILE), 1)
    oldest = row - (WINDOW_LENGTH - 1)

    def passed(item, carried):
        begin, oldest = carried
        near = begin - first_row
        oldest = jnp.where(near <= row, jnp.maximum(oldest, near), oldest)
        return begin + lengths_ref[item], oldest

    _, oldest = lax.fori_loop(0, lengths_ref.shape[0], passed, (jnp.int32(0), oldest))
    key_row = lax.broadcasted_iota(jnp.int32, (TILE, TILE), 0)

    tops = [jnp.full((1, TILE), -jnp.inf, jnp.float32)] * 2
    totals = [jnp.zeros((1, TILE), jnp.float32)] * 2

    causal = key_row <= row
    edge_oldest = jnp.where(causal, oldest, oldest + WINDOW_LENGTH)

    def score(head, item):
        part = dot(key_tile(item, 0), queries_turned[head], (1, 0))
        if item:
            seen = key_row >= oldest - (item - TILES) * TILE
        else:
            last = dot(key_tile(TILES, 0), queries_turned[head], (1, 0))
            part = jnp.where(causal, last, part)
            seen = key_row >= edge_oldest
        part = jnp.where(seen, part, -jnp.inf)
        tops[head] = jnp.maximum(tops[head], jnp.max(part, axis=0, keepdims=True))
        scores[head][item] = part

    def weigh(head, item):
        part = jnp.exp2((scores[head][item] - tops[head]) * (SCORE_SCALE * LOG2_E))
        totals[head] = totals[head] + jnp.sum(part, axis=0, keepdims=True)
        if item == 0:
            last = jnp.where(causal, part, 0.0)
            weights[tiles[TILES], columns[head]] = last.astype(jnp.bfloat16)
            part = jnp.where(causal, 0.0, part)
        weights[tiles[item], columns[head]] = part.astype(jnp.bfloat16)

    def put(head, first, part):
        place = slice((first + head) * width, (first + head + 1) * width)
        out_ref[:, place] = part.astype(jnp.bfloat16).T

    def attend(head, share):
        attended = dot(turned_window(width), weights[:, columns[head]], (1, 0))
        attended = (attended * share).astype(jnp.bfloat16)
        put(head, 0, attended)
        products = attended.astype(jnp.float32) * cotangents_turned[head].astype(jnp.float32)
        return jnp.sum(products, axis=0, keepdims=True)

    def weigh_grad(head, item, row_delta):
        grad = dot(key_tile(item, width), cotangents_turned[head], (1, 0)) - row_delta
        part = weights[tiles[item], columns[head]].astype(jnp.float32)
        part = (part * grad).astype(jnp.bfloat16)
        grad_weights[tiles[item], columns[head]] = part

    def make_query_grad(head, share):
        query_grad = dot(turned_window(0), grad_weights[:, columns[head]], (1, 0))
        put(head, 2, query_grad * (share * SCORE_SCALE))

    def scaled(parts, shares):
        scaled_parts = []
        for part, share in zip(parts, shares):
            down = jnp.broadcast_to(share, (8, TILE)).T[:, :1]
            scaled_parts.append((part.astype(jnp.float32) * down).astype(jnp.bfloat16))
        return jnp.concatenate(scaled_parts, axis=0)

    for item in range(TILES):
        score(0, item)
    for item in range(TILES):
        score(1, item)
        weigh(0, item)
    shares = [1.0 / totals[0]]
    deltas = [attend(0, shares[0])]
    for item in range(TILES):
        weigh(1, item)
    shares.append(1.0 / totals[1])
    deltas.append(attend(1, shares[1]))
    cotangents_scaled = scaled(cotangents, shares)
    queries_scaled = scaled(queries, [share * SCORE_SCALE for share in shares])
    for item in range(SPAN):
        weigh_grad(0, item, deltas[0])
        weigh_grad(1, item, deltas[1])
        add(item, width, dot(weights[tiles[item]], cotangents_scaled, (1, 0)))
        add(item, 0, dot(grad_weights[tiles[item]], queries_scaled, (1, 0)))
    make_query_grad(0, shares[0])
    make_query_grad(1, shares[1])

    @pl.when(step == TILES - 1)
    def _():
        for item, distance in enumerate(BACK_DISTANCES):
            half, part, chunk = item // HALF, item % HALF, member ^ distance
            for halves, place in ((earlier_grads, chunk), (own_grads, MEMBERS + chunk)):
                target = halves[half]
                target[part] = sums[place].astype(jnp.bfloat16)


def attention(doc_lengths, rows, own, earlier):
    width = HEAD_WIDTH
    products = 6 * 2 * WINDOW_LENGTH * 2 * KEYS * width
    half = jax.ShapeDtypeStruct((HALF, ROWS, 2 * width), jnp.bfloat16)
    rows_block = pl.BlockSpec((TILE, 4 * width), lambda i: (i, 0))
    half_block = pl.BlockSpec(half.shape, lambda i: (0, 0, 0))
    outputs = pl.pallas_call(
        attention_kernel,
        grid=(TILES,),
        in_specs=[SCALARS, rows_block] + [half_block] * 4,
        out_specs=[rows_block] + [half_block] * 4,
        out_shape=[jax.ShapeDtypeStruct(rows.shape, jnp.bfloat16)] + [half] * 4,
        scratch_shapes=[
            pltpu.VMEM((2 * MEMBERS, ROWS, 2 * width), jnp.bfloat16),
            pltpu.VMEM((2 * width, 2 * WINDOW_LENGTH), jnp.bfloat16),
            pltpu.VMEM((2 * MEMBERS, ROWS, 2 * width), jnp.float32),
            pltpu.VMEM((KEYS, COLUMNS), jnp.bfloat16),
            pltpu.VMEM((KEYS, COLUMNS), jnp.bfloat16),
        ]
        + [pltpu.VMEM((TILES, TILE, TILE), jnp.float32)] * 2,
        compiler_params=LIMIT,
        cost_estimate=pl.CostEstimate(
            flops=2 * products, bytes_accessed=WINDOW_LENGTH * width * 30, transcendentals=0
        ),
    )(doc_lengths, rows, *own, *earlier)
    return outputs[0], outputs[1:3], outputs[3:]


def by_head(block):
    return block.reshape(ROWS, MEMBERS, block.shape[1] // MEMBERS).transpose(1, 0, 2)


def by_token(blocks):
    return blocks.transpose(1, 0, 2).reshape(ROWS, MEMBERS * blocks.shape[2])


def exchanged(blocks):
    return lax.all_to_all(blocks, "member", split_axis=0, concat_axis=0, tiled=True)


def swapped(pieces, distances):
    moved = []
    for piece, distance in zip(pieces, distances):
        route = [(i, i ^ distance) for i in range(MEMBERS)]
        moved.append(lax.ppermute(piece, "member", route) if distance else piece)
    return moved


def onward(block, direction):
    lower = [(i, i + 1) for i in range(lax.axis_size("stretch") - 1)]
    route = lower if direction > 0 else [(j, i) for i, j in lower]
    return lax.ppermute(block, "stretch", route)


def shards(rotated_query_rows, rotated_key_rows, value_matrix, output_gradient, doc_lengths):
    heavy, light = DISTANCES[:HALF], DISTANCES[HALF:]
    pieces = pack(rotated_key_rows, value_matrix, heavy)
    pieces, rotated_key_rows, value_matrix = lax.optimization_barrier(
        (pieces, rotated_key_rows, value_matrix)
    )
    pieces = swapped(pieces, heavy)
    pieces += swapped(pack(rotated_key_rows, value_matrix, light), light)
    rows = jnp.concatenate([by_head(rotated_query_rows), by_head(output_gradient)], axis=2)
    pieces, rows = lax.optimization_barrier((pieces, rows))
    own = [jnp.stack(pieces[:HALF]), jnp.stack(pieces[HALF:])]
    earlier = [onward(half, 1) for half in own]
    rows = exchanged(rows).reshape(WINDOW_LENGTH, 4 * HEAD_WIDTH)
    results, own_grads, earlier_grads = attention(doc_lengths, rows, own, earlier)
    later = [onward(half, -1) for half in earlier_grads]
    results = exchanged(results.reshape(MEMBERS, ROWS, 4 * HEAD_WIDTH))
    attended = by_token(results[:, :, : 2 * HEAD_WIDTH])
    query_grad = by_token(results[:, :, 2 * HEAD_WIDTH :])
    sums = [
        (own_grads[half].astype(jnp.float32) + later[half].astype(jnp.float32)).astype(
            jnp.bfloat16
        )
        for half in range(2)
    ]
    pieces = [sums[item // HALF][item % HALF] for item in range(MEMBERS)]
    pieces = swapped(pieces, BACK_DISTANCES)
    attended, query_grad, pieces = lax.optimization_barrier((attended, query_grad, pieces))
    return (attended, query_grad, *unpack(pieces))


def solution(mesh):
    grouped = Mesh(mesh.devices.reshape(-1, MEMBERS), ("stretch", "member"))
    spread = P(("stretch", "member"), None)
    return jax.shard_map(
        shards,
        mesh=grouped,
        in_specs=(spread, spread, spread, spread, P()),
        out_specs=(spread, spread, spread, spread),
        check_vma=False,
    )
```
